32 devices in a mesh: blk: 8 (over y, x, core), grp: 4 (over z).
Axes of the slice: x: 2, y: 2, z: 4, core: 2. Of those that a mesh axis runs over, the one named last changes fastest.
Arguments:
- a_tiles: bfloat16 [256, 64, 1024], P(('blk', 'grp')), may hold values from -0.75 to 0.75
- a_cols: int32 [256, 16], P(('blk', 'grp')), may hold values from 0 to 255, as said below
- p_tiles: bfloat16 [256, 64, 256], P(('blk', 'grp')), may hold values from -0.75 to 0.75
- route_list: int32 [256, 256], P(('blk', 'grp')), may hold values from 0 to 255, as said below
- out_slot: int32 [32, 256], P(('blk', 'grp')), may hold values from 0 to 127, as said below
Outputs:
- coarse_blocks: float32 [4096, 4096], P(('blk', 'grp'))
The draws below stay inside these ranges and needn't reach their ends.
Inputs may be any that keep to these rules, and one draw needn't show every extreme that they name: `a_cols`: fine block row f is held by device f // 8 of blk+grp. Every entry in the rows of one device names a fine block row held by a device with the same grp index, and among the 128 entries of one device's rows exactly 16 name rows held by each blk index. `route_list`: A value o * 64 + p sends the partial block to send position p for the device with grp index o and the same blk index. For each device and each o, no position at or above a count is used, the count being at least 16, and 64 for one o of each device. `out_slot`: entry o * 64 + p of row d is the output block, among the 128 of the device with grp index o and the blk index of device d, into which send position p of device d adds; each output block index stands exactly 4 * 64 // 128 times in a row.
All inputs are finite; a program needn't handle non-finite values.
Results may differ from the reference program's by a relative error of at most 0.0029.
Values may be sent and summed in bfloat16 or wider, within the bound.
No kernel may reach another device: no remote copies, remote signals or barrier semaphores. Data moves between devices by JAX's collectives and lax.ppermute only.
A program may use at most 128 MiB of HBM per device.

```python
import jax
import jax.numpy as jnp
from jax import lax

TILE = 64
RF = 8
KA = 16
KP = 4
CAP = 64
OSLOT = 128
NF = 256
N_BLK = 8
N_GRP = 4


def draw_a_cols(key, part):
    base = jax.random.fold_in(key, 101)
    tile_count = RF * KA
    per_peer = tile_count // N_BLK

    def per_device(device):
        device_key = jax.random.fold_in(base, device)
        key_perm, key_row = jax.random.split(device_key)
        ranks = jax.random.permutation(key_perm, tile_count)
        peer_index = ranks // per_peer
        row_index = jax.random.randint(key_row, (tile_count,), 0, RF)
        row_index = jnp.where(ranks == tile_count - 1, RF - 1, jnp.where(ranks == 0, 0, row_index))
        group_index = device % N_GRP
        return ((peer_index * N_GRP + group_index) * RF + row_index).astype(jnp.int32)
    spread = jax.vmap(per_device)(jnp.arange(N_BLK * N_GRP, dtype=jnp.int32))
    return spread.reshape(N_BLK * N_GRP * RF, KA)


def draw_route_list(key, part):
    base = jax.random.fold_in(key, 202)
    part_count = RF * KP * KA * KP
    shift_key = jax.random.fold_in(base, 7)
    shift = jax.random.randint(shift_key, (), 0, N_GRP)
    lowest = max(1, CAP // 4)

    def per_device(device):
        device_key = jax.random.fold_in(base, device + 1000)
        key_count, key_owner, key_pos, key_pick = jax.random.split(device_key, 4)
        counts = jax.random.randint(key_count, (N_GRP,), lowest, CAP + 1)
        fullest = (device + shift) % N_GRP
        counts = jnp.where(jnp.arange(N_GRP) == fullest, CAP, counts)
        owners = jax.random.randint(key_owner, (part_count,), 0, N_GRP)
        positions = jax.random.randint(key_pos, (part_count,), 0, counts[owners])
        chosen = jax.random.randint(key_pick, (), 0, part_count)
        other = (chosen + 1) % part_count
        places = jnp.arange(part_count)
        values = owners * CAP + positions
        values = jnp.where(places == chosen, fullest * CAP + CAP - 1, values)
        values = jnp.where(places == other, 0, values)
        return values.astype(jnp.int32)
    spread = jax.vmap(per_device)(jnp.arange(N_BLK * N_GRP, dtype=jnp.int32))
    return spread.reshape(N_BLK * N_GRP * RF, KP * KA * KP)


def draw_out_slot(key, part):
    base = jax.random.fold_in(key, 303)

    def per_device(device):
        device_key = jax.random.fold_in(base, device)
        ranks = jax.random.permutation(device_key, N_GRP * CAP)
        return (ranks % OSLOT).astype(jnp.int32)
    return jax.vmap(per_device)(jnp.arange(N_BLK * N_GRP, dtype=jnp.int32))


def steps_of(key, extent, pieces, smallest, high):
    def one(position, shards_of):
        heights = jax.random.uniform(jax.random.fold_in(jax.random.fold_in(key, 6), position), (shards_of,), jnp.float32, smallest / len(pieces), high / len(pieces))
        return jnp.repeat(jnp.exp(heights), extent[position] // shards_of).reshape((-1,) + (1,) * (len(extent) - position - 1))

    loudness = one(*pieces[0])
    for cut in pieces[1:]:
        loudness = loudness * one(*cut)
    return loudness


def gaussian(rng, extent, scale, most, pieces=(), held_as=jnp.bfloat16):
    gain = steps_of(rng, extent, pieces, -0.22, 0.18) if pieces else 1.0
    values = jax.random.normal(rng, extent, jnp.float32) * scale * gain
    return jnp.minimum(jnp.maximum(values, -most), most).astype(held_as)


def setup_inputs(seed: int = 0) -> dict:
    seeds = jax.random.split(jax.random.key(seed), 6)
    a_tiles = gaussian(seeds[0], (NF, TILE, KA * TILE), TILE ** -0.5, 0.75, ((0, 32),))
    a_cols = draw_a_cols(jax.random.fold_in(seeds[5], 71), 0)
    p_tiles = gaussian(seeds[2], (NF, TILE, KP * TILE), TILE ** -0.5, 0.75, ((0, 32),))
    route_list = draw_route_list(jax.random.fold_in(seeds[5], 71), 0)
    out_slot = draw_out_slot(jax.random.fold_in(seeds[5], 71), 0)
    return {"a_tiles": a_tiles, "a_cols": a_cols, "p_tiles": p_tiles, "route_list": route_list, "out_slot": out_slot}


def reference(a_tiles, a_cols, p_tiles, route_list, out_slot):
    devices = N_BLK * N_GRP
    a_blocks = a_tiles.reshape(devices * RF, TILE, KA, TILE)

    def device_step(current, device):
        first_row = (device * RF).astype(jnp.int32)
        row_tiles = lax.dynamic_slice_in_dim(a_blocks, first_row, RF, 0)
        col_lists = lax.dynamic_slice_in_dim(a_cols, first_row, RF, 0)
        panel = jnp.take(p_tiles, col_lists.reshape(-1), axis=0).reshape(RF, KA, TILE, KP * TILE)
        product = jnp.einsum("rtks,rkso->rkto", row_tiles.astype(jnp.float32), panel.astype(jnp.float32)).astype(jnp.bfloat16)
        own_rows = lax.dynamic_slice_in_dim(p_tiles, first_row, RF, 0).reshape(RF, TILE, KP, TILE)
        y_five = product.reshape(RF, KA, TILE, KP, TILE)
        partials = jnp.einsum("irsc,ikrqd->iskqcd", own_rows.astype(jnp.float32), y_five.astype(jnp.float32))
        partials = partials.reshape(RF * KP * KA * KP, TILE * TILE)
        destination = lax.dynamic_slice_in_dim(route_list, first_row, RF, 0).reshape(-1)
        slot_row = lax.dynamic_index_in_dim(out_slot, device, 0, keepdims=False)
        segment = ((device // N_GRP) * N_GRP + destination // CAP) * OSLOT + jnp.take(slot_row, destination)
        return current.at[segment.astype(jnp.int32)].add(partials), None

    initial = jnp.zeros((devices * OSLOT, TILE * TILE), jnp.float32)
    summed, _ = lax.scan(device_step, initial, jnp.arange(devices, dtype=jnp.int32))
    return summed
```

```python
import functools

import jax
import jax.numpy as jnp
from jax import lax
from jax.experimental import pallas as pl
from jax.experimental.pallas import tpu as pltpu
from jax.sharding import PartitionSpec as P

OSLOT = 128
LANES = 128
ACCS = 4


def partial_kernel(idx_ref, route_ref, a_ref, lhs_ref, panel_ref, out_ref, *accs):
    row = pl.program_id(0)
    tile = a_ref.shape[1]
    tiles = a_ref.shape[2] // tile
    width = panel_ref.shape[2] // tile
    sub = tile * tile // LANES
    positions = out_ref.shape[0] // sub
    chunk = 256

    @pl.when(row == 0)
    def _():
        def clear(c, carry):
            rows = pl.ds(pl.multiple_of(c * chunk, chunk), chunk)
            for acc in accs:
                acc[rows, :] = jnp.zeros((chunk, LANES), jnp.float32)
            return carry

        lax.fori_loop(0, positions * sub // chunk, clear, 0)

    lo = lax.broadcasted_iota(jnp.int32, (tile, LANES), 1) < tile
    lhs = lhs_ref[0]
    for pair in range(tiles // 2):
        both = a_ref[0, :, pair * LANES:(pair + 1) * LANES]
        none = jnp.zeros_like(both)
        left = jnp.concatenate([jnp.where(lo, both, none), jnp.where(lo, none, both)], axis=0)
        first = row * tiles + pair * 2
        right = jnp.concatenate([panel_ref[idx_ref[first]], panel_ref[idx_ref[first + 1]]], axis=0)
        y = jnp.dot(left, right, preferred_element_type=jnp.float32)
        for half in range(2):
            k = pair * 2 + half
            blocks = []
            for m in range(width // 2):
                x = y[half * tile:(half + 1) * tile, m * LANES:(m + 1) * LANES]
                xr = pltpu.roll(x, tile, 1)
                zero = jnp.zeros_like(x)
                for u, v in ((x, xr), (xr, x)):
                    blocks.append(
                        jnp.concatenate([jnp.where(lo, u, zero), jnp.where(lo, zero, v)], axis=0).astype(jnp.bfloat16)
                    )
            w = jnp.dot(lhs, jnp.concatenate(blocks, axis=1), preferred_element_type=jnp.float32)
            for s in range(width):
                for q in range(width):
                    acc = accs[(s * width + q) % len(accs)]
                    place = route_ref[row * (width * tiles * width) + (s * tiles + k) * width + q]
                    rows = pl.ds(pl.multiple_of(place * sub, sub), sub)
                    acc[rows, :] += w[s * sub:(s + 1) * sub, q * LANES:(q + 1) * LANES]

    @pl.when(row == pl.num_programs(0) - 1)
    def _():
        def merge(c, carry):
            rows = pl.ds(pl.multiple_of(c * chunk, chunk), chunk)
            total = accs[0][rows, :]
            for acc in accs[1:]:
                total = total + acc[rows, :]
            out_ref[rows, :] = total.astype(out_ref.dtype)
            return carry

        lax.fori_loop(0, positions * sub // chunk, merge, 0)


def partial_sums(idx, route, a_tiles, lhs, panel, positions):
    rf, tile, cols = a_tiles.shape
    sub = tile * tile // LANES
    out_rows = positions * sub
    return pl.pallas_call(
        partial_kernel,
        out_shape=jax.ShapeDtypeStruct((out_rows, LANES), jnp.bfloat16),
        grid_spec=pltpu.PrefetchScalarGridSpec(
            num_scalar_prefetch=2,
            grid=(rf,),
            in_specs=[
                pl.BlockSpec((1, tile, cols), lambda i, *_: (i, 0, 0)),
                pl.BlockSpec((1,) + lhs.shape[1:], lambda i, *_: (i, 0, 0)),
                pl.BlockSpec(panel.shape, lambda i, *_: (0, 0, 0), pipeline_mode=pl.Buffered(1)),
            ],
            out_specs=pl.BlockSpec((out_rows, LANES), lambda i, *_: (0, 0)),
            scratch_shapes=[pltpu.VMEM((out_rows, LANES), jnp.float32)] * ACCS,
        ),
        compiler_params=pltpu.CompilerParams(
            dimension_semantics=("arbitrary",), vmem_limit_bytes=56 * 1024 * 1024
        ),
        name="partial_sums",
    )(idx, route, a_tiles, lhs, panel)


def owner_kernel(slot_ref, in_ref, out_ref, *accs):
    sub = out_ref.shape[1] // LANES
    arrivals = in_ref.shape[0] // sub
    chunk = 256
    n_out = out_ref.shape[0]

    def clear(c, carry):
        rows = pl.ds(pl.multiple_of(c * chunk, chunk), chunk)
        for acc in accs:
            acc[rows, :] = jnp.zeros((chunk, LANES), jnp.float32)
        return carry

    lax.fori_loop(0, n_out * sub // chunk, clear, 0)
    step = 8

    def add(c, carry):
        for u in range(step):
            n = c * step + u
            src = pl.ds(pl.multiple_of(n * sub, sub), sub)
            dst = pl.ds(pl.multiple_of(slot_ref[n] * sub, sub), sub)
            accs[u % len(accs)][dst, :] += in_ref[src, :].astype(jnp.float32)
        return carry

    lax.fori_loop(0, arrivals // step, add, 0)

    def emit(c, carry):
        rows = pl.ds(pl.multiple_of(c * 8, 8), 8)
        for t in range(sub):
            total = None
            for acc in accs:
                piece = acc[pl.ds(c * 8 * sub + t, 8, stride=sub), :]
                total = piece if total is None else total + piece
            out_ref[rows, t * LANES:(t + 1) * LANES] = total
        return carry

    lax.fori_loop(0, n_out // 8, emit, 0)


def owner_sums(slots, arrived, sub):
    return pl.pallas_call(
        owner_kernel,
        out_shape=jax.ShapeDtypeStruct((OSLOT, sub * LANES), jnp.float32),
        grid_spec=pltpu.PrefetchScalarGridSpec(
            num_scalar_prefetch=1,
            grid=(1,),
            in_specs=[pl.BlockSpec(arrived.shape, lambda i, *_: (0, 0))],
            out_specs=pl.BlockSpec((OSLOT, sub * LANES), lambda i, *_: (0, 0)),
            scratch_shapes=[pltpu.VMEM((OSLOT * sub, LANES), jnp.float32)] * 2,
        ),
        compiler_params=pltpu.CompilerParams(
            dimension_semantics=("arbitrary",), vmem_limit_bytes=40 * 1024 * 1024
        ),
        name="owner_sums",
    )(slots, arrived)


def body(a_tiles, a_cols, p_tiles, route_list, out_slot):
    groups = lax.axis_size("grp")
    rf, tile, cols = a_tiles.shape
    positions = out_slot.shape[1]
    sub = tile * tile // LANES
    flat_cols = a_cols.reshape(-1)
    panel_row = flat_cols // rf // groups * rf + flat_cols % rf
    panel = lax.all_gather(p_tiles, "blk", axis=0, tiled=True)
    lhs = jnp.swapaxes(p_tiles, 1, 2).reshape(rf, p_tiles.shape[2] // 2, 2 * tile)
    slots = lax.all_to_all(
        out_slot.reshape(groups, positions // groups), "grp", split_axis=0, concat_axis=0, tiled=True
    )
    sums = partial_sums(panel_row, route_list.reshape(-1), a_tiles, lhs, panel, positions)
    arrived = lax.all_to_all(
        sums.reshape(groups, -1, LANES), "grp", split_axis=0, concat_axis=0, tiled=True
    )
    return owner_sums(slots.reshape(-1), arrived.reshape(-1, LANES), sub)


def solution(mesh):
    in_specs = (
        P(("blk", "grp"), None, None),
        P(("blk", "grp"), None),
        P(("blk", "grp"), None, None),
        P(("blk", "grp"), None),
        P(("blk", "grp"), None),
    )
    out_specs = P(("blk", "grp"), None)
    return jax.shard_map(body, mesh=mesh, in_specs=in_specs, out_specs=out_specs, check_vma=False)
```

```python
import functools

import jax
import jax.numpy as jnp
from jax import lax
from jax.experimental import pallas as pl
from jax.experimental.pallas import tpu as pltpu
from jax.sharding import PartitionSpec as P

OSLOT = 128
LANES = 128
ACCS = 4


def partial_kernel(idx_ref, route_ref, a_ref, lhs_ref, *refs):
    n_pieces = len(refs) - ACCS - 4
    pieces, out_ref, accs = refs[:n_pieces], refs[n_pieces], refs[n_pieces + 1:n_pieces + 1 + ACCS]
    panel, y_buf, sems = refs[n_pieces + 1 + ACCS:]
    rf, tile, cols = a_ref.shape
    tiles = cols // tile
    width = panel.shape[2] // tile
    sub = tile * tile // LANES
    table_rows = out_ref.shape[0]
    chunk = 256
    slots = rf * tiles

    copies = []
    for n, piece in enumerate(pieces):
        copy = pltpu.make_async_copy(piece, panel.at[pl.ds(n * rf, rf)], sems.at[n])
        copy.start()
        copies.append(copy)

    def clear(c, carry):
        rows = pl.ds(pl.multiple_of(c * chunk, chunk), chunk)
        for acc in accs:
            acc[rows, :] = jnp.zeros((chunk, LANES), jnp.float32)
        return carry

    lax.fori_loop(0, table_rows // chunk, clear, 0)
    for copy in copies:
        copy.wait()

    lane = lax.broadcasted_iota(jnp.int32, (tile, LANES), 1)
    lo = lane < tile

    def first_step(slot, side):
        row, k = slot // tiles, slot % tiles
        both = a_ref[row, :, pl.ds(pl.multiple_of(k // 2 * LANES, LANES), LANES)]
        start = k % 2 * tile
        left = jnp.where((lane >= start) & (lane < start + tile), both, jnp.zeros_like(both))
        block = panel[idx_ref[slot]]
        right = jnp.concatenate([block, block], axis=0)
        y = jnp.dot(left, right, preferred_element_type=jnp.float32)
        for m in range(width // 2):
            x = y[:, m * LANES:(m + 1) * LANES]
            xr = pltpu.roll(x, tile, 1)
            zero = jnp.zeros_like(x)
            for h, (u, v) in enumerate(((x, xr), (xr, x))):
                at = (2 * m + h) * LANES
                y_buf[side, :tile, at:at + LANES] = jnp.where(lo, u, zero).astype(jnp.bfloat16)
                y_buf[side, tile:, at:at + LANES] = jnp.where(lo, zero, v).astype(jnp.bfloat16)

    def add(slot, w, q):
        row, k = slot // tiles, slot % tiles
        spans = []
        for s in range(width):
            place = route_ref[(row * width + s) * (tiles * width) + k * width + q]
            spans.append(pl.ds(pl.multiple_of(place * sub, sub), sub))
        old = [accs[s][spans[s], :] for s in range(width)]
        for s in range(width):
            accs[s][spans[s], :] = old[s] + w[s * sub:(s + 1) * sub]

    def second_step(slot, side, upcoming):
        row = slot // tiles
        lhs = lhs_ref[row]
        rights = [y_buf[side, :, m * 2 * LANES:(m + 1) * 2 * LANES] for m in range(width // 2)]
        first_step(upcoming, 1 - side)
        for m in range(width // 2):
            w = jnp.dot(lhs, rights[m], preferred_element_type=jnp.float32)
            for h in range(2):
                add(slot, w[:, h * LANES:(h + 1) * LANES], 2 * m + h)

    first_step(0, 0)

    def two(c, carry):
        second_step(2 * c, 0, 2 * c + 1)
        second_step(2 * c + 1, 1, jnp.minimum(2 * c + 2, slots - 1))
        return carry

    lax.fori_loop(0, slots // 2, two, 0)

    def merge(c, carry):
        rows = pl.ds(pl.multiple_of(c * chunk, chunk), chunk)
        total = accs[0][rows, :]
        for acc in accs[1:]:
            total = total + acc[rows, :]
        out_ref[rows, :] = total.astype(out_ref.dtype)
        return carry

    lax.fori_loop(0, table_rows // chunk, merge, 0)


def partial_sums(idx, route, a_tiles, lhs, pieces, positions):
    rf, tile, cols = a_tiles.shape
    sub = tile * tile // LANES
    out_rows = positions * sub
    width = pieces[0].shape[2]
    return pl.pallas_call(
        partial_kernel,
        out_shape=jax.ShapeDtypeStruct((out_rows, LANES), jnp.bfloat16),
        grid_spec=pltpu.PrefetchScalarGridSpec(
            num_scalar_prefetch=2,
            grid=(1,),
            in_specs=[
                pl.BlockSpec(a_tiles.shape, lambda i, *_: (0, 0, 0)),
                pl.BlockSpec(lhs.shape, lambda i, *_: (0, 0, 0)),
            ]
            + [pl.BlockSpec(memory_space=pl.ANY)] * len(pieces),
            out_specs=pl.BlockSpec((out_rows, LANES), lambda i, *_: (0, 0)),
            scratch_shapes=[pltpu.VMEM((out_rows, LANES), jnp.float32)] * ACCS
            + [
                pltpu.VMEM((len(pieces) * rf, tile, width), jnp.bfloat16),
                pltpu.VMEM((2, 2 * tile, 2 * width), jnp.bfloat16),
                pltpu.SemaphoreType.DMA((len(pieces),)),
            ],
        ),
        compiler_params=pltpu.CompilerParams(
            dimension_semantics=("arbitrary",), vmem_limit_bytes=56 * 1024 * 1024
        ),
        name="partial_sums",
    )(idx, route, a_tiles, lhs, *pieces)


def owner_kernel(slot_ref, in_ref, out_ref, *accs):
    sub = out_ref.shape[1] // LANES
    arrivals = in_ref.shape[0] // sub
    chunk = 256
    n_out = out_ref.shape[0]

    def clear(c, carry):
        rows = pl.ds(pl.multiple_of(c * chunk, chunk), chunk)
        for acc in accs:
            acc[rows, :] = jnp.zeros((chunk, LANES), jnp.float32)
        return carry

    lax.fori_loop(0, n_out * sub // chunk, clear, 0)
    step = 8

    def add(c, carry):
        for u in range(step):
            n = c * step + u
            src = pl.ds(pl.multiple_of(n * sub, sub), sub)
            dst = pl.ds(pl.multiple_of(slot_ref[n] * sub, sub), sub)
            accs[u % len(accs)][dst, :] += in_ref[src, :].astype(jnp.float32)
        return carry

    lax.fori_loop(0, arrivals // step, add, 0)

    def emit(c, carry):
        rows = pl.ds(pl.multiple_of(c * 8, 8), 8)
        for t in range(sub):
            total = None
            for acc in accs:
                piece = acc[pl.ds(c * 8 * sub + t, 8, stride=sub), :]
                total = piece if total is None else total + piece
            out_ref[rows, t * LANES:(t + 1) * LANES] = total
        return carry

    lax.fori_loop(0, n_out // 8, emit, 0)


def owner_sums(slots, arrived, sub):
    return pl.pallas_call(
        owner_kernel,
        out_shape=jax.ShapeDtypeStruct((OSLOT, sub * LANES), jnp.float32),
        grid_spec=pltpu.PrefetchScalarGridSpec(
            num_scalar_prefetch=1,
            grid=(1,),
            in_specs=[pl.BlockSpec(arrived.shape, lambda i, *_: (0, 0))],
            out_specs=pl.BlockSpec((OSLOT, sub * LANES), lambda i, *_: (0, 0)),
            scratch_shapes=[pltpu.VMEM((OSLOT * sub, LANES), jnp.float32)] * 2,
        ),
        compiler_params=pltpu.CompilerParams(
            dimension_semantics=("arbitrary",), vmem_limit_bytes=40 * 1024 * 1024
        ),
        name="owner_sums",
    )(slots, arrived)


def gather_pieces(p_tiles):
    size = lax.axis_size("blk")

    def swap(x, d):
        return lax.ppermute(x, "blk", [(i, i ^ d) for i in range(size)])

    pieces = [p_tiles, swap(p_tiles, 1)]
    far = [swap(p_tiles, d) for d in range(2, size, 2)]
    for x in far:
        pieces += [x, swap(x, 1)]
    return pieces


def body(a_tiles, a_cols, p_tiles, route_list, out_slot):
    groups = lax.axis_size("grp")
    rf, tile, cols = a_tiles.shape
    positions = out_slot.shape[1]
    sub = tile * tile // LANES
    flat_cols = a_cols.reshape(-1)
    holder = flat_cols // rf // groups
    panel_row = (holder ^ lax.axis_index("blk")) * rf + flat_cols % rf
    pieces = gather_pieces(p_tiles)
    lhs = jnp.swapaxes(p_tiles, 1, 2).reshape(rf, p_tiles.shape[2] // 2, 2 * tile)
    slots = lax.all_to_all(
        out_slot.reshape(groups, positions // groups), "grp", split_axis=0, concat_axis=0, tiled=True
    )
    sums = partial_sums(panel_row, route_list.reshape(-1), a_tiles, lhs, pieces, positions)
    arrived = lax.all_to_all(
        sums.reshape(groups, -1, LANES), "grp", split_axis=0, concat_axis=0, tiled=True
    )
    return owner_sums(slots.reshape(-1), arrived.reshape(-1, LANES), sub)


def solution(mesh):
    in_specs = (
        P(("blk", "grp"), None, None),
        P(("blk", "grp"), None),
        P(("blk", "grp"), None, None),
        P(("blk", "grp"), None),
        P(("blk", "grp"), None),
    )
    out_specs = P(("blk", "grp"), None)
    return jax.shard_map(body, mesh=mesh, in_specs=in_specs, out_specs=out_specs, check_vma=False)
```

```python
import functools

import jax
import jax.numpy as jnp
from jax import lax
from jax.experimental import pallas as pl
from jax.experimental.pallas import tpu as pltpu
from jax.sharding import PartitionSpec as P

OSLOT = 128
LANES = 128
ACCS = 4
BATCH = 8


def partial_kernel(n_pieces, n_outs, idx_ref, place_ref, a_ref, lhs_ref, *refs):
    pieces, refs = refs[:n_pieces], refs[n_pieces:]
    outs, refs = refs[:n_outs], refs[n_outs:]
    accs, (panel, y_buf, sems) = refs[:ACCS], refs[ACCS:]
    rf, tile, cols = a_ref.shape
    tiles = cols // tile
    width = panel.shape[2] // tile
    sub = tile * tile // LANES
    out_rows = outs[0].shape[0]
    table_rows = n_outs * out_rows
    chunk = 256
    slots = rf * tiles

    copies = []
    for n, piece in enumerate(pieces):
        copy = pltpu.make_async_copy(piece, panel.at[pl.ds(n * rf, rf)], sems.at[n])
        copy.start()
        copies.append(copy)

    def clear(c, carry):
        rows = pl.ds(pl.multiple_of(c * chunk, chunk), chunk)
        for acc in accs:
            acc[rows, :] = jnp.zeros((chunk, LANES), jnp.float32)
        return carry

    lax.fori_loop(0, table_rows // chunk, clear, 0)
    for copy in copies:
        copy.wait()

    lane = lax.broadcasted_iota(jnp.int32, (tile, LANES), 1)
    lo = lane < tile

    def first_product(slot):
        row, k = slot // tiles, slot % tiles
        both = a_ref[row, :, pl.ds(pl.multiple_of(k // 2 * LANES, LANES), LANES)]
        start = k % 2 * tile
        left = jnp.where((lane >= start) & (lane < start + tile), both, jnp.zeros_like(both))
        block = panel[idx_ref[slot]]
        right = jnp.concatenate([block, block], axis=0)
        return jnp.dot(left, right, preferred_element_type=jnp.float32)

    def keep(u, y):
        for m in range(width // 2):
            x = y[:, m * LANES:(m + 1) * LANES]
            xr = pltpu.roll(x, tile, 1)
            zero = jnp.zeros_like(x)
            for h, (p, r) in enumerate(((x, xr), (xr, x))):
                at = (2 * m + h) * LANES
                y_buf[u, :tile, at:at + LANES] = jnp.where(lo, p, zero).astype(jnp.bfloat16)
                y_buf[u, tile:, at:at + LANES] = jnp.where(lo, zero, r).astype(jnp.bfloat16)

    def second_product(slot, u):
        lhs = lhs_ref[slot // tiles]
        return [
            jnp.dot(lhs, y_buf[u, :, m * 2 * LANES:(m + 1) * 2 * LANES], preferred_element_type=jnp.float32)
            for m in range(width // 2)
        ]

    def add(slot, w):
        row, k = slot // tiles, slot % tiles
        for q in range(width):
            spans = []
            for s in range(width):
                place = place_ref[(row * width + s) * (tiles * width) + k * width + q]
                spans.append(pl.ds(pl.multiple_of(place * sub, sub), sub))
            old = [accs[s][spans[s], :] for s in range(width)]
            part = w[q // 2][:, q % 2 * LANES:(q % 2 + 1) * LANES]
            for s in range(width):
                accs[s][spans[s], :] = old[s] + part[s * sub:(s + 1) * sub]

    for u in range(BATCH):
        keep(u, first_product(u))

    def batch(c, carry):
        base = c * BATCH
        upcoming = [first_product(jnp.minimum(base + BATCH + u, slots - 1)) for u in range(BATCH)]
        w = second_product(base, 0)
        for u in range(BATCH):
            after = second_product(base + u + 1, u + 1) if u + 1 < BATCH else None
            add(base + u, w)
            w = after
        for u in range(BATCH):
            keep(u, upcoming[u])
        return carry

    lax.fori_loop(0, slots // BATCH, batch, 0)

    for n, out in enumerate(outs):

        def merge(c, carry):
            rows = pl.ds(pl.multiple_of(n * out_rows + c * chunk, chunk), chunk)
            total = accs[0][rows, :]
            for acc in accs[1:]:
                total = total + acc[rows, :]
            out[pl.ds(pl.multiple_of(c * chunk, chunk), chunk), :] = total.astype(out.dtype)
            return carry

        lax.fori_loop(0, out_rows // chunk, merge, 0)


def partial_sums(idx, places, a_tiles, lhs, pieces, groups, cap):
    rf, tile, cols = a_tiles.shape
    sub = tile * tile // LANES
    width = pieces[0].shape[2]
    return pl.pallas_call(
        functools.partial(partial_kernel, len(pieces), groups),
        out_shape=[jax.ShapeDtypeStruct((cap * sub, LANES), jnp.bfloat16)] * groups,
        grid_spec=pltpu.PrefetchScalarGridSpec(
            num_scalar_prefetch=2,
            grid=(1,),
            in_specs=[
                pl.BlockSpec(a_tiles.shape, lambda i, *_: (0, 0, 0)),
                pl.BlockSpec(lhs.shape, lambda i, *_: (0, 0, 0)),
            ]
            + [pl.BlockSpec(memory_space=pl.ANY)] * len(pieces),
            out_specs=[pl.BlockSpec((cap * sub, LANES), lambda i, *_: (0, 0))] * groups,
            scratch_shapes=[pltpu.VMEM((groups * cap * sub, LANES), jnp.float32)] * ACCS
            + [
                pltpu.VMEM((len(pieces) * rf, tile, width), jnp.bfloat16),
                pltpu.VMEM((BATCH, 2 * tile, 2 * width), jnp.bfloat16),
                pltpu.SemaphoreType.DMA((len(pieces),)),
            ],
        ),
        compiler_params=pltpu.CompilerParams(
            dimension_semantics=("arbitrary",), vmem_limit_bytes=56 * 1024 * 1024
        ),
        name="partial_sums",
    )(idx, places, a_tiles, lhs, *pieces)


def owner_kernel(n_in, slot_ref, *refs):
    ins, out_ref, accs = refs[:n_in], refs[n_in], refs[n_in + 1:]
    sub = out_ref.shape[1] // LANES
    cap = ins[0].shape[0] // sub
    chunk = 256
    n_out = out_ref.shape[0]
    half = len(accs)

    def clear(c, carry):
        rows = pl.ds(pl.multiple_of(c * chunk, chunk), chunk)
        for acc in accs:
            acc[rows, :] = jnp.zeros((chunk, LANES), jnp.float32)
        return carry

    lax.fori_loop(0, n_out * sub // chunk, clear, 0)

    def add(c, carry):
        src = pl.ds(pl.multiple_of(c * sub, sub), sub)
        new = [x[src, :].astype(jnp.float32) for x in ins]
        spans = [pl.ds(pl.multiple_of(slot_ref[n * cap + c] * sub, sub), sub) for n in range(n_in)]
        for first in range(0, n_in, half):
            some = range(first, min(first + half, n_in))
            old = [accs[n - first][spans[n], :] for n in some]
            for n, was in zip(some, old):
                accs[n - first][spans[n], :] = was + new[n]
        return carry

    lax.fori_loop(0, cap, add, 0, unroll=4)

    def emit(c, carry):
        rows = pl.ds(pl.multiple_of(c * 8, 8), 8)
        for t in range(sub):
            total = None
            for acc in accs:
                piece = acc[pl.ds(c * 8 * sub + t, 8, stride=sub), :]
                total = piece if total is None else total + piece
            out_ref[rows, t * LANES:(t + 1) * LANES] = total
        return carry

    lax.fori_loop(0, n_out // 8, emit, 0)


def owner_sums(slots, arrived, sub):
    block = arrived[0].shape
    return pl.pallas_call(
        functools.partial(owner_kernel, len(arrived)),
        out_shape=jax.ShapeDtypeStruct((OSLOT, sub * LANES), jnp.float32),
        grid_spec=pltpu.PrefetchScalarGridSpec(
            num_scalar_prefetch=1,
            grid=(1,),
            in_specs=[pl.BlockSpec(block, lambda i, *_: (0, 0))] * len(arrived),
            out_specs=pl.BlockSpec((OSLOT, sub * LANES), lambda i, *_: (0, 0)),
            scratch_shapes=[pltpu.VMEM((OSLOT * sub, LANES), jnp.float32)] * 2,
        ),
        compiler_params=pltpu.CompilerParams(
            dimension_semantics=("arbitrary",), vmem_limit_bytes=40 * 1024 * 1024
        ),
        name="owner_sums",
    )(slots, *arrived)


def swap(x, axis, d):
    return lax.ppermute(x, axis, [(i, i ^ d) for i in range(lax.axis_size(axis))])


def body(a_tiles, a_cols, p_tiles, route_list, out_slot):
    groups, size = lax.axis_size("grp"), lax.axis_size("blk")
    me = lax.axis_index("grp")
    rf, tile, cols = a_tiles.shape
    cap = out_slot.shape[1] // groups
    sub = tile * tile // LANES
    near = swap(p_tiles, "blk", 1)
    far = [swap(p_tiles, "blk", d) for d in range(2, size, 2)]
    names = out_slot.reshape(groups, cap)
    names = [lax.dynamic_index_in_dim(names, me ^ d, 0, keepdims=False) for d in range(groups)]
    slots = jnp.concatenate([names[0]] + [swap(names[d], "grp", d) for d in range(1, groups)])
    flat_cols = a_cols.reshape(-1)
    holder = flat_cols // rf // groups
    idx = (holder ^ lax.axis_index("blk")) * rf + flat_cols % rf
    lhs = jnp.swapaxes(p_tiles, 1, 2).reshape(rf, p_tiles.shape[2] // 2, 2 * tile)
    flat_route = route_list.reshape(-1)
    places = (flat_route // cap ^ me) * cap + flat_route % cap
    far[0], idx, lhs, places, slots = lax.optimization_barrier((far[0], idx, lhs, places, slots))
    pieces = [p_tiles, near]
    for x in far:
        pieces += [x, swap(x, "blk", 1)]
    sums = partial_sums(idx, places, a_tiles, lhs, pieces, groups, cap)
    arrived = [sums[0]] + [swap(sums[d], "grp", d) for d in range(1, groups)]
    return owner_sums(slots, arrived, sub)


def solution(mesh):
    in_specs = (
        P(("blk", "grp"), None, None),
        P(("blk", "grp"), None),
        P(("blk", "grp"), None, None),
        P(("blk", "grp"), None),
        P(("blk", "grp"), None),
    )
    out_specs = P(("blk", "grp"), None)
    return jax.shard_map(body, mesh=mesh, in_specs=in_specs, out_specs=out_specs, check_vma=False)
```

```python
import functools

import jax
import jax.numpy as jnp
from jax import lax
from jax.experimental import pallas as pl
from jax.experimental.pallas import tpu as pltpu
from jax.sharding import PartitionSpec as P

OSLOT = 128
LANES = 128
ACCS = 4
BATCH = 8


def partial_kernel(n_pieces, n_outs, idx_ref, place_ref, a_ref, lhs_ref, *refs):
    pieces, refs = refs[:n_pieces], refs[n_pieces:]
    outs, refs = refs[:n_outs], refs[n_outs:]
    accs, (panel, y_buf, sems) = refs[:ACCS], refs[ACCS:]
    rf, tile, cols = a_ref.shape
    tiles = cols // tile
    width = panel.shape[2] // tile
    sub = tile * tile // LANES
    out_rows = outs[0].shape[0]
    table_rows = accs[0].shape[0]
    chunk = 256
    slots = rf * tiles

    copies, at = [], 0
    for n, piece in enumerate(pieces):
        copy = pltpu.make_async_copy(piece, panel.at[pl.ds(at, piece.shape[0])], sems.at[n])
        copy.start()
        copies.append(copy)
        at += piece.shape[0]

    def clear(c, carry):
        rows = pl.ds(pl.multiple_of(c * chunk, chunk), chunk)
        for acc in accs:
            acc[rows, :] = jnp.zeros((chunk, LANES), jnp.float32)
        return carry

    lax.fori_loop(0, table_rows // chunk, clear, 0)
    for copy in copies:
        copy.wait()

    lane = lax.broadcasted_iota(jnp.int32, (tile, LANES), 1)
    lo = lane < tile

    def first_product(slot):
        row, k = slot // tiles, slot % tiles
        both = a_ref[row, :, pl.ds(pl.multiple_of(k // 2 * LANES, LANES), LANES)]
        start = k % 2 * tile
        left = jnp.where((lane >= start) & (lane < start + tile), both, jnp.zeros_like(both))
        block = panel[idx_ref[slot]]
        right = jnp.concatenate([block, block], axis=0)
        return jnp.dot(left, right, preferred_element_type=jnp.float32)

    def keep(u, y):
        for m in range(width // 2):
            x = y[:, m * LANES:(m + 1) * LANES]
            xr = pltpu.roll(x, tile, 1)
            zero = jnp.zeros_like(x)
            for h, (p, r) in enumerate(((x, xr), (xr, x))):
                at = (2 * m + h) * LANES
                y_buf[u, :tile, at:at + LANES] = jnp.where(lo, p, zero).astype(jnp.bfloat16)
                y_buf[u, tile:, at:at + LANES] = jnp.where(lo, zero, r).astype(jnp.bfloat16)

    def second_product(slot, u):
        lhs = lhs_ref[slot // tiles]
        return [
            jnp.dot(lhs, y_buf[u, :, m * 2 * LANES:(m + 1) * 2 * LANES], preferred_element_type=jnp.float32)
            for m in range(width // 2)
        ]

    def add(slot, w):
        row, k = slot // tiles, slot % tiles
        for q in range(width):
            spans = []
            for s in range(width):
                place = place_ref[(row * width + s) * (tiles * width) + k * width + q]
                spans.append(pl.ds(pl.multiple_of(place * sub, sub), sub))
            old = [accs[s][spans[s], :] for s in range(width)]
            part = w[q // 2][:, q % 2 * LANES:(q % 2 + 1) * LANES]
            for s in range(width):
                accs[s][spans[s], :] = old[s] + part[s * sub:(s + 1) * sub]

    for u in range(BATCH):
        keep(u, first_product(u))

    def batch(c, carry):
        base = c * BATCH
        upcoming = [first_product(jnp.minimum(base + BATCH + u, slots - 1)) for u in range(BATCH)]
        w = second_product(base, 0)
        for u in range(BATCH):
            after = second_product(base + u + 1, u + 1) if u + 1 < BATCH else None
            add(base + u, w)
            w = after
        for u in range(BATCH):
            keep(u, upcoming[u])
        return carry

    lax.fori_loop(0, slots // BATCH, batch, 0)

    for n, out in enumerate(outs):

        def merge(c, carry):
            rows = pl.ds(pl.multiple_of(n * out_rows + c * chunk, chunk), chunk)
            total = accs[0][rows, :]
            for acc in accs[1:]:
                total = total + acc[rows, :]
            out[pl.ds(pl.multiple_of(c * chunk, chunk), chunk), :] = total.astype(out.dtype)
            return carry

        lax.fori_loop(0, out_rows // chunk, merge, 0)


def partial_sums(idx, places, a_tiles, lhs, pieces, tables, groups, cap):
    rf, tile, cols = a_tiles.shape
    sub = tile * tile // LANES
    width = pieces[0].shape[2]
    return pl.pallas_call(
        functools.partial(partial_kernel, len(pieces), groups),
        out_shape=[jax.ShapeDtypeStruct((cap * sub, LANES), jnp.bfloat16)] * groups,
        grid_spec=pltpu.PrefetchScalarGridSpec(
            num_scalar_prefetch=2,
            grid=(1,),
            in_specs=[
                pl.BlockSpec(a_tiles.shape, lambda i, *_: (0, 0, 0)),
                pl.BlockSpec(lhs.shape, lambda i, *_: (0, 0, 0)),
            ]
            + [pl.BlockSpec(memory_space=pl.ANY)] * len(pieces),
            out_specs=[pl.BlockSpec((cap * sub, LANES), lambda i, *_: (0, 0))] * groups,
            scratch_shapes=[pltpu.VMEM((tables * cap * sub, LANES), jnp.float32)] * ACCS
            + [
                pltpu.VMEM((sum(x.shape[0] for x in pieces), tile, width), jnp.bfloat16),
                pltpu.VMEM((BATCH, 2 * tile, 2 * width), jnp.bfloat16),
                pltpu.SemaphoreType.DMA((len(pieces),)),
            ],
        ),
        compiler_params=pltpu.CompilerParams(
            dimension_semantics=("arbitrary",), vmem_limit_bytes=56 * 1024 * 1024
        ),
        cost_estimate=pl.CostEstimate(flops=1, bytes_accessed=1, transcendentals=0),
        name="partial_sums",
    )(idx, places, a_tiles, lhs, *pieces)


def owner_kernel(n_in, slot_ref, pick_ref, *refs):
    ins, other, out_ref, accs = refs[:n_in], refs[n_in], refs[n_in + 1], refs[n_in + 2:]
    sub = out_ref.shape[1] // LANES
    cap = ins[0].shape[0] // sub
    chunk = 256
    n_out = out_ref.shape[0]
    half = len(accs)

    def clear(c, carry):
        rows = pl.ds(pl.multiple_of(c * chunk, chunk), chunk)
        for acc in accs:
            acc[rows, :] = jnp.zeros((chunk, LANES), jnp.float32)
        return carry

    lax.fori_loop(0, n_out * sub // chunk, clear, 0)

    def add(c, carry):
        src = pl.ds(pl.multiple_of(c * sub, sub), sub)
        new = [x[src, :].astype(jnp.float32) for x in ins]
        new[-1] = jnp.where(pick_ref[0] == 1, new[-1], other[src, :].astype(jnp.float32))
        spans = [pl.ds(pl.multiple_of(slot_ref[n * cap + c] * sub, sub), sub) for n in range(n_in)]
        for first in range(0, n_in, half):
            some = range(first, min(first + half, n_in))
            old = [accs[n - first][spans[n], :] for n in some]
            for n, was in zip(some, old):
                accs[n - first][spans[n], :] = was + new[n]
        return carry

    lax.fori_loop(0, cap, add, 0, unroll=4)

    def emit(c, carry):
        rows = pl.ds(pl.multiple_of(c * 8, 8), 8)
        for t in range(sub):
            total = None
            for acc in accs:
                piece = acc[pl.ds(c * 8 * sub + t, 8, stride=sub), :]
                total = piece if total is None else total + piece
            out_ref[rows, t * LANES:(t + 1) * LANES] = total
        return carry

    lax.fori_loop(0, n_out // 8, emit, 0)


def owner_sums(slots, pick, arrived, other, sub):
    block = other.shape
    return pl.pallas_call(
        functools.partial(owner_kernel, len(arrived)),
        out_shape=jax.ShapeDtypeStruct((OSLOT, sub * LANES), jnp.float32),
        grid_spec=pltpu.PrefetchScalarGridSpec(
            num_scalar_prefetch=2,
            grid=(1,),
            in_specs=[pl.BlockSpec(block, lambda i, *_: (0, 0))] * (len(arrived) + 1),
            out_specs=pl.BlockSpec((OSLOT, sub * LANES), lambda i, *_: (0, 0)),
            scratch_shapes=[pltpu.VMEM((OSLOT * sub, LANES), jnp.float32)] * 2,
        ),
        compiler_params=pltpu.CompilerParams(
            dimension_semantics=("arbitrary",), vmem_limit_bytes=40 * 1024 * 1024
        ),
        name="owner_sums",
    )(slots, pick, *arrived, other)


def swap(x, axis, d):
    return lax.ppermute(x, axis, [(i, i ^ d) for i in range(lax.axis_size(axis))])


def panel_index(a_cols, groups, rf):
    flat = a_cols.reshape(-1)
    d = flat // rf // groups ^ lax.axis_index("blk")
    return (d % 2 * (lax.axis_size("blk") // 2) + d // 2) * rf + flat % rf


def transposed(p_tiles):
    rf, tile, width = p_tiles.shape
    return jnp.swapaxes(p_tiles, 1, 2).reshape(rf, width // 2, 2 * tile)


def direct(p_tiles):
    return [swap(p_tiles, "blk", d) for d in range(2, lax.axis_size("blk"), 2)]


def body(a_tiles, a_cols, p_tiles, route_list, out_slot):
    groups = lax.axis_size("grp")
    me = lax.axis_index("grp")
    rf, tile, cols = a_tiles.shape
    cap = out_slot.shape[1] // groups
    sub = tile * tile // LANES
    n_cols = a_cols.shape[1]

    takes = [(1, 0), (3, 1), (0, 2), (2, 3)]
    far = direct(p_tiles)
    p_took = lax.ppermute(p_tiles, "grp", takes)
    a_took = lax.ppermute(a_tiles, "grp", takes)

    middle = (me == 1) | (me == 2)
    one = middle.astype(jnp.int32)
    names = lax.all_to_all(out_slot.reshape(groups, cap), "grp", split_axis=0, concat_axis=0, tiled=True)
    sources = me ^ jnp.where(middle, jnp.array([0, 2, 1, 3]), jnp.arange(groups))
    slots = names[sources].reshape(-1)
    pick = one.reshape(1)

    idx = panel_index(a_cols, groups, rf)
    lhs = transposed(p_tiles)
    route = route_list.reshape(-1)
    off = route // cap ^ me
    table = jnp.where(middle, jnp.where(off == 0, 0, jnp.where(off == 1, 3, off - 1)), off)
    places = table * cap + route % cap

    ints = jnp.concatenate([a_cols, route_list], axis=1)
    p_near = p_tiles
    far[0], idx, lhs, places, slots, p_near, ints = lax.optimization_barrier(
        (far[0], idx, lhs, places, slots, p_near, ints)
    )
    mine = [p_tiles] + far
    pieces = mine + [swap(x, "blk", 1) for x in [p_near] + far]
    ints_took = lax.ppermute(ints, "grp", takes)
    far_took = direct(p_took)

    own, to_a, to_b = partial_sums(idx, places, a_tiles, lhs, pieces, 4, 3, cap)
    own, to_a, to_b, ints_took, *far_took = lax.optimization_barrier((own, to_a, to_b, ints_took, *far_took))
    from_a = lax.ppermute(to_a, "grp", [(0, 1), (3, 2), (1, 3), (2, 0)])
    from_b = lax.ppermute(to_b, "grp", [(1, 2), (2, 1)])

    idx_took = panel_index(ints_took[:, :n_cols], groups, rf)
    route_took = ints_took[:, n_cols:].reshape(-1)
    off = route_took // cap ^ me
    places_took = jnp.where(off == 0, 0, jnp.where((off == 1) & middle, 1, 2)) * cap + route_took % cap
    lhs_took = transposed(p_took)
    mine_took = jnp.concatenate([p_took] + far_took)
    pieces_took = [mine_took, swap(mine_took, "blk", 1)]
    own_took, to_c = partial_sums(idx_took, places_took, a_took, lhs_took, pieces_took, 3, 2, cap)
    from_c = lax.ppermute(to_c, "grp", [(1, 0), (2, 3)])
    return owner_sums(slots, pick, [own, own_took, from_a, from_b], from_c, sub)


def solution(mesh):
    in_specs = (
        P(("blk", "grp"), None, None),
        P(("blk", "grp"), None),
        P(("blk", "grp"), None, None),
        P(("blk", "grp"), None),
        P(("blk", "grp"), None),
    )
    out_specs = P(("blk", "grp"), None)
    return jax.shard_map(body, mesh=mesh, in_specs=in_specs, out_specs=out_specs, check_vma=False)
```

```python
import functools

import jax
import jax.numpy as jnp
from jax import lax
from jax.experimental import pallas as pl
from jax.experimental.pallas import tpu as pltpu
from jax.sharding import PartitionSpec as P

OSLOT = 128
LANES = 128
ACCS = 4
BATCH = 8


def partial_kernel(n_rows, n_pieces, n_outs, idx_ref, place_ref, lhs_ref, *refs):
    row_parts, refs = refs[:n_rows], refs[n_rows:]
    pieces, refs = refs[:n_pieces], refs[n_pieces:]
    outs, refs = refs[:n_outs], refs[n_outs:]
    accs, (a_ref, panel, y_buf, sems) = refs[:ACCS], refs[ACCS:]
    rf, tile, cols = a_ref.shape
    tiles = cols // tile
    width = panel.shape[2] // tile
    sub = tile * tile // LANES
    out_rows = outs[0].shape[0]
    chunk = 256
    slots = rf * tiles

    copies = []
    for parts, whole in ((row_parts, a_ref), (pieces, panel)):
        at = 0
        for part in parts:
            copy = pltpu.make_async_copy(part, whole.at[pl.ds(at, part.shape[0])], sems.at[len(copies)])
            copy.start()
            copies.append(copy)
            at += part.shape[0]

    def clear(c, carry):
        rows = pl.ds(pl.multiple_of(c * chunk, chunk), chunk)
        for acc in accs:
            acc[rows, :] = jnp.zeros((chunk, LANES), jnp.float32)
        return carry

    lax.fori_loop(0, n_outs * out_rows // chunk, clear, 0)
    for acc in accs:
        acc[n_outs * out_rows:, :] = jnp.zeros((sub, LANES), jnp.float32)
    for copy in copies:
        copy.wait()

    lane = lax.broadcasted_iota(jnp.int32, (tile, LANES), 1)
    lo = lane < tile

    def first_product(slot):
        row, k = slot // tiles, slot % tiles
        both = a_ref[row, :, pl.ds(pl.multiple_of(k // 2 * LANES, LANES), LANES)]
        start = k % 2 * tile
        left = jnp.where((lane >= start) & (lane < start + tile), both, jnp.zeros_like(both))
        block = panel[idx_ref[slot]]
        right = jnp.concatenate([block, block], axis=0)
        return jnp.dot(left, right, preferred_element_type=jnp.float32)

    def keep(u, y):
        for m in range(width // 2):
            x = y[:, m * LANES:(m + 1) * LANES]
            y_buf[u, :, 2 * m * LANES:(2 * m + 1) * LANES] = x.astype(jnp.bfloat16)
            y_buf[u, :, (2 * m + 1) * LANES:(2 * m + 2) * LANES] = pltpu.roll(x, tile, 1).astype(jnp.bfloat16)

    def second_product(slot, u):
        lhs = lhs_ref[slot // tiles]
        w = []
        for m in range(width // 2):
            x = y_buf[u, :, 2 * m * LANES:(2 * m + 1) * LANES]
            xr = y_buf[u, :, (2 * m + 1) * LANES:(2 * m + 2) * LANES]
            none = jnp.zeros_like(x)
            right = jnp.concatenate(
                [
                    jnp.concatenate([jnp.where(lo, x, none), jnp.where(lo, xr, none)], axis=1),
                    jnp.concatenate([jnp.where(lo, none, xr), jnp.where(lo, none, x)], axis=1),
                ],
                axis=0,
            )
            w.append(jnp.dot(lhs, right, preferred_element_type=jnp.float32))
        return w

    def add(slot, w):
        row, k = slot // tiles, slot % tiles
        for q in range(width):
            spans = []
            for s in range(width):
                place = place_ref[(row * width + s) * (tiles * width) + k * width + q]
                spans.append(pl.ds(pl.multiple_of(place * sub, sub), sub))
            old = [accs[s][spans[s], :] for s in range(width)]
            part = w[q // 2][:, q % 2 * LANES:(q % 2 + 1) * LANES]
            for s in range(width):
                accs[s][spans[s], :] = old[s] + part[s * sub:(s + 1) * sub]

    for u in range(BATCH):
        keep(u, first_product(u))

    def batch(c, carry):
        base = c * BATCH
        upcoming = [first_product(jnp.minimum(base + BATCH + u, slots - 1)) for u in range(BATCH)]
        w = second_product(base, 0)
        for u in range(BATCH):
            after = second_product(base + u + 1, u + 1) if u + 1 < BATCH else None
            add(base + u, w)
            w = after
        for u in range(BATCH):
            keep(u, upcoming[u])
        return carry

    lax.fori_loop(0, slots // BATCH, batch, 0)

    for n, out in enumerate(outs):

        def merge(c, carry):
            rows = pl.ds(pl.multiple_of(n * out_rows + c * chunk, chunk), chunk)
            total = accs[0][rows, :]
            for acc in accs[1:]:
                total = total + acc[rows, :]
            out[pl.ds(pl.multiple_of(c * chunk, chunk), chunk), :] = total.astype(out.dtype)
            return carry

        lax.fori_loop(0, out_rows // chunk, merge, 0)


def partial_sums(idx, places, row_parts, lhs, pieces, groups, cap):
    rf = lhs.shape[0]
    tile, cols = row_parts[0].shape[1:]
    sub = tile * tile // LANES
    width = pieces[0].shape[2]
    return pl.pallas_call(
        functools.partial(partial_kernel, len(row_parts), len(pieces), groups),
        out_shape=[jax.ShapeDtypeStruct((cap * sub, LANES), jnp.bfloat16)] * groups,
        grid_spec=pltpu.PrefetchScalarGridSpec(
            num_scalar_prefetch=2,
            grid=(1,),
            in_specs=[pl.BlockSpec(lhs.shape, lambda i, *_: (0, 0, 0))]
            + [pl.BlockSpec(memory_space=pl.ANY)] * (len(row_parts) + len(pieces)),
            out_specs=[pl.BlockSpec((cap * sub, LANES), lambda i, *_: (0, 0))] * groups,
            scratch_shapes=[pltpu.VMEM(((groups * cap + 1) * sub, LANES), jnp.float32)] * ACCS
            + [
                pltpu.VMEM((rf, tile, cols), jnp.bfloat16),
                pltpu.VMEM((sum(x.shape[0] for x in pieces), tile, width), jnp.bfloat16),
                pltpu.VMEM((BATCH, tile, 2 * width), jnp.bfloat16),
                pltpu.SemaphoreType.DMA((len(row_parts) + len(pieces),)),
            ],
        ),
        compiler_params=pltpu.CompilerParams(
            dimension_semantics=("arbitrary",), vmem_limit_bytes=56 * 1024 * 1024
        ),
        name="partial_sums",
    )(idx, places, lhs, *row_parts, *pieces)


def owner_kernel(n_in, slot_ref, pick_ref, *refs):
    ins, other, out_ref, accs = refs[:n_in], refs[n_in], refs[n_in + 1], refs[n_in + 2:]
    sub = out_ref.shape[1] // LANES
    cap = ins[0].shape[0] // sub
    chunk = 256
    n_out = out_ref.shape[0]
    half = len(accs)

    def clear(c, carry):
        rows = pl.ds(pl.multiple_of(c * chunk, chunk), chunk)
        for acc in accs:
            acc[rows, :] = jnp.zeros((chunk, LANES), jnp.float32)
        return carry

    lax.fori_loop(0, n_out * sub // chunk, clear, 0)

    def add(c, carry):
        src = pl.ds(pl.multiple_of(c * sub, sub), sub)
        new = [x[src, :].astype(jnp.float32) for x in ins]
        new[-1] = jnp.where(pick_ref[0] == 1, new[-1], other[src, :].astype(jnp.float32))
        spans = [pl.ds(pl.multiple_of(slot_ref[n * cap + c] * sub, sub), sub) for n in range(n_in)]
        for first in range(0, n_in, half):
            some = range(first, min(first + half, n_in))
            old = [accs[n - first][spans[n], :] for n in some]
            for n, was in zip(some, old):
                accs[n - first][spans[n], :] = was + new[n]
        return carry

    lax.fori_loop(0, cap, add, 0, unroll=4)

    def emit(c, carry):
        rows = pl.ds(pl.multiple_of(c * 8, 8), 8)
        for t in range(sub):
            total = None
            for acc in accs:
                piece = acc[pl.ds(c * 8 * sub + t, 8, stride=sub), :]
                total = piece if total is None else total + piece
            out_ref[rows, t * LANES:(t + 1) * LANES] = total
        return carry

    lax.fori_loop(0, n_out // 8, emit, 0)


def owner_sums(slots, pick, arrived, other, sub):
    block = other.shape
    return pl.pallas_call(
        functools.partial(owner_kernel, len(arrived)),
        out_shape=jax.ShapeDtypeStruct((OSLOT, sub * LANES), jnp.float32),
        grid_spec=pltpu.PrefetchScalarGridSpec(
            num_scalar_prefetch=2,
            grid=(1,),
            in_specs=[pl.BlockSpec(block, lambda i, *_: (0, 0))] * (len(arrived) + 1),
            out_specs=pl.BlockSpec((OSLOT, sub * LANES), lambda i, *_: (0, 0)),
            scratch_shapes=[pltpu.VMEM((OSLOT * sub, LANES), jnp.float32)] * 2,
        ),
        compiler_params=pltpu.CompilerParams(
            dimension_semantics=("arbitrary",), vmem_limit_bytes=40 * 1024 * 1024
        ),
        name="owner_sums",
    )(slots, pick, *arrived, other)


def swap(x, axis, d):
    return lax.ppermute(x, axis, [(i, i ^ d) for i in range(lax.axis_size(axis))])


def panel_index(a_cols, groups, rf):
    flat = a_cols.reshape(-1)
    d = flat // rf // groups ^ lax.axis_index("blk")
    return (d % 2 * (lax.axis_size("blk") // 2) + d // 2) * rf + flat % rf


def transposed(p_tiles):
    rf, tile, width = p_tiles.shape
    return jnp.swapaxes(p_tiles, 1, 2).reshape(rf, width // 2, 2 * tile)


def direct(p_tiles):
    return [swap(p_tiles, "blk", d) for d in range(2, lax.axis_size("blk"), 2)]


def body(a_tiles, a_cols, p_tiles, route_list, out_slot):
    groups = lax.axis_size("grp")
    me = lax.axis_index("grp")
    rf, tile, cols = a_tiles.shape
    cap = out_slot.shape[1] // groups
    sub = tile * tile // LANES
    n_cols = a_cols.shape[1]
    middle = (me == 1) | (me == 2)
    takes = [(1, 0), (3, 1), (0, 2), (2, 3)]

    def take(x):
        return lax.ppermute(x, "grp", takes)

    far = direct(p_tiles)
    p_took = take(p_tiles)
    a_first = take(a_tiles[:rf // 2])
    idx = panel_index(a_cols, groups, rf)
    lhs = transposed(p_tiles)
    route = route_list.reshape(-1)
    off = route // cap ^ me
    spare = 3 * cap
    there = jnp.where(middle, jnp.where(off > 1, off - 1, 0), off) * cap + route % cap
    unused = jnp.where(middle, off == 1, off > 1)
    places = jnp.where(unused, spare, there)

    ints = jnp.concatenate([a_cols, route_list], axis=1)
    p_near = p_tiles
    far[0], idx, lhs, places, p_near, ints = lax.optimization_barrier((far[0], idx, lhs, places, p_near, ints))
    mine = [p_tiles] + far
    pieces = mine + [swap(x, "blk", 1) for x in [p_near] + far]
    ints_took = take(ints)
    far_took = direct(p_took)

    idx_took = panel_index(ints_took[:, :n_cols], groups, rf)
    route_took = ints_took[:, n_cols:].reshape(-1)
    off = route_took // cap ^ me
    used = (off == 0) | ((off == 1) & middle)
    places_took = jnp.where(used, off * cap + route_took % cap, 2 * cap)
    lhs_took = transposed(p_took)

    a_rest = a_tiles[rf // 2:]
    pieces[-1], a_first, idx_took, places_took, lhs_took = lax.optimization_barrier(
        (pieces[-1], a_first, idx_took, places_took, lhs_took)
    )
    a_second = take(a_rest)
    own, to_a, to_b = partial_sums(idx, places, [a_tiles], lhs, pieces, 3, cap)
    own, to_a, to_b, a_second, *far_took = lax.optimization_barrier((own, to_a, to_b, a_second, *far_took))
    from_a = lax.ppermute(to_a, "grp", [(0, 1), (3, 2), (1, 3), (2, 0)])
    from_b = lax.ppermute(to_b, "grp", [(1, 2), (2, 1)])
    mine_took = jnp.concatenate([p_took] + far_took)
    pieces_took = [mine_took, swap(mine_took, "blk", 1)]
    own_took, to_c = partial_sums(idx_took, places_took, [a_first, a_second], lhs_took, pieces_took, 2, cap)
    from_c = lax.ppermute(to_c, "grp", [(1, 0), (2, 3)])

    out_slot, own_took = lax.optimization_barrier((out_slot, own_took))
    names = lax.all_to_all(out_slot.reshape(groups, cap), "grp", split_axis=0, concat_axis=0, tiled=True)
    sources = me ^ jnp.where(middle, jnp.array([0, 2, 1, 3]), jnp.arange(groups))
    slots = names[sources].reshape(-1)
    pick = middle.astype(jnp.int32).reshape(1)
    return owner_sums(slots, pick, [own, own_took, from_a, from_b], from_c, sub)


def solution(mesh):
    in_specs = (
        P(("blk", "grp"), None, None),
        P(("blk", "grp"), None),
        P(("blk", "grp"), None, None),
        P(("blk", "grp"), None),
        P(("blk", "grp"), None),
    )
    out_specs = P(("blk", "grp"), None)
    return jax.shard_map(body, mesh=mesh, in_specs=in_specs, out_specs=out_specs, check_vma=False)
```

```python
import functools

import jax
import jax.numpy as jnp
from jax import lax
from jax.experimental import pallas as pl
from jax.experimental.pallas import tpu as pltpu
from jax.sharding import PartitionSpec as P

OSLOT = 128
LANES = 128
ACCS = 4
BATCH = 8
NAME_ROWS = 16


def partial_kernel(n_rows, n_pieces, n_outs, idx_ref, place_ref, lhs_ref, names_ref, *refs):
    row_parts, refs = refs[:n_rows], refs[n_rows:]
    pieces, refs = refs[:n_pieces], refs[n_pieces:]
    outs, refs = refs[:n_outs], refs[n_outs:]
    accs, (a_ref, panel, y_buf, sems) = refs[:ACCS], refs[ACCS:]
    rf, tile, cols = a_ref.shape
    tiles = cols // tile
    width = panel.shape[2] // tile
    sub = tile * tile // LANES
    out_rows = outs[0].shape[0] - NAME_ROWS
    chunk = 256
    slots = rf * tiles

    copies = []
    for parts, whole in ((row_parts, a_ref), (pieces, panel)):
        at = 0
        for part in parts:
            copy = pltpu.make_async_copy(part, whole.at[pl.ds(at, part.shape[0])], sems.at[len(copies)])
            copy.start()
            copies.append(copy)
            at += part.shape[0]

    def clear(c, carry):
        rows = pl.ds(pl.multiple_of(c * chunk, chunk), chunk)
        for acc in accs:
            acc[rows, :] = jnp.zeros((chunk, LANES), jnp.float32)
        return carry

    lax.fori_loop(0, n_outs * out_rows // chunk, clear, 0)
    for acc in accs:
        acc[n_outs * out_rows:, :] = jnp.zeros((sub, LANES), jnp.float32)
    for copy in copies:
        copy.wait()

    lane = lax.broadcasted_iota(jnp.int32, (tile, LANES), 1)
    lo = lane < tile

    def first_products(slot):
        row, k = slot // tiles, slot % tiles
        both = a_ref[row, :, pl.ds(pl.multiple_of(k * tile, LANES), LANES)]
        none = jnp.zeros_like(both)
        left = jnp.concatenate([jnp.where(lo, both, none), jnp.where(lo, none, both)], axis=0)
        right = jnp.concatenate([panel[idx_ref[slot]], panel[idx_ref[slot + 1]]], axis=0)
        return jnp.dot(left, right, preferred_element_type=jnp.float32)

    def keep(u, y):
        for m in range(width // 2):
            x = y[:, m * LANES:(m + 1) * LANES]
            y_buf[u, :, 2 * m * LANES:(2 * m + 1) * LANES] = x.astype(jnp.bfloat16)
            y_buf[u, :, (2 * m + 1) * LANES:(2 * m + 2) * LANES] = pltpu.roll(x, tile, 1).astype(jnp.bfloat16)

    def second_product(slot, u):
        lhs = lhs_ref[slot // tiles]
        w = []
        for m in range(width // 2):
            x = y_buf[u, :, 2 * m * LANES:(2 * m + 1) * LANES]
            xr = y_buf[u, :, (2 * m + 1) * LANES:(2 * m + 2) * LANES]
            none = jnp.zeros_like(x)
            right = jnp.concatenate(
                [
                    jnp.concatenate([jnp.where(lo, x, none), jnp.where(lo, xr, none)], axis=1),
                    jnp.concatenate([jnp.where(lo, none, xr), jnp.where(lo, none, x)], axis=1),
                ],
                axis=0,
            )
            w.append(jnp.dot(lhs, right, preferred_element_type=jnp.float32))
        return w

    def add(slot, w):
        row, k = slot // tiles, slot % tiles
        for q in range(width):
            spans = []
            for s in range(width):
                place = place_ref[(row * width + s) * (tiles * width) + k * width + q]
                spans.append(pl.ds(pl.multiple_of(place * sub, sub), sub))
            old = [accs[s][spans[s], :] for s in range(width)]
            part = w[q // 2][:, q % 2 * LANES:(q % 2 + 1) * LANES]
            for s in range(width):
                accs[s][spans[s], :] = old[s] + part[s * sub:(s + 1) * sub]

    def keep_two(u, y):
        keep(u, y[:tile])
        keep(u + 1, y[tile:])

    for u in range(0, BATCH, 2):
        keep_two(u, first_products(u))

    def batch(c, carry):
        base = c * BATCH
        following = jnp.minimum(base + BATCH, slots - BATCH)
        upcoming = [first_products(following + u) for u in range(0, BATCH, 2)]
        w = second_product(base, 0)
        for u in range(BATCH):
            after = second_product(base + u + 1, u + 1) if u + 1 < BATCH else None
            add(base + u, w)
            w = after
        for u in range(0, BATCH, 2):
            keep_two(u, upcoming[u // 2])
        return carry

    lax.fori_loop(0, slots // BATCH, batch, 0)

    names = jnp.zeros((NAME_ROWS, LANES), jnp.float32)
    here = lax.broadcasted_iota(jnp.int32, (NAME_ROWS, LANES), 0)
    for n in range(names_ref.shape[1] // LANES):
        part = names_ref[:, n * LANES:(n + 1) * LANES].astype(jnp.float32)
        names = jnp.where(here == n, jnp.broadcast_to(part, names.shape), names)

    for n, out in enumerate(outs):

        def merge(c, carry):
            rows = pl.ds(pl.multiple_of(n * out_rows + c * chunk, chunk), chunk)
            total = accs[0][rows, :]
            for acc in accs[1:]:
                total = total + acc[rows, :]
            out[pl.ds(pl.multiple_of(c * chunk, chunk), chunk), :] = total.astype(out.dtype)
            return carry

        lax.fori_loop(0, out_rows // chunk, merge, 0)
        out[out_rows:, :] = names.astype(out.dtype)


def partial_sums(idx, places, row_parts, lhs, names, pieces, groups, cap):
    rf = lhs.shape[0]
    tile, cols = row_parts[0].shape[1:]
    sub = tile * tile // LANES
    width = pieces[0].shape[2]
    return pl.pallas_call(
        functools.partial(partial_kernel, len(row_parts), len(pieces), groups),
        out_shape=[jax.ShapeDtypeStruct((cap * sub + NAME_ROWS, LANES), jnp.bfloat16)] * groups,
        grid_spec=pltpu.PrefetchScalarGridSpec(
            num_scalar_prefetch=2,
            grid=(1,),
            in_specs=[
                pl.BlockSpec(lhs.shape, lambda i, *_: (0, 0, 0)),
                pl.BlockSpec(names.shape, lambda i, *_: (0, 0)),
            ]
            + [pl.BlockSpec(memory_space=pl.ANY)] * (len(row_parts) + len(pieces)),
            out_specs=[pl.BlockSpec((cap * sub + NAME_ROWS, LANES), lambda i, *_: (0, 0))] * groups,
            scratch_shapes=[pltpu.VMEM(((groups * cap + 1) * sub, LANES), jnp.float32)] * ACCS
            + [
                pltpu.VMEM((rf, tile, cols), jnp.bfloat16),
                pltpu.VMEM((sum(x.shape[0] for x in pieces), tile, width), jnp.bfloat16),
                pltpu.VMEM((BATCH, tile, 2 * width), jnp.bfloat16),
                pltpu.SemaphoreType.DMA((len(row_parts) + len(pieces),)),
            ],
        ),
        compiler_params=pltpu.CompilerParams(
            dimension_semantics=("arbitrary",), vmem_limit_bytes=56 * 1024 * 1024
        ),
        name="partial_sums",
    )(idx, places, lhs, names, *row_parts, *pieces)


def owner_kernel(me_ref, own_names, took_names, own, took, from_a, from_b, from_c, out_ref, *refs):
    accs, (vmem_names, smem_names, sem) = refs[:-3], refs[-3:]
    n_out = out_ref.shape[0]
    sub = out_ref.shape[1] // LANES
    cap = (own.shape[0] - NAME_ROWS) // sub
    chunk = 256
    me, pick = me_ref[0], me_ref[1] == 1

    rows = pl.ds(cap * sub, NAME_ROWS)
    last = jnp.where(pick, from_b[rows, :].astype(jnp.float32), from_c[rows, :].astype(jnp.float32))
    vmem_names[0] = from_a[rows, :].astype(jnp.float32).astype(jnp.int32)
    vmem_names[1] = last.astype(jnp.int32)
    copy = pltpu.make_async_copy(vmem_names, smem_names, sem)
    copy.start()

    def clear(c, carry):
        rows = pl.ds(pl.multiple_of(c * chunk, chunk), chunk)
        for acc in accs:
            acc[rows, :] = jnp.zeros((chunk, LANES), jnp.float32)
        return carry

    lax.fori_loop(0, n_out * sub // chunk, clear, 0)
    copy.wait()

    def add_two(names, blocks):
        spans = [pl.ds(pl.multiple_of(name * sub, sub), sub) for name in names]
        old = [acc[span, :] for acc, span in zip(accs, spans)]
        for acc, span, was, block in zip(accs, spans, old, blocks):
            acc[span, :] = was + block

    def add(c, carry):
        src = pl.ds(pl.multiple_of(c * sub, sub), sub)
        at = me * cap + c
        arrived = [x[src, :].astype(jnp.float32) for x in (own, took, from_a, from_b, from_c)]
        arrived[3:] = [jnp.where(pick, arrived[3], arrived[4])]
        add_two([own_names[0, at], took_names[0, at]], arrived[:2])
        row, lane = at // LANES, at % LANES
        add_two([smem_names[0, row, lane], smem_names[1, row, lane]], arrived[2:])
        return carry

    lax.fori_loop(0, cap, add, 0, unroll=4)

    def emit(c, carry):
        rows = pl.ds(pl.multiple_of(c * 8, 8), 8)
        for t in range(sub):
            total = None
            for acc in accs:
                piece = acc[pl.ds(c * 8 * sub + t, 8, stride=sub), :]
                total = piece if total is None else total + piece
            out_ref[rows, t * LANES:(t + 1) * LANES] = total
        return carry

    lax.fori_loop(0, n_out // 8, emit, 0)


def owner_sums(me, own_names, took_names, tables, sub):
    block = tables[0].shape
    return pl.pallas_call(
        owner_kernel,
        out_shape=jax.ShapeDtypeStruct((OSLOT, sub * LANES), jnp.float32),
        grid_spec=pltpu.PrefetchScalarGridSpec(
            num_scalar_prefetch=3,
            grid=(1,),
            in_specs=[pl.BlockSpec(block, lambda i, *_: (0, 0))] * len(tables),
            out_specs=pl.BlockSpec((OSLOT, sub * LANES), lambda i, *_: (0, 0)),
            scratch_shapes=[pltpu.VMEM((OSLOT * sub, LANES), jnp.float32)] * 2
            + [
                pltpu.VMEM((2, NAME_ROWS, LANES), jnp.int32),
                pltpu.SMEM((2, NAME_ROWS, LANES), jnp.int32),
                pltpu.SemaphoreType.DMA,
            ],
        ),
        compiler_params=pltpu.CompilerParams(
            dimension_semantics=("arbitrary",), vmem_limit_bytes=40 * 1024 * 1024
        ),
        name="owner_sums",
    )(me, own_names, took_names, *tables)


def swap(x, axis, d):
    return lax.ppermute(x, axis, [(i, i ^ d) for i in range(lax.axis_size(axis))])


def panel_index(a_cols, groups, rf):
    flat = a_cols.reshape(-1)
    d = flat // rf // groups ^ lax.axis_index("blk")
    return (d % 2 * (lax.axis_size("blk") // 2) + d // 2) * rf + flat % rf


def transposed(p_tiles):
    rf, tile, width = p_tiles.shape
    return jnp.swapaxes(p_tiles, 1, 2).reshape(rf, width // 2, 2 * tile)


def direct(p_tiles):
    return [swap(p_tiles, "blk", d) for d in range(2, lax.axis_size("blk"), 2)]


def body(a_tiles, a_cols, p_tiles, route_list, out_slot):
    groups = lax.axis_size("grp")
    me = lax.axis_index("grp")
    rf, tile, cols = a_tiles.shape
    cap = out_slot.shape[1] // groups
    sub = tile * tile // LANES
    n_cols = a_cols.shape[1]
    middle = (me == 1) | (me == 2)
    takes = [(1, 0), (3, 1), (0, 2), (2, 3)]

    def take(x):
        return lax.ppermute(x, "grp", takes)

    far = direct(p_tiles)
    p_took = take(p_tiles)
    a_took = take(a_tiles)
    idx = panel_index(a_cols, groups, rf)
    lhs = transposed(p_tiles)
    route = route_list.reshape(-1)
    off = route // cap ^ me
    spare = 3 * cap
    there = jnp.where(middle, jnp.where(off > 1, off - 1, 0), off) * cap + route % cap
    unused = jnp.where(middle, off == 1, off > 1)
    places = jnp.where(unused, spare, there)
    ints = jnp.concatenate([a_cols, route_list], axis=1)
    ints = jnp.concatenate([ints, jnp.pad(out_slot, ((0, 0), (n_cols, 0)))], axis=0)

    far[0], idx, lhs, places, ints = lax.optimization_barrier((far[0], idx, lhs, places, ints))
    ints_took = take(ints)
    far_took = direct(p_took)
    half = len(far) // 2
    mine = [jnp.concatenate([p_tiles] + far[:half]), jnp.concatenate(far[half:])]
    other = [swap(x, "blk", 1) for x in mine]

    idx_took = panel_index(ints_took[:rf, :n_cols], groups, rf)
    route_took = ints_took[:rf, n_cols:].reshape(-1)
    names_took = ints_took[rf:, n_cols:]
    off = route_took // cap ^ me
    used = (off == 0) | ((off == 1) & middle)
    places_took = jnp.where(used, off * cap + route_took % cap, 2 * cap)
    lhs_took = transposed(p_took)

    other[-1], idx_took, places_took, lhs_took, names_took = lax.optimization_barrier(
        (other[-1], idx_took, places_took, lhs_took, names_took)
    )
    own, to_a, to_b = partial_sums(idx, places, [a_tiles], lhs, out_slot, mine + other, 3, cap)
    own, to_a, to_b, a_took, *far_took = lax.optimization_barrier((own, to_a, to_b, a_took, *far_took))
    from_a = lax.ppermute(to_a, "grp", [(0, 1), (3, 2), (1, 3), (2, 0)])
    from_b = lax.ppermute(to_b, "grp", [(1, 2), (2, 1)])
    mine = jnp.concatenate([p_took] + far_took)
    pieces = [mine, swap(mine, "blk", 1)]
    own_took, to_c = partial_sums(idx_took, places_took, [a_took], lhs_took, names_took, pieces, 2, cap)
    from_c = lax.ppermute(to_c, "grp", [(1, 0), (2, 3)])
    about = jnp.stack([me, middle.astype(me.dtype)])
    return owner_sums(about, out_slot, names_took, [own, own_took, from_a, from_b, from_c], sub)


def solution(mesh):
    in_specs = (
        P(("blk", "grp"), None, None),
        P(("blk", "grp"), None),
        P(("blk", "grp"), None, None),
        P(("blk", "grp"), None),
        P(("blk", "grp"), None),
    )
    out_specs = P(("blk", "grp"), None)
    return jax.shard_map(body, mesh=mesh, in_specs=in_specs, out_specs=out_specs, check_vma=False)
```

```python
import functools

import jax
import jax.numpy as jnp
from jax import lax
from jax.experimental import pallas as pl
from jax.experimental.pallas import tpu as pltpu
from jax.sharding import PartitionSpec as P

OSLOT = 128
LANES = 128
ACCS = 4
BATCH = 8
NAME_ROWS = 16


def partial_kernel(n_rows, n_pieces, n_outs, idx_ref, place_ref, lhs_ref, names_ref, *refs):
    row_parts, refs = refs[:n_rows], refs[n_rows:]
    pieces, refs = refs[:n_pieces], refs[n_pieces:]
    outs, refs = refs[:n_outs], refs[n_outs:]
    accs, (a_ref, panel, y_buf, w_buf, sems) = refs[:ACCS], refs[ACCS:]
    rf, tile, cols = a_ref.shape
    tiles = cols // tile
    width = panel.shape[2] // tile
    sub = tile * tile // LANES
    out_rows = outs[0].shape[0] - NAME_ROWS
    chunk = 256
    slots = rf * tiles

    copies = []
    for parts, whole in ((row_parts, a_ref), (pieces, panel)):
        at = 0
        for part in parts:
            copy = pltpu.make_async_copy(part, whole.at[pl.ds(at, part.shape[0])], sems.at[len(copies)])
            copy.start()
            copies.append(copy)
            at += part.shape[0]

    def clear(c, carry):
        rows = pl.ds(pl.multiple_of(c * chunk, chunk), chunk)
        for acc in accs:
            acc[rows, :] = jnp.zeros((chunk, LANES), jnp.float32)
        return carry

    lax.fori_loop(0, n_outs * out_rows // chunk, clear, 0)
    for acc in accs:
        acc[n_outs * out_rows:, :] = jnp.zeros((sub, LANES), jnp.float32)
    for copy in copies:
        copy.wait()

    lane = lax.broadcasted_iota(jnp.int32, (tile, LANES), 1)
    lo = lane < tile

    def first_products(slot):
        row, k = slot // tiles, slot % tiles
        both = a_ref[row, :, pl.ds(pl.multiple_of(k * tile, LANES), LANES)]
        none = jnp.zeros_like(both)
        left = jnp.concatenate([jnp.where(lo, both, none), jnp.where(lo, none, both)], axis=0)
        right = jnp.concatenate([panel[idx_ref[slot]], panel[idx_ref[slot + 1]]], axis=0)
        return jnp.dot(left, right, preferred_element_type=jnp.float32)

    def keep(u, y):
        for m in range(width // 2):
            x = y[:, m * LANES:(m + 1) * LANES]
            y_buf[u, :, 2 * m * LANES:(2 * m + 1) * LANES] = x.astype(jnp.bfloat16)
            y_buf[u, :, (2 * m + 1) * LANES:(2 * m + 2) * LANES] = pltpu.roll(x, tile, 1).astype(jnp.bfloat16)

    def second_product(slot, u):
        lhs = lhs_ref[slot // tiles]
        w = []
        for m in range(width // 2):
            x = y_buf[u, :, 2 * m * LANES:(2 * m + 1) * LANES]
            xr = y_buf[u, :, (2 * m + 1) * LANES:(2 * m + 2) * LANES]
            none = jnp.zeros_like(x)
            right = jnp.concatenate(
                [
                    jnp.concatenate([jnp.where(lo, x, none), jnp.where(lo, xr, none)], axis=1),
                    jnp.concatenate([jnp.where(lo, none, xr), jnp.where(lo, none, x)], axis=1),
                ],
                axis=0,
            )
            w.append(jnp.dot(lhs, right, preferred_element_type=jnp.float32))
        return w

    def add(slot, w):
        row, k = slot // tiles, slot % tiles
        for q in range(width):
            spans = []
            for s in range(width):
                place = place_ref[(row * width + s) * (tiles * width) + k * width + q]
                spans.append(pl.ds(pl.multiple_of(place * sub, sub), sub))
            old = [accs[s][spans[s], :] for s in range(width)]
            part = w[q // 2][:, q % 2 * LANES:(q % 2 + 1) * LANES]
            for s in range(width):
                accs[s][spans[s], :] = old[s] + part[s * sub:(s + 1) * sub]

    def keep_two(u, y):
        keep(u, y[:tile])
        keep(u + 1, y[tile:])

    def hold(w):
        for m, part in enumerate(w):
            w_buf[:, m * 2 * LANES:(m + 1) * 2 * LANES] = part

    for u in range(0, BATCH, 2):
        keep_two(u, first_products(u))
    hold(second_product(0, 0))

    def batch(c, carry):
        base = c * BATCH
        following = jnp.minimum(base + BATCH, slots - BATCH)
        w = [w_buf[:, m * 2 * LANES:(m + 1) * 2 * LANES] for m in range(width // 2)]
        for u in range(BATCH):
            if u % 2 == 0:
                upcoming = first_products(following + u)
            after = second_product(base + u + 1, u + 1) if u + 1 < BATCH else second_product(following, 0)
            add(base + u, w)
            if u % 2 == 1:
                keep_two(u - 1, upcoming)
            w = after
        hold(w)
        return carry

    lax.fori_loop(0, slots // BATCH, batch, 0)

    names = jnp.zeros((NAME_ROWS, LANES), jnp.float32)
    here = lax.broadcasted_iota(jnp.int32, (NAME_ROWS, LANES), 0)
    for n in range(names_ref.shape[1] // LANES):
        part = names_ref[:, n * LANES:(n + 1) * LANES].astype(jnp.float32)
        names = jnp.where(here == n, jnp.broadcast_to(part, names.shape), names)

    for n, out in enumerate(outs):

        def merge(c, carry):
            rows = pl.ds(pl.multiple_of(n * out_rows + c * chunk, chunk), chunk)
            total = accs[0][rows, :]
            for acc in accs[1:]:
                total = total + acc[rows, :]
            out[pl.ds(pl.multiple_of(c * chunk, chunk), chunk), :] = total.astype(out.dtype)
            return carry

        lax.fori_loop(0, out_rows // chunk, merge, 0)
        out[out_rows:, :] = names.astype(out.dtype)


def partial_sums(idx, places, row_parts, lhs, names, pieces, groups, cap):
    rf = lhs.shape[0]
    tile, cols = row_parts[0].shape[1:]
    sub = tile * tile // LANES
    width = pieces[0].shape[2]
    return pl.pallas_call(
        functools.partial(partial_kernel, len(row_parts), len(pieces), groups),
        out_shape=[jax.ShapeDtypeStruct((cap * sub + NAME_ROWS, LANES), jnp.bfloat16)] * groups,
        grid_spec=pltpu.PrefetchScalarGridSpec(
            num_scalar_prefetch=2,
            grid=(1,),
            in_specs=[
                pl.BlockSpec(lhs.shape, lambda i, *_: (0, 0, 0)),
                pl.BlockSpec(names.shape, lambda i, *_: (0, 0)),
            ]
            + [pl.BlockSpec(memory_space=pl.ANY)] * (len(row_parts) + len(pieces)),
            out_specs=[pl.BlockSpec((cap * sub + NAME_ROWS, LANES), lambda i, *_: (0, 0))] * groups,
            scratch_shapes=[pltpu.VMEM(((groups * cap + 1) * sub, LANES), jnp.float32)] * ACCS
            + [
                pltpu.VMEM((rf, tile, cols), jnp.bfloat16),
                pltpu.VMEM((sum(x.shape[0] for x in pieces), tile, width), jnp.bfloat16),
                pltpu.VMEM((BATCH, tile, 2 * width), jnp.bfloat16),
                pltpu.VMEM((width // 2, 2 * width), jnp.float32),
                pltpu.SemaphoreType.DMA((len(row_parts) + len(pieces),)),
            ],
        ),
        compiler_params=pltpu.CompilerParams(
            dimension_semantics=("arbitrary",), vmem_limit_bytes=56 * 1024 * 1024
        ),
        name="partial_sums",
    )(idx, places, lhs, names, *row_parts, *pieces)


def names_of(smem, part, at):
    return smem[part, at // LANES, at % LANES]


def early_kernel(me_ref, own_names, took_names, own, took, from_a, out_ref, *refs):
    accs, (vmem_names, smem_names, sem) = refs[:-3], refs[-3:]
    sub = out_ref.shape[0] // OSLOT
    cap = (own.shape[0] - NAME_ROWS) // sub
    chunk = 256
    me = me_ref[0]

    vmem_names[0] = from_a[pl.ds(cap * sub, NAME_ROWS), :].astype(jnp.float32).astype(jnp.int32)
    copy = pltpu.make_async_copy(vmem_names, smem_names, sem)
    copy.start()

    def clear(c, carry):
        rows = pl.ds(pl.multiple_of(c * chunk, chunk), chunk)
        for acc in accs:
            acc[rows, :] = jnp.zeros((chunk, LANES), jnp.float32)
        return carry

    lax.fori_loop(0, out_ref.shape[0] // chunk, clear, 0)
    copy.wait()

    def add(c, carry):
        src = pl.ds(pl.multiple_of(c * sub, sub), sub)
        at = me * cap + c
        names = [own_names[0, at], took_names[0, at], names_of(smem_names, 0, at)]
        spans = [pl.ds(pl.multiple_of(name * sub, sub), sub) for name in names]
        old = [acc[span, :] for acc, span in zip(accs, spans)]
        for acc, span, was, x in zip(accs, spans, old, (own, took, from_a)):
            acc[span, :] = was + x[src, :].astype(jnp.float32)
        return carry

    lax.fori_loop(0, cap, add, 0, unroll=4)

    def merge(c, carry):
        rows = pl.ds(pl.multiple_of(c * chunk, chunk), chunk)
        total = accs[0][rows, :]
        for acc in accs[1:]:
            total = total + acc[rows, :]
        out_ref[rows, :] = total
        return carry

    lax.fori_loop(0, out_ref.shape[0] // chunk, merge, 0)


def last_kernel(me_ref, table, from_b, from_c, out_ref, acc, vmem_names, smem_names, sems):
    n_out = out_ref.shape[0]
    sub = out_ref.shape[1] // LANES
    cap = (from_b.shape[0] - NAME_ROWS) // sub
    me, pick = me_ref[0], me_ref[1] == 1
    fill = pltpu.make_async_copy(table, acc, sems.at[0])
    fill.start()

    def arrived(rows):
        return jnp.where(pick, from_b[rows, :].astype(jnp.float32), from_c[rows, :].astype(jnp.float32))

    vmem_names[0] = arrived(pl.ds(cap * sub, NAME_ROWS)).astype(jnp.int32)
    copy = pltpu.make_async_copy(vmem_names, smem_names, sems.at[1])
    copy.start()
    copy.wait()
    fill.wait()

    def add(c, carry):
        at = me * cap + c
        span = pl.ds(pl.multiple_of(names_of(smem_names, 0, at) * sub, sub), sub)
        acc[span, :] += arrived(pl.ds(pl.multiple_of(c * sub, sub), sub))
        return carry

    lax.fori_loop(0, cap, add, 0, unroll=4)

    def emit(c, carry):
        rows = pl.ds(pl.multiple_of(c * 8, 8), 8)
        for t in range(sub):
            out_ref[rows, t * LANES:(t + 1) * LANES] = acc[pl.ds(c * 8 * sub + t, 8, stride=sub), :]
        return carry

    lax.fori_loop(0, n_out // 8, emit, 0)


def owner_sums(me, own_names, took_names, own, took, from_a, from_b, from_c, sub):
    block = pl.BlockSpec(own.shape, lambda i, *_: (0, 0))
    table = jax.ShapeDtypeStruct((OSLOT * sub, LANES), jnp.float32)
    names = [pltpu.VMEM((1, NAME_ROWS, LANES), jnp.int32), pltpu.SMEM((1, NAME_ROWS, LANES), jnp.int32)]
    early = pl.pallas_call(
        early_kernel,
        out_shape=table,
        grid_spec=pltpu.PrefetchScalarGridSpec(
            num_scalar_prefetch=3,
            grid=(1,),
            in_specs=[block] * 3,
            out_specs=pl.BlockSpec(table.shape, lambda i, *_: (0, 0)),
            scratch_shapes=[pltpu.VMEM(table.shape, jnp.float32)] * 3 + names + [pltpu.SemaphoreType.DMA],
        ),
        compiler_params=pltpu.CompilerParams(
            dimension_semantics=("arbitrary",), vmem_limit_bytes=40 * 1024 * 1024
        ),
        name="early_sums",
    )(me, own_names, took_names, own, took, from_a)
    return pl.pallas_call(
        last_kernel,
        out_shape=jax.ShapeDtypeStruct((OSLOT, sub * LANES), jnp.float32),
        grid_spec=pltpu.PrefetchScalarGridSpec(
            num_scalar_prefetch=1,
            grid=(1,),
            in_specs=[pl.BlockSpec(memory_space=pl.ANY), block, block],
            out_specs=pl.BlockSpec((OSLOT, sub * LANES), lambda i, *_: (0, 0)),
            scratch_shapes=[pltpu.VMEM(table.shape, jnp.float32)] + names + [pltpu.SemaphoreType.DMA((2,))],
        ),
        compiler_params=pltpu.CompilerParams(
            dimension_semantics=("arbitrary",), vmem_limit_bytes=40 * 1024 * 1024
        ),
        name="owner_sums",
    )(me, early, from_b, from_c)


def swap(x, axis, d):
    return lax.ppermute(x, axis, [(i, i ^ d) for i in range(lax.axis_size(axis))])


def panel_index(a_cols, groups, rf):
    flat = a_cols.reshape(-1)
    d = flat // rf // groups ^ lax.axis_index("blk")
    return (d % 2 * (lax.axis_size("blk") // 2) + d // 2) * rf + flat % rf


def transposed(p_tiles):
    rf, tile, width = p_tiles.shape
    return jnp.swapaxes(p_tiles, 1, 2).reshape(rf, width // 2, 2 * tile)


def direct(p_tiles):
    return [swap(p_tiles, "blk", d) for d in range(2, lax.axis_size("blk"), 2)]


def body(a_tiles, a_cols, p_tiles, route_list, out_slot):
    groups = lax.axis_size("grp")
    me = lax.axis_index("grp")
    rf, tile, cols = a_tiles.shape
    cap = out_slot.shape[1] // groups
    sub = tile * tile // LANES
    n_cols = a_cols.shape[1]
    middle = (me == 1) | (me == 2)
    takes = [(1, 0), (3, 1), (0, 2), (2, 3)]

    def take(x):
        return lax.ppermute(x, "grp", takes)

    ints = jnp.concatenate([a_cols, route_list], axis=1)
    ints_took = take(jnp.concatenate([ints, jnp.pad(out_slot, ((0, 0), (n_cols, 0)))], axis=0))
    a_sent, ints_took = lax.optimization_barrier((a_tiles, ints_took))
    far = direct(p_tiles)
    p_took = take(p_tiles)
    a_took = take(a_sent)
    idx = panel_index(a_cols, groups, rf)
    lhs = transposed(p_tiles)
    route = route_list.reshape(-1)
    off = route // cap ^ me
    spare = 3 * cap
    there = jnp.where(middle, jnp.where(off > 1, off - 1, 0), off) * cap + route % cap
    unused = jnp.where(middle, off == 1, off > 1)
    places = jnp.where(unused, spare, there)
    far[0], idx, lhs, places = lax.optimization_barrier((far[0], idx, lhs, places))
    far_took = direct(p_took)
    half = len(far) // 2
    mine = [jnp.concatenate([p_tiles] + far[:half]), jnp.concatenate(far[half:])]
    other = [swap(x, "blk", 1) for x in mine]

    idx_took = panel_index(ints_took[:rf, :n_cols], groups, rf)
    route_took = ints_took[:rf, n_cols:].reshape(-1)
    names_took = ints_took[rf:, n_cols:]
    off = route_took // cap ^ me
    used = (off == 0) | ((off == 1) & middle)
    places_took = jnp.where(used, off * cap + route_took % cap, 2 * cap)
    lhs_took = transposed(p_took)

    other[-1], idx_took, places_took, lhs_took, names_took = lax.optimization_barrier(
        (other[-1], idx_took, places_took, lhs_took, names_took)
    )
    own, to_a, to_b = partial_sums(idx, places, [a_tiles], lhs, out_slot, mine + other, 3, cap)
    own, to_a, to_b, a_took, *far_took = lax.optimization_barrier((own, to_a, to_b, a_took, *far_took))
    from_a = lax.ppermute(to_a, "grp", [(0, 1), (3, 2), (1, 3), (2, 0)])
    from_b = lax.ppermute(to_b, "grp", [(1, 2), (2, 1)])
    mine = jnp.concatenate([p_took] + far_took)
    pieces = [mine, swap(mine, "blk", 1)]
    own_took, to_c = partial_sums(idx_took, places_took, [a_took], lhs_took, names_took, pieces, 2, cap)
    from_c = lax.ppermute(to_c, "grp", [(1, 0), (2, 3)])
    about = jnp.stack([me, middle.astype(me.dtype)])
    return owner_sums(about, out_slot, names_took, own, own_took, from_a, from_b, from_c, sub)


def solution(mesh):
    in_specs = (
        P(("blk", "grp"), None, None),
        P(("blk", "grp"), None),
        P(("blk", "grp"), None, None),
        P(("blk", "grp"), None),
        P(("blk", "grp"), None),
    )
    out_specs = P(("blk", "grp"), None)
    return jax.shard_map(body, mesh=mesh, in_specs=in_specs, out_specs=out_specs, check_vma=False)
```

```python
import functools

import jax
import jax.numpy as jnp
from jax import lax
from jax.experimental import pallas as pl
from jax.experimental.pallas import tpu as pltpu
from jax.sharding import PartitionSpec as P

OSLOT = 128
LANES = 128
ACCS = 4
BATCH = 8
NAME_ROWS = 16


def log2(n):
    assert n & (n - 1) == 0
    return n.bit_length() - 1


def partial_kernel(n_rows, n_pieces, n_outs, groups, table_of, lhs_ref, ints_ref, *refs):
    row_parts, refs = refs[:n_rows], refs[n_rows:]
    pieces, refs = refs[:n_pieces], refs[n_pieces:]
    outs, refs = refs[:n_outs], refs[n_outs:]
    accs, (a_ref, panel, y_buf, w_buf, *numbers, sems) = refs[:ACCS], refs[ACCS:]
    place_vmem, idx_vmem, place_ref, idx_ref = numbers
    rf, tile, cols = a_ref.shape
    tiles = cols // tile
    width = panel.shape[2] // tile
    sub = tile * tile // LANES
    out_rows = outs[0].shape[0] - NAME_ROWS
    cap = out_rows // sub
    chunk = 8
    per_row = tiles // BATCH

    copies = []
    for parts, whole in ((row_parts, a_ref), (pieces, panel)):
        at = 0
        for part in parts:
            copy = pltpu.make_async_copy(part, whole.at[pl.ds(at, part.shape[0])], sems.at[len(copies)])
            copy.start()
            copies.append(copy)
            at += part.shape[0]

    n_places = width * tiles * width
    me, blk = lax.axis_index("grp"), lax.axis_index("blk")
    route = ints_ref[:rf, :n_places]
    owner = lax.shift_right_logical(route, jnp.int32(log2(cap)))
    table = table_of(owner ^ me, (me == 1) | (me == 2))
    place_vmem[...] = jnp.where(table < n_outs, table * cap + (route & (cap - 1)), n_outs * cap)
    cols = ints_ref[:rf, n_places:]
    d = lax.shift_right_logical(cols, jnp.int32(log2(rf * groups))) ^ blk
    half = panel.shape[0] // (2 * rf)
    idx_vmem[:, :tiles] = ((d & 1) * half + lax.shift_right_logical(d, jnp.int32(1))) * rf + (cols & (rf - 1))
    for n, (src, dst) in enumerate(((place_vmem, place_ref), (idx_vmem, idx_ref))):
        copy = pltpu.make_async_copy(src, dst, sems.at[n_rows + n_pieces + n])
        copy.start()
        copies.append(copy)

    def clear(c, carry):
        blocks = pl.ds(c * chunk, chunk)
        for acc in accs:
            acc[blocks] = jnp.zeros((chunk, sub, LANES), jnp.float32)
        return carry

    lax.fori_loop(0, n_outs * cap // chunk, clear, 0)
    for acc in accs:
        acc[n_outs * cap] = jnp.zeros((sub, LANES), jnp.float32)
    for copy in copies:
        copy.wait()

    lane = lax.broadcasted_iota(jnp.int32, (tile, LANES), 1)
    lo = lane < tile

    def place_of(batch):
        return lax.div(batch, jnp.int32(per_row)), lax.rem(batch, jnp.int32(per_row)) * BATCH

    def first_products(row, first, u):
        both = a_ref[row, :, pl.ds(pl.multiple_of(first * tile + u * tile, LANES), LANES)]
        none = jnp.zeros_like(both)
        left = jnp.concatenate([jnp.where(lo, both, none), jnp.where(lo, none, both)], axis=0)
        right = jnp.concatenate([panel[idx_ref[row, first + u]], panel[idx_ref[row, first + u + 1]]], axis=0)
        return jnp.dot(left, right, preferred_element_type=jnp.float32)

    def keep(u, y):
        for m in range(width // 2):
            x = y[:, m * LANES:(m + 1) * LANES]
            y_buf[u, :, 2 * m * LANES:(2 * m + 1) * LANES] = x.astype(jnp.bfloat16)
            y_buf[u, :, (2 * m + 1) * LANES:(2 * m + 2) * LANES] = pltpu.roll(x, tile, 1).astype(jnp.bfloat16)

    def second_product(row, u):
        lhs = lhs_ref[row]
        w = []
        for m in range(width // 2):
            x = y_buf[u, :, 2 * m * LANES:(2 * m + 1) * LANES]
            xr = y_buf[u, :, (2 * m + 1) * LANES:(2 * m + 2) * LANES]
            none = jnp.zeros_like(x)
            right = jnp.concatenate(
                [
                    jnp.concatenate([jnp.where(lo, x, none), jnp.where(lo, xr, none)], axis=1),
                    jnp.concatenate([jnp.where(lo, none, xr), jnp.where(lo, none, x)], axis=1),
                ],
                axis=0,
            )
            w.append(jnp.dot(lhs, right, preferred_element_type=jnp.float32))
        return w

    def add(row, at, w):
        for q in range(width):
            places = [place_ref[row, at + (s * tiles * width + q)] for s in range(width)]
            old = [acc[place] for acc, place in zip(accs, places)]
            part = w[q // 2][:, q % 2 * LANES:(q % 2 + 1) * LANES]
            for s, place in enumerate(places):
                accs[s][place] = old[s] + part[s * sub:(s + 1) * sub]

    def keep_two(u, y):
        keep(u, y[:tile])
        keep(u + 1, y[tile:])

    def hold(w):
        for m, part in enumerate(w):
            w_buf[:, m * 2 * LANES:(m + 1) * 2 * LANES] = part

    zero = jnp.int32(0)
    for u in range(0, BATCH, 2):
        keep_two(u, first_products(zero, zero, u))
    hold(second_product(zero, 0))

    def batch(c, carry):
        row, first = place_of(c)
        next_row, next_first = place_of(jnp.minimum(c + 1, rf * per_row - 1))
        w = [w_buf[:, m * 2 * LANES:(m + 1) * 2 * LANES] for m in range(width // 2)]
        for u in range(BATCH):
            if u % 2 == 0:
                upcoming = first_products(next_row, next_first, u)
            after = second_product(row, u + 1) if u + 1 < BATCH else second_product(next_row, 0)
            add(row, first * width + u * width, w)
            if u % 2 == 1:
                keep_two(u - 1, upcoming)
            w = after
        hold(w)
        return carry

    lax.fori_loop(0, rf * per_row, batch, 0)

    names = jnp.zeros((NAME_ROWS, LANES), jnp.float32)
    here = lax.broadcasted_iota(jnp.int32, (NAME_ROWS, LANES), 0)
    for n in range(groups * cap // LANES):
        part = ints_ref[rf:, n * LANES:(n + 1) * LANES].astype(jnp.float32)
        names = jnp.where(here == n, jnp.broadcast_to(part, names.shape), names)

    for n, out in enumerate(outs):

        def merge(c, carry):
            blocks = pl.ds(n * cap + c * chunk, chunk)
            total = accs[0][blocks]
            for acc in accs[1:]:
                total = total + acc[blocks]
            rows = pl.ds(pl.multiple_of(c * (chunk * sub), chunk * sub), chunk * sub)
            out[rows, :] = total.reshape(chunk * sub, LANES).astype(out.dtype)
            return carry

        lax.fori_loop(0, cap // chunk, merge, 0)
        out[out_rows:, :] = names.astype(out.dtype)


def partial_sums(ints, row_parts, lhs, pieces, table_of, tables, groups, cap):
    rf = lhs.shape[0]
    tile, cols = row_parts[0].shape[1:]
    sub = tile * tile // LANES
    width = pieces[0].shape[2]
    n_places = ints.shape[1] - cols // tile
    return pl.pallas_call(
        functools.partial(partial_kernel, len(row_parts), len(pieces), tables, groups, table_of),
        out_shape=[jax.ShapeDtypeStruct((cap * sub + NAME_ROWS, LANES), jnp.bfloat16)] * tables,
        grid_spec=pl.GridSpec(
            grid=(1,),
            in_specs=[
                pl.BlockSpec(lhs.shape, lambda i: (0, 0, 0)),
                pl.BlockSpec(ints.shape, lambda i: (0, 0)),
            ]
            + [pl.BlockSpec(memory_space=pl.ANY)] * (len(row_parts) + len(pieces)),
            out_specs=[pl.BlockSpec((cap * sub + NAME_ROWS, LANES), lambda i: (0, 0))] * tables,
            scratch_shapes=[pltpu.VMEM((tables * cap + 1, sub, LANES), jnp.float32)] * ACCS
            + [
                pltpu.VMEM((rf, tile, cols), jnp.bfloat16),
                pltpu.VMEM((sum(x.shape[0] for x in pieces), tile, width), jnp.bfloat16),
                pltpu.VMEM((BATCH, tile, 2 * width), jnp.bfloat16),
                pltpu.VMEM((width // 2, 2 * width), jnp.float32),
                pltpu.VMEM((rf, n_places), jnp.int32),
                pltpu.VMEM((rf, LANES), jnp.int32),
                pltpu.SMEM((rf, n_places), jnp.int32),
                pltpu.SMEM((rf, LANES), jnp.int32),
                pltpu.SemaphoreType.DMA((len(row_parts) + len(pieces) + 2,)),
            ],
        ),
        compiler_params=pltpu.CompilerParams(
            dimension_semantics=("arbitrary",), vmem_limit_bytes=56 * 1024 * 1024
        ),
        cost_estimate=pl.CostEstimate(flops=1, bytes_accessed=1, transcendentals=0),
        name="partial_sums",
    )(lhs, ints, *row_parts, *pieces)


def early_kernel(me_ref, own_names, ints_took, own, took, from_a, out_ref, *refs):
    accs, (vmem_names, smem_names, sem) = refs[:-3], refs[-3:]
    n_out, sub = out_ref.shape[:2]
    cap = (own.shape[0] - NAME_ROWS) // sub
    chunk = 8
    at = me_ref[0] * cap
    row, lane = lax.div(at, jnp.int32(LANES)), lax.rem(at, jnp.int32(LANES))

    vmem_names[...] = from_a[pl.ds(cap * sub, NAME_ROWS), :].astype(jnp.float32).astype(jnp.int32)
    copy = pltpu.make_async_copy(vmem_names, smem_names, sem)
    copy.start()

    def clear(c, carry):
        for acc in accs:
            acc[pl.ds(c * chunk, chunk)] = jnp.zeros((chunk, sub, LANES), jnp.float32)
        return carry

    lax.fori_loop(0, n_out // chunk, clear, 0)
    copy.wait()

    def add(c, carry):
        src = pl.ds(pl.multiple_of(c * sub, sub), sub)
        names = [own_names[0, at + c], ints_took[ints_took.shape[0] - 1, at + c], smem_names[row, lane + c]]
        old = [acc[name] for acc, name in zip(accs, names)]
        for acc, name, was, x in zip(accs, names, old, (own, took, from_a)):
            acc[name] = was + x[src, :].astype(jnp.float32)
        return carry

    lax.fori_loop(0, cap, add, 0, unroll=4)

    def merge(c, carry):
        blocks = pl.ds(c * chunk, chunk)
        total = accs[0][blocks]
        for acc in accs[1:]:
            total = total + acc[blocks]
        out_ref[blocks] = total
        return carry

    lax.fori_loop(0, n_out // chunk, merge, 0)


def last_kernel(me_ref, table, from_b, from_c, out_ref, acc, vmem_names, smem_names, sems):
    n_out, sub = acc.shape[:2]
    cap = (from_b.shape[0] - NAME_ROWS) // sub
    at, pick = me_ref[0] * cap, me_ref[1] == 1
    row, lane = lax.div(at, jnp.int32(LANES)), lax.rem(at, jnp.int32(LANES))
    fill = pltpu.make_async_copy(table, acc, sems.at[0])
    fill.start()

    def arrived(rows):
        return jnp.where(pick, from_b[rows, :].astype(jnp.float32), from_c[rows, :].astype(jnp.float32))

    vmem_names[...] = arrived(pl.ds(cap * sub, NAME_ROWS)).astype(jnp.int32)
    copy = pltpu.make_async_copy(vmem_names, smem_names, sems.at[1])
    copy.start()
    copy.wait()
    fill.wait()

    def add(c, carry):
        acc[smem_names[row, lane + c]] += arrived(pl.ds(pl.multiple_of(c * sub, sub), sub))
        return carry

    lax.fori_loop(0, cap, add, 0, unroll=4)
    flat = acc.reshape(n_out * sub, LANES)

    def emit(c, carry):
        rows = pl.ds(pl.multiple_of(c * 8, 8), 8)
        for t in range(sub):
            out_ref[rows, t * LANES:(t + 1) * LANES] = flat[pl.ds(c * (8 * sub) + t, 8, stride=sub), :]
        return carry

    lax.fori_loop(0, n_out // 8, emit, 0)


def owner_sums(me, own_names, ints_took, own, took, from_a, from_b, from_c, sub):
    block = pl.BlockSpec(own.shape, lambda i, *_: (0, 0))
    table = jax.ShapeDtypeStruct((OSLOT, sub, LANES), jnp.float32)
    names = [pltpu.VMEM((NAME_ROWS, LANES), jnp.int32), pltpu.SMEM((NAME_ROWS, LANES), jnp.int32)]
    early = pl.pallas_call(
        early_kernel,
        out_shape=table,
        grid_spec=pltpu.PrefetchScalarGridSpec(
            num_scalar_prefetch=3,
            grid=(1,),
            in_specs=[block] * 3,
            out_specs=pl.BlockSpec(table.shape, lambda i, *_: (0, 0, 0)),
            scratch_shapes=[pltpu.VMEM(table.shape, jnp.float32)] * 3 + names + [pltpu.SemaphoreType.DMA],
        ),
        compiler_params=pltpu.CompilerParams(
            dimension_semantics=("arbitrary",), vmem_limit_bytes=40 * 1024 * 1024
        ),
        name="early_sums",
    )(me, own_names, ints_took, own, took, from_a)
    return pl.pallas_call(
        last_kernel,
        out_shape=jax.ShapeDtypeStruct((OSLOT, sub * LANES), jnp.float32),
        grid_spec=pltpu.PrefetchScalarGridSpec(
            num_scalar_prefetch=1,
            grid=(1,),
            in_specs=[pl.BlockSpec(memory_space=pl.ANY), block, block],
            out_specs=pl.BlockSpec((OSLOT, sub * LANES), lambda i, *_: (0, 0)),
            scratch_shapes=[pltpu.VMEM(table.shape, jnp.float32)] + names + [pltpu.SemaphoreType.DMA((2,))],
        ),
        compiler_params=pltpu.CompilerParams(
            dimension_semantics=("arbitrary",), vmem_limit_bytes=40 * 1024 * 1024
        ),
        name="owner_sums",
    )(me, early, from_b, from_c)


def swap(x, axis, d):
    return lax.ppermute(x, axis, [(i, i ^ d) for i in range(lax.axis_size(axis))])


def transposed(p_tiles):
    rf, tile, width = p_tiles.shape
    return jnp.swapaxes(p_tiles, 1, 2).reshape(rf, width // 2, 2 * tile)


def direct(p_tiles, later):
    return [swap(later if d & (d - 1) else p_tiles, "blk", d) for d in range(2, lax.axis_size("blk"), 2)]


def body(a_tiles, a_cols, p_tiles, route_list, out_slot):
    groups = lax.axis_size("grp")
    me = lax.axis_index("grp")
    rf, tile, cols = a_tiles.shape
    cap = out_slot.shape[1] // groups
    sub = tile * tile // LANES
    middle = (me == 1) | (me == 2)
    takes = [(1, 0), (3, 1), (0, 2), (2, 3)]

    def take(x):
        return lax.ppermute(x, "grp", takes)

    ints = jnp.concatenate([route_list, a_cols], axis=1)
    ints = jnp.concatenate([ints, jnp.pad(out_slot, ((0, 0), (0, a_cols.shape[1])))], axis=0)
    ints_took = take(ints)
    a_sent, p_later, ints_took = lax.optimization_barrier((a_tiles, p_tiles, ints_took))
    far = direct(p_tiles, p_later)
    p_took = take(p_tiles)
    a_took = take(a_sent)
    lhs = transposed(p_later)
    far[0], p_took, lhs = lax.optimization_barrier((far[0], p_took, lhs))
    far_took = direct(p_took, p_took)
    lhs_took = transposed(p_took)
    half = len(far) // 2
    far[half], lhs_took = lax.optimization_barrier((far[half], lhs_took))
    mine = [jnp.concatenate([p_tiles] + far[:half]), jnp.concatenate(far[half:])]
    other = [swap(x, "blk", 1) for x in mine]
    near_took = swap(p_took, "blk", 1)

    def tables_own(off, middle):
        return jnp.where(middle, jnp.where(off == 0, 0, jnp.where(off == 1, 3, off - 1)), jnp.where(off < 2, off, 3))

    def tables_took(off, middle):
        return jnp.where((off == 0) | ((off == 1) & middle), off, 2)

    own, to_a, to_b = partial_sums(ints, [a_tiles], lhs, mine + other, tables_own, 3, groups, cap)
    own, to_a, to_b, a_took, near_took, *far_took = lax.optimization_barrier(
        (own, to_a, to_b, a_took, near_took, *far_took)
    )
    from_a = lax.ppermute(to_a, "grp", [(0, 1), (3, 2), (1, 3), (2, 0)])
    from_b = lax.ppermute(to_b, "grp", [(1, 2), (2, 1)])
    pieces = [p_took] + far_took + [near_took] + [swap(x, "blk", 1) for x in far_took]
    own_took, to_c = partial_sums(ints_took, [a_took], lhs_took, pieces, tables_took, 2, groups, cap)
    from_c = lax.ppermute(to_c, "grp", [(1, 0), (2, 3)])
    about = jnp.stack([me, middle.astype(me.dtype)])
    return owner_sums(about, out_slot, ints_took, own, own_took, from_a, from_b, from_c, sub)


def solution(mesh):
    in_specs = (
        P(("blk", "grp"), None, None),
        P(("blk", "grp"), None),
        P(("blk", "grp"), None, None),
        P(("blk", "grp"), None),
        P(("blk", "grp"), None),
    )
    out_specs = P(("blk", "grp"), None)
    return jax.shard_map(body, mesh=mesh, in_specs=in_specs, out_specs=out_specs, check_vma=False)
```

```python
import functools

import jax
import jax.numpy as jnp
from jax import lax
from jax.experimental import pallas as pl
from jax.experimental.pallas import tpu as pltpu
from jax.sharding import PartitionSpec as P

OSLOT = 128
LANES = 128
ACCS = 2
BATCH = 8
NAME_ROWS = 16


def log2(n):
    assert n & (n - 1) == 0
    return n.bit_length() - 1


def partial_kernel(n_rows, n_pieces, spans, cap, groups, table_of, lhs_ref, ints_ref, *refs):
    row_parts, refs = refs[:n_rows], refs[n_rows:]
    pieces, refs = refs[:n_pieces], refs[n_pieces:]
    outs, refs = refs[:len(spans)], refs[len(spans):]
    accs, (a_ref, panel, y_buf, w_buf, *numbers, sems) = refs[:ACCS], refs[ACCS:]
    place_vmem, idx_vmem, place_ref, idx_ref = numbers
    rf, tile, cols = a_ref.shape
    tiles = cols // tile
    width = panel.shape[2] // tile
    sub = tile * tile // LANES
    n_tables = accs[0].shape[0] // cap
    chunk = 8
    per_row = tiles // BATCH

    copies = []
    for parts, whole in ((row_parts, a_ref), (pieces, panel)):
        at = 0
        for part in parts:
            copy = pltpu.make_async_copy(part, whole.at[pl.ds(at, part.shape[0])], sems.at[len(copies)])
            copy.start()
            copies.append(copy)
            at += part.shape[0]

    n_places = width * tiles * width
    me, blk = lax.axis_index("grp"), lax.axis_index("blk")
    route = ints_ref[:rf, :n_places]
    owner = lax.shift_right_logical(route, jnp.int32(log2(cap)))
    table = table_of(owner ^ me, (me == 1) | (me == 2))
    place_vmem[...] = jnp.where(table < n_tables, table * cap + (route & (cap - 1)), n_tables * cap)
    cols = ints_ref[:rf, n_places:]
    d = lax.shift_right_logical(cols, jnp.int32(log2(rf * groups))) ^ blk
    half = panel.shape[0] // (2 * rf)
    idx_vmem[:, :tiles] = ((d & 1) * half + lax.shift_right_logical(d, jnp.int32(1))) * rf + (cols & (rf - 1))
    for n, (src, dst) in enumerate(((place_vmem, place_ref), (idx_vmem, idx_ref))):
        copy = pltpu.make_async_copy(src, dst, sems.at[n_rows + n_pieces + n])
        copy.start()
        copies.append(copy)

    def clear(c, carry):
        blocks = pl.ds(c * chunk, chunk)
        for acc in accs:
            acc[blocks] = jnp.zeros((chunk, sub, LANES), jnp.float32)
        return carry

    lax.fori_loop(0, n_tables * cap // chunk, clear, 0)
    for acc in accs:
        acc[n_tables * cap] = jnp.zeros((sub, LANES), jnp.float32)
    for copy in copies:
        copy.wait()

    lane = lax.broadcasted_iota(jnp.int32, (tile, LANES), 1)
    lo = lane < tile

    def place_of(batch):
        return lax.div(batch, jnp.int32(per_row)), lax.rem(batch, jnp.int32(per_row)) * BATCH

    def first_products(row, first, u):
        both = a_ref[row, :, pl.ds(pl.multiple_of(first * tile + u * tile, LANES), LANES)]
        none = jnp.zeros_like(both)
        left = jnp.concatenate([jnp.where(lo, both, none), jnp.where(lo, none, both)], axis=0)
        right = jnp.concatenate([panel[idx_ref[row, first + u]], panel[idx_ref[row, first + u + 1]]], axis=0)
        return jnp.dot(left, right, preferred_element_type=jnp.float32)

    def keep(u, y):
        for m in range(width // 2):
            x = y[:, m * LANES:(m + 1) * LANES]
            y_buf[u, :, 2 * m * LANES:(2 * m + 1) * LANES] = x.astype(jnp.bfloat16)
            y_buf[u, :, (2 * m + 1) * LANES:(2 * m + 2) * LANES] = pltpu.roll(x, tile, 1).astype(jnp.bfloat16)

    def second_product(row, u):
        lhs = lhs_ref[row]
        w = []
        for m in range(width // 2):
            x = y_buf[u, :, 2 * m * LANES:(2 * m + 1) * LANES]
            xr = y_buf[u, :, (2 * m + 1) * LANES:(2 * m + 2) * LANES]
            none = jnp.zeros_like(x)
            right = jnp.concatenate(
                [
                    jnp.concatenate([jnp.where(lo, x, none), jnp.where(lo, xr, none)], axis=1),
                    jnp.concatenate([jnp.where(lo, none, xr), jnp.where(lo, none, x)], axis=1),
                ],
                axis=0,
            )
            w.append(jnp.dot(lhs, right, preferred_element_type=jnp.float32))
        return w

    def add(row, at, w):
        for q in range(width):
            part = w[q // 2][:, q % 2 * LANES:(q % 2 + 1) * LANES]
            for s in range(0, width, ACCS):
                group = range(s, min(s + ACCS, width))
                places = [place_ref[row, at + (n * tiles * width + q)] for n in group]
                old = [acc[place] for acc, place in zip(accs, places)]
                for acc, place, was, n in zip(accs, places, old, group):
                    acc[place] = was + part[n * sub:(n + 1) * sub]

    def keep_two(u, y):
        keep(u, y[:tile])
        keep(u + 1, y[tile:])

    def hold(w):
        for m, part in enumerate(w):
            w_buf[:, m * 2 * LANES:(m + 1) * 2 * LANES] = part

    zero = jnp.int32(0)
    for u in range(0, BATCH, 2):
        keep_two(u, first_products(zero, zero, u))
    hold(second_product(zero, 0))

    def batch(c, carry):
        row, first = place_of(c)
        next_row, next_first = place_of(jnp.minimum(c + 1, rf * per_row - 1))
        w = [w_buf[:, m * 2 * LANES:(m + 1) * 2 * LANES] for m in range(width // 2)]
        for u in range(BATCH):
            if u % 2 == 0:
                upcoming = first_products(next_row, next_first, u)
            after = second_product(row, u + 1) if u + 1 < BATCH else second_product(next_row, 0)
            add(row, first * width + u * width, w)
            if u % 2 == 1:
                keep_two(u - 1, upcoming)
            w = after
        hold(w)
        return carry

    lax.fori_loop(0, rf * per_row, batch, 0)

    names = jnp.zeros((NAME_ROWS, LANES), jnp.float32)
    here = lax.broadcasted_iota(jnp.int32, (NAME_ROWS, LANES), 0)
    for n in range(groups * cap // LANES):
        part = ints_ref[rf:, n * LANES:(n + 1) * LANES].astype(jnp.float32)
        names = jnp.where(here == n, jnp.broadcast_to(part, names.shape), names)

    for (first, count), out in zip(spans, outs):

        def merge(c, carry):
            blocks = pl.ds(first + c * chunk, chunk)
            total = accs[0][blocks]
            for acc in accs[1:]:
                total = total + acc[blocks]
            rows = pl.ds(pl.multiple_of(c * (chunk * sub), chunk * sub), chunk * sub)
            out[rows, :] = total.reshape(chunk * sub, LANES).astype(out.dtype)
            return carry

        lax.fori_loop(0, count // chunk, merge, 0)
        out[count * sub:, :] = names.astype(out.dtype)


def partial_sums(ints, row_parts, lhs, pieces, table_of, tables, spans, groups, cap):
    rf = lhs.shape[0]
    tile, cols = row_parts[0].shape[1:]
    sub = tile * tile // LANES
    width = pieces[0].shape[2]
    n_places = ints.shape[1] - cols // tile
    return pl.pallas_call(
        functools.partial(partial_kernel, len(row_parts), len(pieces), spans, cap, groups, table_of),
        out_shape=[jax.ShapeDtypeStruct((n * sub + NAME_ROWS, LANES), jnp.bfloat16) for _, n in spans],
        grid_spec=pl.GridSpec(
            grid=(1,),
            in_specs=[
                pl.BlockSpec(lhs.shape, lambda i: (0, 0, 0)),
                pl.BlockSpec(ints.shape, lambda i: (0, 0)),
            ]
            + [pl.BlockSpec(memory_space=pl.ANY)] * (len(row_parts) + len(pieces)),
            out_specs=[pl.BlockSpec((n * sub + NAME_ROWS, LANES), lambda i: (0, 0)) for _, n in spans],
            scratch_shapes=[pltpu.VMEM((tables * cap + 1, sub, LANES), jnp.float32)] * ACCS
            + [
                pltpu.VMEM((rf, tile, cols), jnp.bfloat16),
                pltpu.VMEM((sum(x.shape[0] for x in pieces), tile, width), jnp.bfloat16),
                pltpu.VMEM((BATCH, tile, 2 * width), jnp.bfloat16),
                pltpu.VMEM((width // 2, 2 * width), jnp.float32),
                pltpu.VMEM((rf, n_places), jnp.int32),
                pltpu.VMEM((rf, LANES), jnp.int32),
                pltpu.SMEM((rf, n_places), jnp.int32),
                pltpu.SMEM((rf, LANES), jnp.int32),
                pltpu.SemaphoreType.DMA((len(row_parts) + len(pieces) + 2,)),
            ],
        ),
        compiler_params=pltpu.CompilerParams(
            dimension_semantics=("arbitrary",), vmem_limit_bytes=56 * 1024 * 1024
        ),
        cost_estimate=pl.CostEstimate(flops=1, bytes_accessed=1, transcendentals=0),
        name="partial_sums",
    )(lhs, ints, *row_parts, *pieces)


def early_kernel(me_ref, own_names, ints_took, own, took, from_a, from_b, out_ref, *refs):
    accs, (vmem_names, smem_names, sem) = refs[:-3], refs[-3:]
    n_out, sub = out_ref.shape[:2]
    cap, some = [(x.shape[0] - NAME_ROWS) // sub for x in (own, from_b)]
    chunk = 8
    at = me_ref[0] * cap
    row, lane = lax.div(at, jnp.int32(LANES)), lax.rem(at, jnp.int32(LANES))

    for n, (x, count) in enumerate(((from_a, cap), (from_b, some))):
        vmem_names[n] = x[pl.ds(count * sub, NAME_ROWS), :].astype(jnp.float32).astype(jnp.int32)
    copy = pltpu.make_async_copy(vmem_names, smem_names, sem)
    copy.start()

    def clear(c, carry):
        for acc in accs:
            acc[pl.ds(c * chunk, chunk)] = jnp.zeros((chunk, sub, LANES), jnp.float32)
        return carry

    lax.fori_loop(0, n_out // chunk, clear, 0)
    copy.wait()

    def add_to(c, names, tables):
        src = pl.ds(pl.multiple_of(c * sub, sub), sub)
        old = [acc[name] for acc, name in zip(accs, names)]
        for acc, name, was, x in zip(accs, names, old, tables):
            acc[name] = was + x[src, :].astype(jnp.float32)

    def add(c, carry):
        names = [own_names[0, at + c], ints_took[ints_took.shape[0] - 1, at + c], smem_names[0, row, lane + c]]
        add_to(c, names, (own, took, from_a))
        return carry

    def add_some(c, carry):
        add_to(c, [smem_names[1, row, lane + c]], [from_b])
        return carry

    lax.fori_loop(0, cap, add, 0, unroll=4)
    lax.fori_loop(0, some, add_some, 0, unroll=4)

    def merge(c, carry):
        blocks = pl.ds(c * chunk, chunk)
        total = accs[0][blocks]
        for acc in accs[1:]:
            total = total + acc[blocks]
        out_ref[blocks] = total
        return carry

    lax.fori_loop(0, n_out // chunk, merge, 0)


def last_kernel(cap, me_ref, table, from_b, from_c, out_ref, acc, rows_buf, vmem_names, smem_names, sems):
    n_out, sub = acc.shape[:2]
    rest = (from_b.shape[0] - NAME_ROWS) // sub
    at, pick = me_ref[0] * cap, me_ref[1] == 1
    row, lane = lax.div(at, jnp.int32(LANES)), lax.rem(at, jnp.int32(LANES)) + (cap - rest)
    fill = pltpu.make_async_copy(table, acc, sems.at[0])
    fill.start()

    def arrived(rows):
        return jnp.where(pick, from_b[rows, :].astype(jnp.float32), from_c[rows, :].astype(jnp.float32))

    vmem_names[...] = arrived(pl.ds(rest * sub, NAME_ROWS)).astype(jnp.int32)
    copy = pltpu.make_async_copy(vmem_names, smem_names, sems.at[1])
    copy.start()
    copy.wait()
    fill.wait()

    def add(c, carry):
        acc[smem_names[row, lane + c]] += arrived(pl.ds(pl.multiple_of(c * sub, sub), sub))
        return carry

    lax.fori_loop(0, rest, add, 0, unroll=4)
    flat = acc.reshape(n_out * sub, LANES)

    def emit(c, carry):
        rows = pl.ds(pl.multiple_of(c * 8, 8), 8)
        for t in range(sub):
            rows_buf[rows, t * LANES:(t + 1) * LANES] = flat[pl.ds(c * (8 * sub) + t, 8, stride=sub), :]
        return carry

    parts = sems.shape[0] - 2
    height = n_out // parts
    copies = []
    for n in range(parts):
        lax.fori_loop(n * height // 8, (n + 1) * height // 8, emit, 0)
        rows = pl.ds(n * height, height)
        copies.append(pltpu.make_async_copy(rows_buf.at[rows], out_ref.at[rows], sems.at[2 + n]))
        copies[-1].start()
    for copy in copies:
        copy.wait()


def owner_sums(me, own_names, ints_took, own, took, from_a, from_b, last_b, last_c, cap, sub):
    def whole(x):
        return pl.BlockSpec(x.shape, lambda i, *_: (0,) * len(x.shape))

    table = jax.ShapeDtypeStruct((OSLOT, sub, LANES), jnp.float32)
    early = pl.pallas_call(
        early_kernel,
        out_shape=table,
        grid_spec=pltpu.PrefetchScalarGridSpec(
            num_scalar_prefetch=3,
            grid=(1,),
            in_specs=[whole(x) for x in (own, took, from_a, from_b)],
            out_specs=whole(table),
            scratch_shapes=[pltpu.VMEM(table.shape, jnp.float32)] * 3
            + [
                pltpu.VMEM((2, NAME_ROWS, LANES), jnp.int32),
                pltpu.SMEM((2, NAME_ROWS, LANES), jnp.int32),
                pltpu.SemaphoreType.DMA,
            ],
        ),
        compiler_params=pltpu.CompilerParams(
            dimension_semantics=("arbitrary",), vmem_limit_bytes=40 * 1024 * 1024
        ),
        name="early_sums",
    )(me, own_names, ints_took, own, took, from_a, from_b)
    return pl.pallas_call(
        functools.partial(last_kernel, cap),
        out_shape=jax.ShapeDtypeStruct((OSLOT, sub * LANES), jnp.float32),
        grid_spec=pltpu.PrefetchScalarGridSpec(
            num_scalar_prefetch=1,
            grid=(1,),
            in_specs=[pl.BlockSpec(memory_space=pl.ANY), whole(last_b), whole(last_c)],
            out_specs=pl.BlockSpec(memory_space=pl.ANY),
            scratch_shapes=[
                pltpu.VMEM(table.shape, jnp.float32),
                pltpu.VMEM((OSLOT, sub * LANES), jnp.float32),
                pltpu.VMEM((NAME_ROWS, LANES), jnp.int32),
                pltpu.SMEM((NAME_ROWS, LANES), jnp.int32),
                pltpu.SemaphoreType.DMA((2 + 4,)),
            ],
        ),
        compiler_params=pltpu.CompilerParams(
            dimension_semantics=("arbitrary",), vmem_limit_bytes=40 * 1024 * 1024
        ),
        name="owner_sums",
    )(me, early, last_b, last_c)


def swap(x, axis, d):
    return lax.ppermute(x, axis, [(i, i ^ d) for i in range(lax.axis_size(axis))])


def transposed(p_tiles):
    rf, tile, width = p_tiles.shape
    return jnp.swapaxes(p_tiles, 1, 2).reshape(rf, width // 2, 2 * tile)


def direct(p_tiles):
    return [swap(p_tiles, "blk", d) for d in range(2, lax.axis_size("blk"), 2)]


def body(a_tiles, a_cols, p_tiles, route_list, out_slot):
    groups = lax.axis_size("grp")
    me = lax.axis_index("grp")
    rf, tile, cols = a_tiles.shape
    cap = out_slot.shape[1] // groups
    sub = tile * tile // LANES
    middle = (me == 1) | (me == 2)
    takes = [(1, 0), (3, 1), (0, 2), (2, 3)]

    def take(x):
        return lax.ppermute(x, "grp", takes)

    ints = jnp.concatenate([route_list, a_cols], axis=1)
    ints = jnp.concatenate([ints, jnp.pad(out_slot, ((0, 0), (0, a_cols.shape[1])))], axis=0)
    ints_took = take(ints)
    a_sent, p_later, ints_took = lax.optimization_barrier((a_tiles, p_tiles, ints_took))
    far = direct(p_tiles)
    p_took = take(p_tiles)
    a_took = take(a_sent)
    lhs = transposed(p_later)
    far[0], p_took, lhs = lax.optimization_barrier((far[0], p_took, lhs))
    far_took = direct(p_took)
    lhs_took = transposed(p_took)
    half = len(far) // 2
    far[half], lhs_took = lax.optimization_barrier((far[half], lhs_took))
    mine = [jnp.concatenate([p_tiles] + far[:half]), jnp.concatenate(far[half:])]
    other = [swap(x, "blk", 1) for x in mine]
    near_took = swap(p_took, "blk", 1)

    def tables_own(off, middle):
        ends = jnp.where(off < 2, off, jnp.where(off == 3, 2, 3))
        return jnp.where(middle, jnp.where(off == 0, 0, jnp.where(off == 1, 3, off - 1)), ends)

    def tables_took(off, middle):
        return jnp.where((off == 0) | ((off == 1) & middle), off, 2)

    first = cap // 4
    spans = ((0, cap), (cap, cap), (2 * cap, first), (2 * cap + first, cap - first))
    own, to_a, to_b, last_b = partial_sums(
        ints, [a_tiles], lhs, mine + other, tables_own, 3, spans, groups, cap
    )
    own, to_a, to_b, last_b, a_took, near_took, *far_took = lax.optimization_barrier(
        (own, to_a, to_b, last_b, a_took, near_took, *far_took)
    )
    from_b = lax.ppermute(to_b, "grp", [(1, 2), (2, 1), (0, 3), (3, 0)])
    from_a = lax.ppermute(to_a, "grp", [(0, 1), (3, 2), (1, 3), (2, 0)])
    last_b = lax.ppermute(last_b, "grp", [(1, 2), (2, 1)])
    relayed = [swap(x, "blk", 1) for x in far_took]
    relayed[-1], from_b = lax.optimization_barrier((relayed[-1], from_b))
    pieces = [p_took] + far_took + [near_took] + relayed
    spans = ((0, cap), (cap + first, cap - first))
    own_took, last_c = partial_sums(ints_took, [a_took], lhs_took, pieces, tables_took, 2, spans, groups, cap)
    last_c = lax.ppermute(last_c, "grp", [(1, 0), (2, 3)])
    about = jnp.stack([me, middle.astype(me.dtype)])
    return owner_sums(about, out_slot, ints_took, own, own_took, from_a, from_b, last_b, last_c, cap, sub)


def solution(mesh):
    in_specs = (
        P(("blk", "grp"), None, None),
        P(("blk", "grp"), None),
        P(("blk", "grp"), None, None),
        P(("blk", "grp"), None),
        P(("blk", "grp"), None),
    )
    out_specs = P(("blk", "grp"), None)
    return jax.shard_map(body, mesh=mesh, in_specs=in_specs, out_specs=out_specs, check_vma=False)
```

```python
import functools

import jax
import jax.numpy as jnp
from jax import lax
from jax.experimental import pallas as pl
from jax.experimental.pallas import tpu as pltpu
from jax.sharding import PartitionSpec as P

OSLOT = 128
LANES = 128
ACCS = 4
AHEAD = 2
NAME_ROWS = 16


def log2(n):
    assert n & (n - 1) == 0
    return n.bit_length() - 1


def partial_kernel(n_rows, n_pieces, spans, cap, groups, table_of, lhs_ref, ints_ref, *refs):
    row_parts, refs = refs[:n_rows], refs[n_rows:]
    pieces, refs = refs[:n_pieces], refs[n_pieces:]
    outs, refs = refs[:len(spans)], refs[len(spans):]
    accs, (a_ref, panel, y_buf, w_buf, *numbers, sems) = refs[:ACCS], refs[ACCS:]
    place_vmem, idx_vmem, place_ref, idx_ref = numbers
    rf, tile, cols = a_ref.shape
    tiles = cols // tile
    width = panel.shape[2] // tile
    sub = tile * tile // LANES
    n_tables = accs[0].shape[0] // cap
    chunk = 8

    copies = []
    for parts, whole in ((row_parts, a_ref), (pieces, panel)):
        at = 0
        for part in parts:
            copy = pltpu.make_async_copy(part, whole.at[pl.ds(at, part.shape[0])], sems.at[len(copies)])
            copy.start()
            copies.append(copy)
            at += part.shape[0]

    n_places = width * tiles * width
    me, blk = lax.axis_index("grp"), lax.axis_index("blk")
    route = ints_ref[:rf, :n_places]
    owner = lax.shift_right_logical(route, jnp.int32(log2(cap)))
    table = table_of(owner ^ me, (me == 1) | (me == 2))
    place_vmem[...] = jnp.where(table < n_tables, table * cap + (route & (cap - 1)), n_tables * cap)
    cols = ints_ref[:rf, n_places:]
    d = lax.shift_right_logical(cols, jnp.int32(log2(rf * groups))) ^ blk
    half = panel.shape[0] // (2 * rf)
    idx_vmem[:, :tiles] = ((d & 1) * half + lax.shift_right_logical(d, jnp.int32(1))) * rf + (cols & (rf - 1))
    for n, (src, dst) in enumerate(((place_vmem, place_ref), (idx_vmem, idx_ref))):
        copy = pltpu.make_async_copy(src, dst, sems.at[n_rows + n_pieces + n])
        copy.start()
        copies.append(copy)

    def clear(c, carry):
        blocks = pl.ds(c * chunk, chunk)
        for acc in accs:
            acc[blocks] = jnp.zeros((chunk, sub, LANES), jnp.float32)
        return carry

    lax.fori_loop(0, n_tables * cap // chunk, clear, 0)
    for acc in accs:
        acc[n_tables * cap] = jnp.zeros((sub, LANES), jnp.float32)
    for copy in copies:
        copy.wait()

    lane = lax.broadcasted_iota(jnp.int32, (tile, LANES), 1)
    lo = lane < tile

    def first_products(row, k):
        both = a_ref[row, :, k * tile:k * tile + LANES]
        none = jnp.zeros_like(both)
        left = jnp.concatenate([jnp.where(lo, both, none), jnp.where(lo, none, both)], axis=0)
        right = jnp.concatenate([panel[idx_ref[row, k]], panel[idx_ref[row, k + 1]]], axis=0)
        return jnp.dot(left, right, preferred_element_type=jnp.float32)

    def keep(u, y):
        for m in range(width // 2):
            x = y[:, m * LANES:(m + 1) * LANES]
            y_buf[u, :, 2 * m * LANES:(2 * m + 1) * LANES] = x.astype(jnp.bfloat16)
            y_buf[u, :, (2 * m + 1) * LANES:(2 * m + 2) * LANES] = pltpu.roll(x, tile, 1).astype(jnp.bfloat16)

    def second_product(row, u):
        lhs = lhs_ref[row]
        w = []
        for m in range(width // 2):
            x = y_buf[u, :, 2 * m * LANES:(2 * m + 1) * LANES]
            xr = y_buf[u, :, (2 * m + 1) * LANES:(2 * m + 2) * LANES]
            none = jnp.zeros_like(x)
            right = jnp.concatenate(
                [
                    jnp.concatenate([jnp.where(lo, x, none), jnp.where(lo, xr, none)], axis=1),
                    jnp.concatenate([jnp.where(lo, none, xr), jnp.where(lo, none, x)], axis=1),
                ],
                axis=0,
            )
            w.append(jnp.dot(lhs, right, preferred_element_type=jnp.float32))
        return w

    def add(row, k, w):
        for q in range(width):
            part = w[q // 2][:, q % 2 * LANES:(q % 2 + 1) * LANES]
            for s in range(0, width, ACCS):
                group = range(s, min(s + ACCS, width))
                places = [place_ref[row, (n * tiles + k) * width + q] for n in group]
                old = [acc[place] for acc, place in zip(accs, places)]
                for acc, place, was, n in zip(accs, places, old, group):
                    acc[place] = was + part[n * sub:(n + 1) * sub]

    def keep_two(u, y):
        keep(u, y[:tile])
        keep(u + 1, y[tile:])

    def hold(n, w):
        for m, part in enumerate(w):
            w_buf[n, :, m * 2 * LANES:(m + 1) * 2 * LANES] = part

    def held(n):
        return [w_buf[n, :, m * 2 * LANES:(m + 1) * 2 * LANES] for m in range(width // 2)]

    for k in range(0, tiles, 2):
        keep_two(k, first_products(0, k))
    for n in range(AHEAD):
        hold(n, second_product(0, n))

    def block_row(row, carry):
        following = jnp.minimum(row + 1, rf - 1)
        w = [held(n) for n in range(AHEAD)]
        for k in range(tiles):
            if k % 2 == 0:
                upcoming = first_products(following, k)
            ahead = k + AHEAD
            w.append(second_product(row, ahead) if ahead < tiles else second_product(following, ahead - tiles))
            add(row, k, w.pop(0))
            if k % 2 == 1:
                keep_two(k - 1, upcoming)
        for n in range(AHEAD):
            hold(n, w[n])
        return carry

    lax.fori_loop(0, rf, block_row, 0)

    names = jnp.zeros((NAME_ROWS, LANES), jnp.float32)
    here = lax.broadcasted_iota(jnp.int32, (NAME_ROWS, LANES), 0)
    for n in range(groups * cap // LANES):
        part = ints_ref[rf:, n * LANES:(n + 1) * LANES].astype(jnp.float32)
        names = jnp.where(here == n, jnp.broadcast_to(part, names.shape), names)

    for (first, count), out in zip(spans, outs):

        def merge(c, carry):
            blocks = pl.ds(first + c * chunk, chunk)
            total = accs[0][blocks]
            for acc in accs[1:]:
                total = total + acc[blocks]
            rows = pl.ds(pl.multiple_of(c * (chunk * sub), chunk * sub), chunk * sub)
            out[rows, :] = total.reshape(chunk * sub, LANES).astype(out.dtype)
            return carry

        lax.fori_loop(0, count // chunk, merge, 0)
        out[count * sub:, :] = names.astype(out.dtype)


def partial_sums(ints, row_parts, lhs, pieces, table_of, tables, spans, groups, cap):
    rf = lhs.shape[0]
    tile, cols = row_parts[0].shape[1:]
    sub = tile * tile // LANES
    width = pieces[0].shape[2]
    n_places = ints.shape[1] - cols // tile
    return pl.pallas_call(
        functools.partial(partial_kernel, len(row_parts), len(pieces), spans, cap, groups, table_of),
        out_shape=[jax.ShapeDtypeStruct((n * sub + NAME_ROWS, LANES), jnp.bfloat16) for _, n in spans],
        grid_spec=pl.GridSpec(
            grid=(1,),
            in_specs=[
                pl.BlockSpec(lhs.shape, lambda i: (0, 0, 0)),
                pl.BlockSpec(ints.shape, lambda i: (0, 0)),
            ]
            + [pl.BlockSpec(memory_space=pl.ANY)] * (len(row_parts) + len(pieces)),
            out_specs=[pl.BlockSpec((n * sub + NAME_ROWS, LANES), lambda i: (0, 0)) for _, n in spans],
            scratch_shapes=[pltpu.VMEM((tables * cap + 1, sub, LANES), jnp.float32)] * ACCS
            + [
                pltpu.VMEM((rf, tile, cols), jnp.bfloat16),
                pltpu.VMEM((sum(x.shape[0] for x in pieces), tile, width), jnp.bfloat16),
                pltpu.VMEM((cols // tile, tile, 2 * width), jnp.bfloat16),
                pltpu.VMEM((AHEAD, width // 2, 2 * width), jnp.float32),
                pltpu.VMEM((rf, n_places), jnp.int32),
                pltpu.VMEM((rf, LANES), jnp.int32),
                pltpu.SMEM((rf, n_places), jnp.int32),
                pltpu.SMEM((rf, LANES), jnp.int32),
                pltpu.SemaphoreType.DMA((len(row_parts) + len(pieces) + 2,)),
            ],
        ),
        compiler_params=pltpu.CompilerParams(
            dimension_semantics=("arbitrary",), vmem_limit_bytes=56 * 1024 * 1024
        ),
        cost_estimate=pl.CostEstimate(flops=1, bytes_accessed=1, transcendentals=0),
        name="partial_sums",
    )(lhs, ints, *row_parts, *pieces)


def early_kernel(me_ref, own_names, ints_took, own, took, from_a, from_b, out_ref, *refs):
    accs, (vmem_names, smem_names, sem) = refs[:-3], refs[-3:]
    n_out, sub = out_ref.shape[:2]
    cap, some = [(x.shape[0] - NAME_ROWS) // sub for x in (own, from_b)]
    chunk = 8
    at = me_ref[0] * cap
    row, lane = lax.div(at, jnp.int32(LANES)), lax.rem(at, jnp.int32(LANES))

    for n, (x, count) in enumerate(((from_a, cap), (from_b, some))):
        vmem_names[n] = x[pl.ds(count * sub, NAME_ROWS), :].astype(jnp.float32).astype(jnp.int32)
    copy = pltpu.make_async_copy(vmem_names, smem_names, sem)
    copy.start()

    def clear(c, carry):
        for acc in accs:
            acc[pl.ds(c * chunk, chunk)] = jnp.zeros((chunk, sub, LANES), jnp.float32)
        return carry

    lax.fori_loop(0, n_out // chunk, clear, 0)
    copy.wait()

    def add_to(c, names, tables):
        src = pl.ds(pl.multiple_of(c * sub, sub), sub)
        old = [acc[name] for acc, name in zip(accs, names)]
        for acc, name, was, x in zip(accs, names, old, tables):
            acc[name] = was + x[src, :].astype(jnp.float32)

    def add(c, carry):
        names = [own_names[0, at + c], ints_took[ints_took.shape[0] - 1, at + c], smem_names[0, row, lane + c]]
        add_to(c, names, (own, took, from_a))
        return carry

    def add_some(c, carry):
        add_to(c, [smem_names[1, row, lane + c]], [from_b])
        return carry

    lax.fori_loop(0, cap, add, 0, unroll=4)
    lax.fori_loop(0, some, add_some, 0, unroll=4)

    def merge(c, carry):
        blocks = pl.ds(c * chunk, chunk)
        total = accs[0][blocks]
        for acc in accs[1:]:
            total = total + acc[blocks]
        out_ref[blocks] = total
        return carry

    lax.fori_loop(0, n_out // chunk, merge, 0)


def last_kernel(cap, me_ref, table, from_b, from_c, out_ref, acc, rows_buf, vmem_names, smem_names, sems):
    n_out, sub = acc.shape[:2]
    rest = (from_b.shape[0] - NAME_ROWS) // sub
    at, pick = me_ref[0] * cap, me_ref[1] == 1
    row, lane = lax.div(at, jnp.int32(LANES)), lax.rem(at, jnp.int32(LANES)) + (cap - rest)
    fill = pltpu.make_async_copy(table, acc, sems.at[0])
    fill.start()

    def arrived(rows):
        return jnp.where(pick, from_b[rows, :].astype(jnp.float32), from_c[rows, :].astype(jnp.float32))

    vmem_names[...] = arrived(pl.ds(rest * sub, NAME_ROWS)).astype(jnp.int32)
    copy = pltpu.make_async_copy(vmem_names, smem_names, sems.at[1])
    copy.start()
    copy.wait()
    fill.wait()

    def add(c, carry):
        acc[smem_names[row, lane + c]] += arrived(pl.ds(pl.multiple_of(c * sub, sub), sub))
        return carry

    lax.fori_loop(0, rest, add, 0, unroll=4)
    flat = acc.reshape(n_out * sub, LANES)

    def emit(c, carry):
        rows = pl.ds(pl.multiple_of(c * 8, 8), 8)
        for t in range(sub):
            rows_buf[rows, t * LANES:(t + 1) * LANES] = flat[pl.ds(c * (8 * sub) + t, 8, stride=sub), :]
        return carry

    parts = sems.shape[0] - 2
    height = n_out // parts
    copies = []
    for n in range(parts):
        lax.fori_loop(n * height // 8, (n + 1) * height // 8, emit, 0)
        rows = pl.ds(n * height, height)
        copies.append(pltpu.make_async_copy(rows_buf.at[rows], out_ref.at[rows], sems.at[2 + n]))
        copies[-1].start()
    for copy in copies:
        copy.wait()


def owner_sums(me, own_names, ints_took, own, took, from_a, from_b, last_b, last_c, cap, sub):
    def whole(x):
        return pl.BlockSpec(x.shape, lambda i, *_: (0,) * len(x.shape))

    table = jax.ShapeDtypeStruct((OSLOT, sub, LANES), jnp.float32)
    early = pl.pallas_call(
        early_kernel,
        out_shape=table,
        grid_spec=pltpu.PrefetchScalarGridSpec(
            num_scalar_prefetch=3,
            grid=(1,),
            in_specs=[whole(x) for x in (own, took, from_a, from_b)],
            out_specs=whole(table),
            scratch_shapes=[pltpu.VMEM(table.shape, jnp.float32)] * 3
            + [
                pltpu.VMEM((2, NAME_ROWS, LANES), jnp.int32),
                pltpu.SMEM((2, NAME_ROWS, LANES), jnp.int32),
                pltpu.SemaphoreType.DMA,
            ],
        ),
        compiler_params=pltpu.CompilerParams(
            dimension_semantics=("arbitrary",), vmem_limit_bytes=40 * 1024 * 1024
        ),
        name="early_sums",
    )(me, own_names, ints_took, own, took, from_a, from_b)
    return pl.pallas_call(
        functools.partial(last_kernel, cap),
        out_shape=jax.ShapeDtypeStruct((OSLOT, sub * LANES), jnp.float32),
        grid_spec=pltpu.PrefetchScalarGridSpec(
            num_scalar_prefetch=1,
            grid=(1,),
            in_specs=[pl.BlockSpec(memory_space=pl.ANY), whole(last_b), whole(last_c)],
            out_specs=pl.BlockSpec(memory_space=pl.ANY),
            scratch_shapes=[
                pltpu.VMEM(table.shape, jnp.float32),
                pltpu.VMEM((OSLOT, sub * LANES), jnp.float32),
                pltpu.VMEM((NAME_ROWS, LANES), jnp.int32),
                pltpu.SMEM((NAME_ROWS, LANES), jnp.int32),
                pltpu.SemaphoreType.DMA((2 + 4,)),
            ],
        ),
        compiler_params=pltpu.CompilerParams(
            dimension_semantics=("arbitrary",), vmem_limit_bytes=40 * 1024 * 1024
        ),
        name="owner_sums",
    )(me, early, last_b, last_c)


def swap(x, axis, d):
    return lax.ppermute(x, axis, [(i, i ^ d) for i in range(lax.axis_size(axis))])


def transposed(p_tiles):
    rf, tile, width = p_tiles.shape
    return jnp.swapaxes(p_tiles, 1, 2).reshape(rf, width // 2, 2 * tile)


def direct(p_tiles):
    return [swap(p_tiles, "blk", d) for d in range(2, lax.axis_size("blk"), 2)]


def body(a_tiles, a_cols, p_tiles, route_list, out_slot):
    groups = lax.axis_size("grp")
    me = lax.axis_index("grp")
    rf, tile, cols = a_tiles.shape
    cap = out_slot.shape[1] // groups
    sub = tile * tile // LANES
    middle = (me == 1) | (me == 2)
    takes = [(1, 0), (3, 1), (0, 2), (2, 3)]

    def take(x):
        return lax.ppermute(x, "grp", takes)

    ints = jnp.concatenate([route_list, a_cols], axis=1)
    ints = jnp.concatenate([ints, jnp.pad(out_slot, ((0, 0), (0, a_cols.shape[1])))], axis=0)
    ints_took = take(ints)
    a_sent, p_later, ints_took = lax.optimization_barrier((a_tiles, p_tiles, ints_took))
    far = direct(p_tiles)
    p_took = take(p_tiles)
    a_took = take(a_sent)
    lhs = transposed(p_later)
    far[0], p_took, lhs = lax.optimization_barrier((far[0], p_took, lhs))
    far_took = direct(p_took)
    lhs_took = transposed(p_took)
    half = len(far) // 2
    far[half], lhs_took = lax.optimization_barrier((far[half], lhs_took))
    mine = [jnp.concatenate([p_tiles] + far[:half]), jnp.concatenate(far[half:])]
    other = [swap(x, "blk", 1) for x in mine]
    near_took = swap(p_took, "blk", 1)

    def tables_own(off, middle):
        ends = jnp.where(off < 2, off, jnp.where(off == 3, 2, 3))
        return jnp.where(middle, jnp.where(off == 0, 0, jnp.where(off == 1, 3, off - 1)), ends)

    def tables_took(off, middle):
        return jnp.where((off == 0) | ((off == 1) & middle), off, 2)

    first = cap // 4
    spans = ((0, cap), (cap, cap), (2 * cap, first), (2 * cap + first, cap - first))
    own, to_a, to_b, last_b = partial_sums(
        ints, [a_tiles], lhs, mine + other, tables_own, 3, spans, groups, cap
    )
    own, to_a, to_b, last_b, a_took, near_took, *far_took = lax.optimization_barrier(
        (own, to_a, to_b, last_b, a_took, near_took, *far_took)
    )
    from_b = lax.ppermute(to_b, "grp", [(1, 2), (2, 1), (0, 3), (3, 0)])
    from_a = lax.ppermute(to_a, "grp", [(0, 1), (3, 2), (1, 3), (2, 0)])
    last_b = lax.ppermute(last_b, "grp", [(1, 2), (2, 1)])
    pieces = [p_took] + far_took + [near_took] + [swap(x, "blk", 1) for x in far_took]
    spans = ((0, cap), (cap + first, cap - first))
    own_took, last_c = partial_sums(ints_took, [a_took], lhs_took, pieces, tables_took, 2, spans, groups, cap)
    own_took, last_c, from_b = lax.optimization_barrier((own_took, last_c, from_b))
    last_c = lax.ppermute(last_c, "grp", [(1, 0), (2, 3)])
    about = jnp.stack([me, middle.astype(me.dtype)])
    return owner_sums(about, out_slot, ints_took, own, own_took, from_a, from_b, last_b, last_c, cap, sub)


def solution(mesh):
    in_specs = (
        P(("blk", "grp"), None, None),
        P(("blk", "grp"), None),
        P(("blk", "grp"), None, None),
        P(("blk", "grp"), None),
        P(("blk", "grp"), None),
    )
    out_specs = P(("blk", "grp"), None)
    return jax.shard_map(body, mesh=mesh, in_specs=in_specs, out_specs=out_specs, check_vma=False)
```

```python
import functools

import jax
import jax.numpy as jnp
from jax import lax
from jax.experimental import pallas as pl
from jax.experimental.pallas import tpu as pltpu
from jax.sharding import PartitionSpec as P

OSLOT = 128
LANES = 128
ACCS = 4
AHEAD = 2
NAME_ROWS = 16
PART = 256


def log2(n):
    assert n & (n - 1) == 0
    return n.bit_length() - 1


def numbers_kernel(p_ref, route_ref, slot_ref, cols_ref, out_ref, wide):
    rf = p_ref.shape[0]
    out_ref[:rf] = p_ref[...]
    wide[...] = jnp.zeros_like(wide)
    cols = cols_ref[...]
    parts = (route_ref[...], slot_ref[...], lax.shift_right_logical(cols, jnp.int32(log2(PART))), cols & (PART - 1))
    for n, part in enumerate(parts):
        wide[n * rf:n * rf + part.shape[0], :part.shape[1]] = part.astype(jnp.float32)
    out_ref[rf] = wide[...].astype(out_ref.dtype)


def with_numbers(p_tiles, route_list, out_slot, a_cols):
    rf, tile, width = p_tiles.shape
    return pl.pallas_call(
        numbers_kernel,
        out_shape=jax.ShapeDtypeStruct((rf + 1, tile, width), p_tiles.dtype),
        scratch_shapes=[pltpu.VMEM((tile, width), jnp.float32)],
        compiler_params=pltpu.CompilerParams(vmem_limit_bytes=8 * 1024 * 1024),
        cost_estimate=pl.CostEstimate(flops=1, bytes_accessed=1, transcendentals=0),
        name="with_numbers",
    )(p_tiles, route_list, out_slot, a_cols)


def partial_kernel(n_rows, n_pieces, spans, cap, groups, table_of, lhs_in, packed, *refs):
    row_parts, refs = refs[:n_rows], refs[n_rows:]
    pieces, refs = refs[:n_pieces], refs[n_pieces:]
    outs, refs = refs[:len(spans)], refs[len(spans):]
    accs, (a_ref, lhs_ref, panel, y_buf, w_buf, *rest, sems) = refs[:ACCS], refs[ACCS:]
    packed_ref, place_vmem, idx_vmem, place_ref, idx_ref = rest
    rf, tile, cols = a_ref.shape
    tiles = cols // tile
    width = panel.shape[2] // tile
    sub = tile * tile // LANES
    n_tables = accs[0].shape[0] // cap
    chunk = 8

    copies = [
        pltpu.make_async_copy(packed.at[rf], packed_ref, sems.at[0]),
        pltpu.make_async_copy(lhs_in, lhs_ref, sems.at[1]),
    ]
    for parts, whole in ((row_parts, a_ref), (pieces, panel)):
        at = 0
        for part in parts:
            height = part.shape[0] // rf * rf if whole is panel else part.shape[0]
            copies.append(
                pltpu.make_async_copy(part.at[pl.ds(0, height)], whole.at[pl.ds(at, height)], sems.at[len(copies)])
            )
            at += height
    for copy in copies:
        copy.start()
    copies.pop(0).wait()

    me, blk = lax.axis_index("grp"), lax.axis_index("blk")
    numbers = packed_ref[...].astype(jnp.float32).astype(jnp.int32)
    route, names = numbers[:rf], numbers[rf:rf + 1].astype(jnp.float32)
    owner = lax.shift_right_logical(route, jnp.int32(log2(cap)))
    table = table_of(owner ^ me, (me == 1) | (me == 2))
    place_vmem[...] = jnp.where(table < n_tables, table * cap + (route & (cap - 1)), n_tables * cap)
    cols = numbers[2 * rf:3 * rf] * PART + numbers[3 * rf:4 * rf]
    d = lax.shift_right_logical(cols, jnp.int32(log2(rf * groups))) ^ blk
    half = panel.shape[0] // (2 * rf)
    idx_vmem[...] = ((d & 1) * half + lax.shift_right_logical(d, jnp.int32(1))) * rf + (cols & (rf - 1))
    for n, (src, dst) in enumerate(((place_vmem, place_ref), (idx_vmem, idx_ref))):
        copy = pltpu.make_async_copy(src, dst, sems.at[2 + n_rows + n_pieces + n])
        copy.start()
        copies.append(copy)

    def clear(c, carry):
        blocks = pl.ds(c * chunk, chunk)
        for acc in accs:
            acc[blocks] = jnp.zeros((chunk, sub, LANES), jnp.float32)
        return carry

    lax.fori_loop(0, n_tables * cap // chunk, clear, 0)
    for acc in accs:
        acc[n_tables * cap] = jnp.zeros((sub, LANES), jnp.float32)
    for copy in copies:
        copy.wait()

    lane = lax.broadcasted_iota(jnp.int32, (tile, LANES), 1)
    lo = lane < tile

    def first_products(row, k):
        both = a_ref[row, :, k * tile:k * tile + LANES]
        none = jnp.zeros_like(both)
        left = jnp.concatenate([jnp.where(lo, both, none), jnp.where(lo, none, both)], axis=0)
        right = jnp.concatenate([panel[idx_ref[row, k]], panel[idx_ref[row, k + 1]]], axis=0)
        return jnp.dot(left, right, preferred_element_type=jnp.float32)

    def keep(u, y):
        for m in range(width // 2):
            x = y[:, m * LANES:(m + 1) * LANES]
            y_buf[u, :, 2 * m * LANES:(2 * m + 1) * LANES] = x.astype(jnp.bfloat16)
            y_buf[u, :, (2 * m + 1) * LANES:(2 * m + 2) * LANES] = pltpu.roll(x, tile, 1).astype(jnp.bfloat16)

    def second_product(row, u):
        lhs = lhs_ref[row]
        w = []
        for m in range(width // 2):
            x = y_buf[u, :, 2 * m * LANES:(2 * m + 1) * LANES]
            xr = y_buf[u, :, (2 * m + 1) * LANES:(2 * m + 2) * LANES]
            none = jnp.zeros_like(x)
            right = jnp.concatenate(
                [
                    jnp.concatenate([jnp.where(lo, x, none), jnp.where(lo, xr, none)], axis=1),
                    jnp.concatenate([jnp.where(lo, none, xr), jnp.where(lo, none, x)], axis=1),
                ],
                axis=0,
            )
            w.append(jnp.dot(lhs, right, preferred_element_type=jnp.float32))
        return w

    def add(row, k, w):
        for q in range(width):
            part = w[q // 2][:, q % 2 * LANES:(q % 2 + 1) * LANES]
            for s in range(0, width, ACCS):
                group = range(s, min(s + ACCS, width))
                places = [place_ref[row, (n * tiles + k) * width + q] for n in group]
                old = [acc[place] for acc, place in zip(accs, places)]
                for acc, place, was, n in zip(accs, places, old, group):
                    acc[place] = was + part[n * sub:(n + 1) * sub]

    def keep_two(u, y):
        keep(u, y[:tile])
        keep(u + 1, y[tile:])

    def hold(n, w):
        for m, part in enumerate(w):
            w_buf[n, :, m * 2 * LANES:(m + 1) * 2 * LANES] = part

    def held(n):
        return [w_buf[n, :, m * 2 * LANES:(m + 1) * 2 * LANES] for m in range(width // 2)]

    for k in range(0, tiles, 2):
        keep_two(k, first_products(0, k))
    for n in range(AHEAD):
        hold(n, second_product(0, n))

    def block_row(row, carry):
        following = jnp.minimum(row + 1, rf - 1)
        w = [held(n) for n in range(AHEAD)]
        for k in range(tiles):
            if k % 2 == 0:
                upcoming = first_products(following, k)
            ahead = k + AHEAD
            w.append(second_product(row, ahead) if ahead < tiles else second_product(following, ahead - tiles))
            add(row, k, w.pop(0))
            if k % 2 == 1:
                keep_two(k - 1, upcoming)
        for n in range(AHEAD):
            hold(n, w[n])
        return carry

    lax.fori_loop(0, rf, block_row, 0)

    named = jnp.zeros((NAME_ROWS, LANES), jnp.float32)
    here = lax.broadcasted_iota(jnp.int32, named.shape, 0)
    for n in range(groups * cap // LANES):
        part = names[:, n * LANES:(n + 1) * LANES]
        named = jnp.where(here == n, jnp.broadcast_to(part, named.shape), named)

    for (first, count), out in zip(spans, outs):

        def merge(c, carry):
            blocks = pl.ds(first + c * chunk, chunk)
            total = accs[0][blocks]
            for acc in accs[1:]:
                total = total + acc[blocks]
            rows = pl.ds(pl.multiple_of(c * (chunk * sub), chunk * sub), chunk * sub)
            out[rows, :] = total.reshape(chunk * sub, LANES).astype(out.dtype)
            return carry

        lax.fori_loop(0, count // chunk, merge, 0)
        out[count * sub:, :] = named.astype(out.dtype)


def partial_sums(packed, row_parts, lhs, pieces, table_of, tables, spans, groups, cap):
    rf = lhs.shape[0]
    tile, cols = row_parts[0].shape[1:]
    sub = tile * tile // LANES
    width = pieces[0].shape[2]
    rows = sum(x.shape[0] // rf * rf for x in pieces)
    operands = [lhs, packed] + row_parts + pieces
    panel_bytes = rows * tile * width * 2
    return pl.pallas_call(
        functools.partial(partial_kernel, len(row_parts), len(pieces), spans, cap, groups, table_of),
        out_shape=[jax.ShapeDtypeStruct((n * sub + NAME_ROWS, LANES), jnp.bfloat16) for _, n in spans],
        grid_spec=pl.GridSpec(
            grid=(1,),
            in_specs=[pl.BlockSpec(memory_space=pl.ANY)] * len(operands),
            out_specs=[pl.BlockSpec((n * sub + NAME_ROWS, LANES), lambda i: (0, 0)) for _, n in spans],
            scratch_shapes=[pltpu.VMEM((tables * cap + 1, sub, LANES), jnp.float32)] * ACCS
            + [
                pltpu.VMEM((rf, tile, cols), jnp.bfloat16),
                pltpu.VMEM(lhs.shape, jnp.bfloat16),
                pltpu.VMEM((rows, tile, width), jnp.bfloat16),
                pltpu.VMEM((cols // tile, tile, 2 * width), jnp.bfloat16),
                pltpu.VMEM((AHEAD, width // 2, 2 * width), jnp.float32),
                pltpu.VMEM(packed.shape[1:], jnp.bfloat16),
                pltpu.VMEM((rf, width), jnp.int32),
                pltpu.VMEM((rf, width), jnp.int32),
                pltpu.SMEM((rf, width), jnp.int32),
                pltpu.SMEM((rf, width), jnp.int32),
                pltpu.SemaphoreType.DMA((len(operands) + 2,)),
            ],
        ),
        compiler_params=pltpu.CompilerParams(
            dimension_semantics=("arbitrary",), vmem_limit_bytes=26 * 1024 * 1024 + panel_bytes
        ),
        cost_estimate=pl.CostEstimate(flops=1, bytes_accessed=1, transcendentals=0),
        name="partial_sums",
    )(*operands)


def early_kernel(me_ref, *refs):
    tables, out_ref, accs, (vmem_names, smem_names, sem) = refs[:4], refs[4], refs[5:-3], refs[-3:]
    n_out, sub = out_ref.shape[:2]
    counts = [(x.shape[0] - NAME_ROWS) // sub for x in tables]
    cap, some = counts[0], counts[-1]
    chunk = 8
    at = me_ref[0] * cap
    row, lane = lax.div(at, jnp.int32(LANES)), lax.rem(at, jnp.int32(LANES))

    for n, (x, count) in enumerate(zip(tables, counts)):
        vmem_names[n] = x[pl.ds(count * sub, NAME_ROWS), :].astype(jnp.float32).astype(jnp.int32)
    copy = pltpu.make_async_copy(vmem_names, smem_names, sem)
    copy.start()

    def clear(c, carry):
        for acc in accs:
            acc[pl.ds(c * chunk, chunk)] = jnp.zeros((chunk, sub, LANES), jnp.float32)
        return carry

    lax.fori_loop(0, n_out // chunk, clear, 0)
    copy.wait()

    def add_to(c, numbers):
        src = pl.ds(pl.multiple_of(c * sub, sub), sub)
        names = [smem_names[n, row, lane + c] for n in numbers]
        old = [acc[name] for acc, name in zip(accs, names)]
        for acc, name, was, n in zip(accs, names, old, numbers):
            acc[name] = was + tables[n][src, :].astype(jnp.float32)

    def add(c, carry):
        add_to(c, (0, 1, 2))
        return carry

    def add_some(c, carry):
        add_to(c, (3,))
        return carry

    lax.fori_loop(0, cap, add, 0, unroll=4)
    lax.fori_loop(0, some, add_some, 0, unroll=4)

    def merge(c, carry):
        blocks = pl.ds(c * chunk, chunk)
        total = accs[0][blocks]
        for acc in accs[1:]:
            total = total + acc[blocks]
        out_ref[blocks] = total
        return carry

    lax.fori_loop(0, n_out // chunk, merge, 0)


def last_kernel(cap, me_ref, table, from_b, from_c, out_ref, acc, rows_buf, vmem_names, smem_names, sems):
    n_out, sub = acc.shape[:2]
    rest = (from_b.shape[0] - NAME_ROWS) // sub
    at, pick = me_ref[0] * cap, me_ref[1] == 1
    row, lane = lax.div(at, jnp.int32(LANES)), lax.rem(at, jnp.int32(LANES)) + (cap - rest)
    fill = pltpu.make_async_copy(table, acc, sems.at[0])
    fill.start()

    def arrived(rows):
        return jnp.where(pick, from_b[rows, :].astype(jnp.float32), from_c[rows, :].astype(jnp.float32))

    vmem_names[...] = arrived(pl.ds(rest * sub, NAME_ROWS)).astype(jnp.int32)
    copy = pltpu.make_async_copy(vmem_names, smem_names, sems.at[1])
    copy.start()
    copy.wait()
    fill.wait()

    def add(c, carry):
        acc[smem_names[row, lane + c]] += arrived(pl.ds(pl.multiple_of(c * sub, sub), sub))
        return carry

    lax.fori_loop(0, rest, add, 0, unroll=4)
    flat = acc.reshape(n_out * sub, LANES)

    def emit(c, carry):
        rows = pl.ds(pl.multiple_of(c * 8, 8), 8)
        for t in range(sub):
            rows_buf[rows, t * LANES:(t + 1) * LANES] = flat[pl.ds(c * (8 * sub) + t, 8, stride=sub), :]
        return carry

    parts = sems.shape[0] - 2
    height = n_out // parts
    copies = []
    for n in range(parts):
        lax.fori_loop(n * height // 8, (n + 1) * height // 8, emit, 0)
        rows = pl.ds(n * height, height)
        copies.append(pltpu.make_async_copy(rows_buf.at[rows], out_ref.at[rows], sems.at[2 + n]))
        copies[-1].start()
    for copy in copies:
        copy.wait()


def owner_sums(me, tables, last_b, last_c, cap, sub):
    def whole(x):
        return pl.BlockSpec(x.shape, lambda i, *_: (0,) * len(x.shape))

    table = jax.ShapeDtypeStruct((OSLOT, sub, LANES), jnp.float32)
    early = pl.pallas_call(
        early_kernel,
        out_shape=table,
        grid_spec=pltpu.PrefetchScalarGridSpec(
            num_scalar_prefetch=1,
            grid=(1,),
            in_specs=[whole(x) for x in tables],
            out_specs=whole(table),
            scratch_shapes=[pltpu.VMEM(table.shape, jnp.float32)] * (len(tables) - 1)
            + [
                pltpu.VMEM((len(tables), NAME_ROWS, LANES), jnp.int32),
                pltpu.SMEM((len(tables), NAME_ROWS, LANES), jnp.int32),
                pltpu.SemaphoreType.DMA,
            ],
        ),
        compiler_params=pltpu.CompilerParams(
            dimension_semantics=("arbitrary",), vmem_limit_bytes=20 * 1024 * 1024
        ),
        name="early_sums",
    )(me, *tables)
    return pl.pallas_call(
        functools.partial(last_kernel, cap),
        out_shape=jax.ShapeDtypeStruct((OSLOT, sub * LANES), jnp.float32),
        grid_spec=pltpu.PrefetchScalarGridSpec(
            num_scalar_prefetch=1,
            grid=(1,),
            in_specs=[pl.BlockSpec(memory_space=pl.ANY), whole(last_b), whole(last_c)],
            out_specs=pl.BlockSpec(memory_space=pl.ANY),
            scratch_shapes=[
                pltpu.VMEM(table.shape, jnp.float32),
                pltpu.VMEM((OSLOT, sub * LANES), jnp.float32),
                pltpu.VMEM((NAME_ROWS, LANES), jnp.int32),
                pltpu.SMEM((NAME_ROWS, LANES), jnp.int32),
                pltpu.SemaphoreType.DMA((2 + 4,)),
            ],
        ),
        compiler_params=pltpu.CompilerParams(
            dimension_semantics=("arbitrary",), vmem_limit_bytes=20 * 1024 * 1024
        ),
        name="owner_sums",
    )(me, early, last_b, last_c)


def swap(x, axis, d):
    return lax.ppermute(x, axis, [(i, i ^ d) for i in range(lax.axis_size(axis))])


def transposed(p_tiles):
    rf, tile, width = p_tiles.shape
    return jnp.swapaxes(p_tiles, 1, 2).reshape(rf, width // 2, 2 * tile)


def direct(p_tiles):
    return [swap(p_tiles, "blk", d) for d in range(2, lax.axis_size("blk"), 2)]


def body(a_tiles, a_cols, p_tiles, route_list, out_slot):
    groups = lax.axis_size("grp")
    me = lax.axis_index("grp")
    rf, tile, cols = a_tiles.shape
    cap = out_slot.shape[1] // groups
    sub = tile * tile // LANES
    middle = (me == 1) | (me == 2)
    takes = [(1, 0), (3, 1), (0, 2), (2, 3)]

    def take(x):
        return lax.ppermute(x, "grp", takes)

    packed = with_numbers(p_tiles, route_list, out_slot, a_cols)
    far = direct(p_tiles)
    p_took = take(packed)
    a_took = take(a_tiles)
    lhs = transposed(p_tiles)
    far[0], p_took, lhs = lax.optimization_barrier((far[0], p_took, lhs))
    far_took = direct(p_took)
    lhs_took = transposed(p_took[:rf])
    half = len(far) // 2
    far[half], lhs_took = lax.optimization_barrier((far[half], lhs_took))
    mine = [jnp.concatenate([p_tiles] + far[:half]), jnp.concatenate(far[half:])]
    other = [swap(x, "blk", 1) for x in mine]
    near_took = swap(p_took, "blk", 1)

    def tables_own(off, middle):
        ends = jnp.where(off < 2, off, jnp.where(off == 3, 2, 3))
        return jnp.where(middle, jnp.where(off == 0, 0, jnp.where(off == 1, 3, off - 1)), ends)

    def tables_took(off, middle):
        return jnp.where((off == 0) | ((off == 1) & middle), off, 2)

    first = cap // 4
    spans = ((0, cap), (cap, cap), (2 * cap, first), (2 * cap + first, cap - first))
    own, to_a, to_b, last_b = partial_sums(
        packed, [a_tiles], lhs, mine + other, tables_own, 3, spans, groups, cap
    )
    own, to_a, to_b, last_b, a_took, near_took, *far_took = lax.optimization_barrier(
        (own, to_a, to_b, last_b, a_took, near_took, *far_took)
    )
    from_b = lax.ppermute(to_b, "grp", [(1, 2), (2, 1), (0, 3), (3, 0)])
    from_a = lax.ppermute(to_a, "grp", [(0, 1), (3, 2), (1, 3), (2, 0)])
    last_b = lax.ppermute(last_b, "grp", [(1, 2), (2, 1)])
    pieces = [p_took] + far_took + [near_took] + [swap(x, "blk", 1) for x in far_took]
    spans = ((0, cap), (cap + first, cap - first))
    own_took, last_c = partial_sums(p_took, [a_took], lhs_took, pieces, tables_took, 2, spans, groups, cap)
    own_took, last_c, from_b = lax.optimization_barrier((own_took, last_c, from_b))
    last_c = lax.ppermute(last_c, "grp", [(1, 0), (2, 3)])
    about = jnp.stack([me, middle.astype(me.dtype)])
    return owner_sums(about, [own, own_took, from_a, from_b], last_b, last_c, cap, sub)


def solution(mesh):
    in_specs = (
        P(("blk", "grp"), None, None),
        P(("blk", "grp"), None),
        P(("blk", "grp"), None, None),
        P(("blk", "grp"), None),
        P(("blk", "grp"), None),
    )
    out_specs = P(("blk", "grp"), None)
    return jax.shard_map(body, mesh=mesh, in_specs=in_specs, out_specs=out_specs, check_vma=False)
```

```python
import functools

import jax
import jax.numpy as jnp
from jax import lax
from jax.experimental import pallas as pl
from jax.experimental.pallas import tpu as pltpu
from jax.sharding import PartitionSpec as P

OSLOT = 128
LANES = 128
ACCS = 4
AHEAD = 2
NAME_ROWS = 16


def log2(n):
    assert n & (n - 1) == 0
    return n.bit_length() - 1


def partial_kernel(n_rows, n_pieces, spans, cap, groups, table_of, ints, *refs):
    row_parts, refs = refs[:n_rows], refs[n_rows:]
    pieces, refs = refs[:n_pieces], refs[n_pieces:]
    outs, refs = refs[:len(spans)], refs[len(spans):]
    accs, (a_ref, lhs_ref, panel, y_buf, w_buf, *rest, sems) = refs[:ACCS], refs[ACCS:]
    ints_ref, place_vmem, idx_vmem, place_ref, idx_ref = rest
    rf, tile, cols = a_ref.shape
    tiles = cols // tile
    width = panel.shape[2] // tile
    sub = tile * tile // LANES
    n_tables = accs[0].shape[0] // cap
    chunk = 8

    copies = [pltpu.make_async_copy(ints, ints_ref, sems.at[0])]
    for parts, whole in ((row_parts, a_ref), (pieces, panel)):
        at = 0
        for part in parts:
            height = part.shape[0]
            copies.append(
                pltpu.make_async_copy(part, whole.at[pl.ds(at, height)], sems.at[len(copies)])
            )
            at += height
    for copy in copies:
        copy.start()
    copies.pop(0).wait()

    me, blk = lax.axis_index("grp"), lax.axis_index("blk")
    n_places = width * tiles * width
    route, names = ints_ref[:rf, :n_places], ints_ref[rf:, :n_places].astype(jnp.float32)
    owner = lax.shift_right_logical(route, jnp.int32(log2(cap)))
    table = table_of(owner ^ me, (me == 1) | (me == 2))
    place_vmem[...] = jnp.where(table < n_tables, table * cap + (route & (cap - 1)), n_tables * cap)
    cols = ints_ref[:rf, n_places:]
    d = lax.shift_right_logical(cols, jnp.int32(log2(rf * groups))) ^ blk
    half = panel.shape[0] // (2 * rf)
    idx_vmem[:, :tiles] = ((d & 1) * half + lax.shift_right_logical(d, jnp.int32(1))) * rf + (cols & (rf - 1))
    for n, (src, dst) in enumerate(((place_vmem, place_ref), (idx_vmem, idx_ref))):
        copy = pltpu.make_async_copy(src, dst, sems.at[1 + n_rows + n_pieces + n])
        copy.start()
        copies.append(copy)

    def clear(c, carry):
        blocks = pl.ds(c * chunk, chunk)
        for acc in accs:
            acc[blocks] = jnp.zeros((chunk, sub, LANES), jnp.float32)
        return carry

    lax.fori_loop(0, n_tables * cap // chunk, clear, 0)
    for acc in accs:
        acc[n_tables * cap] = jnp.zeros((sub, LANES), jnp.float32)
    for copy in copies:
        copy.wait()

    columns = width * tile
    from_col = lax.broadcasted_iota(jnp.int32, (columns, columns), 0)
    to_col = lax.broadcasted_iota(jnp.int32, (columns, columns), 1)
    wanted = jnp.where(to_col < columns // 2, 2 * to_col, 2 * to_col - columns + 1)
    chosen = jnp.where(from_col == wanted, 1.0, 0.0).astype(jnp.bfloat16)
    for row in range(rf):
        split = jnp.dot(panel[row], chosen, preferred_element_type=jnp.float32)
        stacked = jnp.concatenate([split[:, :columns // 2], split[:, columns // 2:]], axis=0)
        lhs_ref[row] = jnp.transpose(stacked).astype(jnp.bfloat16)

    lane = lax.broadcasted_iota(jnp.int32, (tile, LANES), 1)
    lo = lane < tile

    def first_products(row, k):
        both = a_ref[row, :, k * tile:k * tile + LANES]
        none = jnp.zeros_like(both)
        left = jnp.concatenate([jnp.where(lo, both, none), jnp.where(lo, none, both)], axis=0)
        right = jnp.concatenate([panel[idx_ref[row, k]], panel[idx_ref[row, k + 1]]], axis=0)
        return jnp.dot(left, right, preferred_element_type=jnp.float32)

    def keep(u, y):
        for m in range(width // 2):
            x = y[:, m * LANES:(m + 1) * LANES]
            y_buf[u, :, 2 * m * LANES:(2 * m + 1) * LANES] = x.astype(jnp.bfloat16)
            y_buf[u, :, (2 * m + 1) * LANES:(2 * m + 2) * LANES] = pltpu.roll(x, tile, 1).astype(jnp.bfloat16)

    def second_product(row, u):
        lhs = lhs_ref[row]
        w = []
        for m in range(width // 2):
            x = y_buf[u, :, 2 * m * LANES:(2 * m + 1) * LANES]
            xr = y_buf[u, :, (2 * m + 1) * LANES:(2 * m + 2) * LANES]
            none = jnp.zeros_like(x)
            right = jnp.concatenate(
                [
                    jnp.concatenate([jnp.where(lo, x, none), jnp.where(lo, xr, none)], axis=1),
                    jnp.concatenate([jnp.where(lo, none, xr), jnp.where(lo, none, x)], axis=1),
                ],
                axis=0,
            )
            w.append(jnp.dot(lhs, right, preferred_element_type=jnp.float32))
        return w

    def add(row, k, w):
        for q in range(width):
            part = w[q // 2][:, q % 2 * LANES:(q % 2 + 1) * LANES]
            for s in range(0, width, ACCS):
                group = range(s, min(s + ACCS, width))
                places = [place_ref[row, (n * tiles + k) * width + q] for n in group]
                old = [acc[place] for acc, place in zip(accs, places)]
                for acc, place, was, n in zip(accs, places, old, group):
                    acc[place] = was + part[n * sub:(n + 1) * sub]

    def keep_two(u, y):
        keep(u, y[:tile])
        keep(u + 1, y[tile:])

    def hold(n, w):
        for m, part in enumerate(w):
            w_buf[n, :, m * 2 * LANES:(m + 1) * 2 * LANES] = part

    def held(n):
        return [w_buf[n, :, m * 2 * LANES:(m + 1) * 2 * LANES] for m in range(width // 2)]

    for k in range(0, tiles, 2):
        keep_two(k, first_products(0, k))
    for n in range(AHEAD):
        hold(n, second_product(0, n))

    def block_row(row, carry):
        following = jnp.minimum(row + 1, rf - 1)
        w = [held(n) for n in range(AHEAD)]
        for k in range(tiles):
            if k % 2 == 0:
                upcoming = first_products(following, k)
            ahead = k + AHEAD
            w.append(second_product(row, ahead) if ahead < tiles else second_product(following, ahead - tiles))
            add(row, k, w.pop(0))
            if k % 2 == 1:
                keep_two(k - 1, upcoming)
        for n in range(AHEAD):
            hold(n, w[n])
        return carry

    lax.fori_loop(0, rf, block_row, 0)

    named = jnp.zeros((NAME_ROWS, LANES), jnp.float32)
    here = lax.broadcasted_iota(jnp.int32, named.shape, 0)
    for n in range(groups * cap // LANES):
        part = names[:, n * LANES:(n + 1) * LANES]
        named = jnp.where(here == n, jnp.broadcast_to(part, named.shape), named)

    for (first, count), out in zip(spans, outs):

        def merge(c, carry):
            blocks = pl.ds(first + c * chunk, chunk)
            total = accs[0][blocks]
            for acc in accs[1:]:
                total = total + acc[blocks]
            rows = pl.ds(pl.multiple_of(c * (chunk * sub), chunk * sub), chunk * sub)
            out[rows, :] = total.reshape(chunk * sub, LANES).astype(out.dtype)
            return carry

        lax.fori_loop(0, count // chunk, merge, 0)
        out[count * sub:, :] = named.astype(out.dtype)


def partial_sums(ints, row_parts, pieces, table_of, tables, spans, groups, cap):
    rf, tile, cols = row_parts[0].shape
    sub = tile * tile // LANES
    width = pieces[0].shape[2]
    rows = sum(x.shape[0] for x in pieces)
    n_places = ints.shape[1] - cols // tile
    operands = [ints] + row_parts + pieces
    panel_bytes = rows * tile * width * 2
    return pl.pallas_call(
        functools.partial(partial_kernel, len(row_parts), len(pieces), spans, cap, groups, table_of),
        out_shape=[jax.ShapeDtypeStruct((n * sub + NAME_ROWS, LANES), jnp.bfloat16) for _, n in spans],
        grid_spec=pl.GridSpec(
            grid=(1,),
            in_specs=[pl.BlockSpec(memory_space=pl.ANY)] * len(operands),
            out_specs=[pl.BlockSpec((n * sub + NAME_ROWS, LANES), lambda i: (0, 0)) for _, n in spans],
            scratch_shapes=[pltpu.VMEM((tables * cap + 1, sub, LANES), jnp.float32)] * ACCS
            + [
                pltpu.VMEM((rf, tile, cols), jnp.bfloat16),
                pltpu.VMEM((rf, width // 2, 2 * tile), jnp.bfloat16),
                pltpu.VMEM((rows, tile, width), jnp.bfloat16),
                pltpu.VMEM((cols // tile, tile, 2 * width), jnp.bfloat16),
                pltpu.VMEM((AHEAD, width // 2, 2 * width), jnp.float32),
                pltpu.VMEM(ints.shape, jnp.int32),
                pltpu.VMEM((rf, n_places), jnp.int32),
                pltpu.VMEM((rf, LANES), jnp.int32),
                pltpu.SMEM((rf, n_places), jnp.int32),
                pltpu.SMEM((rf, LANES), jnp.int32),
                pltpu.SemaphoreType.DMA((len(operands) + 2,)),
            ],
        ),
        compiler_params=pltpu.CompilerParams(
            dimension_semantics=("arbitrary",), vmem_limit_bytes=26 * 1024 * 1024 + panel_bytes
        ),
        cost_estimate=pl.CostEstimate(flops=1, bytes_accessed=1, transcendentals=0),
        name="partial_sums",
    )(*operands)


def early_kernel(me_ref, *refs):
    tables, out_ref, accs, (vmem_names, smem_names, sem) = refs[:4], refs[4], refs[5:-3], refs[-3:]
    n_out, sub = out_ref.shape[:2]
    counts = [(x.shape[0] - NAME_ROWS) // sub for x in tables]
    cap, some = counts[0], counts[-1]
    chunk = 8
    at = me_ref[0] * cap
    row, lane = lax.div(at, jnp.int32(LANES)), lax.rem(at, jnp.int32(LANES))

    for n, (x, count) in enumerate(zip(tables, counts)):
        vmem_names[n] = x[pl.ds(count * sub, NAME_ROWS), :].astype(jnp.float32).astype(jnp.int32)
    copy = pltpu.make_async_copy(vmem_names, smem_names, sem)
    copy.start()

    def clear(c, carry):
        for acc in accs:
            acc[pl.ds(c * chunk, chunk)] = jnp.zeros((chunk, sub, LANES), jnp.float32)
        return carry

    lax.fori_loop(0, n_out // chunk, clear, 0)
    copy.wait()

    def add_to(c, numbers):
        src = pl.ds(pl.multiple_of(c * sub, sub), sub)
        names = [smem_names[n, row, lane + c] for n in numbers]
        old = [acc[name] for acc, name in zip(accs, names)]
        for acc, name, was, n in zip(accs, names, old, numbers):
            acc[name] = was + tables[n][src, :].astype(jnp.float32)

    def add(c, carry):
        add_to(c, (0, 1, 2))
        return carry

    def add_some(c, carry):
        add_to(c, (3,))
        return carry

    lax.fori_loop(0, cap, add, 0, unroll=4)
    lax.fori_loop(0, some, add_some, 0, unroll=4)

    def merge(c, carry):
        blocks = pl.ds(c * chunk, chunk)
        total = accs[0][blocks]
        for acc in accs[1:]:
            total = total + acc[blocks]
        out_ref[blocks] = total
        return carry

    lax.fori_loop(0, n_out // chunk, merge, 0)


def last_kernel(cap, me_ref, table, from_b, from_c, out_ref, acc, rows_buf, vmem_names, smem_names, sems):
    n_out, sub = acc.shape[:2]
    rest = (from_b.shape[0] - NAME_ROWS) // sub
    at, pick = me_ref[0] * cap, me_ref[1] == 1
    row, lane = lax.div(at, jnp.int32(LANES)), lax.rem(at, jnp.int32(LANES)) + (cap - rest)
    fill = pltpu.make_async_copy(table, acc, sems.at[0])
    fill.start()

    def arrived(rows):
        return jnp.where(pick, from_b[rows, :].astype(jnp.float32), from_c[rows, :].astype(jnp.float32))

    vmem_names[...] = arrived(pl.ds(rest * sub, NAME_ROWS)).astype(jnp.int32)
    copy = pltpu.make_async_copy(vmem_names, smem_names, sems.at[1])
    copy.start()
    copy.wait()
    fill.wait()

    def add(c, carry):
        acc[smem_names[row, lane + c]] += arrived(pl.ds(pl.multiple_of(c * sub, sub), sub))
        return carry

    lax.fori_loop(0, rest, add, 0, unroll=4)
    flat = acc.reshape(n_out * sub, LANES)

    def emit(c, carry):
        rows = pl.ds(pl.multiple_of(c * 8, 8), 8)
        for t in range(sub):
            rows_buf[rows, t * LANES:(t + 1) * LANES] = flat[pl.ds(c * (8 * sub) + t, 8, stride=sub), :]
        return carry

    parts = sems.shape[0] - 2
    height = n_out // parts
    copies = []
    for n in range(parts):
        lax.fori_loop(n * height // 8, (n + 1) * height // 8, emit, 0)
        rows = pl.ds(n * height, height)
        copies.append(pltpu.make_async_copy(rows_buf.at[rows], out_ref.at[rows], sems.at[2 + n]))
        copies[-1].start()
    for copy in copies:
        copy.wait()


def owner_sums(me, tables, last_b, last_c, cap, sub):
    def whole(x):
        return pl.BlockSpec(x.shape, lambda i, *_: (0,) * len(x.shape))

    table = jax.ShapeDtypeStruct((OSLOT, sub, LANES), jnp.float32)
    early = pl.pallas_call(
        early_kernel,
        out_shape=table,
        grid_spec=pltpu.PrefetchScalarGridSpec(
            num_scalar_prefetch=1,
            grid=(1,),
            in_specs=[whole(x) for x in tables],
            out_specs=whole(table),
            scratch_shapes=[pltpu.VMEM(table.shape, jnp.float32)] * (len(tables) - 1)
            + [
                pltpu.VMEM((len(tables), NAME_ROWS, LANES), jnp.int32),
                pltpu.SMEM((len(tables), NAME_ROWS, LANES), jnp.int32),
                pltpu.SemaphoreType.DMA,
            ],
        ),
        compiler_params=pltpu.CompilerParams(
            dimension_semantics=("arbitrary",), vmem_limit_bytes=20 * 1024 * 1024
        ),
        name="early_sums",
    )(me, *tables)
    return pl.pallas_call(
        functools.partial(last_kernel, cap),
        out_shape=jax.ShapeDtypeStruct((OSLOT, sub * LANES), jnp.float32),
        grid_spec=pltpu.PrefetchScalarGridSpec(
            num_scalar_prefetch=1,
            grid=(1,),
            in_specs=[pl.BlockSpec(memory_space=pl.ANY), whole(last_b), whole(last_c)],
            out_specs=pl.BlockSpec(memory_space=pl.ANY),
            scratch_shapes=[
                pltpu.VMEM(table.shape, jnp.float32),
                pltpu.VMEM((OSLOT, sub * LANES), jnp.float32),
                pltpu.VMEM((NAME_ROWS, LANES), jnp.int32),
                pltpu.SMEM((NAME_ROWS, LANES), jnp.int32),
                pltpu.SemaphoreType.DMA((2 + 4,)),
            ],
        ),
        compiler_params=pltpu.CompilerParams(
            dimension_semantics=("arbitrary",), vmem_limit_bytes=20 * 1024 * 1024
        ),
        name="owner_sums",
    )(me, early, last_b, last_c)


def swap(x, axis, d):
    return lax.ppermute(x, axis, [(i, i ^ d) for i in range(lax.axis_size(axis))])


def direct(p_tiles):
    return [swap(p_tiles, "blk", d) for d in range(2, lax.axis_size("blk"), 2)]


def body(a_tiles, a_cols, p_tiles, route_list, out_slot):
    groups = lax.axis_size("grp")
    me = lax.axis_index("grp")
    rf, tile, cols = a_tiles.shape
    cap = out_slot.shape[1] // groups
    sub = tile * tile // LANES
    middle = (me == 1) | (me == 2)
    takes = [(1, 0), (3, 1), (0, 2), (2, 3)]

    def take(x):
        return lax.ppermute(x, "grp", takes)

    ints = jnp.concatenate([route_list, a_cols], axis=1)
    ints = jnp.concatenate([ints, jnp.pad(out_slot, ((0, 0), (0, a_cols.shape[1])))], axis=0)
    ints_took = take(ints)
    a_sent, ints_took = lax.optimization_barrier((a_tiles, ints_took))
    far = direct(p_tiles)
    p_took = take(p_tiles)
    a_took = take(a_sent)
    far[0], p_took = lax.optimization_barrier((far[0], p_took))
    far_took = direct(p_took)
    half = len(far) // 2
    mine = [jnp.concatenate([p_tiles] + far[:half]), jnp.concatenate(far[half:])]
    other = [swap(x, "blk", 1) for x in mine]
    near_took = swap(p_took, "blk", 1)

    def tables_own(off, middle):
        ends = jnp.where(off < 2, off, jnp.where(off == 3, 2, 3))
        return jnp.where(middle, jnp.where(off == 0, 0, jnp.where(off == 1, 3, off - 1)), ends)

    def tables_took(off, middle):
        return jnp.where((off == 0) | ((off == 1) & middle), off, 2)

    first = cap // 4
    spans = ((0, cap), (cap, cap), (2 * cap, first), (2 * cap + first, cap - first))
    own, to_a, to_b, last_b = partial_sums(
        ints, [a_tiles], mine + other, tables_own, 3, spans, groups, cap
    )
    own, to_a, to_b, last_b, a_took, near_took, *far_took = lax.optimization_barrier(
        (own, to_a, to_b, last_b, a_took, near_took, *far_took)
    )
    from_b = lax.ppermute(to_b, "grp", [(1, 2), (2, 1), (0, 3), (3, 0)])
    from_a = lax.ppermute(to_a, "grp", [(0, 1), (3, 2), (1, 3), (2, 0)])
    last_b = lax.ppermute(last_b, "grp", [(1, 2), (2, 1)])
    pieces = [p_took] + far_took + [near_took] + [swap(x, "blk", 1) for x in far_took]
    spans = ((0, cap), (cap + first, cap - first))
    own_took, last_c = partial_sums(ints_took, [a_took], pieces, tables_took, 2, spans, groups, cap)
    own_took, last_c, from_b = lax.optimization_barrier((own_took, last_c, from_b))
    last_c = lax.ppermute(last_c, "grp", [(1, 0), (2, 3)])
    about = jnp.stack([me, middle.astype(me.dtype)])
    return owner_sums(about, [own, own_took, from_a, from_b], last_b, last_c, cap, sub)


def solution(mesh):
    in_specs = (
        P(("blk", "grp"), None, None),
        P(("blk", "grp"), None),
        P(("blk", "grp"), None, None),
        P(("blk", "grp"), None),
        P(("blk", "grp"), None),
    )
    out_specs = P(("blk", "grp"), None)
    return jax.shard_map(body, mesh=mesh, in_specs=in_specs, out_specs=out_specs, check_vma=False)
```

```python
import functools

import jax
import jax.numpy as jnp
from jax import lax
from jax.experimental import pallas as pl
from jax.experimental.pallas import tpu as pltpu
from jax.sharding import PartitionSpec as P

OSLOT = 128
LANES = 128
ACCS = 4
AHEAD = 2
NAME_ROWS = 16
PART = 256


def log2(n):
    assert n & (n - 1) == 0
    return n.bit_length() - 1


def numbers_kernel(p_ref, route_ref, slot_ref, cols_ref, out_ref, wide):
    rf = p_ref.shape[0]
    out_ref[:rf] = p_ref[...]
    wide[...] = jnp.zeros_like(wide)
    cols = cols_ref[...]
    parts = (route_ref[...], slot_ref[...], lax.shift_right_logical(cols, jnp.int32(log2(PART))), cols & (PART - 1))
    for n, part in enumerate(parts):
        wide[n * rf:n * rf + part.shape[0], :part.shape[1]] = part.astype(jnp.float32)
    out_ref[rf] = wide[...].astype(out_ref.dtype)


def with_numbers(p_tiles, route_list, out_slot, a_cols):
    rf, tile, width = p_tiles.shape
    return pl.pallas_call(
        numbers_kernel,
        out_shape=jax.ShapeDtypeStruct((rf + 1, tile, width), p_tiles.dtype),
        scratch_shapes=[pltpu.VMEM((tile, width), jnp.float32)],
        compiler_params=pltpu.CompilerParams(vmem_limit_bytes=56 * 1024 * 1024),
        cost_estimate=pl.CostEstimate(flops=1, bytes_accessed=1, transcendentals=0),
        name="with_numbers",
    )(p_tiles, route_list, out_slot, a_cols)


def partial_kernel(n_rows, n_pieces, spans, cap, groups, table_of, packed, *refs):
    row_parts, refs = refs[:n_rows], refs[n_rows:]
    pieces, refs = refs[:n_pieces], refs[n_pieces:]
    outs, refs = refs[:len(spans)], refs[len(spans):]
    accs, (a_ref, lhs_ref, panel, y_buf, w_buf, *rest, sems) = refs[:ACCS], refs[ACCS:]
    packed_ref, place_vmem, idx_vmem, place_ref, idx_ref = rest
    rf, tile, cols = a_ref.shape
    tiles = cols // tile
    width = panel.shape[2] // tile
    sub = tile * tile // LANES
    n_tables = accs[0].shape[0] // cap
    chunk = 8

    copies = [pltpu.make_async_copy(packed.at[rf], packed_ref, sems.at[0])]
    for parts, whole in ((row_parts, a_ref), (pieces, panel)):
        at = 0
        for part in parts:
            height = part.shape[0] // rf * rf
            copies.append(
                pltpu.make_async_copy(part.at[pl.ds(0, height)], whole.at[pl.ds(at, height)], sems.at[len(copies)])
            )
            at += height
    for copy in copies:
        copy.start()
    copies.pop(0).wait()

    me, blk = lax.axis_index("grp"), lax.axis_index("blk")
    numbers = packed_ref[...].astype(jnp.float32).astype(jnp.int32)
    route, names = numbers[:rf], numbers[rf:rf + 1].astype(jnp.float32)
    owner = lax.shift_right_logical(route, jnp.int32(log2(cap)))
    table = table_of(owner ^ me, (me == 1) | (me == 2))
    place_vmem[...] = jnp.where(table < n_tables, table * cap + (route & (cap - 1)), n_tables * cap)
    cols = numbers[2 * rf:3 * rf] * PART + numbers[3 * rf:4 * rf]
    d = lax.shift_right_logical(cols, jnp.int32(log2(rf * groups))) ^ blk
    half = panel.shape[0] // (2 * rf)
    idx_vmem[...] = ((d & 1) * half + lax.shift_right_logical(d, jnp.int32(1))) * rf + (cols & (rf - 1))
    for n, (src, dst) in enumerate(((place_vmem, place_ref), (idx_vmem, idx_ref))):
        copy = pltpu.make_async_copy(src, dst, sems.at[1 + n_rows + n_pieces + n])
        copy.start()
        copies.append(copy)

    def clear(c, carry):
        blocks = pl.ds(c * chunk, chunk)
        for acc in accs:
            acc[blocks] = jnp.zeros((chunk, sub, LANES), jnp.float32)
        return carry

    lax.fori_loop(0, n_tables * cap // chunk, clear, 0)
    for acc in accs:
        acc[n_tables * cap] = jnp.zeros((sub, LANES), jnp.float32)
    for copy in copies:
        copy.wait()

    columns = width * tile
    from_col = lax.broadcasted_iota(jnp.int32, (columns, columns), 0)
    to_col = lax.broadcasted_iota(jnp.int32, (columns, columns), 1)
    wanted = jnp.where(to_col < columns // 2, 2 * to_col, 2 * to_col - columns + 1)
    chosen = jnp.where(from_col == wanted, 1.0, 0.0).astype(jnp.bfloat16)
    for row in range(rf):
        split = jnp.dot(panel[row], chosen, preferred_element_type=jnp.float32)
        stacked = jnp.concatenate([split[:, :columns // 2], split[:, columns // 2:]], axis=0)
        lhs_ref[row] = jnp.transpose(stacked).astype(jnp.bfloat16)

    lane = lax.broadcasted_iota(jnp.int32, (tile, LANES), 1)
    lo = lane < tile

    def first_products(row, k):
        both = a_ref[row, :, k * tile:k * tile + LANES]
        none = jnp.zeros_like(both)
        left = jnp.concatenate([jnp.where(lo, both, none), jnp.where(lo, none, both)], axis=0)
        right = jnp.concatenate([panel[idx_ref[row, k]], panel[idx_ref[row, k + 1]]], axis=0)
        return jnp.dot(left, right, preferred_element_type=jnp.float32)

    def keep(u, y):
        for m in range(width // 2):
            x = y[:, m * LANES:(m + 1) * LANES]
            y_buf[u, :, 2 * m * LANES:(2 * m + 1) * LANES] = x.astype(jnp.bfloat16)
            y_buf[u, :, (2 * m + 1) * LANES:(2 * m + 2) * LANES] = pltpu.roll(x, tile, 1).astype(jnp.bfloat16)

    def second_product(row, u):
        lhs = lhs_ref[row]
        w = []
        for m in range(width // 2):
            x = y_buf[u, :, 2 * m * LANES:(2 * m + 1) * LANES]
            xr = y_buf[u, :, (2 * m + 1) * LANES:(2 * m + 2) * LANES]
            none = jnp.zeros_like(x)
            right = jnp.concatenate(
                [
                    jnp.concatenate([jnp.where(lo, x, none), jnp.where(lo, xr, none)], axis=1),
                    jnp.concatenate([jnp.where(lo, none, xr), jnp.where(lo, none, x)], axis=1),
                ],
                axis=0,
            )
            w.append(jnp.dot(lhs, right, preferred_element_type=jnp.float32))
        return w

    def add(row, k, w):
        for q in range(width):
            part = w[q // 2][:, q % 2 * LANES:(q % 2 + 1) * LANES]
            for s in range(0, width, ACCS):
                group = range(s, min(s + ACCS, width))
                places = [place_ref[row, (n * tiles + k) * width + q] for n in group]
                old = [acc[place] for acc, place in zip(accs, places)]
                for acc, place, was, n in zip(accs, places, old, group):
                    acc[place] = was + part[n * sub:(n + 1) * sub]

    def keep_two(u, y):
        keep(u, y[:tile])
        keep(u + 1, y[tile:])

    def hold(n, w):
        for m, part in enumerate(w):
            w_buf[n, :, m * 2 * LANES:(m + 1) * 2 * LANES] = part

    def held(n):
        return [w_buf[n, :, m * 2 * LANES:(m + 1) * 2 * LANES] for m in range(width // 2)]

    for k in range(0, tiles, 2):
        keep_two(k, first_products(0, k))
    for n in range(AHEAD):
        hold(n, second_product(0, n))

    def block_row(row, carry):
        following = jnp.minimum(row + 1, rf - 1)
        w = [held(n) for n in range(AHEAD)]
        for k in range(tiles):
            if k % 2 == 0:
                upcoming = first_products(following, k)
            ahead = k + AHEAD
            w.append(second_product(row, ahead) if ahead < tiles else second_product(following, ahead - tiles))
            add(row, k, w.pop(0))
            if k % 2 == 1:
                keep_two(k - 1, upcoming)
        for n in range(AHEAD):
            hold(n, w[n])
        return carry

    lax.fori_loop(0, rf, block_row, 0)

    named = jnp.zeros((NAME_ROWS, LANES), jnp.float32)
    here = lax.broadcasted_iota(jnp.int32, named.shape, 0)
    for n in range(groups * cap // LANES):
        part = names[:, n * LANES:(n + 1) * LANES]
        named = jnp.where(here == n, jnp.broadcast_to(part, named.shape), named)

    for (first, count), out in zip(spans, outs):

        def merge(c, carry):
            blocks = pl.ds(first + c * chunk, chunk)
            total = accs[0][blocks]
            for acc in accs[1:]:
                total = total + acc[blocks]
            rows = pl.ds(pl.multiple_of(c * (chunk * sub), chunk * sub), chunk * sub)
            out[rows, :] = total.reshape(chunk * sub, LANES).astype(out.dtype)
            return carry

        lax.fori_loop(0, count // chunk, merge, 0)
        out[count * sub:, :] = named.astype(out.dtype)


def partial_sums(packed, row_parts, pieces, table_of, tables, spans, groups, cap):
    rf, tile, cols = row_parts[0].shape
    sub = tile * tile // LANES
    width = pieces[0].shape[2]
    rows = sum(x.shape[0] // rf * rf for x in pieces)
    operands = [packed] + row_parts + pieces
    panel_bytes = rows * tile * width * 2
    return pl.pallas_call(
        functools.partial(partial_kernel, len(row_parts), len(pieces), spans, cap, groups, table_of),
        out_shape=[jax.ShapeDtypeStruct((n * sub + NAME_ROWS, LANES), jnp.bfloat16) for _, n in spans],
        grid_spec=pl.GridSpec(
            grid=(1,),
            in_specs=[pl.BlockSpec(memory_space=pl.ANY)] * len(operands),
            out_specs=[pl.BlockSpec((n * sub + NAME_ROWS, LANES), lambda i: (0, 0)) for _, n in spans],
            scratch_shapes=[pltpu.VMEM((tables * cap + 1, sub, LANES), jnp.float32)] * ACCS
            + [
                pltpu.VMEM((rf, tile, cols), jnp.bfloat16),
                pltpu.VMEM((rf, width // 2, 2 * tile), jnp.bfloat16),
                pltpu.VMEM((rows, tile, width), jnp.bfloat16),
                pltpu.VMEM((cols // tile, tile, 2 * width), jnp.bfloat16),
                pltpu.VMEM((AHEAD, width // 2, 2 * width), jnp.float32),
                pltpu.VMEM(packed.shape[1:], jnp.bfloat16),
                pltpu.VMEM((rf, width), jnp.int32),
                pltpu.VMEM((rf, width), jnp.int32),
                pltpu.SMEM((rf, width), jnp.int32),
                pltpu.SMEM((rf, width), jnp.int32),
                pltpu.SemaphoreType.DMA((len(operands) + 2,)),
            ],
        ),
        compiler_params=pltpu.CompilerParams(
            dimension_semantics=("arbitrary",), vmem_limit_bytes=26 * 1024 * 1024 + panel_bytes
        ),
        cost_estimate=pl.CostEstimate(flops=1, bytes_accessed=1, transcendentals=0),
        name="partial_sums",
    )(*operands)


def early_kernel(me_ref, *refs):
    tables, out_ref, accs, (vmem_names, smem_names, sem) = refs[:4], refs[4], refs[5:-3], refs[-3:]
    n_out, sub = out_ref.shape[:2]
    counts = [(x.shape[0] - NAME_ROWS) // sub for x in tables]
    cap, some = counts[0], counts[-1]
    chunk = 8
    at = me_ref[0] * cap
    row, lane = lax.div(at, jnp.int32(LANES)), lax.rem(at, jnp.int32(LANES))

    for n, (x, count) in enumerate(zip(tables, counts)):
        vmem_names[n] = x[pl.ds(count * sub, NAME_ROWS), :].astype(jnp.float32).astype(jnp.int32)
    copy = pltpu.make_async_copy(vmem_names, smem_names, sem)
    copy.start()

    def clear(c, carry):
        for acc in accs:
            acc[pl.ds(c * chunk, chunk)] = jnp.zeros((chunk, sub, LANES), jnp.float32)
        return carry

    lax.fori_loop(0, n_out // chunk, clear, 0)
    copy.wait()

    def add_to(c, numbers):
        src = pl.ds(pl.multiple_of(c * sub, sub), sub)
        names = [smem_names[n, row, lane + c] for n in numbers]
        old = [acc[name] for acc, name in zip(accs, names)]
        for acc, name, was, n in zip(accs, names, old, numbers):
            acc[name] = was + tables[n][src, :].astype(jnp.float32)

    def add(c, carry):
        add_to(c, (0, 1, 2))
        return carry

    def add_some(c, carry):
        add_to(c, (3,))
        return carry

    lax.fori_loop(0, cap, add, 0, unroll=4)
    lax.fori_loop(0, some, add_some, 0, unroll=4)

    def merge(c, carry):
        blocks = pl.ds(c * chunk, chunk)
        total = accs[0][blocks]
        for acc in accs[1:]:
            total = total + acc[blocks]
        out_ref[blocks] = total
        return carry

    lax.fori_loop(0, n_out // chunk, merge, 0)


def last_kernel(cap, me_ref, table, from_b, from_c, out_ref, acc, rows_buf, vmem_names, smem_names, sems):
    n_out, sub = acc.shape[:2]
    rest = (from_b.shape[0] - NAME_ROWS) // sub
    at, pick = me_ref[0] * cap, me_ref[1] == 1
    row, lane = lax.div(at, jnp.int32(LANES)), lax.rem(at, jnp.int32(LANES)) + (cap - rest)
    fill = pltpu.make_async_copy(table, acc, sems.at[0])
    fill.start()

    def arrived(rows):
        return jnp.where(pick, from_b[rows, :].astype(jnp.float32), from_c[rows, :].astype(jnp.float32))

    vmem_names[...] = arrived(pl.ds(rest * sub, NAME_ROWS)).astype(jnp.int32)
    copy = pltpu.make_async_copy(vmem_names, smem_names, sems.at[1])
    copy.start()
    copy.wait()
    fill.wait()

    def add(c, carry):
        acc[smem_names[row, lane + c]] += arrived(pl.ds(pl.multiple_of(c * sub, sub), sub))
        return carry

    lax.fori_loop(0, rest, add, 0, unroll=4)
    flat = acc.reshape(n_out * sub, LANES)

    def emit(c, carry):
        rows = pl.ds(pl.multiple_of(c * 8, 8), 8)
        for t in range(sub):
            rows_buf[rows, t * LANES:(t + 1) * LANES] = flat[pl.ds(c * (8 * sub) + t, 8, stride=sub), :]
        return carry

    parts = sems.shape[0] - 2
    height = n_out // parts
    copies = []
    for n in range(parts):
        lax.fori_loop(n * height // 8, (n + 1) * height // 8, emit, 0)
        rows = pl.ds(n * height, height)
        copies.append(pltpu.make_async_copy(rows_buf.at[rows], out_ref.at[rows], sems.at[2 + n]))
        copies[-1].start()
    for copy in copies:
        copy.wait()


def owner_sums(me, tables, last_b, last_c, cap, sub):
    def whole(x):
        return pl.BlockSpec(x.shape, lambda i, *_: (0,) * len(x.shape))

    table = jax.ShapeDtypeStruct((OSLOT, sub, LANES), jnp.float32)
    early = pl.pallas_call(
        early_kernel,
        out_shape=table,
        grid_spec=pltpu.PrefetchScalarGridSpec(
            num_scalar_prefetch=1,
            grid=(1,),
            in_specs=[whole(x) for x in tables],
            out_specs=whole(table),
            scratch_shapes=[pltpu.VMEM(table.shape, jnp.float32)] * (len(tables) - 1)
            + [
                pltpu.VMEM((len(tables), NAME_ROWS, LANES), jnp.int32),
                pltpu.SMEM((len(tables), NAME_ROWS, LANES), jnp.int32),
                pltpu.SemaphoreType.DMA,
            ],
        ),
        compiler_params=pltpu.CompilerParams(
            dimension_semantics=("arbitrary",), vmem_limit_bytes=20 * 1024 * 1024
        ),
        name="early_sums",
    )(me, *tables)
    return pl.pallas_call(
        functools.partial(last_kernel, cap),
        out_shape=jax.ShapeDtypeStruct((OSLOT, sub * LANES), jnp.float32),
        grid_spec=pltpu.PrefetchScalarGridSpec(
            num_scalar_prefetch=1,
            grid=(1,),
            in_specs=[pl.BlockSpec(memory_space=pl.ANY), whole(last_b), whole(last_c)],
            out_specs=pl.BlockSpec(memory_space=pl.ANY),
            scratch_shapes=[
                pltpu.VMEM(table.shape, jnp.float32),
                pltpu.VMEM((OSLOT, sub * LANES), jnp.float32),
                pltpu.VMEM((NAME_ROWS, LANES), jnp.int32),
                pltpu.SMEM((NAME_ROWS, LANES), jnp.int32),
                pltpu.SemaphoreType.DMA((2 + 4,)),
            ],
        ),
        compiler_params=pltpu.CompilerParams(
            dimension_semantics=("arbitrary",), vmem_limit_bytes=20 * 1024 * 1024
        ),
        name="owner_sums",
    )(me, early, last_b, last_c)


def swap(x, axis, d):
    return lax.ppermute(x, axis, [(i, i ^ d) for i in range(lax.axis_size(axis))])


def direct(p_tiles):
    return [swap(p_tiles, "blk", d) for d in range(2, lax.axis_size("blk"), 2)]


def body(a_tiles, a_cols, p_tiles, route_list, out_slot):
    groups = lax.axis_size("grp")
    me = lax.axis_index("grp")
    rf, tile, cols = a_tiles.shape
    cap = out_slot.shape[1] // groups
    sub = tile * tile // LANES
    middle = (me == 1) | (me == 2)
    takes = [(1, 0), (3, 1), (0, 2), (2, 3)]

    def take(x):
        return lax.ppermute(x, "grp", takes)

    packed = with_numbers(p_tiles, route_list, out_slot, a_cols)
    far = direct(p_tiles)
    p_took = take(packed)
    a_took = take(a_tiles)
    far[0], p_took = lax.optimization_barrier((far[0], p_took))
    far_took = direct(p_took)
    half = len(far) // 2
    mine = [jnp.concatenate([p_tiles] + far[:half]), jnp.concatenate(far[half:])]
    other = [swap(x, "blk", 1) for x in mine]
    near_took = swap(p_took, "blk", 1)

    def tables_own(off, middle):
        ends = jnp.where(off < 2, off, jnp.where(off == 3, 2, 3))
        return jnp.where(middle, jnp.where(off == 0, 0, jnp.where(off == 1, 3, off - 1)), ends)

    def tables_took(off, middle):
        return jnp.where((off == 0) | ((off == 1) & middle), off, 2)

    first = cap // 4
    spans = ((0, cap), (cap, cap), (2 * cap, first), (2 * cap + first, cap - first))
    own, to_a, to_b, last_b = partial_sums(
        packed, [a_tiles], mine + other, tables_own, 3, spans, groups, cap
    )
    own, a_took, near_took, *far_took = lax.optimization_barrier((own, a_took, near_took, *far_took))
    from_b = lax.ppermute(to_b, "grp", [(1, 2), (2, 1), (0, 3), (3, 0)])
    from_a = lax.ppermute(to_a, "grp", [(0, 1), (3, 2), (1, 3), (2, 0)])
    last_b = lax.ppermute(last_b, "grp", [(1, 2), (2, 1)])
    pieces = [p_took] + far_took + [near_took] + [swap(x, "blk", 1) for x in far_took]
    spans = ((0, cap), (cap + first, cap - first))
    own_took, last_c = partial_sums(p_took, [a_took], pieces, tables_took, 2, spans, groups, cap)
    own_took, last_c, from_b = lax.optimization_barrier((own_took, last_c, from_b))
    last_c = lax.ppermute(last_c, "grp", [(1, 0), (2, 3)])
    about = jnp.stack([me, middle.astype(me.dtype)])
    return owner_sums(about, [own, own_took, from_a, from_b], last_b, last_c, cap, sub)


def solution(mesh):
    in_specs = (
        P(("blk", "grp"), None, None),
        P(("blk", "grp"), None),
        P(("blk", "grp"), None, None),
        P(("blk", "grp"), None),
        P(("blk", "grp"), None),
    )
    out_specs = P(("blk", "grp"), None)
    return jax.shard_map(body, mesh=mesh, in_specs=in_specs, out_specs=out_specs, check_vma=False)
```

```python
import functools

import jax
import jax.numpy as jnp
from jax import lax
from jax.experimental import pallas as pl
from jax.experimental.pallas import tpu as pltpu
from jax.sharding import PartitionSpec as P

OSLOT = 128
LANES = 128
ACCS = 4
AHEAD = 2
NAME_ROWS = 16


def log2(n):
    assert n & (n - 1) == 0
    return n.bit_length() - 1


def partial_kernel(n_rows, n_pieces, spans, cap, groups, table_of, ints, *refs):
    row_parts, refs = refs[:n_rows], refs[n_rows:]
    pieces, refs = refs[:n_pieces], refs[n_pieces:]
    outs, refs = refs[:len(spans)], refs[len(spans):]
    accs, (a_ref, lhs_ref, panel, y_buf, w_buf, *rest, sems) = refs[:ACCS], refs[ACCS:]
    ints_ref, place_vmem, idx_vmem, place_ref, idx_ref = rest
    rf, tile, cols = a_ref.shape
    tiles = cols // tile
    width = panel.shape[2] // tile
    sub = tile * tile // LANES
    n_tables = accs[0].shape[0] // cap
    chunk = 8

    copies = [pltpu.make_async_copy(ints, ints_ref, sems.at[0])]
    for parts, whole in ((row_parts, a_ref), (pieces, panel)):
        at = 0
        for part in parts:
            height = part.shape[0]
            copies.append(
                pltpu.make_async_copy(part, whole.at[pl.ds(at, height)], sems.at[len(copies)])
            )
            at += height
    for copy in copies:
        copy.start()
    copies.pop(0).wait()

    me, blk = lax.axis_index("grp"), lax.axis_index("blk")
    n_places = width * tiles * width
    route, names = ints_ref[:rf, :n_places], ints_ref[rf:, :n_places].astype(jnp.float32)
    owner = lax.shift_right_logical(route, jnp.int32(log2(cap)))
    table = table_of(owner ^ me, (me == 1) | (me == 2))
    place_vmem[...] = jnp.where(table < n_tables, table * cap + (route & (cap - 1)), n_tables * cap)
    cols = ints_ref[:rf, n_places:]
    d = lax.shift_right_logical(cols, jnp.int32(log2(rf * groups))) ^ blk
    half = panel.shape[0] // (2 * rf)
    idx_vmem[:, :tiles] = ((d & 1) * half + lax.shift_right_logical(d, jnp.int32(1))) * rf + (cols & (rf - 1))
    for n, (src, dst) in enumerate(((place_vmem, place_ref), (idx_vmem, idx_ref))):
        copy = pltpu.make_async_copy(src, dst, sems.at[1 + n_rows + n_pieces + n])
        copy.start()
        copies.append(copy)

    def clear(c, carry):
        blocks = pl.ds(c * chunk, chunk)
        for acc in accs:
            acc[blocks] = jnp.zeros((chunk, sub, LANES), jnp.float32)
        return carry

    lax.fori_loop(0, n_tables * cap // chunk, clear, 0)
    for acc in accs:
        acc[n_tables * cap] = jnp.zeros((sub, LANES), jnp.float32)
    for copy in copies:
        copy.wait()

    columns = width * tile
    from_col = lax.broadcasted_iota(jnp.int32, (columns, columns), 0)
    to_col = lax.broadcasted_iota(jnp.int32, (columns, columns), 1)
    wanted = jnp.where(to_col < columns // 2, 2 * to_col, 2 * to_col - columns + 1)
    chosen = jnp.where(from_col == wanted, 1.0, 0.0).astype(jnp.bfloat16)
    for row in range(rf):
        split = jnp.dot(panel[row], chosen, preferred_element_type=jnp.float32)
        stacked = jnp.concatenate([split[:, :columns // 2], split[:, columns // 2:]], axis=0)
        lhs_ref[row] = jnp.transpose(stacked).astype(jnp.bfloat16)

    lane = lax.broadcasted_iota(jnp.int32, (tile, LANES), 1)
    lo = lane < tile

    def first_products(row, k):
        both = a_ref[row, :, k * tile:k * tile + LANES]
        none = jnp.zeros_like(both)
        left = jnp.concatenate([jnp.where(lo, both, none), jnp.where(lo, none, both)], axis=0)
        right = jnp.concatenate([panel[idx_ref[row, k]], panel[idx_ref[row, k + 1]]], axis=0)
        return jnp.dot(left, right, preferred_element_type=jnp.float32)

    def keep(u, y):
        for m in range(width // 2):
            x = y[:, m * LANES:(m + 1) * LANES]
            y_buf[u, :, 2 * m * LANES:(2 * m + 1) * LANES] = x.astype(jnp.bfloat16)
            y_buf[u, :, (2 * m + 1) * LANES:(2 * m + 2) * LANES] = pltpu.roll(x, tile, 1).astype(jnp.bfloat16)

    def second_product(row, u):
        lhs = lhs_ref[row]
        w = []
        for m in range(width // 2):
            x = y_buf[u, :, 2 * m * LANES:(2 * m + 1) * LANES]
            xr = y_buf[u, :, (2 * m + 1) * LANES:(2 * m + 2) * LANES]
            none = jnp.zeros_like(x)
            right = jnp.concatenate(
                [
                    jnp.concatenate([jnp.where(lo, x, none), jnp.where(lo, xr, none)], axis=1),
                    jnp.concatenate([jnp.where(lo, none, xr), jnp.where(lo, none, x)], axis=1),
                ],
                axis=0,
            )
            w.append(jnp.dot(lhs, right, preferred_element_type=jnp.float32))
        return w

    def add(row, k, w):
        for q in range(width):
            part = w[q // 2][:, q % 2 * LANES:(q % 2 + 1) * LANES]
            for s in range(0, width, ACCS):
                group = range(s, min(s + ACCS, width))
                places = [place_ref[row, (n * tiles + k) * width + q] for n in group]
                old = [acc[place] for acc, place in zip(accs, places)]
                for acc, place, was, n in zip(accs, places, old, group):
                    acc[place] = was + part[n * sub:(n + 1) * sub]

    def keep_two(u, y):
        keep(u, y[:tile])
        keep(u + 1, y[tile:])

    def hold(n, w):
        for m, part in enumerate(w):
            w_buf[n, :, m * 2 * LANES:(m + 1) * 2 * LANES] = part

    def held(n):
        return [w_buf[n, :, m * 2 * LANES:(m + 1) * 2 * LANES] for m in range(width // 2)]

    for k in range(0, tiles, 2):
        keep_two(k, first_products(0, k))
    for n in range(AHEAD):
        hold(n, second_product(0, n))

    def block_row(row, carry):
        following = jnp.minimum(row + 1, rf - 1)
        w = [held(n) for n in range(AHEAD)]
        for k in range(tiles):
            if k % 2 == 0:
                upcoming = first_products(following, k)
            ahead = k + AHEAD
            w.append(second_product(row, ahead) if ahead < tiles else second_product(following, ahead - tiles))
            add(row, k, w.pop(0))
            if k % 2 == 1:
                keep_two(k - 1, upcoming)
        for n in range(AHEAD):
            hold(n, w[n])
        return carry

    lax.fori_loop(0, rf, block_row, 0)

    named = jnp.zeros((NAME_ROWS, LANES), jnp.float32)
    here = lax.broadcasted_iota(jnp.int32, named.shape, 0)
    for n in range(groups * cap // LANES):
        part = names[:, n * LANES:(n + 1) * LANES]
        named = jnp.where(here == n, jnp.broadcast_to(part, named.shape), named)

    for (first, count), out in zip(spans, outs):

        def merge(c, carry):
            blocks = pl.ds(first + c * chunk, chunk)
            total = accs[0][blocks]
            for acc in accs[1:]:
                total = total + acc[blocks]
            rows = pl.ds(pl.multiple_of(c * (chunk * sub), chunk * sub), chunk * sub)
            out[rows, :] = total.reshape(chunk * sub, LANES).astype(out.dtype)
            return carry

        lax.fori_loop(0, count // chunk, merge, 0)
        out[count * sub:, :] = named.astype(out.dtype)


def partial_sums(ints, row_parts, pieces, table_of, tables, spans, groups, cap):
    rf, tile, cols = row_parts[0].shape
    sub = tile * tile // LANES
    width = pieces[0].shape[2]
    rows = sum(x.shape[0] for x in pieces)
    n_places = ints.shape[1] - cols // tile
    operands = [ints] + row_parts + pieces
    panel_bytes = rows * tile * width * 2
    return pl.pallas_call(
        functools.partial(partial_kernel, len(row_parts), len(pieces), spans, cap, groups, table_of),
        out_shape=[jax.ShapeDtypeStruct((n * sub + NAME_ROWS, LANES), jnp.bfloat16) for _, n in spans],
        grid_spec=pl.GridSpec(
            grid=(1,),
            in_specs=[pl.BlockSpec(memory_space=pl.ANY)] * len(operands),
            out_specs=[pl.BlockSpec((n * sub + NAME_ROWS, LANES), lambda i: (0, 0)) for _, n in spans],
            scratch_shapes=[pltpu.VMEM((tables * cap + 1, sub, LANES), jnp.float32)] * ACCS
            + [
                pltpu.VMEM((rf, tile, cols), jnp.bfloat16),
                pltpu.VMEM((rf, width // 2, 2 * tile), jnp.bfloat16),
                pltpu.VMEM((rows, tile, width), jnp.bfloat16),
                pltpu.VMEM((cols // tile, tile, 2 * width), jnp.bfloat16),
                pltpu.VMEM((AHEAD, width // 2, 2 * width), jnp.float32),
                pltpu.VMEM(ints.shape, jnp.int32),
                pltpu.VMEM((rf, n_places), jnp.int32),
                pltpu.VMEM((rf, LANES), jnp.int32),
                pltpu.SMEM((rf, n_places), jnp.int32),
                pltpu.SMEM((rf, LANES), jnp.int32),
                pltpu.SemaphoreType.DMA((len(operands) + 2,)),
            ],
        ),
        compiler_params=pltpu.CompilerParams(
            dimension_semantics=("arbitrary",), vmem_limit_bytes=26 * 1024 * 1024 + panel_bytes
        ),
        cost_estimate=pl.CostEstimate(flops=1, bytes_accessed=1, transcendentals=0),
        name="partial_sums",
    )(*operands)


def early_kernel(me_ref, *refs):
    tables, out_ref, accs, (vmem_names, smem_names, sem) = refs[:4], refs[4], refs[5:-3], refs[-3:]
    n_out, sub = out_ref.shape[:2]
    counts = [(x.shape[0] - NAME_ROWS) // sub for x in tables]
    cap, some = counts[0], counts[-1]
    chunk = 8
    at = me_ref[0] * cap
    row, lane = lax.div(at, jnp.int32(LANES)), lax.rem(at, jnp.int32(LANES))

    for n, (x, count) in enumerate(zip(tables, counts)):
        vmem_names[n] = x[pl.ds(count * sub, NAME_ROWS), :].astype(jnp.float32).astype(jnp.int32)
    copy = pltpu.make_async_copy(vmem_names, smem_names, sem)
    copy.start()

    def clear(c, carry):
        for acc in accs:
            acc[pl.ds(c * chunk, chunk)] = jnp.zeros((chunk, sub, LANES), jnp.float32)
        return carry

    lax.fori_loop(0, n_out // chunk, clear, 0)
    copy.wait()

    def add_to(c, numbers):
        src = pl.ds(pl.multiple_of(c * sub, sub), sub)
        names = [smem_names[n, row, lane + c] for n in numbers]
        old = [acc[name] for acc, name in zip(accs, names)]
        for acc, name, was, n in zip(accs, names, old, numbers):
            acc[name] = was + tables[n][src, :].astype(jnp.float32)

    def add(c, carry):
        add_to(c, (0, 1, 2))
        return carry

    def add_some(c, carry):
        add_to(c, (3,))
        return carry

    lax.fori_loop(0, cap, add, 0, unroll=4)
    lax.fori_loop(0, some, add_some, 0, unroll=4)

    def merge(c, carry):
        blocks = pl.ds(c * chunk, chunk)
        total = accs[0][blocks]
        for acc in accs[1:]:
            total = total + acc[blocks]
        out_ref[blocks] = total
        return carry

    lax.fori_loop(0, n_out // chunk, merge, 0)


def last_kernel(cap, me_ref, table, from_b, from_c, out_ref, acc, rows_buf, vmem_names, smem_names, sems):
    n_out, sub = acc.shape[:2]
    rest = (from_b.shape[0] - NAME_ROWS) // sub
    at, pick = me_ref[0] * cap, me_ref[1] == 1
    row, lane = lax.div(at, jnp.int32(LANES)), lax.rem(at, jnp.int32(LANES)) + (cap - rest)
    fill = pltpu.make_async_copy(table, acc, sems.at[0])
    fill.start()

    def arrived(rows):
        return jnp.where(pick, from_b[rows, :].astype(jnp.float32), from_c[rows, :].astype(jnp.float32))

    vmem_names[...] = arrived(pl.ds(rest * sub, NAME_ROWS)).astype(jnp.int32)
    copy = pltpu.make_async_copy(vmem_names, smem_names, sems.at[1])
    copy.start()
    copy.wait()
    fill.wait()

    def add(c, carry):
        acc[smem_names[row, lane + c]] += arrived(pl.ds(pl.multiple_of(c * sub, sub), sub))
        return carry

    lax.fori_loop(0, rest, add, 0, unroll=4)
    flat = acc.reshape(n_out * sub, LANES)

    def emit(c, carry):
        rows = pl.ds(pl.multiple_of(c * 8, 8), 8)
        for t in range(sub):
            rows_buf[rows, t * LANES:(t + 1) * LANES] = flat[pl.ds(c * (8 * sub) + t, 8, stride=sub), :]
        return carry

    parts = sems.shape[0] - 2
    height = n_out // parts
    copies = []
    for n in range(parts):
        lax.fori_loop(n * height // 8, (n + 1) * height // 8, emit, 0)
        rows = pl.ds(n * height, height)
        copies.append(pltpu.make_async_copy(rows_buf.at[rows], out_ref.at[rows], sems.at[2 + n]))
        copies[-1].start()
    for copy in copies:
        copy.wait()


def owner_sums(me, tables, last_b, last_c, cap, sub):
    def whole(x):
        return pl.BlockSpec(x.shape, lambda i, *_: (0,) * len(x.shape))

    table = jax.ShapeDtypeStruct((OSLOT, sub, LANES), jnp.float32)
    early = pl.pallas_call(
        early_kernel,
        out_shape=table,
        grid_spec=pltpu.PrefetchScalarGridSpec(
            num_scalar_prefetch=1,
            grid=(1,),
            in_specs=[whole(x) for x in tables],
            out_specs=whole(table),
            scratch_shapes=[pltpu.VMEM(table.shape, jnp.float32)] * (len(tables) - 1)
            + [
                pltpu.VMEM((len(tables), NAME_ROWS, LANES), jnp.int32),
                pltpu.SMEM((len(tables), NAME_ROWS, LANES), jnp.int32),
                pltpu.SemaphoreType.DMA,
            ],
        ),
        compiler_params=pltpu.CompilerParams(
            dimension_semantics=("arbitrary",), vmem_limit_bytes=20 * 1024 * 1024
        ),
        name="early_sums",
    )(me, *tables)
    return pl.pallas_call(
        functools.partial(last_kernel, cap),
        out_shape=jax.ShapeDtypeStruct((OSLOT, sub * LANES), jnp.float32),
        grid_spec=pltpu.PrefetchScalarGridSpec(
            num_scalar_prefetch=1,
            grid=(1,),
            in_specs=[pl.BlockSpec(memory_space=pl.ANY), whole(last_b), whole(last_c)],
            out_specs=pl.BlockSpec(memory_space=pl.ANY),
            scratch_shapes=[
                pltpu.VMEM(table.shape, jnp.float32),
                pltpu.VMEM((OSLOT, sub * LANES), jnp.float32),
                pltpu.VMEM((NAME_ROWS, LANES), jnp.int32),
                pltpu.SMEM((NAME_ROWS, LANES), jnp.int32),
                pltpu.SemaphoreType.DMA((2 + 4,)),
            ],
        ),
        compiler_params=pltpu.CompilerParams(
            dimension_semantics=("arbitrary",), vmem_limit_bytes=20 * 1024 * 1024
        ),
        name="owner_sums",
    )(me, early, last_b, last_c)


def swap(x, axis, d):
    return lax.ppermute(x, axis, [(i, i ^ d) for i in range(lax.axis_size(axis))])


def direct(p_tiles):
    return [swap(p_tiles, "blk", d) for d in range(2, lax.axis_size("blk"), 2)]


def body(a_tiles, a_cols, p_tiles, route_list, out_slot):
    groups = lax.axis_size("grp")
    me = lax.axis_index("grp")
    rf, tile, cols = a_tiles.shape
    cap = out_slot.shape[1] // groups
    sub = tile * tile // LANES
    middle = (me == 1) | (me == 2)
    takes = [(1, 0), (3, 1), (0, 2), (2, 3)]

    def take(x):
        return lax.ppermute(x, "grp", takes)

    ints = jnp.concatenate([route_list, a_cols], axis=1)
    ints = jnp.concatenate([ints, jnp.pad(out_slot, ((0, 0), (0, a_cols.shape[1])))], axis=0)
    ints_took = take(ints)
    far = direct(p_tiles)
    p_took = take(p_tiles)
    a_took = take(a_tiles)
    far[0], p_took = lax.optimization_barrier((far[0], p_took))
    far_took = direct(p_took)
    half = len(far) // 2
    mine = [jnp.concatenate([p_tiles] + far[:half]), jnp.concatenate(far[half:])]
    other = [swap(x, "blk", 1) for x in mine]

    def tables_own(off, middle):
        ends = jnp.where(off < 2, off, jnp.where(off == 3, 2, 3))
        return jnp.where(middle, jnp.where(off == 0, 0, jnp.where(off == 1, 3, off - 1)), ends)

    def tables_took(off, middle):
        return jnp.where((off == 0) | ((off == 1) & middle), off, 2)

    first = cap // 4
    spans = ((0, cap), (cap, cap), (2 * cap, first), (2 * cap + first, cap - first))
    own, to_a, to_b, last_b = partial_sums(
        ints, [a_tiles], mine + other, tables_own, 3, spans, groups, cap
    )
    own, a_took, ints_took, p_took, *far_took = lax.optimization_barrier((own, a_took, ints_took, p_took, *far_took))
    from_b = lax.ppermute(to_b, "grp", [(1, 2), (2, 1), (0, 3), (3, 0)])
    from_a = lax.ppermute(to_a, "grp", [(0, 1), (3, 2), (1, 3), (2, 0)])
    last_b = lax.ppermute(last_b, "grp", [(1, 2), (2, 1)])
    took = [p_took] + far_took
    pieces = took + [swap(x, "blk", 1) for x in took]
    spans = ((0, cap), (cap + first, cap - first))
    own_took, last_c = partial_sums(ints_took, [a_took], pieces, tables_took, 2, spans, groups, cap)
    own_took, last_c, from_b = lax.optimization_barrier((own_took, last_c, from_b))
    last_c = lax.ppermute(last_c, "grp", [(1, 0), (2, 3)])
    about = jnp.stack([me, middle.astype(me.dtype)])
    return owner_sums(about, [own, own_took, from_a, from_b], last_b, last_c, cap, sub)


def solution(mesh):
    in_specs = (
        P(("blk", "grp"), None, None),
        P(("blk", "grp"), None),
        P(("blk", "grp"), None, None),
        P(("blk", "grp"), None),
        P(("blk", "grp"), None),
    )
    out_specs = P(("blk", "grp"), None)
    return jax.shard_map(body, mesh=mesh, in_specs=in_specs, out_specs=out_specs, check_vma=False)
```

```python
import functools

import jax
import jax.numpy as jnp
from jax import lax
from jax.experimental import pallas as pl
from jax.experimental.pallas import tpu as pltpu
from jax.sharding import PartitionSpec as P

OSLOT = 128
LANES = 128
ACCS = 4
AHEAD = 2
NAME_ROWS = 16


def log2(n):
    assert n & (n - 1) == 0
    return n.bit_length() - 1


def partial_kernel(n_rows, n_pieces, spans, cap, groups, table_of, ints, *refs):
    row_parts, refs = refs[:n_rows], refs[n_rows:]
    pieces, refs = refs[:n_pieces], refs[n_pieces:]
    outs, refs = refs[:len(spans)], refs[len(spans):]
    accs, (a_ref, lhs_ref, panel, y_buf, w_buf, *rest, sems) = refs[:ACCS], refs[ACCS:]
    ints_ref, place_vmem, idx_vmem, place_ref, idx_ref = rest
    rf, tile, cols = a_ref.shape
    tiles = cols // tile
    width = panel.shape[2] // tile
    sub = tile * tile // LANES
    n_tables = accs[0].shape[0] // cap
    chunk = 8

    copies = [pltpu.make_async_copy(ints, ints_ref, sems.at[0])]
    for parts, whole in ((row_parts, a_ref), (pieces, panel)):
        at = 0
        for part in parts:
            height = part.shape[0]
            copies.append(
                pltpu.make_async_copy(part, whole.at[pl.ds(at, height)], sems.at[len(copies)])
            )
            at += height
    for copy in copies:
        copy.start()
    copies.pop(0).wait()

    me, blk = lax.axis_index("grp"), lax.axis_index("blk")
    n_places = width * tiles * width
    route, names = ints_ref[:rf, :n_places], ints_ref[rf:, :n_places].astype(jnp.float32)
    owner = lax.shift_right_logical(route, jnp.int32(log2(cap)))
    table = table_of(owner ^ me, (me == 1) | (me == 2))
    place_vmem[...] = jnp.where(table < n_tables, table * cap + (route & (cap - 1)), n_tables * cap)
    cols = ints_ref[:rf, n_places:]
    d = lax.shift_right_logical(cols, jnp.int32(log2(rf * groups))) ^ blk
    half = panel.shape[0] // (2 * rf)
    idx_vmem[:, :tiles] = ((d & 1) * half + lax.shift_right_logical(d, jnp.int32(1))) * rf + (cols & (rf - 1))
    for n, (src, dst) in enumerate(((place_vmem, place_ref), (idx_vmem, idx_ref))):
        copy = pltpu.make_async_copy(src, dst, sems.at[1 + n_rows + n_pieces + n])
        copy.start()
        copies.append(copy)

    def clear(c, carry):
        blocks = pl.ds(c * chunk, chunk)
        for acc in accs:
            acc[blocks] = jnp.zeros((chunk, sub, LANES), jnp.float32)
        return carry

    lax.fori_loop(0, n_tables * cap // chunk, clear, 0)
    for acc in accs:
        acc[n_tables * cap] = jnp.zeros((sub, LANES), jnp.float32)
    for copy in copies:
        copy.wait()

    columns = width * tile
    from_col = lax.broadcasted_iota(jnp.int32, (columns, columns), 0)
    to_col = lax.broadcasted_iota(jnp.int32, (columns, columns), 1)
    wanted = jnp.where(to_col < columns // 2, 2 * to_col, 2 * to_col - columns + 1)
    chosen = jnp.where(from_col == wanted, 1.0, 0.0).astype(jnp.bfloat16)
    for row in range(rf):
        split = jnp.dot(panel[row], chosen, preferred_element_type=jnp.float32)
        stacked = jnp.concatenate([split[:, :columns // 2], split[:, columns // 2:]], axis=0)
        lhs_ref[row] = jnp.transpose(stacked).astype(jnp.bfloat16)

    lane = lax.broadcasted_iota(jnp.int32, (tile, LANES), 1)
    lo = lane < tile

    def first_products(row, k):
        both = a_ref[row, :, k * tile:k * tile + LANES]
        none = jnp.zeros_like(both)
        left = jnp.concatenate([jnp.where(lo, both, none), jnp.where(lo, none, both)], axis=0)
        right = jnp.concatenate([panel[idx_ref[row, k]], panel[idx_ref[row, k + 1]]], axis=0)
        return jnp.dot(left, right, preferred_element_type=jnp.float32)

    def keep(u, y):
        for m in range(width // 2):
            x = y[:, m * LANES:(m + 1) * LANES]
            y_buf[u, :, 2 * m * LANES:(2 * m + 1) * LANES] = x.astype(jnp.bfloat16)
            y_buf[u, :, (2 * m + 1) * LANES:(2 * m + 2) * LANES] = pltpu.roll(x, tile, 1).astype(jnp.bfloat16)

    def second_product(row, u):
        lhs = lhs_ref[row]
        w = []
        for m in range(width // 2):
            x = y_buf[u, :, 2 * m * LANES:(2 * m + 1) * LANES]
            xr = y_buf[u, :, (2 * m + 1) * LANES:(2 * m + 2) * LANES]
            none = jnp.zeros_like(x)
            right = jnp.concatenate(
                [
                    jnp.concatenate([jnp.where(lo, x, none), jnp.where(lo, xr, none)], axis=1),
                    jnp.concatenate([jnp.where(lo, none, xr), jnp.where(lo, none, x)], axis=1),
                ],
                axis=0,
            )
            w.append(jnp.dot(lhs, right, preferred_element_type=jnp.float32))
        return w

    def add(row, k, w):
        for q in range(width):
            part = w[q // 2][:, q % 2 * LANES:(q % 2 + 1) * LANES]
            for s in range(0, width, ACCS):
                group = range(s, min(s + ACCS, width))
                places = [place_ref[row, (n * tiles + k) * width + q] for n in group]
                old = [acc[place] for acc, place in zip(accs, places)]
                for acc, place, was, n in zip(accs, places, old, group):
                    acc[place] = was + part[n * sub:(n + 1) * sub]

    def keep_two(u, y):
        keep(u, y[:tile])
        keep(u + 1, y[tile:])

    def hold(n, w):
        for m, part in enumerate(w):
            w_buf[n, :, m * 2 * LANES:(m + 1) * 2 * LANES] = part

    def held(n):
        return [w_buf[n, :, m * 2 * LANES:(m + 1) * 2 * LANES] for m in range(width // 2)]

    for k in range(0, tiles, 2):
        keep_two(k, first_products(0, k))
    for n in range(AHEAD):
        hold(n, second_product(0, n))

    def block_row(row, carry):
        following = jnp.minimum(row + 1, rf - 1)
        w = [held(n) for n in range(AHEAD)]
        for k in range(tiles):
            if k % 2 == 0:
                upcoming = first_products(following, k)
            ahead = k + AHEAD
            w.append(second_product(row, ahead) if ahead < tiles else second_product(following, ahead - tiles))
            add(row, k, w.pop(0))
            if k % 2 == 1:
                keep_two(k - 1, upcoming)
        for n in range(AHEAD):
            hold(n, w[n])
        return carry

    lax.fori_loop(0, rf, block_row, 0)

    named = jnp.zeros((NAME_ROWS, LANES), jnp.float32)
    here = lax.broadcasted_iota(jnp.int32, named.shape, 0)
    for n in range(groups * cap // LANES):
        part = names[:, n * LANES:(n + 1) * LANES]
        named = jnp.where(here == n, jnp.broadcast_to(part, named.shape), named)

    for (first, count), out in zip(spans, outs):

        def merge(c, carry):
            blocks = pl.ds(first + c * chunk, chunk)
            total = accs[0][blocks]
            for acc in accs[1:]:
                total = total + acc[blocks]
            rows = pl.ds(pl.multiple_of(c * (chunk * sub), chunk * sub), chunk * sub)
            out[rows, :] = total.reshape(chunk * sub, LANES).astype(out.dtype)
            return carry

        lax.fori_loop(0, count // chunk, merge, 0)
        out[count * sub:, :] = named.astype(out.dtype)


def partial_sums(ints, row_parts, pieces, table_of, tables, spans, groups, cap):
    rf, tile, cols = row_parts[0].shape
    sub = tile * tile // LANES
    width = pieces[0].shape[2]
    rows = sum(x.shape[0] for x in pieces)
    n_places = ints.shape[1] - cols // tile
    operands = [ints] + row_parts + pieces
    panel_bytes = rows * tile * width * 2
    return pl.pallas_call(
        functools.partial(partial_kernel, len(row_parts), len(pieces), spans, cap, groups, table_of),
        out_shape=[jax.ShapeDtypeStruct((n * sub + NAME_ROWS, LANES), jnp.bfloat16) for _, n in spans],
        grid_spec=pl.GridSpec(
            grid=(1,),
            in_specs=[pl.BlockSpec(memory_space=pl.ANY)] * len(operands),
            out_specs=[pl.BlockSpec((n * sub + NAME_ROWS, LANES), lambda i: (0, 0)) for _, n in spans],
            scratch_shapes=[pltpu.VMEM((tables * cap + 1, sub, LANES), jnp.float32)] * ACCS
            + [
                pltpu.VMEM((rf, tile, cols), jnp.bfloat16),
                pltpu.VMEM((rf, width // 2, 2 * tile), jnp.bfloat16),
                pltpu.VMEM((rows, tile, width), jnp.bfloat16),
                pltpu.VMEM((cols // tile, tile, 2 * width), jnp.bfloat16),
                pltpu.VMEM((AHEAD, width // 2, 2 * width), jnp.float32),
                pltpu.VMEM(ints.shape, jnp.int32),
                pltpu.VMEM((rf, n_places), jnp.int32),
                pltpu.VMEM((rf, LANES), jnp.int32),
                pltpu.SMEM((rf, n_places), jnp.int32),
                pltpu.SMEM((rf, LANES), jnp.int32),
                pltpu.SemaphoreType.DMA((len(operands) + 2,)),
            ],
        ),
        compiler_params=pltpu.CompilerParams(
            dimension_semantics=("arbitrary",), vmem_limit_bytes=26 * 1024 * 1024 + panel_bytes
        ),
        cost_estimate=pl.CostEstimate(flops=1, bytes_accessed=1, transcendentals=0),
        name="partial_sums",
    )(*operands)


def early_kernel(me_ref, *refs):
    tables, out_ref, accs, (vmem_names, smem_names, sem) = refs[:4], refs[4], refs[5:-3], refs[-3:]
    n_out, sub = out_ref.shape[:2]
    counts = [(x.shape[0] - NAME_ROWS) // sub for x in tables]
    cap, some = counts[0], counts[-1]
    chunk = 8
    at = me_ref[0] * cap
    row, lane = lax.div(at, jnp.int32(LANES)), lax.rem(at, jnp.int32(LANES))

    for n, (x, count) in enumerate(zip(tables, counts)):
        vmem_names[n] = x[pl.ds(count * sub, NAME_ROWS), :].astype(jnp.float32).astype(jnp.int32)
    copy = pltpu.make_async_copy(vmem_names, smem_names, sem)
    copy.start()

    def clear(c, carry):
        for acc in accs:
            acc[pl.ds(c * chunk, chunk)] = jnp.zeros((chunk, sub, LANES), jnp.float32)
        return carry

    lax.fori_loop(0, n_out // chunk, clear, 0)
    copy.wait()

    def add_to(c, numbers):
        src = pl.ds(pl.multiple_of(c * sub, sub), sub)
        names = [smem_names[n, row, lane + c] for n in numbers]
        old = [acc[name] for acc, name in zip(accs, names)]
        for acc, name, was, n in zip(accs, names, old, numbers):
            acc[name] = was + tables[n][src, :].astype(jnp.float32)

    def add(c, carry):
        add_to(c, (0, 1, 2))
        return carry

    def add_some(c, carry):
        add_to(c, (3,))
        return carry

    lax.fori_loop(0, cap, add, 0, unroll=4)
    lax.fori_loop(0, some, add_some, 0, unroll=4)

    def merge(c, carry):
        blocks = pl.ds(c * chunk, chunk)
        total = accs[0][blocks]
        for acc in accs[1:]:
            total = total + acc[blocks]
        out_ref[blocks] = total
        return carry

    lax.fori_loop(0, n_out // chunk, merge, 0)


def last_kernel(me_ref, table, from_b, from_c, out_ref, acc, rows_buf, vmem_names, smem_names, sems):
    n_out, sub = acc.shape[:2]
    cap, rest = [(x.shape[0] - NAME_ROWS) // sub for x in (from_b, from_c)]
    pick = me_ref[1] == 1
    count = jnp.where(pick, cap, rest)
    at = me_ref[0] * cap
    row, lane = lax.div(at, jnp.int32(LANES)), lax.rem(at, jnp.int32(LANES)) + (cap - count)
    fill = pltpu.make_async_copy(table, acc, sems.at[0])
    fill.start()

    def arrived(rows_b, rows_c):
        return jnp.where(pick, from_b[rows_b, :].astype(jnp.float32), from_c[rows_c, :].astype(jnp.float32))

    vmem_names[...] = arrived(pl.ds(cap * sub, NAME_ROWS), pl.ds(rest * sub, NAME_ROWS)).astype(jnp.int32)
    copy = pltpu.make_async_copy(vmem_names, smem_names, sems.at[1])
    copy.start()
    copy.wait()
    fill.wait()

    def add(c, carry):
        for u in range(4):
            n = c * 4 + u
            rows_b = pl.ds(pl.multiple_of(n * sub, sub), sub)
            rows_c = pl.ds(pl.multiple_of(jnp.minimum(n, rest - 1) * sub, sub), sub)
            acc[smem_names[row, lane + n]] += arrived(rows_b, rows_c)
        return carry

    lax.fori_loop(0, lax.div(count, jnp.int32(4)), add, 0)
    flat = acc.reshape(n_out * sub, LANES)

    def emit(c, carry):
        rows = pl.ds(pl.multiple_of(c * 8, 8), 8)
        for t in range(sub):
            rows_buf[rows, t * LANES:(t + 1) * LANES] = flat[pl.ds(c * (8 * sub) + t, 8, stride=sub), :]
        return carry

    parts = sems.shape[0] - 2
    height = n_out // parts
    copies = []
    for n in range(parts):
        lax.fori_loop(n * height // 8, (n + 1) * height // 8, emit, 0)
        rows = pl.ds(n * height, height)
        copies.append(pltpu.make_async_copy(rows_buf.at[rows], out_ref.at[rows], sems.at[2 + n]))
        copies[-1].start()
    for copy in copies:
        copy.wait()


def owner_sums(me, tables, from_b, from_c, sub):
    def whole(x):
        return pl.BlockSpec(x.shape, lambda i, *_: (0,) * len(x.shape))

    table = jax.ShapeDtypeStruct((OSLOT, sub, LANES), jnp.float32)
    early = pl.pallas_call(
        early_kernel,
        out_shape=table,
        grid_spec=pltpu.PrefetchScalarGridSpec(
            num_scalar_prefetch=1,
            grid=(1,),
            in_specs=[whole(x) for x in tables],
            out_specs=whole(table),
            scratch_shapes=[pltpu.VMEM(table.shape, jnp.float32)] * (len(tables) - 1)
            + [
                pltpu.VMEM((len(tables), NAME_ROWS, LANES), jnp.int32),
                pltpu.SMEM((len(tables), NAME_ROWS, LANES), jnp.int32),
                pltpu.SemaphoreType.DMA,
            ],
        ),
        compiler_params=pltpu.CompilerParams(
            dimension_semantics=("arbitrary",), vmem_limit_bytes=20 * 1024 * 1024
        ),
        name="early_sums",
    )(me, *tables)
    return pl.pallas_call(
        last_kernel,
        out_shape=jax.ShapeDtypeStruct((OSLOT, sub * LANES), jnp.float32),
        grid_spec=pltpu.PrefetchScalarGridSpec(
            num_scalar_prefetch=1,
            grid=(1,),
            in_specs=[pl.BlockSpec(memory_space=pl.ANY), whole(from_b), whole(from_c)],
            out_specs=pl.BlockSpec(memory_space=pl.ANY),
            scratch_shapes=[
                pltpu.VMEM(table.shape, jnp.float32),
                pltpu.VMEM((OSLOT, sub * LANES), jnp.float32),
                pltpu.VMEM((NAME_ROWS, LANES), jnp.int32),
                pltpu.SMEM((NAME_ROWS, LANES), jnp.int32),
                pltpu.SemaphoreType.DMA((2 + 4,)),
            ],
        ),
        compiler_params=pltpu.CompilerParams(
            dimension_semantics=("arbitrary",), vmem_limit_bytes=20 * 1024 * 1024
        ),
        name="owner_sums",
    )(me, early, from_b, from_c)


def swap(x, axis, d):
    return lax.ppermute(x, axis, [(i, i ^ d) for i in range(lax.axis_size(axis))])


def direct(p_tiles):
    return [swap(p_tiles, "blk", d) for d in range(2, lax.axis_size("blk"), 2)]


def body(a_tiles, a_cols, p_tiles, route_list, out_slot):
    groups = lax.axis_size("grp")
    me = lax.axis_index("grp")
    rf, tile, cols = a_tiles.shape
    cap = out_slot.shape[1] // groups
    sub = tile * tile // LANES
    middle = (me == 1) | (me == 2)
    takes = [(1, 0), (3, 1), (0, 2), (2, 3)]

    def take(x):
        return lax.ppermute(x, "grp", takes)

    ints = jnp.concatenate([route_list, a_cols], axis=1)
    ints = jnp.concatenate([ints, jnp.pad(out_slot, ((0, 0), (0, a_cols.shape[1])))], axis=0)
    ints_took = take(ints)
    far = direct(p_tiles)
    p_took = take(p_tiles)
    a_took = take(a_tiles)
    far[0], p_took = lax.optimization_barrier((far[0], p_took))
    far_took = direct(p_took)
    mine = [p_tiles, jnp.concatenate(far)]
    other = [swap(x, "blk", 1) for x in mine]

    def tables_own(off, middle):
        ends = jnp.where(off < 2, off, jnp.where(off == 3, 2, 3))
        return jnp.where(middle, jnp.where(off == 0, 0, jnp.where(off == 1, 3, off - 1)), ends)

    def tables_took(off, middle):
        return jnp.where((off == 0) | ((off == 1) & middle), off, 2)

    first = cap // 4
    spans = ((0, cap), (cap, cap), (2 * cap, cap), (2 * cap, first))
    own, to_a, to_b, to_d = partial_sums(ints, [a_tiles], mine + other, tables_own, 3, spans, groups, cap)
    own, a_took, ints_took, p_took, *far_took = lax.optimization_barrier((own, a_took, ints_took, p_took, *far_took))
    from_d = lax.ppermute(to_d, "grp", [(0, 3), (3, 0)])
    from_a = lax.ppermute(to_a, "grp", [(0, 1), (3, 2), (1, 3), (2, 0)])
    from_b = lax.ppermute(to_b, "grp", [(1, 2), (2, 1)])
    took = [p_took] + far_took
    pieces = took + [swap(x, "blk", 1) for x in took]
    spans = ((0, cap), (cap + first, cap - first))
    own_took, to_c = partial_sums(ints_took, [a_took], pieces, tables_took, 2, spans, groups, cap)
    own_took, to_c, from_d = lax.optimization_barrier((own_took, to_c, from_d))
    from_c = lax.ppermute(to_c, "grp", [(1, 0), (2, 3)])
    about = jnp.stack([me, middle.astype(me.dtype)])
    return owner_sums(about, [own, own_took, from_a, from_d], from_b, from_c, sub)


def solution(mesh):
    in_specs = (
        P(("blk", "grp"), None, None),
        P(("blk", "grp"), None),
        P(("blk", "grp"), None, None),
        P(("blk", "grp"), None),
        P(("blk", "grp"), None),
    )
    out_specs = P(("blk", "grp"), None)
    return jax.shard_map(body, mesh=mesh, in_specs=in_specs, out_specs=out_specs, check_vma=False)
```

```python
import functools

import jax
import jax.numpy as jnp
from jax import lax
from jax.experimental import pallas as pl
from jax.experimental.pallas import tpu as pltpu
from jax.sharding import PartitionSpec as P

OSLOT = 128
LANES = 128
ACCS = 4
AHEAD = 2
NAME_ROWS = 16
PART = 256


def log2(n):
    assert n & (n - 1) == 0
    return n.bit_length() - 1


def numbers_kernel(a_ref, route_ref, slot_ref, cols_ref, out_ref, wide):
    rf = a_ref.shape[0]
    out_ref[:rf] = a_ref[...]
    wide[...] = jnp.zeros_like(wide)
    cols = cols_ref[...]
    parts = (route_ref[...], slot_ref[...], lax.shift_right_logical(cols, jnp.int32(log2(PART))), cols & (PART - 1))
    for n, part in enumerate(parts):
        wide[n * rf:n * rf + part.shape[0], :part.shape[1]] = part.astype(jnp.float32)
    out_ref[rf] = wide[...].astype(out_ref.dtype)


def with_numbers(a_tiles, route_list, out_slot, a_cols):
    rf, tile, width = a_tiles.shape
    return pl.pallas_call(
        numbers_kernel,
        out_shape=jax.ShapeDtypeStruct((rf + 1, tile, width), a_tiles.dtype),
        scratch_shapes=[pltpu.VMEM((tile, width), jnp.float32)],
        compiler_params=pltpu.CompilerParams(vmem_limit_bytes=56 * 1024 * 1024),
        cost_estimate=pl.CostEstimate(flops=1, bytes_accessed=1, transcendentals=0),
        name="with_numbers",
    )(a_tiles, route_list, out_slot, a_cols)


def partial_kernel(n_pieces, spans, cap, groups, table_of, rows_in, *refs):
    pieces, refs = refs[:n_pieces], refs[n_pieces:]
    outs, refs = refs[:len(spans)], refs[len(spans):]
    accs, (a_ref, lhs_ref, panel, y_buf, w_buf, *rest, sems) = refs[:ACCS], refs[ACCS:]
    packed_ref, place_vmem, idx_vmem, place_ref, idx_ref = rest
    rf, tile, cols = a_ref.shape
    tiles = cols // tile
    width = panel.shape[2] // tile
    sub = tile * tile // LANES
    n_tables = accs[0].shape[0] // cap
    chunk = 8

    n_places = width * tiles * width
    copies = [
        pltpu.make_async_copy(rows_in.at[rf, :, pl.ds(0, n_places)], packed_ref, sems.at[0]),
        pltpu.make_async_copy(rows_in.at[pl.ds(0, rf)], a_ref, sems.at[1]),
    ]
    at = 0
    for piece in pieces:
        height = piece.shape[0]
        copies.append(pltpu.make_async_copy(piece, panel.at[pl.ds(at, height)], sems.at[len(copies)]))
        at += height
    for copy in copies:
        copy.start()
    copies.pop(0).wait()

    me, blk = lax.axis_index("grp"), lax.axis_index("blk")
    numbers = packed_ref[...].astype(jnp.float32).astype(jnp.int32)
    route, names = numbers[:rf], numbers[rf:rf + 1].astype(jnp.float32)
    owner = lax.shift_right_logical(route, jnp.int32(log2(cap)))
    table = table_of(owner ^ me, (me == 1) | (me == 2))
    place_vmem[...] = jnp.where(table < n_tables, table * cap + (route & (cap - 1)), n_tables * cap)
    cols = numbers[2 * rf:3 * rf] * PART + numbers[3 * rf:4 * rf]
    d = lax.shift_right_logical(cols, jnp.int32(log2(rf * groups))) ^ blk
    half = panel.shape[0] // (2 * rf)
    idx_vmem[...] = ((d & 1) * half + lax.shift_right_logical(d, jnp.int32(1))) * rf + (cols & (rf - 1))
    for n, (src, dst) in enumerate(((place_vmem, place_ref), (idx_vmem, idx_ref))):
        copy = pltpu.make_async_copy(src, dst, sems.at[2 + n_pieces + n])
        copy.start()
        copies.append(copy)

    def clear(c, carry):
        blocks = pl.ds(c * chunk, chunk)
        for acc in accs:
            acc[blocks] = jnp.zeros((chunk, sub, LANES), jnp.float32)
        return carry

    lax.fori_loop(0, n_tables * cap // chunk, clear, 0)
    for acc in accs:
        acc[n_tables * cap] = jnp.zeros((sub, LANES), jnp.float32)
    for copy in copies:
        copy.wait()

    columns = width * tile
    from_col = lax.broadcasted_iota(jnp.int32, (columns, columns), 0)
    to_col = lax.broadcasted_iota(jnp.int32, (columns, columns), 1)
    wanted = jnp.where(to_col < columns // 2, 2 * to_col, 2 * to_col - columns + 1)
    chosen = jnp.where(from_col == wanted, 1.0, 0.0).astype(jnp.bfloat16)
    for row in range(rf):
        split = jnp.dot(panel[row], chosen, preferred_element_type=jnp.float32)
        stacked = jnp.concatenate([split[:, :columns // 2], split[:, columns // 2:]], axis=0)
        lhs_ref[row] = jnp.transpose(stacked).astype(jnp.bfloat16)

    lane = lax.broadcasted_iota(jnp.int32, (tile, LANES), 1)
    lo = lane < tile

    def first_products(row, k):
        both = a_ref[row, :, k * tile:k * tile + LANES]
        none = jnp.zeros_like(both)
        left = jnp.concatenate([jnp.where(lo, both, none), jnp.where(lo, none, both)], axis=0)
        right = jnp.concatenate([panel[idx_ref[row, k]], panel[idx_ref[row, k + 1]]], axis=0)
        return jnp.dot(left, right, preferred_element_type=jnp.float32)

    def keep(u, y):
        for m in range(width // 2):
            x = y[:, m * LANES:(m + 1) * LANES]
            y_buf[u, :, 2 * m * LANES:(2 * m + 1) * LANES] = x.astype(jnp.bfloat16)
            y_buf[u, :, (2 * m + 1) * LANES:(2 * m + 2) * LANES] = pltpu.roll(x, tile, 1).astype(jnp.bfloat16)

    def second_product(row, u):
        lhs = lhs_ref[row]
        w = []
        for m in range(width // 2):
            x = y_buf[u, :, 2 * m * LANES:(2 * m + 1) * LANES]
            xr = y_buf[u, :, (2 * m + 1) * LANES:(2 * m + 2) * LANES]
            none = jnp.zeros_like(x)
            right = jnp.concatenate(
                [
                    jnp.concatenate([jnp.where(lo, x, none), jnp.where(lo, xr, none)], axis=1),
                    jnp.concatenate([jnp.where(lo, none, xr), jnp.where(lo, none, x)], axis=1),
                ],
                axis=0,
            )
            w.append(jnp.dot(lhs, right, preferred_element_type=jnp.float32))
        return w

    def add(row, k, w):
        for q in range(width):
            part = w[q // 2][:, q % 2 * LANES:(q % 2 + 1) * LANES]
            for s in range(0, width, ACCS):
                group = range(s, min(s + ACCS, width))
                places = [place_ref[row, (n * tiles + k) * width + q] for n in group]
                old = [acc[place] for acc, place in zip(accs, places)]
                for acc, place, was, n in zip(accs, places, old, group):
                    acc[place] = was + part[n * sub:(n + 1) * sub]

    def keep_two(u, y):
        keep(u, y[:tile])
        keep(u + 1, y[tile:])

    def hold(n, w):
        for m, part in enumerate(w):
            w_buf[n, :, m * 2 * LANES:(m + 1) * 2 * LANES] = part

    def held(n):
        return [w_buf[n, :, m * 2 * LANES:(m + 1) * 2 * LANES] for m in range(width // 2)]

    for k in range(0, tiles, 2):
        keep_two(k, first_products(0, k))
    for n in range(AHEAD):
        hold(n, second_product(0, n))

    def block_row(row, carry):
        following = jnp.minimum(row + 1, rf - 1)
        w = [held(n) for n in range(AHEAD)]
        for k in range(tiles):
            if k % 2 == 0:
                upcoming = first_products(following, k)
            ahead = k + AHEAD
            w.append(second_product(row, ahead) if ahead < tiles else second_product(following, ahead - tiles))
            add(row, k, w.pop(0))
            if k % 2 == 1:
                keep_two(k - 1, upcoming)
        for n in range(AHEAD):
            hold(n, w[n])
        return carry

    lax.fori_loop(0, rf, block_row, 0)

    named = jnp.zeros((NAME_ROWS, LANES), jnp.float32)
    here = lax.broadcasted_iota(jnp.int32, named.shape, 0)
    for n in range(groups * cap // LANES):
        part = names[:, n * LANES:(n + 1) * LANES]
        named = jnp.where(here == n, jnp.broadcast_to(part, named.shape), named)

    for (first, count), out in zip(spans, outs):

        def merge(c, carry):
            blocks = pl.ds(first + c * chunk, chunk)
            total = accs[0][blocks]
            for acc in accs[1:]:
                total = total + acc[blocks]
            rows = pl.ds(pl.multiple_of(c * (chunk * sub), chunk * sub), chunk * sub)
            out[rows, :] = total.reshape(chunk * sub, LANES).astype(out.dtype)
            return carry

        lax.fori_loop(0, count // chunk, merge, 0)
        out[count * sub:, :] = named.astype(out.dtype)


def partial_sums(rows_in, pieces, table_of, tables, spans, groups, cap):
    rf, tile, cols = rows_in.shape[0] - 1, *rows_in.shape[1:]
    sub = tile * tile // LANES
    width = pieces[0].shape[2]
    rows = sum(x.shape[0] for x in pieces)
    n_places = (width // tile) ** 2 * (cols // tile)
    operands = [rows_in] + pieces
    panel_bytes = rows * tile * width * 2
    return pl.pallas_call(
        functools.partial(partial_kernel, len(pieces), spans, cap, groups, table_of),
        out_shape=[jax.ShapeDtypeStruct((n * sub + NAME_ROWS, LANES), jnp.bfloat16) for _, n in spans],
        grid_spec=pl.GridSpec(
            grid=(1,),
            in_specs=[pl.BlockSpec(memory_space=pl.ANY)] * len(operands),
            out_specs=[pl.BlockSpec((n * sub + NAME_ROWS, LANES), lambda i: (0, 0)) for _, n in spans],
            scratch_shapes=[pltpu.VMEM((tables * cap + 1, sub, LANES), jnp.float32)] * ACCS
            + [
                pltpu.VMEM((rf, tile, cols), jnp.bfloat16),
                pltpu.VMEM((rf, width // 2, 2 * tile), jnp.bfloat16),
                pltpu.VMEM((rows, tile, width), jnp.bfloat16),
                pltpu.VMEM((cols // tile, tile, 2 * width), jnp.bfloat16),
                pltpu.VMEM((AHEAD, width // 2, 2 * width), jnp.float32),
                pltpu.VMEM((tile, n_places), jnp.bfloat16),
                pltpu.VMEM((rf, n_places), jnp.int32),
                pltpu.VMEM((rf, n_places), jnp.int32),
                pltpu.SMEM((rf, n_places), jnp.int32),
                pltpu.SMEM((rf, n_places), jnp.int32),
                pltpu.SemaphoreType.DMA((len(operands) + 3,)),
            ],
        ),
        compiler_params=pltpu.CompilerParams(
            dimension_semantics=("arbitrary",), vmem_limit_bytes=26 * 1024 * 1024 + panel_bytes
        ),
        cost_estimate=pl.CostEstimate(flops=1, bytes_accessed=1, transcendentals=0),
        name="partial_sums",
    )(*operands)


def early_kernel(me_ref, *refs):
    tables, out_ref, accs, (vmem_names, smem_names, sem) = refs[:4], refs[4], refs[5:-3], refs[-3:]
    n_out, sub = out_ref.shape[:2]
    counts = [(x.shape[0] - NAME_ROWS) // sub for x in tables]
    cap, some = counts[0], counts[-1]
    chunk = 8
    at = me_ref[0] * cap
    row, lane = lax.div(at, jnp.int32(LANES)), lax.rem(at, jnp.int32(LANES))

    for n, (x, count) in enumerate(zip(tables, counts)):
        vmem_names[n] = x[pl.ds(count * sub, NAME_ROWS), :].astype(jnp.float32).astype(jnp.int32)
    copy = pltpu.make_async_copy(vmem_names, smem_names, sem)
    copy.start()

    def clear(c, carry):
        for acc in accs:
            acc[pl.ds(c * chunk, chunk)] = jnp.zeros((chunk, sub, LANES), jnp.float32)
        return carry

    lax.fori_loop(0, n_out // chunk, clear, 0)
    copy.wait()

    def add_to(c, numbers):
        src = pl.ds(pl.multiple_of(c * sub, sub), sub)
        names = [smem_names[n, row, lane + c] for n in numbers]
        old = [acc[name] for acc, name in zip(accs, names)]
        for acc, name, was, n in zip(accs, names, old, numbers):
            acc[name] = was + tables[n][src, :].astype(jnp.float32)

    def add(c, carry):
        add_to(c, (0, 1, 2))
        return carry

    def add_some(c, carry):
        add_to(c, (3,))
        return carry

    lax.fori_loop(0, cap, add, 0, unroll=4)
    lax.fori_loop(0, some, add_some, 0, unroll=4)

    def merge(c, carry):
        blocks = pl.ds(c * chunk, chunk)
        total = accs[0][blocks]
        for acc in accs[1:]:
            total = total + acc[blocks]
        out_ref[blocks] = total
        return carry

    lax.fori_loop(0, n_out // chunk, merge, 0)


def last_kernel(me_ref, table, from_b, from_c, out_ref, acc, rows_buf, vmem_names, smem_names, sems):
    n_out, sub = acc.shape[:2]
    cap, rest = [(x.shape[0] - NAME_ROWS) // sub for x in (from_b, from_c)]
    pick = me_ref[1] == 1
    count = jnp.where(pick, cap, rest)
    at = me_ref[0] * cap
    row, lane = lax.div(at, jnp.int32(LANES)), lax.rem(at, jnp.int32(LANES)) + (cap - count)
    fill = pltpu.make_async_copy(table, acc, sems.at[0])
    fill.start()

    def arrived(rows_b, rows_c):
        return jnp.where(pick, from_b[rows_b, :].astype(jnp.float32), from_c[rows_c, :].astype(jnp.float32))

    vmem_names[...] = arrived(pl.ds(cap * sub, NAME_ROWS), pl.ds(rest * sub, NAME_ROWS)).astype(jnp.int32)
    copy = pltpu.make_async_copy(vmem_names, smem_names, sems.at[1])
    copy.start()
    copy.wait()
    fill.wait()

    def add(c, carry):
        for u in range(4):
            n = c * 4 + u
            rows_b = pl.ds(pl.multiple_of(n * sub, sub), sub)
            rows_c = pl.ds(pl.multiple_of(jnp.minimum(n, rest - 1) * sub, sub), sub)
            acc[smem_names[row, lane + n]] += arrived(rows_b, rows_c)
        return carry

    lax.fori_loop(0, lax.div(count, jnp.int32(4)), add, 0)
    flat = acc.reshape(n_out * sub, LANES)

    def emit(c, carry):
        rows = pl.ds(pl.multiple_of(c * 8, 8), 8)
        for t in range(sub):
            rows_buf[rows, t * LANES:(t + 1) * LANES] = flat[pl.ds(c * (8 * sub) + t, 8, stride=sub), :]
        return carry

    parts = sems.shape[0] - 2
    height = n_out // parts
    copies = []
    for n in range(parts):
        lax.fori_loop(n * height // 8, (n + 1) * height // 8, emit, 0)
        rows = pl.ds(n * height, height)
        copies.append(pltpu.make_async_copy(rows_buf.at[rows], out_ref.at[rows], sems.at[2 + n]))
        copies[-1].start()
    for copy in copies:
        copy.wait()


def owner_sums(me, tables, from_b, from_c, sub):
    def whole(x):
        return pl.BlockSpec(x.shape, lambda i, *_: (0,) * len(x.shape))

    table = jax.ShapeDtypeStruct((OSLOT, sub, LANES), jnp.float32)
    early = pl.pallas_call(
        early_kernel,
        out_shape=table,
        grid_spec=pltpu.PrefetchScalarGridSpec(
            num_scalar_prefetch=1,
            grid=(1,),
            in_specs=[whole(x) for x in tables],
            out_specs=whole(table),
            scratch_shapes=[pltpu.VMEM(table.shape, jnp.float32)] * (len(tables) - 1)
            + [
                pltpu.VMEM((len(tables), NAME_ROWS, LANES), jnp.int32),
                pltpu.SMEM((len(tables), NAME_ROWS, LANES), jnp.int32),
                pltpu.SemaphoreType.DMA,
            ],
        ),
        compiler_params=pltpu.CompilerParams(
            dimension_semantics=("arbitrary",), vmem_limit_bytes=20 * 1024 * 1024
        ),
        name="early_sums",
    )(me, *tables)
    return pl.pallas_call(
        last_kernel,
        out_shape=jax.ShapeDtypeStruct((OSLOT, sub * LANES), jnp.float32),
        grid_spec=pltpu.PrefetchScalarGridSpec(
            num_scalar_prefetch=1,
            grid=(1,),
            in_specs=[pl.BlockSpec(memory_space=pl.ANY), whole(from_b), whole(from_c)],
            out_specs=pl.BlockSpec(memory_space=pl.ANY),
            scratch_shapes=[
                pltpu.VMEM(table.shape, jnp.float32),
                pltpu.VMEM((OSLOT, sub * LANES), jnp.float32),
                pltpu.VMEM((NAME_ROWS, LANES), jnp.int32),
                pltpu.SMEM((NAME_ROWS, LANES), jnp.int32),
                pltpu.SemaphoreType.DMA((2 + 4,)),
            ],
        ),
        compiler_params=pltpu.CompilerParams(
            dimension_semantics=("arbitrary",), vmem_limit_bytes=20 * 1024 * 1024
        ),
        name="owner_sums",
    )(me, early, from_b, from_c)


def swap(x, axis, d):
    return lax.ppermute(x, axis, [(i, i ^ d) for i in range(lax.axis_size(axis))])


def direct(p_tiles):
    return [swap(p_tiles, "blk", d) for d in range(2, lax.axis_size("blk"), 2)]


def body(a_tiles, a_cols, p_tiles, route_list, out_slot):
    groups = lax.axis_size("grp")
    me = lax.axis_index("grp")
    rf, tile, cols = a_tiles.shape
    cap = out_slot.shape[1] // groups
    sub = tile * tile // LANES
    middle = (me == 1) | (me == 2)
    takes = [(1, 0), (3, 1), (0, 2), (2, 3)]

    def take(x):
        return lax.ppermute(x, "grp", takes)

    rows_sent = with_numbers(a_tiles, route_list, out_slot, a_cols)
    far = direct(p_tiles)
    p_took = take(p_tiles)
    a_took = take(rows_sent)
    far[0], p_took = lax.optimization_barrier((far[0], p_took))
    far_took = direct(p_took)
    mine = [p_tiles, jnp.concatenate(far)]
    other = [swap(x, "blk", 1) for x in mine]

    def tables_own(off, middle):
        ends = jnp.where(off < 2, off, jnp.where(off == 3, 2, 3))
        return jnp.where(middle, jnp.where(off == 0, 0, jnp.where(off == 1, 3, off - 1)), ends)

    def tables_took(off, middle):
        return jnp.where((off == 0) | ((off == 1) & middle), off, 2)

    first = cap // 4
    spans = ((0, cap), (cap, cap), (2 * cap, cap), (2 * cap, first))
    own, to_a, to_b, to_d = partial_sums(rows_sent, mine + other, tables_own, 3, spans, groups, cap)
    own, a_took, p_took, *far_took = lax.optimization_barrier((own, a_took, p_took, *far_took))
    from_d = lax.ppermute(to_d, "grp", [(0, 3), (3, 0)])
    from_a = lax.ppermute(to_a, "grp", [(0, 1), (3, 2), (1, 3), (2, 0)])
    from_b = lax.ppermute(to_b, "grp", [(1, 2), (2, 1)])
    took = [p_took] + far_took
    pieces = took + [swap(x, "blk", 1) for x in took]
    spans = ((0, cap), (cap + first, cap - first))
    own_took, to_c = partial_sums(a_took, pieces, tables_took, 2, spans, groups, cap)
    own_took, to_c, from_d = lax.optimization_barrier((own_took, to_c, from_d))
    from_c = lax.ppermute(to_c, "grp", [(1, 0), (2, 3)])
    about = jnp.stack([me, middle.astype(me.dtype)])
    return owner_sums(about, [own, own_took, from_a, from_d], from_b, from_c, sub)


def solution(mesh):
    in_specs = (
        P(("blk", "grp"), None, None),
        P(("blk", "grp"), None),
        P(("blk", "grp"), None, None),
        P(("blk", "grp"), None),
        P(("blk", "grp"), None),
    )
    out_specs = P(("blk", "grp"), None)
    return jax.shard_map(body, mesh=mesh, in_specs=in_specs, out_specs=out_specs, check_vma=False)
```

```python
import functools

import jax
import jax.numpy as jnp
from jax import lax
from jax.experimental import pallas as pl
from jax.experimental.pallas import tpu as pltpu
from jax.sharding import PartitionSpec as P

OSLOT = 128
LANES = 128
ACCS = 4
AHEAD = 2
NAME_ROWS = 16
PART = 256


def log2(n):
    assert n & (n - 1) == 0
    return n.bit_length() - 1


def number_columns(n_places):
    return 0, n_places, 2 * n_places, 2 * n_places + LANES


def numbers_kernel(a_ref, route_ref, slot_ref, cols_ref, out_ref, wide):
    rf, tile, width = a_ref.shape
    out_ref[:rf * tile, :] = a_ref[...].reshape(rf * tile, width)
    wide[...] = jnp.zeros_like(wide)
    cols = cols_ref[...]
    parts = (route_ref[...], slot_ref[...], lax.shift_right_logical(cols, jnp.int32(log2(PART))), cols & (PART - 1))
    for at, part in zip(number_columns(route_ref.shape[1]), parts):
        wide[:part.shape[0], at:at + part.shape[1]] = part.astype(jnp.float32)
    out_ref[rf * tile:, :] = wide[...].astype(out_ref.dtype)


def with_numbers(a_tiles, route_list, out_slot, a_cols):
    rf, tile, width = a_tiles.shape
    return pl.pallas_call(
        numbers_kernel,
        out_shape=jax.ShapeDtypeStruct((rf * tile + NAME_ROWS, width), a_tiles.dtype),
        scratch_shapes=[pltpu.VMEM((NAME_ROWS, width), jnp.float32)],
        compiler_params=pltpu.CompilerParams(vmem_limit_bytes=56 * 1024 * 1024),
        cost_estimate=pl.CostEstimate(flops=1, bytes_accessed=1, transcendentals=0),
        name="with_numbers",
    )(a_tiles, route_list, out_slot, a_cols)


def partial_kernel(n_pieces, spans, cap, groups, table_of, rows_in, *refs):
    pieces, refs = refs[:n_pieces], refs[n_pieces:]
    outs, refs = refs[:len(spans)], refs[len(spans):]
    accs, (a_ref, lhs_ref, panel, y_buf, w_buf, *rest, sems) = refs[:ACCS], refs[ACCS:]
    packed_ref, place_vmem, idx_vmem, place_ref, idx_ref = rest
    tile = panel.shape[1]
    rf, tiles = a_ref.shape[0] // tile, a_ref.shape[1] // tile
    width = panel.shape[2] // tile
    sub = tile * tile // LANES
    n_tables = accs[0].shape[0] // cap
    chunk = 8

    n_places = width * tiles * width
    copies = [
        pltpu.make_async_copy(rows_in.at[pl.ds(rf * tile, NAME_ROWS)], packed_ref, sems.at[0]),
        pltpu.make_async_copy(rows_in.at[pl.ds(0, rf * tile)], a_ref, sems.at[1]),
    ]
    at = 0
    for piece in pieces:
        height = piece.shape[0]
        copies.append(pltpu.make_async_copy(piece, panel.at[pl.ds(at, height)], sems.at[len(copies)]))
        at += height
    for copy in copies:
        copy.start()
    copies.pop(0).wait()

    me, blk = lax.axis_index("grp"), lax.axis_index("blk")
    numbers = packed_ref[...].astype(jnp.float32).astype(jnp.int32)
    at_route, at_slot, at_high, at_low = number_columns(n_places)
    route = numbers[:rf, at_route:at_route + n_places]
    names = numbers[:1, at_slot:at_slot + n_places].astype(jnp.float32)
    owner = lax.shift_right_logical(route, jnp.int32(log2(cap)))
    table = table_of(owner ^ me, (me == 1) | (me == 2))
    place_vmem[...] = jnp.where(table < n_tables, table * cap + (route & (cap - 1)), n_tables * cap)
    cols = numbers[:rf, at_high:at_high + LANES] * PART + numbers[:rf, at_low:at_low + LANES]
    d = lax.shift_right_logical(cols, jnp.int32(log2(rf * groups))) ^ blk
    half = panel.shape[0] // (2 * rf)
    idx_vmem[...] = ((d & 1) * half + lax.shift_right_logical(d, jnp.int32(1))) * rf + (cols & (rf - 1))
    for n, (src, dst) in enumerate(((place_vmem, place_ref), (idx_vmem, idx_ref))):
        copy = pltpu.make_async_copy(src, dst, sems.at[2 + n_pieces + n])
        copy.start()
        copies.append(copy)

    def clear(c, carry):
        blocks = pl.ds(c * chunk, chunk)
        for acc in accs:
            acc[blocks] = jnp.zeros((chunk, sub, LANES), jnp.float32)
        return carry

    lax.fori_loop(0, n_tables * cap // chunk, clear, 0)
    for acc in accs:
        acc[n_tables * cap] = jnp.zeros((sub, LANES), jnp.float32)
    for copy in copies:
        copy.wait()

    columns = width * tile
    from_col = lax.broadcasted_iota(jnp.int32, (columns, columns), 0)
    to_col = lax.broadcasted_iota(jnp.int32, (columns, columns), 1)
    wanted = jnp.where(to_col < columns // 2, 2 * to_col, 2 * to_col - columns + 1)
    chosen = jnp.where(from_col == wanted, 1.0, 0.0).astype(jnp.bfloat16)
    for row in range(rf):
        split = jnp.dot(panel[row], chosen, preferred_element_type=jnp.float32)
        stacked = jnp.concatenate([split[:, :columns // 2], split[:, columns // 2:]], axis=0)
        lhs_ref[row] = jnp.transpose(stacked).astype(jnp.bfloat16)

    lane = lax.broadcasted_iota(jnp.int32, (tile, LANES), 1)
    lo = lane < tile

    def first_products(row, k):
        both = a_ref[pl.ds(pl.multiple_of(row * tile, tile), tile), k * tile:k * tile + LANES]
        none = jnp.zeros_like(both)
        left = jnp.concatenate([jnp.where(lo, both, none), jnp.where(lo, none, both)], axis=0)
        right = jnp.concatenate([panel[idx_ref[row, k]], panel[idx_ref[row, k + 1]]], axis=0)
        return jnp.dot(left, right, preferred_element_type=jnp.float32)

    def keep(u, y):
        for m in range(width // 2):
            x = y[:, m * LANES:(m + 1) * LANES]
            y_buf[u, :, 2 * m * LANES:(2 * m + 1) * LANES] = x.astype(jnp.bfloat16)
            y_buf[u, :, (2 * m + 1) * LANES:(2 * m + 2) * LANES] = pltpu.roll(x, tile, 1).astype(jnp.bfloat16)

    def second_product(row, u):
        lhs = lhs_ref[row]
        w = []
        for m in range(width // 2):
            x = y_buf[u, :, 2 * m * LANES:(2 * m + 1) * LANES]
            xr = y_buf[u, :, (2 * m + 1) * LANES:(2 * m + 2) * LANES]
            none = jnp.zeros_like(x)
            right = jnp.concatenate(
                [
                    jnp.concatenate([jnp.where(lo, x, none), jnp.where(lo, xr, none)], axis=1),
                    jnp.concatenate([jnp.where(lo, none, xr), jnp.where(lo, none, x)], axis=1),
                ],
                axis=0,
            )
            w.append(jnp.dot(lhs, right, preferred_element_type=jnp.float32))
        return w

    def add(row, k, w):
        for q in range(width):
            part = w[q // 2][:, q % 2 * LANES:(q % 2 + 1) * LANES]
            for s in range(0, width, ACCS):
                group = range(s, min(s + ACCS, width))
                places = [place_ref[row, (n * tiles + k) * width + q] for n in group]
                old = [acc[place] for acc, place in zip(accs, places)]
                for acc, place, was, n in zip(accs, places, old, group):
                    acc[place] = was + part[n * sub:(n + 1) * sub]

    def keep_two(u, y):
        keep(u, y[:tile])
        keep(u + 1, y[tile:])

    def hold(n, w):
        for m, part in enumerate(w):
            w_buf[n, :, m * 2 * LANES:(m + 1) * 2 * LANES] = part

    def held(n):
        return [w_buf[n, :, m * 2 * LANES:(m + 1) * 2 * LANES] for m in range(width // 2)]

    for k in range(0, tiles, 2):
        keep_two(k, first_products(0, k))
    for n in range(AHEAD):
        hold(n, second_product(0, n))

    def block_row(row, carry):
        following = jnp.minimum(row + 1, rf - 1)
        w = [held(n) for n in range(AHEAD)]
        for k in range(tiles):
            if k % 2 == 0:
                upcoming = first_products(following, k)
            ahead = k + AHEAD
            w.append(second_product(row, ahead) if ahead < tiles else second_product(following, ahead - tiles))
            add(row, k, w.pop(0))
            if k % 2 == 1:
                keep_two(k - 1, upcoming)
        for n in range(AHEAD):
            hold(n, w[n])
        return carry

    lax.fori_loop(0, rf, block_row, 0)

    named = jnp.zeros((NAME_ROWS, LANES), jnp.float32)
    here = lax.broadcasted_iota(jnp.int32, named.shape, 0)
    for n in range(groups * cap // LANES):
        part = names[:, n * LANES:(n + 1) * LANES]
        named = jnp.where(here == n, jnp.broadcast_to(part, named.shape), named)

    for (first, count), out in zip(spans, outs):

        def merge(c, carry):
            blocks = pl.ds(first + c * chunk, chunk)
            total = accs[0][blocks]
            for acc in accs[1:]:
                total = total + acc[blocks]
            rows = pl.ds(pl.multiple_of(c * (chunk * sub), chunk * sub), chunk * sub)
            out[rows, :] = total.reshape(chunk * sub, LANES).astype(out.dtype)
            return carry

        lax.fori_loop(0, count // chunk, merge, 0)
        out[count * sub:, :] = named.astype(out.dtype)


def partial_sums(rows_in, pieces, table_of, tables, spans, groups, cap):
    tile, cols = pieces[0].shape[1], rows_in.shape[1]
    rf = (rows_in.shape[0] - NAME_ROWS) // tile
    sub = tile * tile // LANES
    width = pieces[0].shape[2]
    rows = sum(x.shape[0] for x in pieces)
    n_places = (width // tile) ** 2 * (cols // tile)
    operands = [rows_in] + pieces
    panel_bytes = rows * tile * width * 2
    return pl.pallas_call(
        functools.partial(partial_kernel, len(pieces), spans, cap, groups, table_of),
        out_shape=[jax.ShapeDtypeStruct((n * sub + NAME_ROWS, LANES), jnp.bfloat16) for _, n in spans],
        grid_spec=pl.GridSpec(
            grid=(1,),
            in_specs=[pl.BlockSpec(memory_space=pl.ANY)] * len(operands),
            out_specs=[pl.BlockSpec((n * sub + NAME_ROWS, LANES), lambda i: (0, 0)) for _, n in spans],
            scratch_shapes=[pltpu.VMEM((tables * cap + 1, sub, LANES), jnp.float32)] * ACCS
            + [
                pltpu.VMEM((rf * tile, cols), jnp.bfloat16),
                pltpu.VMEM((rf, width // 2, 2 * tile), jnp.bfloat16),
                pltpu.VMEM((rows, tile, width), jnp.bfloat16),
                pltpu.VMEM((cols // tile, tile, 2 * width), jnp.bfloat16),
                pltpu.VMEM((AHEAD, width // 2, 2 * width), jnp.float32),
                pltpu.VMEM((NAME_ROWS, cols), jnp.bfloat16),
                pltpu.VMEM((rf, n_places), jnp.int32),
                pltpu.VMEM((rf, LANES), jnp.int32),
                pltpu.SMEM((rf, n_places), jnp.int32),
                pltpu.SMEM((rf, LANES), jnp.int32),
                pltpu.SemaphoreType.DMA((len(operands) + 3,)),
            ],
        ),
        compiler_params=pltpu.CompilerParams(
            dimension_semantics=("arbitrary",), vmem_limit_bytes=26 * 1024 * 1024 + panel_bytes
        ),
        cost_estimate=pl.CostEstimate(flops=1, bytes_accessed=1, transcendentals=0),
        name="partial_sums",
    )(*operands)


def early_kernel(me_ref, *refs):
    tables, out_ref, accs, (vmem_names, smem_names, sem) = refs[:3], refs[3], refs[4:-3], refs[-3:]
    n_out, sub = out_ref.shape[:2]
    cap = (tables[0].shape[0] - NAME_ROWS) // sub
    chunk = 8
    at = me_ref[0] * cap
    row, lane = lax.div(at, jnp.int32(LANES)), lax.rem(at, jnp.int32(LANES))

    for n, x in enumerate(tables):
        vmem_names[n] = x[pl.ds(cap * sub, NAME_ROWS), :].astype(jnp.float32).astype(jnp.int32)
    copy = pltpu.make_async_copy(vmem_names, smem_names, sem)
    copy.start()

    def clear(c, carry):
        for acc in accs:
            acc[pl.ds(c * chunk, chunk)] = jnp.zeros((chunk, sub, LANES), jnp.float32)
        return carry

    lax.fori_loop(0, n_out // chunk, clear, 0)
    copy.wait()

    def add(c, carry):
        src = pl.ds(pl.multiple_of(c * sub, sub), sub)
        names = [smem_names[n, row, lane + c] for n in range(len(tables))]
        old = [acc[name] for acc, name in zip(accs, names)]
        for acc, name, was, x in zip(accs, names, old, tables):
            acc[name] = was + x[src, :].astype(jnp.float32)
        return carry

    lax.fori_loop(0, cap, add, 0, unroll=4)

    def merge(c, carry):
        blocks = pl.ds(c * chunk, chunk)
        total = accs[0][blocks]
        for acc in accs[1:]:
            total = total + acc[blocks]
        out_ref[blocks] = total
        return carry

    lax.fori_loop(0, n_out // chunk, merge, 0)


def last_kernel(me_ref, table, from_b, from_c, from_d, out_ref, acc, rows_buf, vmem_names, smem_names, sems):
    n_out, sub = acc.shape[:2]
    cap, rest, first = [(x.shape[0] - NAME_ROWS) // sub for x in (from_b, from_c, from_d)]
    pick = me_ref[1] == 1
    at = me_ref[0] * cap
    row, lane = lax.div(at, jnp.int32(LANES)), lax.rem(at, jnp.int32(LANES))
    fill = pltpu.make_async_copy(table, acc, sems.at[0])
    fill.start()

    def arrived(rows_b, other, rows):
        return jnp.where(pick, from_b[rows_b, :].astype(jnp.float32), other[rows, :].astype(jnp.float32))

    names = arrived(pl.ds(cap * sub, NAME_ROWS), from_c, pl.ds(rest * sub, NAME_ROWS))
    vmem_names[...] = names.astype(jnp.int32)
    copy = pltpu.make_async_copy(vmem_names, smem_names, sems.at[1])
    copy.start()
    copy.wait()
    fill.wait()

    for start, count, other in ((0, first, from_d), (first, rest, from_c)):

        def add(c, carry):
            rows_b = pl.ds(pl.multiple_of((start + c) * sub, sub), sub)
            rows = pl.ds(pl.multiple_of(c * sub, sub), sub)
            acc[smem_names[row, lane + (start + c)]] += arrived(rows_b, other, rows)
            return carry

        lax.fori_loop(0, count, add, 0, unroll=4)
    flat = acc.reshape(n_out * sub, LANES)

    def emit(c, carry):
        rows = pl.ds(pl.multiple_of(c * 8, 8), 8)
        for t in range(sub):
            rows_buf[rows, t * LANES:(t + 1) * LANES] = flat[pl.ds(c * (8 * sub) + t, 8, stride=sub), :]
        return carry

    parts = sems.shape[0] - 2
    height = n_out // parts
    copies = []
    for n in range(parts):
        lax.fori_loop(n * height // 8, (n + 1) * height // 8, emit, 0)
        rows = pl.ds(n * height, height)
        copies.append(pltpu.make_async_copy(rows_buf.at[rows], out_ref.at[rows], sems.at[2 + n]))
        copies[-1].start()
    for copy in copies:
        copy.wait()


def owner_sums(me, tables, lasts, sub):
    def whole(x):
        return pl.BlockSpec(x.shape, lambda i, *_: (0,) * len(x.shape))

    table = jax.ShapeDtypeStruct((OSLOT, sub, LANES), jnp.float32)
    early = pl.pallas_call(
        early_kernel,
        out_shape=table,
        grid_spec=pltpu.PrefetchScalarGridSpec(
            num_scalar_prefetch=1,
            grid=(1,),
            in_specs=[whole(x) for x in tables],
            out_specs=whole(table),
            scratch_shapes=[pltpu.VMEM(table.shape, jnp.float32)] * len(tables)
            + [
                pltpu.VMEM((len(tables), NAME_ROWS, LANES), jnp.int32),
                pltpu.SMEM((len(tables), NAME_ROWS, LANES), jnp.int32),
                pltpu.SemaphoreType.DMA,
            ],
        ),
        compiler_params=pltpu.CompilerParams(
            dimension_semantics=("arbitrary",), vmem_limit_bytes=20 * 1024 * 1024
        ),
        name="early_sums",
    )(me, *tables)
    return pl.pallas_call(
        last_kernel,
        out_shape=jax.ShapeDtypeStruct((OSLOT, sub * LANES), jnp.float32),
        grid_spec=pltpu.PrefetchScalarGridSpec(
            num_scalar_prefetch=1,
            grid=(1,),
            in_specs=[pl.BlockSpec(memory_space=pl.ANY)] + [whole(x) for x in lasts],
            out_specs=pl.BlockSpec(memory_space=pl.ANY),
            scratch_shapes=[
                pltpu.VMEM(table.shape, jnp.float32),
                pltpu.VMEM((OSLOT, sub * LANES), jnp.float32),
                pltpu.VMEM((NAME_ROWS, LANES), jnp.int32),
                pltpu.SMEM((NAME_ROWS, LANES), jnp.int32),
                pltpu.SemaphoreType.DMA((2 + 4,)),
            ],
        ),
        compiler_params=pltpu.CompilerParams(
            dimension_semantics=("arbitrary",), vmem_limit_bytes=20 * 1024 * 1024
        ),
        name="owner_sums",
    )(me, early, *lasts)


def swap(x, axis, d):
    return lax.ppermute(x, axis, [(i, i ^ d) for i in range(lax.axis_size(axis))])


def direct(p_tiles):
    return [swap(p_tiles, "blk", d) for d in range(2, lax.axis_size("blk"), 2)]


def body(a_tiles, a_cols, p_tiles, route_list, out_slot):
    groups = lax.axis_size("grp")
    me = lax.axis_index("grp")
    rf, tile, cols = a_tiles.shape
    cap = out_slot.shape[1] // groups
    sub = tile * tile // LANES
    middle = (me == 1) | (me == 2)
    takes = [(1, 0), (3, 1), (0, 2), (2, 3)]

    def take(x):
        return lax.ppermute(x, "grp", takes)

    rows_sent = with_numbers(a_tiles, route_list, out_slot, a_cols)
    far = direct(p_tiles)
    p_took = take(p_tiles)
    a_took = take(rows_sent)
    far[0], p_took = lax.optimization_barrier((far[0], p_took))
    far_took = direct(p_took)
    mine = [p_tiles, jnp.concatenate(far)]
    other = [swap(x, "blk", 1) for x in mine]

    def tables_own(off, middle):
        ends = jnp.where(off < 2, off, jnp.where(off == 3, 2, 3))
        return jnp.where(middle, jnp.where(off == 0, 0, jnp.where(off == 1, 3, off - 1)), ends)

    def tables_took(off, middle):
        return jnp.where((off == 0) | ((off == 1) & middle), off, 2)

    first = cap // 4
    spans = ((0, cap), (cap, cap), (2 * cap, cap), (2 * cap, first))
    own, to_a, to_b, to_d = partial_sums(rows_sent, mine + other, tables_own, 3, spans, groups, cap)
    own, a_took, p_took, *far_took = lax.optimization_barrier((own, a_took, p_took, *far_took))
    from_a = lax.ppermute(to_a, "grp", [(0, 1), (3, 2), (1, 3), (2, 0)])
    from_b = lax.ppermute(to_b, "grp", [(1, 2), (2, 1)])
    took = [p_took] + far_took
    pieces = took + [swap(x, "blk", 1) for x in took]
    spans = ((0, cap), (cap + first, cap - first))
    own_took, to_c = partial_sums(a_took, pieces, tables_took, 2, spans, groups, cap)
    from_c = lax.ppermute(to_c, "grp", [(1, 0), (2, 3)])
    to_d, to_c = lax.optimization_barrier((to_d, to_c))
    from_d = lax.ppermute(to_d, "grp", [(0, 3), (3, 0)])
    about = jnp.stack([me, middle.astype(me.dtype)])
    return owner_sums(about, [own, own_took, from_a], [from_b, from_c, from_d], sub)


def solution(mesh):
    in_specs = (
        P(("blk", "grp"), None, None),
        P(("blk", "grp"), None),
        P(("blk", "grp"), None, None),
        P(("blk", "grp"), None),
        P(("blk", "grp"), None),
    )
    out_specs = P(("blk", "grp"), None)
    return jax.shard_map(body, mesh=mesh, in_specs=in_specs, out_specs=out_specs, check_vma=False)
```

```python
import functools

import jax
import jax.numpy as jnp
from jax import lax
from jax.experimental import pallas as pl
from jax.experimental.pallas import tpu as pltpu
from jax.sharding import PartitionSpec as P

OSLOT = 128
LANES = 128
ACCS = 4
AHEAD = 2
NAME_ROWS = 16
PART = 256
PARTS = 2


def log2(n):
    assert n & (n - 1) == 0
    return n.bit_length() - 1


def number_columns(n_places):
    return 0, n_places, 2 * n_places, 2 * n_places + LANES


def numbers_kernel(a_ref, route_ref, slot_ref, cols_ref, out_ref, wide):
    rf, tile, width = a_ref.shape
    out_ref[:rf * tile, :] = a_ref[...].reshape(rf * tile, width)
    wide[...] = jnp.zeros_like(wide)
    cols = cols_ref[...]
    parts = (route_ref[...], slot_ref[...], lax.shift_right_logical(cols, jnp.int32(log2(PART))), cols & (PART - 1))
    for at, part in zip(number_columns(route_ref.shape[1]), parts):
        wide[:part.shape[0], at:at + part.shape[1]] = part.astype(jnp.float32)
    out_ref[rf * tile:, :] = wide[...].astype(out_ref.dtype)


def with_numbers(a_tiles, route_list, out_slot, a_cols):
    rf, tile, width = a_tiles.shape
    return pl.pallas_call(
        numbers_kernel,
        out_shape=jax.ShapeDtypeStruct((rf * tile + NAME_ROWS, width), a_tiles.dtype),
        scratch_shapes=[pltpu.VMEM((NAME_ROWS, width), jnp.float32)],
        compiler_params=pltpu.CompilerParams(vmem_limit_bytes=56 * 1024 * 1024),
        cost_estimate=pl.CostEstimate(flops=1, bytes_accessed=1, transcendentals=0),
        name="with_numbers",
    )(a_tiles, route_list, out_slot, a_cols)


def partial_kernel(n_pieces, spans, cap, groups, table_of, rows_in, *refs):
    pieces, refs = refs[:n_pieces], refs[n_pieces:]
    outs, refs = refs[:len(spans)], refs[len(spans):]
    accs, (a_ref, lhs_ref, panel, y_buf, w_buf, *rest, sems) = refs[:ACCS], refs[ACCS:]
    packed_ref, place_vmem, idx_vmem, place_ref, idx_ref = rest
    tile = panel.shape[1]
    rf, tiles = a_ref.shape[0] // tile, a_ref.shape[1] // tile
    width = panel.shape[2] // tile
    sub = tile * tile // LANES
    n_tables = accs[0].shape[0] // cap
    chunk = 8

    n_places = width * tiles * width
    copies = [
        pltpu.make_async_copy(rows_in.at[pl.ds(rf * tile, NAME_ROWS)], packed_ref, sems.at[0]),
    ]
    for n in range(0, rf, PARTS):
        part = pl.ds(n * tile, PARTS * tile)
        copies.append(pltpu.make_async_copy(rows_in.at[part], a_ref.at[part], sems.at[len(copies)]))
    at = 0
    for piece in pieces:
        for n in range(0, piece.shape[0], rf):
            part, whole = piece.at[pl.ds(n, rf)], panel.at[pl.ds(at, rf)]
            copies.append(pltpu.make_async_copy(part, whole, sems.at[len(copies)]))
            at += rf
    for copy in copies:
        copy.start()
    copies.pop(0).wait()

    me, blk = lax.axis_index("grp"), lax.axis_index("blk")
    numbers = packed_ref[...].astype(jnp.float32).astype(jnp.int32)
    at_route, at_slot, at_high, at_low = number_columns(n_places)
    route = numbers[:rf, at_route:at_route + n_places]
    names = numbers[:1, at_slot:at_slot + n_places].astype(jnp.float32)
    owner = lax.shift_right_logical(route, jnp.int32(log2(cap)))
    table = table_of(owner ^ me, (me == 1) | (me == 2))
    place_vmem[...] = jnp.where(table < n_tables, table * cap + (route & (cap - 1)), n_tables * cap)
    cols = numbers[:rf, at_high:at_high + LANES] * PART + numbers[:rf, at_low:at_low + LANES]
    d = lax.shift_right_logical(cols, jnp.int32(log2(rf * groups))) ^ blk
    half = panel.shape[0] // (2 * rf)
    idx_vmem[...] = ((d & 1) * half + lax.shift_right_logical(d, jnp.int32(1))) * rf + (cols & (rf - 1))
    for n, (src, dst) in enumerate(((place_vmem, place_ref), (idx_vmem, idx_ref))):
        copy = pltpu.make_async_copy(src, dst, sems.at[sems.shape[0] - 2 + n])
        copy.start()
        copies.append(copy)

    def clear(c, carry):
        blocks = pl.ds(c * chunk, chunk)
        for acc in accs:
            acc[blocks] = jnp.zeros((chunk, sub, LANES), jnp.float32)
        return carry

    lax.fori_loop(0, n_tables * cap // chunk, clear, 0)
    for acc in accs:
        acc[n_tables * cap] = jnp.zeros((sub, LANES), jnp.float32)
    for copy in copies:
        copy.wait()

    columns = width * tile
    from_col = lax.broadcasted_iota(jnp.int32, (columns, columns), 0)
    to_col = lax.broadcasted_iota(jnp.int32, (columns, columns), 1)
    wanted = jnp.where(to_col < columns // 2, 2 * to_col, 2 * to_col - columns + 1)
    chosen = jnp.where(from_col == wanted, 1.0, 0.0).astype(jnp.bfloat16)
    for row in range(rf):
        split = jnp.dot(panel[row], chosen, preferred_element_type=jnp.float32)
        stacked = jnp.concatenate([split[:, :columns // 2], split[:, columns // 2:]], axis=0)
        lhs_ref[row] = jnp.transpose(stacked).astype(jnp.bfloat16)

    lane = lax.broadcasted_iota(jnp.int32, (tile, LANES), 1)
    lo = lane < tile

    def first_products(row, k):
        both = a_ref[pl.ds(pl.multiple_of(row * tile, tile), tile), k * tile:k * tile + LANES]
        none = jnp.zeros_like(both)
        left = jnp.concatenate([jnp.where(lo, both, none), jnp.where(lo, none, both)], axis=0)
        right = jnp.concatenate([panel[idx_ref[row, k]], panel[idx_ref[row, k + 1]]], axis=0)
        return jnp.dot(left, right, preferred_element_type=jnp.float32)

    def keep(u, y):
        for m in range(width // 2):
            x = y[:, m * LANES:(m + 1) * LANES]
            y_buf[u, :, 2 * m * LANES:(2 * m + 1) * LANES] = x.astype(jnp.bfloat16)
            y_buf[u, :, (2 * m + 1) * LANES:(2 * m + 2) * LANES] = pltpu.roll(x, tile, 1).astype(jnp.bfloat16)

    def second_product(row, u):
        lhs = lhs_ref[row]
        w = []
        for m in range(width // 2):
            x = y_buf[u, :, 2 * m * LANES:(2 * m + 1) * LANES]
            xr = y_buf[u, :, (2 * m + 1) * LANES:(2 * m + 2) * LANES]
            none = jnp.zeros_like(x)
            right = jnp.concatenate(
                [
                    jnp.concatenate([jnp.where(lo, x, none), jnp.where(lo, xr, none)], axis=1),
                    jnp.concatenate([jnp.where(lo, none, xr), jnp.where(lo, none, x)], axis=1),
                ],
                axis=0,
            )
            w.append(jnp.dot(lhs, right, preferred_element_type=jnp.float32))
        return w

    def add(row, k, w):
        for q in range(width):
            part = w[q // 2][:, q % 2 * LANES:(q % 2 + 1) * LANES]
            for s in range(0, width, ACCS):
                group = range(s, min(s + ACCS, width))
                places = [place_ref[row, (n * tiles + k) * width + q] for n in group]
                old = [acc[place] for acc, place in zip(accs, places)]
                for acc, place, was, n in zip(accs, places, old, group):
                    acc[place] = was + part[n * sub:(n + 1) * sub]

    def keep_two(u, y):
        keep(u, y[:tile])
        keep(u + 1, y[tile:])

    def hold(n, w):
        for m, part in enumerate(w):
            w_buf[n, :, m * 2 * LANES:(m + 1) * 2 * LANES] = part

    def held(n):
        return [w_buf[n, :, m * 2 * LANES:(m + 1) * 2 * LANES] for m in range(width // 2)]

    for k in range(0, tiles, 2):
        keep_two(k, first_products(0, k))
    for n in range(AHEAD):
        hold(n, second_product(0, n))

    def block_row(row, carry):
        following = jnp.minimum(row + 1, rf - 1)
        w = [held(n) for n in range(AHEAD)]
        for k in range(tiles):
            if k % 2 == 0:
                upcoming = first_products(following, k)
            ahead = k + AHEAD
            w.append(second_product(row, ahead) if ahead < tiles else second_product(following, ahead - tiles))
            add(row, k, w.pop(0))
            if k % 2 == 1:
                keep_two(k - 1, upcoming)
        for n in range(AHEAD):
            hold(n, w[n])
        return carry

    lax.fori_loop(0, rf, block_row, 0)

    named = jnp.zeros((NAME_ROWS, LANES), jnp.float32)
    here = lax.broadcasted_iota(jnp.int32, named.shape, 0)
    for n in range(groups * cap // LANES):
        part = names[:, n * LANES:(n + 1) * LANES]
        named = jnp.where(here == n, jnp.broadcast_to(part, named.shape), named)

    for (first, count), out in zip(spans, outs):

        def merge(c, carry):
            blocks = pl.ds(first + c * chunk, chunk)
            total = accs[0][blocks]
            for acc in accs[1:]:
                total = total + acc[blocks]
            rows = pl.ds(pl.multiple_of(c * (chunk * sub), chunk * sub), chunk * sub)
            out[rows, :] = total.reshape(chunk * sub, LANES).astype(out.dtype)
            return carry

        lax.fori_loop(0, count // chunk, merge, 0)
        out[count * sub:, :] = named.astype(out.dtype)


def partial_sums(rows_in, pieces, table_of, tables, spans, groups, cap):
    tile, cols = pieces[0].shape[1], rows_in.shape[1]
    rf = (rows_in.shape[0] - NAME_ROWS) // tile
    sub = tile * tile // LANES
    width = pieces[0].shape[2]
    rows = sum(x.shape[0] for x in pieces)
    n_places = (width // tile) ** 2 * (cols // tile)
    operands = [rows_in] + pieces
    panel_bytes = rows * tile * width * 2
    return pl.pallas_call(
        functools.partial(partial_kernel, len(pieces), spans, cap, groups, table_of),
        out_shape=[jax.ShapeDtypeStruct((n * sub + NAME_ROWS, LANES), jnp.bfloat16) for _, n in spans],
        grid_spec=pl.GridSpec(
            grid=(1,),
            in_specs=[pl.BlockSpec(memory_space=pl.ANY)] * len(operands),
            out_specs=[pl.BlockSpec((n * sub + NAME_ROWS, LANES), lambda i: (0, 0)) for _, n in spans],
            scratch_shapes=[pltpu.VMEM((tables * cap + 1, sub, LANES), jnp.float32)] * ACCS
            + [
                pltpu.VMEM((rf * tile, cols), jnp.bfloat16),
                pltpu.VMEM((rf, width // 2, 2 * tile), jnp.bfloat16),
                pltpu.VMEM((rows, tile, width), jnp.bfloat16),
                pltpu.VMEM((cols // tile, tile, 2 * width), jnp.bfloat16),
                pltpu.VMEM((AHEAD, width // 2, 2 * width), jnp.float32),
                pltpu.VMEM((NAME_ROWS, cols), jnp.bfloat16),
                pltpu.VMEM((rf, n_places), jnp.int32),
                pltpu.VMEM((rf, LANES), jnp.int32),
                pltpu.SMEM((rf, n_places), jnp.int32),
                pltpu.SMEM((rf, LANES), jnp.int32),
                pltpu.SemaphoreType.DMA((3 + rf // PARTS + rows // rf,)),
            ],
        ),
        compiler_params=pltpu.CompilerParams(
            dimension_semantics=("arbitrary",), vmem_limit_bytes=26 * 1024 * 1024 + panel_bytes
        ),
        cost_estimate=pl.CostEstimate(flops=1, bytes_accessed=1, transcendentals=0),
        name="partial_sums",
    )(*operands)


def early_kernel(*refs):
    tables, out_ref, accs, (vmem_names, smem_names, sem) = refs[:3], refs[3], refs[4:-3], refs[-3:]
    n_out, sub = out_ref.shape[:2]
    cap = (tables[0].shape[0] - NAME_ROWS) // sub
    chunk = 8
    at = lax.axis_index("grp") * cap
    row, lane = lax.div(at, jnp.int32(LANES)), lax.rem(at, jnp.int32(LANES))

    for n, x in enumerate(tables):
        vmem_names[n] = x[pl.ds(cap * sub, NAME_ROWS), :].astype(jnp.float32).astype(jnp.int32)
    copy = pltpu.make_async_copy(vmem_names, smem_names, sem)
    copy.start()

    def clear(c, carry):
        for acc in accs:
            acc[pl.ds(c * chunk, chunk)] = jnp.zeros((chunk, sub, LANES), jnp.float32)
        return carry

    lax.fori_loop(0, n_out // chunk, clear, 0)
    copy.wait()

    def add(c, carry):
        src = pl.ds(pl.multiple_of(c * sub, sub), sub)
        names = [smem_names[n, row, lane + c] for n in range(len(tables))]
        old = [acc[name] for acc, name in zip(accs, names)]
        for acc, name, was, x in zip(accs, names, old, tables):
            acc[name] = was + x[src, :].astype(jnp.float32)
        return carry

    lax.fori_loop(0, cap, add, 0, unroll=4)

    def merge(c, carry):
        blocks = pl.ds(c * chunk, chunk)
        total = accs[0][blocks]
        for acc in accs[1:]:
            total = total + acc[blocks]
        out_ref[blocks] = total
        return carry

    lax.fori_loop(0, n_out // chunk, merge, 0)


def last_kernel(table, from_b, from_c, out_ref, acc, late, rows_buf, vmem_names, smem_names, sems):
    n_out, sub = acc.shape[:2]
    cap = (late.shape[0] - NAME_ROWS) // sub
    me = lax.axis_index("grp")
    at = me * cap
    row, lane = lax.div(at, jnp.int32(LANES)), lax.rem(at, jnp.int32(LANES))
    parts = (sems.shape[0] - 2) // 3

    def late_copies(table_in):
        spans = [pl.ds(cap * sub, NAME_ROWS)]
        spans += [pl.ds(n * (cap // parts) * sub, cap // parts * sub) for n in range(parts)]
        return [
            pltpu.make_async_copy(table_in.at[span], late.at[span], sems.at[n]) for n, span in enumerate(spans)
        ]

    middle = (me == 1) | (me == 2)

    @pl.when(middle)
    def _():
        for copy in late_copies(from_b):
            copy.start()

    @pl.when(jnp.logical_not(middle))
    def _():
        for copy in late_copies(from_c):
            copy.start()

    height = n_out // parts
    blocks = [pl.ds(n * height, height) for n in range(parts)]
    fills = [
        pltpu.make_async_copy(table.at[span], acc.at[span], sems.at[1 + parts + n]) for n, span in enumerate(blocks)
    ]
    for copy in fills:
        copy.start()
    waiting = late_copies(from_b)
    waiting.pop(0).wait()
    vmem_names[...] = late[pl.ds(cap * sub, NAME_ROWS), :].astype(jnp.float32).astype(jnp.int32)
    copy = pltpu.make_async_copy(vmem_names, smem_names, sems.at[1 + 2 * parts])
    copy.start()
    for other in waiting + fills + [copy]:
        other.wait()

    def add(c, carry):
        acc[smem_names[row, lane + c]] += late[pl.ds(pl.multiple_of(c * sub, sub), sub), :].astype(jnp.float32)
        return carry

    lax.fori_loop(0, cap, add, 0, unroll=4)
    flat = acc.reshape(n_out * sub, LANES)

    def emit(c, carry):
        rows = pl.ds(pl.multiple_of(c * 8, 8), 8)
        for t in range(sub):
            rows_buf[rows, t * LANES:(t + 1) * LANES] = flat[pl.ds(c * (8 * sub) + t, 8, stride=sub), :]
        return carry

    copies = []
    for n, rows in enumerate(blocks):
        lax.fori_loop(n * height // 8, (n + 1) * height // 8, emit, 0)
        copies.append(pltpu.make_async_copy(rows_buf.at[rows], out_ref.at[rows], sems.at[2 + 2 * parts + n]))
        copies[-1].start()
    for copy in copies:
        copy.wait()


def owner_sums(tables, from_b, from_c, sub):
    def whole(x):
        return pl.BlockSpec(x.shape, lambda i: (0,) * len(x.shape))

    table = jax.ShapeDtypeStruct((OSLOT, sub, LANES), jnp.float32)
    names = (NAME_ROWS, LANES)
    early = pl.pallas_call(
        early_kernel,
        out_shape=table,
        grid_spec=pl.GridSpec(
            grid=(1,),
            in_specs=[whole(x) for x in tables],
            out_specs=whole(table),
            scratch_shapes=[pltpu.VMEM(table.shape, jnp.float32)] * len(tables)
            + [
                pltpu.VMEM((len(tables),) + names, jnp.int32),
                pltpu.SMEM((len(tables),) + names, jnp.int32),
                pltpu.SemaphoreType.DMA,
            ],
        ),
        compiler_params=pltpu.CompilerParams(
            dimension_semantics=("arbitrary",), vmem_limit_bytes=20 * 1024 * 1024
        ),
        name="early_sums",
    )(*tables)
    return pl.pallas_call(
        last_kernel,
        out_shape=jax.ShapeDtypeStruct((OSLOT, sub * LANES), jnp.float32),
        grid_spec=pl.GridSpec(
            grid=(1,),
            in_specs=[pl.BlockSpec(memory_space=pl.ANY)] * 3,
            out_specs=pl.BlockSpec(memory_space=pl.ANY),
            scratch_shapes=[
                pltpu.VMEM(table.shape, jnp.float32),
                pltpu.VMEM(from_b.shape, jnp.bfloat16),
                pltpu.VMEM((OSLOT, sub * LANES), jnp.float32),
                pltpu.VMEM(names, jnp.int32),
                pltpu.SMEM(names, jnp.int32),
                pltpu.SemaphoreType.DMA((2 + 3 * 4,)),
            ],
        ),
        compiler_params=pltpu.CompilerParams(
            dimension_semantics=("arbitrary",), vmem_limit_bytes=20 * 1024 * 1024
        ),
        name="owner_sums",
    )(early, from_b, from_c)


def swap(x, axis, d):
    return lax.ppermute(x, axis, [(i, i ^ d) for i in range(lax.axis_size(axis))])


def direct(p_tiles):
    return [swap(p_tiles, "blk", d) for d in range(2, lax.axis_size("blk"), 2)]


def body(a_tiles, a_cols, p_tiles, route_list, out_slot):
    groups = lax.axis_size("grp")
    rf, tile, cols = a_tiles.shape
    cap = out_slot.shape[1] // groups
    sub = tile * tile // LANES
    takes = [(1, 0), (3, 1), (0, 2), (2, 3)]

    def take(x):
        return lax.ppermute(x, "grp", takes)

    rows_sent = with_numbers(a_tiles, route_list, out_slot, a_cols)
    far = direct(p_tiles)
    p_took = take(p_tiles)
    a_took = take(rows_sent)
    far[0], p_took = lax.optimization_barrier((far[0], p_took))
    far_took = direct(p_took)
    mine = [p_tiles, jnp.concatenate(far)]
    other = [swap(x, "blk", 1) for x in mine]

    def tables_own(off, middle):
        return jnp.where(middle, jnp.where(off == 0, 0, jnp.where(off == 1, 3, off - 1)), jnp.where(off < 2, off, 3))

    def tables_took(off, middle):
        return jnp.where((off == 0) | ((off == 1) & middle), off, 2)

    spans = ((0, cap), (cap, cap), (2 * cap, cap))
    own, to_a, to_b = partial_sums(rows_sent, mine + other, tables_own, 3, spans, groups, cap)
    own, p_took, *far_took = lax.optimization_barrier((own, p_took, *far_took))
    to_a, to_b, a_took = lax.optimization_barrier((to_a, to_b, a_took))
    from_a = lax.ppermute(to_a, "grp", [(0, 1), (3, 2), (1, 3), (2, 0)])
    from_b = lax.ppermute(to_b, "grp", [(1, 2), (2, 1)])
    took = [p_took] + far_took
    pieces = took + [swap(x, "blk", 1) for x in took]
    spans = ((0, cap), (cap, cap))
    own_took, to_c = partial_sums(a_took, pieces, tables_took, 2, spans, groups, cap)
    from_c = lax.ppermute(to_c, "grp", [(1, 0), (2, 3)])
    return owner_sums([own, own_took, from_a], from_b, from_c, sub)


def solution(mesh):
    in_specs = (
        P(("blk", "grp"), None, None),
        P(("blk", "grp"), None),
        P(("blk", "grp"), None, None),
        P(("blk", "grp"), None),
        P(("blk", "grp"), None),
    )
    out_specs = P(("blk", "grp"), None)
    return jax.shard_map(body, mesh=mesh, in_specs=in_specs, out_specs=out_specs, check_vma=False)
```

```python
import functools

import jax
import jax.numpy as jnp
from jax import lax
from jax.experimental import pallas as pl
from jax.experimental.pallas import tpu as pltpu
from jax.sharding import PartitionSpec as P

OSLOT = 128
LANES = 128
ACCS = 4
AHEAD = 2
NAME_ROWS = 16
PART = 256
PARTS = 2


def log2(n):
    assert n & (n - 1) == 0
    return n.bit_length() - 1


def number_columns(n_places):
    return 0, n_places, 2 * n_places, 2 * n_places + LANES


def numbers_kernel(a_ref, route_ref, slot_ref, cols_ref, out_ref, wide, packed, sems):
    rf, tile, _ = a_ref.shape
    copies = [
        pltpu.make_async_copy(a_ref.at[n], out_ref.at[pl.ds(n * tile, tile)], sems.at[n]) for n in range(rf)
    ]
    for copy in copies:
        copy.start()
    wide[...] = jnp.zeros_like(wide)
    cols = cols_ref[...]
    parts = (route_ref[...], slot_ref[...], lax.shift_right_logical(cols, jnp.int32(log2(PART))), cols & (PART - 1))
    for at, part in zip(number_columns(route_ref.shape[1]), parts):
        wide[:part.shape[0], at:at + part.shape[1]] = part.astype(jnp.float32)
    packed[...] = wide[...].astype(packed.dtype)
    copies.append(pltpu.make_async_copy(packed, out_ref.at[pl.ds(rf * tile, NAME_ROWS)], sems.at[rf]))
    copies[-1].start()
    for copy in copies:
        copy.wait()


def with_numbers(a_tiles, route_list, out_slot, a_cols):
    rf, tile, width = a_tiles.shape
    whole = pl.BlockSpec(memory_space=pltpu.VMEM)
    return pl.pallas_call(
        numbers_kernel,
        out_shape=jax.ShapeDtypeStruct((rf * tile + NAME_ROWS, width), a_tiles.dtype),
        in_specs=[pl.BlockSpec(memory_space=pl.ANY)] + [whole] * 3,
        out_specs=pl.BlockSpec(memory_space=pl.ANY),
        scratch_shapes=[
            pltpu.VMEM((NAME_ROWS, width), jnp.float32),
            pltpu.VMEM((NAME_ROWS, width), a_tiles.dtype),
            pltpu.SemaphoreType.DMA((rf + 1,)),
        ],
        compiler_params=pltpu.CompilerParams(vmem_limit_bytes=56 * 1024 * 1024),
        cost_estimate=pl.CostEstimate(flops=1, bytes_accessed=1, transcendentals=0),
        name="with_numbers",
    )(a_tiles, route_list, out_slot, a_cols)


def partial_kernel(n_pieces, spans, cap, groups, table_of, rows_in, *refs):
    pieces, refs = refs[:n_pieces], refs[n_pieces:]
    outs, refs = refs[:len(spans)], refs[len(spans):]
    stages, refs = refs[:len(spans)], refs[len(spans):]
    accs, (a_ref, lhs_ref, panel, y_buf, w_buf, *rest, out_sems, sems) = refs[:ACCS], refs[ACCS:]
    packed_ref, place_vmem, idx_vmem, place_ref, idx_ref = rest
    tile = panel.shape[1]
    rf, tiles = a_ref.shape[0] // tile, a_ref.shape[1] // tile
    width = panel.shape[2] // tile
    sub = tile * tile // LANES
    n_tables = accs[0].shape[0] // cap
    chunk = 8

    n_places = width * tiles * width
    copies = [
        pltpu.make_async_copy(rows_in.at[pl.ds(rf * tile, NAME_ROWS)], packed_ref, sems.at[0]),
    ]
    for n in range(0, rf, PARTS):
        part = pl.ds(n * tile, PARTS * tile)
        copies.append(pltpu.make_async_copy(rows_in.at[part], a_ref.at[part], sems.at[len(copies)]))
    at = 0
    for piece in pieces:
        for n in range(0, piece.shape[0], rf):
            part, whole = piece.at[pl.ds(n, rf)], panel.at[pl.ds(at, rf)]
            copies.append(pltpu.make_async_copy(part, whole, sems.at[len(copies)]))
            at += rf
    for copy in copies:
        copy.start()
    copies.pop(0).wait()

    me, blk = lax.axis_index("grp"), lax.axis_index("blk")
    numbers = packed_ref[...].astype(jnp.float32).astype(jnp.int32)
    at_route, at_slot, at_high, at_low = number_columns(n_places)
    route = numbers[:rf, at_route:at_route + n_places]
    names = numbers[:1, at_slot:at_slot + n_places].astype(jnp.float32)
    owner = lax.shift_right_logical(route, jnp.int32(log2(cap)))
    table = table_of(owner ^ me, (me == 1) | (me == 2))
    place_vmem[...] = jnp.where(table < n_tables, table * cap + (route & (cap - 1)), n_tables * cap)
    cols = numbers[:rf, at_high:at_high + LANES] * PART + numbers[:rf, at_low:at_low + LANES]
    d = lax.shift_right_logical(cols, jnp.int32(log2(rf * groups))) ^ blk
    half = panel.shape[0] // (2 * rf)
    idx_vmem[...] = ((d & 1) * half + lax.shift_right_logical(d, jnp.int32(1))) * rf + (cols & (rf - 1))
    for n, (src, dst) in enumerate(((place_vmem, place_ref), (idx_vmem, idx_ref))):
        copy = pltpu.make_async_copy(src, dst, sems.at[sems.shape[0] - 2 + n])
        copy.start()
        copies.append(copy)

    def clear(c, carry):
        blocks = pl.ds(c * chunk, chunk)
        for acc in accs:
            acc[blocks] = jnp.zeros((chunk, sub, LANES), jnp.float32)
        return carry

    lax.fori_loop(0, n_tables * cap // chunk, clear, 0)
    for acc in accs:
        acc[n_tables * cap] = jnp.zeros((sub, LANES), jnp.float32)
    for copy in copies:
        copy.wait()

    columns = width * tile
    from_col = lax.broadcasted_iota(jnp.int32, (columns, columns), 0)
    to_col = lax.broadcasted_iota(jnp.int32, (columns, columns), 1)
    wanted = jnp.where(to_col < columns // 2, 2 * to_col, 2 * to_col - columns + 1)
    chosen = jnp.where(from_col == wanted, 1.0, 0.0).astype(jnp.bfloat16)
    for row in range(rf):
        split = jnp.dot(panel[row], chosen, preferred_element_type=jnp.float32)
        stacked = jnp.concatenate([split[:, :columns // 2], split[:, columns // 2:]], axis=0)
        lhs_ref[row] = jnp.transpose(stacked).astype(jnp.bfloat16)

    lane = lax.broadcasted_iota(jnp.int32, (tile, LANES), 1)
    lo = lane < tile

    def first_products(row, k):
        both = a_ref[pl.ds(pl.multiple_of(row * tile, tile), tile), k * tile:k * tile + LANES]
        none = jnp.zeros_like(both)
        left = jnp.concatenate([jnp.where(lo, both, none), jnp.where(lo, none, both)], axis=0)
        right = jnp.concatenate([panel[idx_ref[row, k]], panel[idx_ref[row, k + 1]]], axis=0)
        return jnp.dot(left, right, preferred_element_type=jnp.float32)

    def keep(u, y):
        for m in range(width // 2):
            x = y[:, m * LANES:(m + 1) * LANES]
            y_buf[u, :, 2 * m * LANES:(2 * m + 1) * LANES] = x.astype(jnp.bfloat16)
            y_buf[u, :, (2 * m + 1) * LANES:(2 * m + 2) * LANES] = pltpu.roll(x, tile, 1).astype(jnp.bfloat16)

    def second_product(row, u):
        lhs = lhs_ref[row]
        w = []
        for m in range(width // 2):
            x = y_buf[u, :, 2 * m * LANES:(2 * m + 1) * LANES]
            xr = y_buf[u, :, (2 * m + 1) * LANES:(2 * m + 2) * LANES]
            none = jnp.zeros_like(x)
            right = jnp.concatenate(
                [
                    jnp.concatenate([jnp.where(lo, x, none), jnp.where(lo, xr, none)], axis=1),
                    jnp.concatenate([jnp.where(lo, none, xr), jnp.where(lo, none, x)], axis=1),
                ],
                axis=0,
            )
            w.append(jnp.dot(lhs, right, preferred_element_type=jnp.float32))
        return w

    def add(row, k, w):
        for q in range(width):
            part = w[q // 2][:, q % 2 * LANES:(q % 2 + 1) * LANES]
            for s in range(0, width, ACCS):
                group = range(s, min(s + ACCS, width))
                places = [place_ref[row, (n * tiles + k) * width + q] for n in group]
                old = [acc[place] for acc, place in zip(accs, places)]
                for acc, place, was, n in zip(accs, places, old, group):
                    acc[place] = was + part[n * sub:(n + 1) * sub]

    def keep_two(u, y):
        keep(u, y[:tile])
        keep(u + 1, y[tile:])

    def hold(n, w):
        for m, part in enumerate(w):
            w_buf[n, :, m * 2 * LANES:(m + 1) * 2 * LANES] = part

    def held(n):
        return [w_buf[n, :, m * 2 * LANES:(m + 1) * 2 * LANES] for m in range(width // 2)]

    for k in range(0, tiles, 2):
        keep_two(k, first_products(0, k))
    for n in range(AHEAD):
        hold(n, second_product(0, n))

    def block_row(row, carry):
        following = jnp.minimum(row + 1, rf - 1)
        w = [held(n) for n in range(AHEAD)]
        for k in range(tiles):
            if k % 2 == 0:
                upcoming = first_products(following, k)
            ahead = k + AHEAD
            w.append(second_product(row, ahead) if ahead < tiles else second_product(following, ahead - tiles))
            add(row, k, w.pop(0))
            if k % 2 == 1:
                keep_two(k - 1, upcoming)
        for n in range(AHEAD):
            hold(n, w[n])
        return carry

    lax.fori_loop(0, rf, block_row, 0)

    named = jnp.zeros((NAME_ROWS, LANES), jnp.float32)
    here = lax.broadcasted_iota(jnp.int32, named.shape, 0)
    for n in range(groups * cap // LANES):
        part = names[:, n * LANES:(n + 1) * LANES]
        named = jnp.where(here == n, jnp.broadcast_to(part, named.shape), named)

    leaving = []
    for (first, count), stage, out in zip(spans, stages, outs):

        def merge(c, carry):
            blocks = pl.ds(first + c * chunk, chunk)
            total = accs[0][blocks]
            for acc in accs[1:]:
                total = total + acc[blocks]
            rows = pl.ds(pl.multiple_of(c * (chunk * sub), chunk * sub), chunk * sub)
            stage[rows, :] = total.reshape(chunk * sub, LANES).astype(stage.dtype)
            return carry

        stage[count * sub:, :] = named.astype(stage.dtype)
        lax.fori_loop(0, count // chunk, merge, 0)
        leaving.append(pltpu.make_async_copy(stage, out, out_sems.at[len(leaving)]))
        leaving[-1].start()
    for copy in leaving:
        copy.wait()


def partial_sums(rows_in, pieces, table_of, tables, spans, groups, cap):
    tile, cols = pieces[0].shape[1], rows_in.shape[1]
    rf = (rows_in.shape[0] - NAME_ROWS) // tile
    sub = tile * tile // LANES
    width = pieces[0].shape[2]
    rows = sum(x.shape[0] for x in pieces)
    n_places = (width // tile) ** 2 * (cols // tile)
    operands = [rows_in] + pieces
    panel_bytes = rows * tile * width * 2
    return pl.pallas_call(
        functools.partial(partial_kernel, len(pieces), spans, cap, groups, table_of),
        out_shape=[jax.ShapeDtypeStruct((n * sub + NAME_ROWS, LANES), jnp.bfloat16) for _, n in spans],
        grid_spec=pl.GridSpec(
            grid=(1,),
            in_specs=[pl.BlockSpec(memory_space=pl.ANY)] * len(operands),
            out_specs=[pl.BlockSpec(memory_space=pl.ANY)] * len(spans),
            scratch_shapes=[pltpu.VMEM((n * sub + NAME_ROWS, LANES), jnp.bfloat16) for _, n in spans]
            + [pltpu.VMEM((tables * cap + 1, sub, LANES), jnp.float32)] * ACCS
            + [
                pltpu.VMEM((rf * tile, cols), jnp.bfloat16),
                pltpu.VMEM((rf, width // 2, 2 * tile), jnp.bfloat16),
                pltpu.VMEM((rows, tile, width), jnp.bfloat16),
                pltpu.VMEM((cols // tile, tile, 2 * width), jnp.bfloat16),
                pltpu.VMEM((AHEAD, width // 2, 2 * width), jnp.float32),
                pltpu.VMEM((NAME_ROWS, cols), jnp.bfloat16),
                pltpu.VMEM((rf, n_places), jnp.int32),
                pltpu.VMEM((rf, LANES), jnp.int32),
                pltpu.SMEM((rf, n_places), jnp.int32),
                pltpu.SMEM((rf, LANES), jnp.int32),
                pltpu.SemaphoreType.DMA((len(spans),)),
                pltpu.SemaphoreType.DMA((3 + rf // PARTS + rows // rf,)),
            ],
        ),
        compiler_params=pltpu.CompilerParams(
            dimension_semantics=("arbitrary",), vmem_limit_bytes=26 * 1024 * 1024 + panel_bytes
        ),
        cost_estimate=pl.CostEstimate(flops=1, bytes_accessed=1, transcendentals=0),
        name="partial_sums",
    )(*operands)


def early_kernel(*refs):
    tables, out_ref, accs, (vmem_names, smem_names, sem) = refs[:3], refs[3], refs[4:-3], refs[-3:]
    n_out, sub = out_ref.shape[:2]
    cap = (tables[0].shape[0] - NAME_ROWS) // sub
    chunk = 8
    at = lax.axis_index("grp") * cap
    row, lane = lax.div(at, jnp.int32(LANES)), lax.rem(at, jnp.int32(LANES))

    for n, x in enumerate(tables):
        vmem_names[n] = x[pl.ds(cap * sub, NAME_ROWS), :].astype(jnp.float32).astype(jnp.int32)
    copy = pltpu.make_async_copy(vmem_names, smem_names, sem)
    copy.start()

    def clear(c, carry):
        for acc in accs:
            acc[pl.ds(c * chunk, chunk)] = jnp.zeros((chunk, sub, LANES), jnp.float32)
        return carry

    lax.fori_loop(0, n_out // chunk, clear, 0)
    copy.wait()

    def add(c, carry):
        src = pl.ds(pl.multiple_of(c * sub, sub), sub)
        names = [smem_names[n, row, lane + c] for n in range(len(tables))]
        old = [acc[name] for acc, name in zip(accs, names)]
        for acc, name, was, x in zip(accs, names, old, tables):
            acc[name] = was + x[src, :].astype(jnp.float32)
        return carry

    lax.fori_loop(0, cap, add, 0, unroll=4)

    def merge(c, carry):
        blocks = pl.ds(c * chunk, chunk)
        total = accs[0][blocks]
        for acc in accs[1:]:
            total = total + acc[blocks]
        out_ref[blocks] = total
        return carry

    lax.fori_loop(0, n_out // chunk, merge, 0)


def last_kernel(table, from_b, from_c, out_ref, acc, late, rows_buf, vmem_names, smem_names, sems):
    n_out, sub = acc.shape[:2]
    cap = (late.shape[0] - NAME_ROWS) // sub
    me = lax.axis_index("grp")
    at = me * cap
    row, lane = lax.div(at, jnp.int32(LANES)), lax.rem(at, jnp.int32(LANES))
    parts = (sems.shape[0] - 2) // 3

    def late_copies(table_in):
        spans = [pl.ds(cap * sub, NAME_ROWS)]
        spans += [pl.ds(n * (cap // parts) * sub, cap // parts * sub) for n in range(parts)]
        return [
            pltpu.make_async_copy(table_in.at[span], late.at[span], sems.at[n]) for n, span in enumerate(spans)
        ]

    middle = (me == 1) | (me == 2)

    @pl.when(middle)
    def _():
        for copy in late_copies(from_b):
            copy.start()

    @pl.when(jnp.logical_not(middle))
    def _():
        for copy in late_copies(from_c):
            copy.start()

    height = n_out // parts
    blocks = [pl.ds(n * height, height) for n in range(parts)]
    fills = [
        pltpu.make_async_copy(table.at[span], acc.at[span], sems.at[1 + parts + n]) for n, span in enumerate(blocks)
    ]
    for copy in fills:
        copy.start()
    waiting = late_copies(from_b)
    waiting.pop(0).wait()
    vmem_names[...] = late[pl.ds(cap * sub, NAME_ROWS), :].astype(jnp.float32).astype(jnp.int32)
    copy = pltpu.make_async_copy(vmem_names, smem_names, sems.at[1 + 2 * parts])
    copy.start()
    for other in waiting + fills + [copy]:
        other.wait()

    def add(c, carry):
        acc[smem_names[row, lane + c]] += late[pl.ds(pl.multiple_of(c * sub, sub), sub), :].astype(jnp.float32)
        return carry

    lax.fori_loop(0, cap, add, 0, unroll=4)
    flat = acc.reshape(n_out * sub, LANES)

    def emit(c, carry):
        rows = pl.ds(pl.multiple_of(c * 8, 8), 8)
        for t in range(sub):
            rows_buf[rows, t * LANES:(t + 1) * LANES] = flat[pl.ds(c * (8 * sub) + t, 8, stride=sub), :]
        return carry

    copies = []
    for n, rows in enumerate(blocks):
        lax.fori_loop(n * height // 8, (n + 1) * height // 8, emit, 0)
        copies.append(pltpu.make_async_copy(rows_buf.at[rows], out_ref.at[rows], sems.at[2 + 2 * parts + n]))
        copies[-1].start()
    for copy in copies:
        copy.wait()


def owner_sums(tables, from_b, from_c, sub):
    def whole(x):
        return pl.BlockSpec(x.shape, lambda i: (0,) * len(x.shape))

    table = jax.ShapeDtypeStruct((OSLOT, sub, LANES), jnp.float32)
    names = (NAME_ROWS, LANES)
    early = pl.pallas_call(
        early_kernel,
        out_shape=table,
        grid_spec=pl.GridSpec(
            grid=(1,),
            in_specs=[whole(x) for x in tables],
            out_specs=whole(table),
            scratch_shapes=[pltpu.VMEM(table.shape, jnp.float32)] * len(tables)
            + [
                pltpu.VMEM((len(tables),) + names, jnp.int32),
                pltpu.SMEM((len(tables),) + names, jnp.int32),
                pltpu.SemaphoreType.DMA,
            ],
        ),
        compiler_params=pltpu.CompilerParams(
            dimension_semantics=("arbitrary",), vmem_limit_bytes=20 * 1024 * 1024
        ),
        name="early_sums",
    )(*tables)
    return pl.pallas_call(
        last_kernel,
        out_shape=jax.ShapeDtypeStruct((OSLOT, sub * LANES), jnp.float32),
        grid_spec=pl.GridSpec(
            grid=(1,),
            in_specs=[pl.BlockSpec(memory_space=pl.ANY)] * 3,
            out_specs=pl.BlockSpec(memory_space=pl.ANY),
            scratch_shapes=[
                pltpu.VMEM(table.shape, jnp.float32),
                pltpu.VMEM(from_b.shape, jnp.bfloat16),
                pltpu.VMEM((OSLOT, sub * LANES), jnp.float32),
                pltpu.VMEM(names, jnp.int32),
                pltpu.SMEM(names, jnp.int32),
                pltpu.SemaphoreType.DMA((2 + 3 * 4,)),
            ],
        ),
        compiler_params=pltpu.CompilerParams(
            dimension_semantics=("arbitrary",), vmem_limit_bytes=20 * 1024 * 1024
        ),
        name="owner_sums",
    )(early, from_b, from_c)


def swap(x, axis, d):
    return lax.ppermute(x, axis, [(i, i ^ d) for i in range(lax.axis_size(axis))])


def direct(p_tiles):
    return [swap(p_tiles, "blk", d) for d in range(2, lax.axis_size("blk"), 2)]


def body(a_tiles, a_cols, p_tiles, route_list, out_slot):
    groups = lax.axis_size("grp")
    rf, tile, cols = a_tiles.shape
    cap = out_slot.shape[1] // groups
    sub = tile * tile // LANES
    takes = [(1, 0), (3, 1), (0, 2), (2, 3)]

    def take(x):
        return lax.ppermute(x, "grp", takes)

    rows_sent = with_numbers(a_tiles, route_list, out_slot, a_cols)
    far = direct(p_tiles)
    p_took = take(p_tiles)
    a_took = take(rows_sent)
    far[0], p_took = lax.optimization_barrier((far[0], p_took))
    far_took = direct(p_took)
    mine = [p_tiles, jnp.concatenate(far)]
    other = [swap(x, "blk", 1) for x in mine]

    def tables_own(off, middle):
        return jnp.where(middle, jnp.where(off == 0, 0, jnp.where(off == 1, 3, off - 1)), jnp.where(off < 2, off, 3))

    def tables_took(off, middle):
        return jnp.where((off == 0) | ((off == 1) & middle), off, 2)

    spans = ((0, cap), (cap, cap), (2 * cap, cap))
    own, to_a, to_b = partial_sums(rows_sent, mine + other, tables_own, 3, spans, groups, cap)
    own, p_took, *far_took = lax.optimization_barrier((own, p_took, *far_took))
    to_a, to_b, a_took = lax.optimization_barrier((to_a, to_b, a_took))
    from_a = lax.ppermute(to_a, "grp", [(0, 1), (3, 2), (1, 3), (2, 0)])
    from_b = lax.ppermute(to_b, "grp", [(1, 2), (2, 1)])
    took = [p_took] + far_took
    pieces = took + [swap(x, "blk", 1) for x in took]
    spans = ((0, cap), (cap, cap))
    own_took, to_c = partial_sums(a_took, pieces, tables_took, 2, spans, groups, cap)
    from_c = lax.ppermute(to_c, "grp", [(1, 0), (2, 3)])
    return owner_sums([own, own_took, from_a], from_b, from_c, sub)


def solution(mesh):
    in_specs = (
        P(("blk", "grp"), None, None),
        P(("blk", "grp"), None),
        P(("blk", "grp"), None, None),
        P(("blk", "grp"), None),
        P(("blk", "grp"), None),
    )
    out_specs = P(("blk", "grp"), None)
    return jax.shard_map(body, mesh=mesh, in_specs=in_specs, out_specs=out_specs, check_vma=False)
```

```python
import functools

import jax
import jax.numpy as jnp
from jax import lax
from jax.experimental import pallas as pl
from jax.experimental.pallas import tpu as pltpu
from jax.sharding import PartitionSpec as P

OSLOT = 128
LANES = 128
ACCS = 4
AHEAD = 2
NAME_ROWS = 16
PART = 256
PARTS = 2


def log2(n):
    assert n & (n - 1) == 0
    return n.bit_length() - 1


def number_columns(n_places):
    return 0, n_places, 2 * n_places, 2 * n_places + LANES


def numbers_kernel(a_ref, route_ref, slot_ref, cols_ref, out_ref, held, wide, packed, sems):
    rf, tile, _ = a_ref.shape
    into, out = [], []
    for n in range(rf):
        rows = pl.ds(n * tile, tile)
        into.append(pltpu.make_async_copy(a_ref.at[n], held.at[n], sems.at[n]))
        out.append(pltpu.make_async_copy(held.at[n], out_ref.at[rows], sems.at[rf + n]))
        into[-1].start()
    wide[...] = jnp.zeros_like(wide)
    cols = cols_ref[...]
    parts = (route_ref[...], slot_ref[...], lax.shift_right_logical(cols, jnp.int32(log2(PART))), cols & (PART - 1))
    for at, part in zip(number_columns(route_ref.shape[1]), parts):
        wide[:part.shape[0], at:at + part.shape[1]] = part.astype(jnp.float32)
    packed[...] = wide[...].astype(packed.dtype)
    last = pltpu.make_async_copy(packed, out_ref.at[pl.ds(rf * tile, NAME_ROWS)], sems.at[2 * rf])
    last.start()
    for arriving, leaving in zip(into, out):
        arriving.wait()
        leaving.start()
    for copy in out + [last]:
        copy.wait()


def with_numbers(a_tiles, route_list, out_slot, a_cols):
    rf, tile, width = a_tiles.shape
    whole = pl.BlockSpec(memory_space=pltpu.VMEM)
    return pl.pallas_call(
        numbers_kernel,
        out_shape=jax.ShapeDtypeStruct((rf * tile + NAME_ROWS, width), a_tiles.dtype),
        in_specs=[pl.BlockSpec(memory_space=pl.ANY)] + [whole] * 3,
        out_specs=pl.BlockSpec(memory_space=pl.ANY),
        scratch_shapes=[
            pltpu.VMEM(a_tiles.shape, a_tiles.dtype),
            pltpu.VMEM((NAME_ROWS, width), jnp.float32),
            pltpu.VMEM((NAME_ROWS, width), a_tiles.dtype),
            pltpu.SemaphoreType.DMA((2 * rf + 1,)),
        ],
        compiler_params=pltpu.CompilerParams(vmem_limit_bytes=56 * 1024 * 1024),
        cost_estimate=pl.CostEstimate(flops=1, bytes_accessed=1, transcendentals=0),
        name="with_numbers",
    )(a_tiles, route_list, out_slot, a_cols)


def partial_kernel(n_pieces, spans, cap, groups, table_of, rows_in, *refs):
    pieces, refs = refs[:n_pieces], refs[n_pieces:]
    outs, refs = refs[:len(spans)], refs[len(spans):]
    accs, (a_ref, lhs_ref, panel, y_buf, w_buf, *rest, sems) = refs[:ACCS], refs[ACCS:]
    packed_ref, place_vmem, idx_vmem, place_ref, idx_ref = rest
    tile = panel.shape[1]
    rf, tiles = a_ref.shape[0] // tile, a_ref.shape[1] // tile
    width = panel.shape[2] // tile
    sub = tile * tile // LANES
    n_tables = accs[0].shape[0] // cap
    chunk = 8

    n_places = width * tiles * width
    copies = [
        pltpu.make_async_copy(rows_in.at[pl.ds(rf * tile, NAME_ROWS)], packed_ref, sems.at[0]),
    ]
    for n in range(0, rf, PARTS):
        part = pl.ds(n * tile, PARTS * tile)
        copies.append(pltpu.make_async_copy(rows_in.at[part], a_ref.at[part], sems.at[len(copies)]))
    at = 0
    for piece in pieces:
        for n in range(0, piece.shape[0], rf):
            part, whole = piece.at[pl.ds(n, rf)], panel.at[pl.ds(at, rf)]
            copies.append(pltpu.make_async_copy(part, whole, sems.at[len(copies)]))
            at += rf
    for copy in copies:
        copy.start()
    copies.pop(0).wait()

    me, blk = lax.axis_index("grp"), lax.axis_index("blk")
    numbers = packed_ref[...].astype(jnp.float32).astype(jnp.int32)
    at_route, at_slot, at_high, at_low = number_columns(n_places)
    route = numbers[:rf, at_route:at_route + n_places]
    names = numbers[:1, at_slot:at_slot + n_places].astype(jnp.float32)
    owner = lax.shift_right_logical(route, jnp.int32(log2(cap)))
    table = table_of(owner ^ me, (me == 1) | (me == 2))
    place_vmem[...] = jnp.where(table < n_tables, table * cap + (route & (cap - 1)), n_tables * cap)
    cols = numbers[:rf, at_high:at_high + LANES] * PART + numbers[:rf, at_low:at_low + LANES]
    d = lax.shift_right_logical(cols, jnp.int32(log2(rf * groups))) ^ blk
    half = panel.shape[0] // (2 * rf)
    idx_vmem[...] = ((d & 1) * half + lax.shift_right_logical(d, jnp.int32(1))) * rf + (cols & (rf - 1))
    for n, (src, dst) in enumerate(((place_vmem, place_ref), (idx_vmem, idx_ref))):
        copy = pltpu.make_async_copy(src, dst, sems.at[sems.shape[0] - 2 + n])
        copy.start()
        copies.append(copy)

    def clear(c, carry):
        blocks = pl.ds(c * chunk, chunk)
        for acc in accs:
            acc[blocks] = jnp.zeros((chunk, sub, LANES), jnp.float32)
        return carry

    lax.fori_loop(0, n_tables * cap // chunk, clear, 0)
    for acc in accs:
        acc[n_tables * cap] = jnp.zeros((sub, LANES), jnp.float32)
    for copy in copies:
        copy.wait()

    columns = width * tile
    from_col = lax.broadcasted_iota(jnp.int32, (columns, columns), 0)
    to_col = lax.broadcasted_iota(jnp.int32, (columns, columns), 1)
    wanted = jnp.where(to_col < columns // 2, 2 * to_col, 2 * to_col - columns + 1)
    chosen = jnp.where(from_col == wanted, 1.0, 0.0).astype(jnp.bfloat16)
    for row in range(rf):
        split = jnp.dot(panel[row], chosen, preferred_element_type=jnp.float32)
        stacked = jnp.concatenate([split[:, :columns // 2], split[:, columns // 2:]], axis=0)
        lhs_ref[row] = jnp.transpose(stacked).astype(jnp.bfloat16)

    lane = lax.broadcasted_iota(jnp.int32, (tile, LANES), 1)
    lo = lane < tile

    def first_products(row, k):
        both = a_ref[pl.ds(pl.multiple_of(row * tile, tile), tile), k * tile:k * tile + LANES]
        none = jnp.zeros_like(both)
        left = jnp.concatenate([jnp.where(lo, both, none), jnp.where(lo, none, both)], axis=0)
        right = jnp.concatenate([panel[idx_ref[row, k]], panel[idx_ref[row, k + 1]]], axis=0)
        return jnp.dot(left, right, preferred_element_type=jnp.float32)

    def keep(u, y):
        for m in range(width // 2):
            x = y[:, m * LANES:(m + 1) * LANES]
            y_buf[u, :, 2 * m * LANES:(2 * m + 1) * LANES] = x.astype(jnp.bfloat16)
            y_buf[u, :, (2 * m + 1) * LANES:(2 * m + 2) * LANES] = pltpu.roll(x, tile, 1).astype(jnp.bfloat16)

    def second_product(row, u):
        lhs = lhs_ref[row]
        w = []
        for m in range(width // 2):
            x = y_buf[u, :, 2 * m * LANES:(2 * m + 1) * LANES]
            xr = y_buf[u, :, (2 * m + 1) * LANES:(2 * m + 2) * LANES]
            none = jnp.zeros_like(x)
            right = jnp.concatenate(
                [
                    jnp.concatenate([jnp.where(lo, x, none), jnp.where(lo, xr, none)], axis=1),
                    jnp.concatenate([jnp.where(lo, none, xr), jnp.where(lo, none, x)], axis=1),
                ],
                axis=0,
            )
            w.append(jnp.dot(lhs, right, preferred_element_type=jnp.float32))
        return w

    def add(row, k, w):
        for q in range(width):
            part = w[q // 2][:, q % 2 * LANES:(q % 2 + 1) * LANES]
            for s in range(0, width, ACCS):
                group = range(s, min(s + ACCS, width))
                places = [place_ref[row, (n * tiles + k) * width + q] for n in group]
                old = [acc[place] for acc, place in zip(accs, places)]
                for acc, place, was, n in zip(accs, places, old, group):
                    acc[place] = was + part[n * sub:(n + 1) * sub]

    def keep_two(u, y):
        keep(u, y[:tile])
        keep(u + 1, y[tile:])

    def hold(n, w):
        for m, part in enumerate(w):
            w_buf[n, :, m * 2 * LANES:(m + 1) * 2 * LANES] = part

    def held(n):
        return [w_buf[n, :, m * 2 * LANES:(m + 1) * 2 * LANES] for m in range(width // 2)]

    for k in range(0, tiles, 2):
        keep_two(k, first_products(0, k))
    for n in range(AHEAD):
        hold(n, second_product(0, n))

    def block_row(row, carry):
        following = jnp.minimum(row + 1, rf - 1)
        w = [held(n) for n in range(AHEAD)]
        for k in range(tiles):
            if k % 2 == 0:
                upcoming = first_products(following, k)
            ahead = k + AHEAD
            w.append(second_product(row, ahead) if ahead < tiles else second_product(following, ahead - tiles))
            add(row, k, w.pop(0))
            if k % 2 == 1:
                keep_two(k - 1, upcoming)
        for n in range(AHEAD):
            hold(n, w[n])
        return carry

    lax.fori_loop(0, rf, block_row, 0)

    named = jnp.zeros((NAME_ROWS, LANES), jnp.float32)
    here = lax.broadcasted_iota(jnp.int32, named.shape, 0)
    for n in range(groups * cap // LANES):
        part = names[:, n * LANES:(n + 1) * LANES]
        named = jnp.where(here == n, jnp.broadcast_to(part, named.shape), named)

    for (first, count), out in zip(spans, outs):

        def merge(c, carry):
            blocks = pl.ds(first + c * chunk, chunk)
            total = accs[0][blocks]
            for acc in accs[1:]:
                total = total + acc[blocks]
            rows = pl.ds(pl.multiple_of(c * (chunk * sub), chunk * sub), chunk * sub)
            out[rows, :] = total.reshape(chunk * sub, LANES).astype(out.dtype)
            return carry

        lax.fori_loop(0, count // chunk, merge, 0)
        out[count * sub:, :] = named.astype(out.dtype)


def partial_sums(rows_in, pieces, table_of, tables, spans, groups, cap):
    tile, cols = pieces[0].shape[1], rows_in.shape[1]
    rf = (rows_in.shape[0] - NAME_ROWS) // tile
    sub = tile * tile // LANES
    width = pieces[0].shape[2]
    rows = sum(x.shape[0] for x in pieces)
    n_places = (width // tile) ** 2 * (cols // tile)
    operands = [rows_in] + pieces
    panel_bytes = rows * tile * width * 2
    return pl.pallas_call(
        functools.partial(partial_kernel, len(pieces), spans, cap, groups, table_of),
        out_shape=[jax.ShapeDtypeStruct((n * sub + NAME_ROWS, LANES), jnp.bfloat16) for _, n in spans],
        grid_spec=pl.GridSpec(
            grid=(1,),
            in_specs=[pl.BlockSpec(memory_space=pl.ANY)] * len(operands),
            out_specs=[pl.BlockSpec((n * sub + NAME_ROWS, LANES), lambda i: (0, 0)) for _, n in spans],
            scratch_shapes=[pltpu.VMEM((tables * cap + 1, sub, LANES), jnp.float32)] * ACCS
            + [
                pltpu.VMEM((rf * tile, cols), jnp.bfloat16),
                pltpu.VMEM((rf, width // 2, 2 * tile), jnp.bfloat16),
                pltpu.VMEM((rows, tile, width), jnp.bfloat16),
                pltpu.VMEM((cols // tile, tile, 2 * width), jnp.bfloat16),
                pltpu.VMEM((AHEAD, width // 2, 2 * width), jnp.float32),
                pltpu.VMEM((NAME_ROWS, cols), jnp.bfloat16),
                pltpu.VMEM((rf, n_places), jnp.int32),
                pltpu.VMEM((rf, LANES), jnp.int32),
                pltpu.SMEM((rf, n_places), jnp.int32),
                pltpu.SMEM((rf, LANES), jnp.int32),
                pltpu.SemaphoreType.DMA((3 + rf // PARTS + rows // rf,)),
            ],
        ),
        compiler_params=pltpu.CompilerParams(
            dimension_semantics=("arbitrary",), vmem_limit_bytes=26 * 1024 * 1024 + panel_bytes
        ),
        cost_estimate=pl.CostEstimate(flops=1, bytes_accessed=1, transcendentals=0),
        name="partial_sums",
    )(*operands)


def early_kernel(*refs):
    tables, out_ref, accs, (vmem_names, smem_names, sem) = refs[:3], refs[3], refs[4:-3], refs[-3:]
    n_out, sub = out_ref.shape[:2]
    cap = (tables[0].shape[0] - NAME_ROWS) // sub
    chunk = 8
    at = lax.axis_index("grp") * cap
    row, lane = lax.div(at, jnp.int32(LANES)), lax.rem(at, jnp.int32(LANES))

    for n, x in enumerate(tables):
        vmem_names[n] = x[pl.ds(cap * sub, NAME_ROWS), :].astype(jnp.float32).astype(jnp.int32)
    copy = pltpu.make_async_copy(vmem_names, smem_names, sem)
    copy.start()

    def clear(c, carry):
        for acc in accs:
            acc[pl.ds(c * chunk, chunk)] = jnp.zeros((chunk, sub, LANES), jnp.float32)
        return carry

    lax.fori_loop(0, n_out // chunk, clear, 0)
    copy.wait()

    def add(c, carry):
        src = pl.ds(pl.multiple_of(c * sub, sub), sub)
        names = [smem_names[n, row, lane + c] for n in range(len(tables))]
        old = [acc[name] for acc, name in zip(accs, names)]
        for acc, name, was, x in zip(accs, names, old, tables):
            acc[name] = was + x[src, :].astype(jnp.float32)
        return carry

    lax.fori_loop(0, cap, add, 0, unroll=4)

    def merge(c, carry):
        blocks = pl.ds(c * chunk, chunk)
        total = accs[0][blocks]
        for acc in accs[1:]:
            total = total + acc[blocks]
        out_ref[blocks] = total
        return carry

    lax.fori_loop(0, n_out // chunk, merge, 0)


def last_kernel(table, from_b, from_c, out_ref, acc, late, rows_buf, vmem_names, smem_names, sems):
    n_out, sub = acc.shape[:2]
    cap = (late.shape[0] - NAME_ROWS) // sub
    me = lax.axis_index("grp")
    at = me * cap
    row, lane = lax.div(at, jnp.int32(LANES)), lax.rem(at, jnp.int32(LANES))
    parts = (sems.shape[0] - 2) // 3

    def late_copies(table_in):
        spans = [pl.ds(cap * sub, NAME_ROWS)]
        spans += [pl.ds(n * (cap // parts) * sub, cap // parts * sub) for n in range(parts)]
        return [
            pltpu.make_async_copy(table_in.at[span], late.at[span], sems.at[n]) for n, span in enumerate(spans)
        ]

    middle = (me == 1) | (me == 2)

    @pl.when(middle)
    def _():
        for copy in late_copies(from_b):
            copy.start()

    @pl.when(jnp.logical_not(middle))
    def _():
        for copy in late_copies(from_c):
            copy.start()

    height = n_out // parts
    blocks = [pl.ds(n * height, height) for n in range(parts)]
    fills = [
        pltpu.make_async_copy(table.at[span], acc.at[span], sems.at[1 + parts + n]) for n, span in enumerate(blocks)
    ]
    for copy in fills:
        copy.start()
    waiting = late_copies(from_b)
    waiting.pop(0).wait()
    vmem_names[...] = late[pl.ds(cap * sub, NAME_ROWS), :].astype(jnp.float32).astype(jnp.int32)
    copy = pltpu.make_async_copy(vmem_names, smem_names, sems.at[1 + 2 * parts])
    copy.start()
    for other in waiting + fills + [copy]:
        other.wait()

    def add(c, carry):
        acc[smem_names[row, lane + c]] += late[pl.ds(pl.multiple_of(c * sub, sub), sub), :].astype(jnp.float32)
        return carry

    lax.fori_loop(0, cap, add, 0, unroll=4)
    flat = acc.reshape(n_out * sub, LANES)

    def emit(c, carry):
        rows = pl.ds(pl.multiple_of(c * 8, 8), 8)
        for t in range(sub):
            rows_buf[rows, t * LANES:(t + 1) * LANES] = flat[pl.ds(c * (8 * sub) + t, 8, stride=sub), :]
        return carry

    copies = []
    for n, rows in enumerate(blocks):
        lax.fori_loop(n * height // 8, (n + 1) * height // 8, emit, 0)
        copies.append(pltpu.make_async_copy(rows_buf.at[rows], out_ref.at[rows], sems.at[2 + 2 * parts + n]))
        copies[-1].start()
    for copy in copies:
        copy.wait()


def owner_sums(tables, from_b, from_c, sub):
    def whole(x):
        return pl.BlockSpec(x.shape, lambda i: (0,) * len(x.shape))

    table = jax.ShapeDtypeStruct((OSLOT, sub, LANES), jnp.float32)
    names = (NAME_ROWS, LANES)
    early = pl.pallas_call(
        early_kernel,
        out_shape=table,
        grid_spec=pl.GridSpec(
            grid=(1,),
            in_specs=[whole(x) for x in tables],
            out_specs=whole(table),
            scratch_shapes=[pltpu.VMEM(table.shape, jnp.float32)] * len(tables)
            + [
                pltpu.VMEM((len(tables),) + names, jnp.int32),
                pltpu.SMEM((len(tables),) + names, jnp.int32),
                pltpu.SemaphoreType.DMA,
            ],
        ),
        compiler_params=pltpu.CompilerParams(
            dimension_semantics=("arbitrary",), vmem_limit_bytes=20 * 1024 * 1024
        ),
        name="early_sums",
    )(*tables)
    return pl.pallas_call(
        last_kernel,
        out_shape=jax.ShapeDtypeStruct((OSLOT, sub * LANES), jnp.float32),
        grid_spec=pl.GridSpec(
            grid=(1,),
            in_specs=[pl.BlockSpec(memory_space=pl.ANY)] * 3,
            out_specs=pl.BlockSpec(memory_space=pl.ANY),
            scratch_shapes=[
                pltpu.VMEM(table.shape, jnp.float32),
                pltpu.VMEM(from_b.shape, jnp.bfloat16),
                pltpu.VMEM((OSLOT, sub * LANES), jnp.float32),
                pltpu.VMEM(names, jnp.int32),
                pltpu.SMEM(names, jnp.int32),
                pltpu.SemaphoreType.DMA((2 + 3 * 4,)),
            ],
        ),
        compiler_params=pltpu.CompilerParams(
            dimension_semantics=("arbitrary",), vmem_limit_bytes=20 * 1024 * 1024
        ),
        name="owner_sums",
    )(early, from_b, from_c)


def swap(x, axis, d):
    return lax.ppermute(x, axis, [(i, i ^ d) for i in range(lax.axis_size(axis))])


def direct(p_tiles):
    return [swap(p_tiles, "blk", d) for d in range(2, lax.axis_size("blk"), 2)]


def body(a_tiles, a_cols, p_tiles, route_list, out_slot):
    groups = lax.axis_size("grp")
    rf, tile, cols = a_tiles.shape
    cap = out_slot.shape[1] // groups
    sub = tile * tile // LANES
    takes = [(1, 0), (3, 1), (0, 2), (2, 3)]

    def take(x):
        return lax.ppermute(x, "grp", takes)

    rows_sent = with_numbers(a_tiles, route_list, out_slot, a_cols)
    far = direct(p_tiles)
    p_took = take(p_tiles)
    a_took = take(rows_sent)
    far[0], p_took = lax.optimization_barrier((far[0], p_took))
    far_took = direct(p_took)
    mine = [p_tiles, jnp.concatenate(far)]
    other = [swap(x, "blk", 1) for x in mine]

    def tables_own(off, middle):
        return jnp.where(middle, jnp.where(off == 0, 0, jnp.where(off == 1, 3, off - 1)), jnp.where(off < 2, off, 3))

    def tables_took(off, middle):
        return jnp.where((off == 0) | ((off == 1) & middle), off, 2)

    spans = ((0, cap), (cap, cap), (2 * cap, cap))
    own, to_a, to_b = partial_sums(rows_sent, mine + other, tables_own, 3, spans, groups, cap)
    own, p_took, *far_took = lax.optimization_barrier((own, p_took, *far_took))
    to_a, a_took = lax.optimization_barrier((to_a, a_took))
    from_a = lax.ppermute(to_a, "grp", [(0, 1), (3, 2), (1, 3), (2, 0)])
    took = [p_took] + far_took
    pieces = took + [swap(x, "blk", 1) for x in took]
    spans = ((0, cap), (cap, cap))
    own_took, to_c = partial_sums(a_took, pieces, tables_took, 2, spans, groups, cap)
    to_b, to_c = lax.optimization_barrier((to_b, to_c))
    from_b = lax.ppermute(to_b, "grp", [(1, 2), (2, 1)])
    from_c = lax.ppermute(to_c, "grp", [(1, 0), (2, 3)])
    return owner_sums([own, own_took, from_a], from_b, from_c, sub)


def solution(mesh):
    in_specs = (
        P(("blk", "grp"), None, None),
        P(("blk", "grp"), None),
        P(("blk", "grp"), None, None),
        P(("blk", "grp"), None),
        P(("blk", "grp"), None),
    )
    out_specs = P(("blk", "grp"), None)
    return jax.shard_map(body, mesh=mesh, in_specs=in_specs, out_specs=out_specs, check_vma=False)
```

```python
import functools

import jax
import jax.numpy as jnp
from jax import lax
from jax.experimental import pallas as pl
from jax.experimental.pallas import tpu as pltpu
from jax.sharding import PartitionSpec as P

OSLOT = 128
LANES = 128
ACCS = 4
AHEAD = 2
NAME_ROWS = 16
PART = 256
PARTS = 2


def log2(n):
    assert n & (n - 1) == 0
    return n.bit_length() - 1


def number_columns(n_places):
    return 0, n_places, 2 * n_places, 2 * n_places + LANES


def numbers_kernel(a_ref, route_ref, slot_ref, cols_ref, out_ref, wide):
    rf, tile, width = a_ref.shape
    out_ref[:rf * tile, :] = a_ref[...].reshape(rf * tile, width)
    wide[...] = jnp.zeros_like(wide)
    cols = cols_ref[...]
    parts = (route_ref[...], slot_ref[...], lax.shift_right_logical(cols, jnp.int32(log2(PART))), cols & (PART - 1))
    for at, part in zip(number_columns(route_ref.shape[1]), parts):
        wide[:part.shape[0], at:at + part.shape[1]] = part.astype(jnp.float32)
    out_ref[rf * tile:, :] = wide[...].astype(out_ref.dtype)


def with_numbers(a_tiles, route_list, out_slot, a_cols):
    rf, tile, width = a_tiles.shape
    return pl.pallas_call(
        numbers_kernel,
        out_shape=jax.ShapeDtypeStruct((rf * tile + NAME_ROWS, width), a_tiles.dtype),
        scratch_shapes=[pltpu.VMEM((NAME_ROWS, width), jnp.float32)],
        compiler_params=pltpu.CompilerParams(vmem_limit_bytes=56 * 1024 * 1024),
        cost_estimate=pl.CostEstimate(flops=1, bytes_accessed=1, transcendentals=0),
        name="with_numbers",
    )(a_tiles, route_list, out_slot, a_cols)


def partial_kernel(n_pieces, spans, cap, groups, table_of, rows_in, *refs):
    pieces, refs = refs[:n_pieces], refs[n_pieces:]
    outs, refs = refs[:len(spans)], refs[len(spans):]
    accs, (a_ref, lhs_ref, panel, y_buf, w_buf, *rest, sems) = refs[:ACCS], refs[ACCS:]
    packed_ref, place_vmem, idx_vmem, place_ref, idx_ref = rest
    tile = panel.shape[1]
    rf, tiles = a_ref.shape[0] // tile, a_ref.shape[1] // tile
    width = panel.shape[2] // tile
    sub = tile * tile // LANES
    n_tables = accs[0].shape[0] // cap
    chunk = 8

    n_places = width * tiles * width
    copies = [
        pltpu.make_async_copy(rows_in.at[pl.ds(rf * tile, NAME_ROWS)], packed_ref, sems.at[0]),
    ]
    for n in range(0, rf, PARTS):
        part = pl.ds(n * tile, PARTS * tile)
        copies.append(pltpu.make_async_copy(rows_in.at[part], a_ref.at[part], sems.at[len(copies)]))
    at = 0
    for piece in pieces:
        for n in range(0, piece.shape[0], rf):
            part, whole = piece.at[pl.ds(n, rf)], panel.at[pl.ds(at, rf)]
            copies.append(pltpu.make_async_copy(part, whole, sems.at[len(copies)]))
            at += rf
    for copy in copies:
        copy.start()
    copies.pop(0).wait()

    me, blk = lax.axis_index("grp"), lax.axis_index("blk")
    numbers = packed_ref[...].astype(jnp.float32).astype(jnp.int32)
    at_route, at_slot, at_high, at_low = number_columns(n_places)
    route = numbers[:rf, at_route:at_route + n_places]
    names = numbers[:1, at_slot:at_slot + n_places].astype(jnp.float32)
    owner = lax.shift_right_logical(route, jnp.int32(log2(cap)))
    table = table_of(owner ^ me, (me == 1) | (me == 2))
    place_vmem[...] = jnp.where(table < n_tables, table * cap + (route & (cap - 1)), n_tables * cap)
    cols = numbers[:rf, at_high:at_high + LANES] * PART + numbers[:rf, at_low:at_low + LANES]
    d = lax.shift_right_logical(cols, jnp.int32(log2(rf * groups))) ^ blk
    half = panel.shape[0] // (2 * rf)
    idx_vmem[...] = ((d & 1) * half + lax.shift_right_logical(d, jnp.int32(1))) * rf + (cols & (rf - 1))
    for n, (src, dst) in enumerate(((place_vmem, place_ref), (idx_vmem, idx_ref))):
        copy = pltpu.make_async_copy(src, dst, sems.at[sems.shape[0] - 2 + n])
        copy.start()
        copies.append(copy)

    def clear(c, carry):
        blocks = pl.ds(c * chunk, chunk)
        for acc in accs:
            acc[blocks] = jnp.zeros((chunk, sub, LANES), jnp.float32)
        return carry

    lax.fori_loop(0, n_tables * cap // chunk, clear, 0)
    for acc in accs:
        acc[n_tables * cap] = jnp.zeros((sub, LANES), jnp.float32)
    for copy in copies:
        copy.wait()

    columns = width * tile
    from_col = lax.broadcasted_iota(jnp.int32, (columns, columns), 0)
    to_col = lax.broadcasted_iota(jnp.int32, (columns, columns), 1)
    wanted = jnp.where(to_col < columns // 2, 2 * to_col, 2 * to_col - columns + 1)
    chosen = jnp.where(from_col == wanted, 1.0, 0.0).astype(jnp.bfloat16)
    for row in range(rf):
        split = jnp.dot(panel[row], chosen, preferred_element_type=jnp.float32)
        stacked = jnp.concatenate([split[:, :columns // 2], split[:, columns // 2:]], axis=0)
        lhs_ref[row] = jnp.transpose(stacked).astype(jnp.bfloat16)

    lane = lax.broadcasted_iota(jnp.int32, (tile, LANES), 1)
    lo = lane < tile

    def first_products(row, k):
        both = a_ref[pl.ds(pl.multiple_of(row * tile, tile), tile), k * tile:k * tile + LANES]
        none = jnp.zeros_like(both)
        left = jnp.concatenate([jnp.where(lo, both, none), jnp.where(lo, none, both)], axis=0)
        right = jnp.concatenate([panel[idx_ref[row, k]], panel[idx_ref[row, k + 1]]], axis=0)
        return jnp.dot(left, right, preferred_element_type=jnp.float32)

    def keep(u, y):
        for m in range(width // 2):
            x = y[:, m * LANES:(m + 1) * LANES]
            y_buf[u, :, 2 * m * LANES:(2 * m + 1) * LANES] = x.astype(jnp.bfloat16)
            y_buf[u, :, (2 * m + 1) * LANES:(2 * m + 2) * LANES] = pltpu.roll(x, tile, 1).astype(jnp.bfloat16)

    def second_product(row, u):
        lhs = lhs_ref[row]
        w = []
        for m in range(width // 2):
            x = y_buf[u, :, 2 * m * LANES:(2 * m + 1) * LANES]
            xr = y_buf[u, :, (2 * m + 1) * LANES:(2 * m + 2) * LANES]
            none = jnp.zeros_like(x)
            right = jnp.concatenate(
                [
                    jnp.concatenate([jnp.where(lo, x, none), jnp.where(lo, xr, none)], axis=1),
                    jnp.concatenate([jnp.where(lo, none, xr), jnp.where(lo, none, x)], axis=1),
                ],
                axis=0,
            )
            w.append(jnp.dot(lhs, right, preferred_element_type=jnp.float32))
        return w

    def add(row, k, w):
        for q in range(width):
            part = w[q // 2][:, q % 2 * LANES:(q % 2 + 1) * LANES]
            for s in range(0, width, ACCS):
                group = range(s, min(s + ACCS, width))
                places = [place_ref[row, (n * tiles + k) * width + q] for n in group]
                old = [acc[place] for acc, place in zip(accs, places)]
                for acc, place, was, n in zip(accs, places, old, group):
                    acc[place] = was + part[n * sub:(n + 1) * sub]

    def keep_two(u, y):
        keep(u, y[:tile])
        keep(u + 1, y[tile:])

    def hold(n, w):
        for m, part in enumerate(w):
            w_buf[n, :, m * 2 * LANES:(m + 1) * 2 * LANES] = part

    def held(n):
        return [w_buf[n, :, m * 2 * LANES:(m + 1) * 2 * LANES] for m in range(width // 2)]

    for k in range(0, tiles, 2):
        keep_two(k, first_products(0, k))
    for n in range(AHEAD):
        hold(n, second_product(0, n))

    def block_row(row, carry):
        following = jnp.minimum(row + 1, rf - 1)
        w = [held(n) for n in range(AHEAD)]
        for k in range(tiles):
            if k % 2 == 0:
                upcoming = first_products(following, k)
            ahead = k + AHEAD
            w.append(second_product(row, ahead) if ahead < tiles else second_product(following, ahead - tiles))
            add(row, k, w.pop(0))
            if k % 2 == 1:
                keep_two(k - 1, upcoming)
        for n in range(AHEAD):
            hold(n, w[n])
        return carry

    lax.fori_loop(0, rf, block_row, 0)

    named = jnp.zeros((NAME_ROWS, LANES), jnp.float32)
    here = lax.broadcasted_iota(jnp.int32, named.shape, 0)
    for n in range(groups * cap // LANES):
        part = names[:, n * LANES:(n + 1) * LANES]
        named = jnp.where(here == n, jnp.broadcast_to(part, named.shape), named)

    for (first, count), out in zip(spans, outs):

        def merge(c, carry):
            blocks = pl.ds(first + c * chunk, chunk)
            total = accs[0][blocks]
            for acc in accs[1:]:
                total = total + acc[blocks]
            rows = pl.ds(pl.multiple_of(c * (chunk * sub), chunk * sub), chunk * sub)
            out[rows, :] = total.reshape(chunk * sub, LANES).astype(out.dtype)
            return carry

        lax.fori_loop(0, count // chunk, merge, 0)
        out[count * sub:, :] = named.astype(out.dtype)


def partial_sums(rows_in, pieces, table_of, tables, spans, groups, cap):
    tile, cols = pieces[0].shape[1], rows_in.shape[1]
    rf = (rows_in.shape[0] - NAME_ROWS) // tile
    sub = tile * tile // LANES
    width = pieces[0].shape[2]
    rows = sum(x.shape[0] for x in pieces)
    n_places = (width // tile) ** 2 * (cols // tile)
    operands = [rows_in] + pieces
    panel_bytes = rows * tile * width * 2
    return pl.pallas_call(
        functools.partial(partial_kernel, len(pieces), spans, cap, groups, table_of),
        out_shape=[jax.ShapeDtypeStruct((n * sub + NAME_ROWS, LANES), jnp.bfloat16) for _, n in spans],
        grid_spec=pl.GridSpec(
            grid=(1,),
            in_specs=[pl.BlockSpec(memory_space=pl.ANY)] * len(operands),
            out_specs=[pl.BlockSpec((n * sub + NAME_ROWS, LANES), lambda i: (0, 0)) for _, n in spans],
            scratch_shapes=[pltpu.VMEM((tables * cap + 1, sub, LANES), jnp.float32)] * ACCS
            + [
                pltpu.VMEM((rf * tile, cols), jnp.bfloat16),
                pltpu.VMEM((rf, width // 2, 2 * tile), jnp.bfloat16),
                pltpu.VMEM((rows, tile, width), jnp.bfloat16),
                pltpu.VMEM((cols // tile, tile, 2 * width), jnp.bfloat16),
                pltpu.VMEM((AHEAD, width // 2, 2 * width), jnp.float32),
                pltpu.VMEM((NAME_ROWS, cols), jnp.bfloat16),
                pltpu.VMEM((rf, n_places), jnp.int32),
                pltpu.VMEM((rf, LANES), jnp.int32),
                pltpu.SMEM((rf, n_places), jnp.int32),
                pltpu.SMEM((rf, LANES), jnp.int32),
                pltpu.SemaphoreType.DMA((3 + rf // PARTS + rows // rf,)),
            ],
        ),
        compiler_params=pltpu.CompilerParams(
            dimension_semantics=("arbitrary",), vmem_limit_bytes=26 * 1024 * 1024 + panel_bytes
        ),
        cost_estimate=pl.CostEstimate(flops=1, bytes_accessed=1, transcendentals=0),
        name="partial_sums",
    )(*operands)


def early_kernel(*refs):
    tables, out_ref, accs, (vmem_names, smem_names, sem) = refs[:3], refs[3], refs[4:-3], refs[-3:]
    n_out, sub = out_ref.shape[:2]
    cap = (tables[0].shape[0] - NAME_ROWS) // sub
    chunk = 8
    at = lax.axis_index("grp") * cap
    row, lane = lax.div(at, jnp.int32(LANES)), lax.rem(at, jnp.int32(LANES))

    for n, x in enumerate(tables):
        vmem_names[n] = x[pl.ds(cap * sub, NAME_ROWS), :].astype(jnp.float32).astype(jnp.int32)
    copy = pltpu.make_async_copy(vmem_names, smem_names, sem)
    copy.start()

    def clear(c, carry):
        for acc in accs:
            acc[pl.ds(c * chunk, chunk)] = jnp.zeros((chunk, sub, LANES), jnp.float32)
        return carry

    lax.fori_loop(0, n_out // chunk, clear, 0)
    copy.wait()

    def add(c, carry):
        src = pl.ds(pl.multiple_of(c * sub, sub), sub)
        names = [smem_names[n, row, lane + c] for n in range(len(tables))]
        old = [acc[name] for acc, name in zip(accs, names)]
        for acc, name, was, x in zip(accs, names, old, tables):
            acc[name] = was + x[src, :].astype(jnp.float32)
        return carry

    lax.fori_loop(0, cap, add, 0, unroll=4)

    def merge(c, carry):
        blocks = pl.ds(c * chunk, chunk)
        total = accs[0][blocks]
        for acc in accs[1:]:
            total = total + acc[blocks]
        out_ref[blocks] = total
        return carry

    lax.fori_loop(0, n_out // chunk, merge, 0)


def last_kernel(table, from_c, from_b, out_ref, acc, late, rows_buf, vmem_names, smem_names, sems):
    n_out, sub = acc.shape[:2]
    cap = (late.shape[0] - NAME_ROWS) // sub
    me = lax.axis_index("grp")
    at = me * cap
    row, lane = lax.div(at, jnp.int32(LANES)), lax.rem(at, jnp.int32(LANES))
    parts = (sems.shape[0] - 2) // 3

    def late_copies(table_in):
        spans = [pl.ds(cap * sub, NAME_ROWS)]
        spans += [pl.ds(n * (cap // parts) * sub, cap // parts * sub) for n in range(parts)]
        return [
            pltpu.make_async_copy(table_in.at[span], late.at[span], sems.at[n]) for n, span in enumerate(spans)
        ]

    middle = (me == 1) | (me == 2)

    @pl.when(middle)
    def _():
        for copy in late_copies(from_b):
            copy.start()

    @pl.when(jnp.logical_not(middle))
    def _():
        for copy in late_copies(from_c):
            copy.start()

    height = n_out // parts
    blocks = [pl.ds(n * height, height) for n in range(parts)]
    fills = [
        pltpu.make_async_copy(table.at[span], acc.at[span], sems.at[1 + parts + n]) for n, span in enumerate(blocks)
    ]
    for copy in fills:
        copy.start()
    waiting = late_copies(from_b)
    waiting.pop(0).wait()
    vmem_names[...] = late[pl.ds(cap * sub, NAME_ROWS), :].astype(jnp.float32).astype(jnp.int32)
    copy = pltpu.make_async_copy(vmem_names, smem_names, sems.at[1 + 2 * parts])
    copy.start()
    for other in waiting + fills + [copy]:
        other.wait()

    def add(c, carry):
        acc[smem_names[row, lane + c]] += late[pl.ds(pl.multiple_of(c * sub, sub), sub), :].astype(jnp.float32)
        return carry

    lax.fori_loop(0, cap, add, 0, unroll=4)
    flat = acc.reshape(n_out * sub, LANES)

    def emit(c, carry):
        rows = pl.ds(pl.multiple_of(c * 8, 8), 8)
        for t in range(sub):
            rows_buf[rows, t * LANES:(t + 1) * LANES] = flat[pl.ds(c * (8 * sub) + t, 8, stride=sub), :]
        return carry

    copies = []
    for n, rows in enumerate(blocks):
        lax.fori_loop(n * height // 8, (n + 1) * height // 8, emit, 0)
        copies.append(pltpu.make_async_copy(rows_buf.at[rows], out_ref.at[rows], sems.at[2 + 2 * parts + n]))
        copies[-1].start()
    for copy in copies:
        copy.wait()


def owner_sums(tables, from_c, from_b, sub):
    def whole(x):
        return pl.BlockSpec(x.shape, lambda i: (0,) * len(x.shape))

    table = jax.ShapeDtypeStruct((OSLOT, sub, LANES), jnp.float32)
    names = (NAME_ROWS, LANES)
    early = pl.pallas_call(
        early_kernel,
        out_shape=table,
        grid_spec=pl.GridSpec(
            grid=(1,),
            in_specs=[whole(x) for x in tables],
            out_specs=whole(table),
            scratch_shapes=[pltpu.VMEM(table.shape, jnp.float32)] * len(tables)
            + [
                pltpu.VMEM((len(tables),) + names, jnp.int32),
                pltpu.SMEM((len(tables),) + names, jnp.int32),
                pltpu.SemaphoreType.DMA,
            ],
        ),
        compiler_params=pltpu.CompilerParams(
            dimension_semantics=("arbitrary",), vmem_limit_bytes=20 * 1024 * 1024
        ),
        name="early_sums",
    )(*tables)
    return pl.pallas_call(
        last_kernel,
        out_shape=jax.ShapeDtypeStruct((OSLOT, sub * LANES), jnp.float32),
        grid_spec=pl.GridSpec(
            grid=(1,),
            in_specs=[pl.BlockSpec(memory_space=pl.ANY)] * 3,
            out_specs=pl.BlockSpec(memory_space=pl.ANY),
            scratch_shapes=[
                pltpu.VMEM(table.shape, jnp.float32),
                pltpu.VMEM(from_b.shape, jnp.bfloat16),
                pltpu.VMEM((OSLOT, sub * LANES), jnp.float32),
                pltpu.VMEM(names, jnp.int32),
                pltpu.SMEM(names, jnp.int32),
                pltpu.SemaphoreType.DMA((2 + 3 * 4,)),
            ],
        ),
        compiler_params=pltpu.CompilerParams(
            dimension_semantics=("arbitrary",), vmem_limit_bytes=20 * 1024 * 1024
        ),
        name="owner_sums",
    )(early, from_c, from_b)


def swap(x, axis, d):
    return lax.ppermute(x, axis, [(i, i ^ d) for i in range(lax.axis_size(axis))])


def direct(p_tiles):
    return [swap(p_tiles, "blk", d) for d in range(2, lax.axis_size("blk"), 2)]


def body(a_tiles, a_cols, p_tiles, route_list, out_slot):
    groups = lax.axis_size("grp")
    rf, tile, cols = a_tiles.shape
    cap = out_slot.shape[1] // groups
    sub = tile * tile // LANES
    takes = [(1, 0), (3, 1), (0, 2), (2, 3)]

    def take(x):
        return lax.ppermute(x, "grp", takes)

    rows_sent = with_numbers(a_tiles, route_list, out_slot, a_cols)
    far = direct(p_tiles)
    p_took = take(p_tiles)
    a_took = take(rows_sent)
    far[0], p_took = lax.optimization_barrier((far[0], p_took))
    far_took = direct(p_took)
    mine = [p_tiles, jnp.concatenate(far)]
    other = [swap(x, "blk", 1) for x in mine]

    def tables_own(off, middle):
        return jnp.where(middle, jnp.where(off == 0, 0, jnp.where(off == 1, 3, off - 1)), jnp.where(off < 2, off, 3))

    def tables_took(off, middle):
        return jnp.where((off == 0) | ((off == 1) & middle), off, 2)

    spans = ((0, cap), (cap, cap), (2 * cap, cap))
    own, to_a, to_b = partial_sums(rows_sent, mine + other, tables_own, 3, spans, groups, cap)
    own, p_took, *far_took = lax.optimization_barrier((own, p_took, *far_took))
    to_a, a_took = lax.optimization_barrier((to_a, a_took))
    from_a = lax.ppermute(to_a, "grp", [(0, 1), (3, 2), (1, 3), (2, 0)])
    took = [p_took] + far_took
    pieces = took + [swap(x, "blk", 1) for x in took]
    spans = ((0, cap), (cap, cap))
    own_took, to_c = partial_sums(a_took, pieces, tables_took, 2, spans, groups, cap)
    from_c = lax.ppermute(to_c, "grp", [(1, 0), (2, 3)])
    to_b, own_took = lax.optimization_barrier((to_b, own_took))
    from_b = lax.ppermute(to_b, "grp", [(1, 2), (2, 1)])
    return owner_sums([own, own_took, from_a], from_c, from_b, sub)


def solution(mesh):
    in_specs = (
        P(("blk", "grp"), None, None),
        P(("blk", "grp"), None),
        P(("blk", "grp"), None, None),
        P(("blk", "grp"), None),
        P(("blk", "grp"), None),
    )
    out_specs = P(("blk", "grp"), None)
    return jax.shard_map(body, mesh=mesh, in_specs=in_specs, out_specs=out_specs, check_vma=False)
```

```python
import functools

import jax
import jax.numpy as jnp
from jax import lax
from jax.experimental import pallas as pl
from jax.experimental.pallas import tpu as pltpu
from jax.sharding import PartitionSpec as P

OSLOT = 128
LANES = 128
ACCS = 4
AHEAD = 2
NAME_ROWS = 16
PART = 256
PARTS = 2


def log2(n):
    assert n & (n - 1) == 0
    return n.bit_length() - 1


def number_columns(n_places):
    return 0, n_places, 2 * n_places, 2 * n_places + LANES


def numbers_kernel(a_ref, route_ref, slot_ref, cols_ref, out_ref, wide):
    rf, tile, width = a_ref.shape
    out_ref[:rf * tile, :] = a_ref[...].reshape(rf * tile, width)
    wide[...] = jnp.zeros_like(wide)
    cols = cols_ref[...]
    parts = (route_ref[...], slot_ref[...], lax.shift_right_logical(cols, jnp.int32(log2(PART))), cols & (PART - 1))
    for at, part in zip(number_columns(route_ref.shape[1]), parts):
        wide[:part.shape[0], at:at + part.shape[1]] = part.astype(jnp.float32)
    out_ref[rf * tile:, :] = wide[...].astype(out_ref.dtype)


def with_numbers(a_tiles, route_list, out_slot, a_cols):
    rf, tile, width = a_tiles.shape
    return pl.pallas_call(
        numbers_kernel,
        out_shape=jax.ShapeDtypeStruct((rf * tile + NAME_ROWS, width), a_tiles.dtype),
        scratch_shapes=[pltpu.VMEM((NAME_ROWS, width), jnp.float32)],
        compiler_params=pltpu.CompilerParams(vmem_limit_bytes=56 * 1024 * 1024),
        cost_estimate=pl.CostEstimate(flops=1, bytes_accessed=1, transcendentals=0),
        name="with_numbers",
    )(a_tiles, route_list, out_slot, a_cols)


def partial_kernel(n_pieces, spans, cap, groups, table_of, rows_in, *refs):
    pieces, refs = refs[:n_pieces], refs[n_pieces:]
    outs, refs = refs[:len(spans)], refs[len(spans):]
    accs, (a_ref, lhs_ref, panel, y_buf, w_buf, *rest, sems) = refs[:ACCS], refs[ACCS:]
    packed_ref, place_vmem, idx_vmem, place_ref, idx_ref = rest
    tile = panel.shape[1]
    rf, tiles = a_ref.shape[0] // tile, a_ref.shape[1] // tile
    width = panel.shape[2] // tile
    sub = tile * tile // LANES
    n_tables = accs[0].shape[0] // cap
    chunk = 8

    n_places = width * tiles * width
    copies = [
        pltpu.make_async_copy(rows_in.at[pl.ds(rf * tile, NAME_ROWS)], packed_ref, sems.at[0]),
    ]
    for n in range(0, rf, PARTS):
        part = pl.ds(n * tile, PARTS * tile)
        copies.append(pltpu.make_async_copy(rows_in.at[part], a_ref.at[part], sems.at[len(copies)]))
    at = 0
    for piece in pieces:
        for n in range(0, piece.shape[0], rf):
            part, whole = piece.at[pl.ds(n, rf)], panel.at[pl.ds(at, rf)]
            copies.append(pltpu.make_async_copy(part, whole, sems.at[len(copies)]))
            at += rf
    for copy in copies:
        copy.start()
    copies.pop(0).wait()

    me, blk = lax.axis_index("grp"), lax.axis_index("blk")
    numbers = packed_ref[...].astype(jnp.float32).astype(jnp.int32)
    at_route, at_slot, at_high, at_low = number_columns(n_places)
    route = numbers[:rf, at_route:at_route + n_places]
    names = numbers[:1, at_slot:at_slot + n_places].astype(jnp.float32)
    owner = lax.shift_right_logical(route, jnp.int32(log2(cap)))
    table = table_of(owner ^ me, (me == 1) | (me == 2))
    place_vmem[...] = jnp.where(table < n_tables, table * cap + (route & (cap - 1)), n_tables * cap)
    cols = numbers[:rf, at_high:at_high + LANES] * PART + numbers[:rf, at_low:at_low + LANES]
    d = lax.shift_right_logical(cols, jnp.int32(log2(rf * groups))) ^ blk
    half = panel.shape[0] // (2 * rf)
    idx_vmem[...] = ((d & 1) * half + lax.shift_right_logical(d, jnp.int32(1))) * rf + (cols & (rf - 1))
    for n, (src, dst) in enumerate(((place_vmem, place_ref), (idx_vmem, idx_ref))):
        copy = pltpu.make_async_copy(src, dst, sems.at[sems.shape[0] - 2 + n])
        copy.start()
        copies.append(copy)

    def clear(c, carry):
        blocks = pl.ds(c * chunk, chunk)
        for acc in accs:
            acc[blocks] = jnp.zeros((chunk, sub, LANES), jnp.float32)
        return carry

    lax.fori_loop(0, n_tables * cap // chunk, clear, 0)
    for acc in accs:
        acc[n_tables * cap] = jnp.zeros((sub, LANES), jnp.float32)
    for copy in copies:
        copy.wait()

    columns = width * tile
    from_col = lax.broadcasted_iota(jnp.int32, (columns, columns), 0)
    to_col = lax.broadcasted_iota(jnp.int32, (columns, columns), 1)
    wanted = jnp.where(to_col < columns // 2, 2 * to_col, 2 * to_col - columns + 1)
    chosen = jnp.where(from_col == wanted, 1.0, 0.0).astype(jnp.bfloat16)
    for row in range(rf):
        split = jnp.dot(panel[row], chosen, preferred_element_type=jnp.float32)
        stacked = jnp.concatenate([split[:, :columns // 2], split[:, columns // 2:]], axis=0)
        lhs_ref[row] = jnp.transpose(stacked).astype(jnp.bfloat16)

    lane = lax.broadcasted_iota(jnp.int32, (tile, LANES), 1)
    lo = lane < tile

    def first_products(row, k):
        both = a_ref[pl.ds(pl.multiple_of(row * tile, tile), tile), k * tile:k * tile + LANES]
        none = jnp.zeros_like(both)
        left = jnp.concatenate([jnp.where(lo, both, none), jnp.where(lo, none, both)], axis=0)
        right = jnp.concatenate([panel[idx_ref[row, k]], panel[idx_ref[row, k + 1]]], axis=0)
        return jnp.dot(left, right, preferred_element_type=jnp.float32)

    def keep(u, y):
        for m in range(width // 2):
            x = y[:, m * LANES:(m + 1) * LANES]
            y_buf[u, :, 2 * m * LANES:(2 * m + 1) * LANES] = x.astype(jnp.bfloat16)
            y_buf[u, :, (2 * m + 1) * LANES:(2 * m + 2) * LANES] = pltpu.roll(x, tile, 1).astype(jnp.bfloat16)

    def second_product(row, u):
        lhs = lhs_ref[row]
        w = []
        for m in range(width // 2):
            x = y_buf[u, :, 2 * m * LANES:(2 * m + 1) * LANES]
            xr = y_buf[u, :, (2 * m + 1) * LANES:(2 * m + 2) * LANES]
            none = jnp.zeros_like(x)
            right = jnp.concatenate(
                [
                    jnp.concatenate([jnp.where(lo, x, none), jnp.where(lo, xr, none)], axis=1),
                    jnp.concatenate([jnp.where(lo, none, xr), jnp.where(lo, none, x)], axis=1),
                ],
                axis=0,
            )
            w.append(jnp.dot(lhs, right, preferred_element_type=jnp.float32))
        return w

    def add(row, k, w):
        for q in range(width):
            part = w[q // 2][:, q % 2 * LANES:(q % 2 + 1) * LANES]
            for s in range(0, width, ACCS):
                group = range(s, min(s + ACCS, width))
                places = [place_ref[row, (n * tiles + k) * width + q] for n in group]
                old = [acc[place] for acc, place in zip(accs, places)]
                for acc, place, was, n in zip(accs, places, old, group):
                    acc[place] = was + part[n * sub:(n + 1) * sub]

    def keep_two(u, y):
        keep(u, y[:tile])
        keep(u + 1, y[tile:])

    def hold(n, w):
        for m, part in enumerate(w):
            w_buf[n, :, m * 2 * LANES:(m + 1) * 2 * LANES] = part

    def held(n):
        return [w_buf[n, :, m * 2 * LANES:(m + 1) * 2 * LANES] for m in range(width // 2)]

    for k in range(0, tiles, 2):
        keep_two(k, first_products(0, k))
    for n in range(AHEAD):
        hold(n, second_product(0, n))

    def block_row(row, carry):
        following = jnp.minimum(row + 1, rf - 1)
        w = [held(n) for n in range(AHEAD)]
        for k in range(tiles):
            if k % 2 == 0:
                upcoming = first_products(following, k)
            ahead = k + AHEAD
            w.append(second_product(row, ahead) if ahead < tiles else second_product(following, ahead - tiles))
            add(row, k, w.pop(0))
            if k % 2 == 1:
                keep_two(k - 1, upcoming)
        for n in range(AHEAD):
            hold(n, w[n])
        return carry

    lax.fori_loop(0, rf, block_row, 0)

    named = jnp.zeros((NAME_ROWS, LANES), jnp.float32)
    here = lax.broadcasted_iota(jnp.int32, named.shape, 0)
    for n in range(groups * cap // LANES):
        part = names[:, n * LANES:(n + 1) * LANES]
        named = jnp.where(here == n, jnp.broadcast_to(part, named.shape), named)

    for (first, count), out in zip(spans, outs):

        def merge(c, carry):
            blocks = pl.ds(first + c * chunk, chunk)
            total = accs[0][blocks]
            for acc in accs[1:]:
                total = total + acc[blocks]
            rows = pl.ds(pl.multiple_of(c * (chunk * sub), chunk * sub), chunk * sub)
            out[rows, :] = total.reshape(chunk * sub, LANES).astype(out.dtype)
            return carry

        lax.fori_loop(0, count // chunk, merge, 0)
        out[count * sub:, :] = named.astype(out.dtype)


def partial_sums(rows_in, pieces, table_of, tables, spans, groups, cap):
    tile, cols = pieces[0].shape[1], rows_in.shape[1]
    rf = (rows_in.shape[0] - NAME_ROWS) // tile
    sub = tile * tile // LANES
    width = pieces[0].shape[2]
    rows = sum(x.shape[0] for x in pieces)
    n_places = (width // tile) ** 2 * (cols // tile)
    operands = [rows_in] + pieces
    panel_bytes = rows * tile * width * 2
    return pl.pallas_call(
        functools.partial(partial_kernel, len(pieces), spans, cap, groups, table_of),
        out_shape=[jax.ShapeDtypeStruct((n * sub + NAME_ROWS, LANES), jnp.bfloat16) for _, n in spans],
        grid_spec=pl.GridSpec(
            grid=(1,),
            in_specs=[pl.BlockSpec(memory_space=pl.ANY)] * len(operands),
            out_specs=[pl.BlockSpec((n * sub + NAME_ROWS, LANES), lambda i: (0, 0)) for _, n in spans],
            scratch_shapes=[pltpu.VMEM((tables * cap + 1, sub, LANES), jnp.float32)] * ACCS
            + [
                pltpu.VMEM((rf * tile, cols), jnp.bfloat16),
                pltpu.VMEM((rf, width // 2, 2 * tile), jnp.bfloat16),
                pltpu.VMEM((rows, tile, width), jnp.bfloat16),
                pltpu.VMEM((cols // tile, tile, 2 * width), jnp.bfloat16),
                pltpu.VMEM((AHEAD, width // 2, 2 * width), jnp.float32),
                pltpu.VMEM((NAME_ROWS, cols), jnp.bfloat16),
                pltpu.VMEM((rf, n_places), jnp.int32),
                pltpu.VMEM((rf, LANES), jnp.int32),
                pltpu.SMEM((rf, n_places), jnp.int32),
                pltpu.SMEM((rf, LANES), jnp.int32),
                pltpu.SemaphoreType.DMA((3 + rf // PARTS + rows // rf,)),
            ],
        ),
        compiler_params=pltpu.CompilerParams(
            dimension_semantics=("arbitrary",), vmem_limit_bytes=26 * 1024 * 1024 + panel_bytes
        ),
        cost_estimate=pl.CostEstimate(flops=1, bytes_accessed=1, transcendentals=0),
        name="partial_sums",
    )(*operands)


def early_kernel(*refs):
    tables, out_ref, accs, (vmem_names, smem_names, sem) = refs[:3], refs[3], refs[4:-3], refs[-3:]
    n_out, sub = out_ref.shape[:2]
    cap = (tables[0].shape[0] - NAME_ROWS) // sub
    chunk = 8
    at = lax.axis_index("grp") * cap
    row, lane = lax.div(at, jnp.int32(LANES)), lax.rem(at, jnp.int32(LANES))

    for n, x in enumerate(tables):
        vmem_names[n] = x[pl.ds(cap * sub, NAME_ROWS), :].astype(jnp.float32).astype(jnp.int32)
    copy = pltpu.make_async_copy(vmem_names, smem_names, sem)
    copy.start()

    def clear(c, carry):
        for acc in accs:
            acc[pl.ds(c * chunk, chunk)] = jnp.zeros((chunk, sub, LANES), jnp.float32)
        return carry

    lax.fori_loop(0, n_out // chunk, clear, 0)
    copy.wait()

    def add(c, carry):
        src = pl.ds(pl.multiple_of(c * sub, sub), sub)
        names = [smem_names[n, row, lane + c] for n in range(len(tables))]
        old = [acc[name] for acc, name in zip(accs, names)]
        for acc, name, was, x in zip(accs, names, old, tables):
            acc[name] = was + x[src, :].astype(jnp.float32)
        return carry

    lax.fori_loop(0, cap, add, 0, unroll=4)

    def merge(c, carry):
        blocks = pl.ds(c * chunk, chunk)
        total = accs[0][blocks]
        for acc in accs[1:]:
            total = total + acc[blocks]
        out_ref[blocks] = total
        return carry

    lax.fori_loop(0, n_out // chunk, merge, 0)


def last_kernel(names, table, from_b, from_c, out_ref, acc, late, rows_buf, sems):
    n_out, sub = acc.shape[:2]
    cap = late.shape[0] // sub
    me = lax.axis_index("grp")
    at = me * cap
    parts = sems.shape[0] // 3

    def late_copies(table_in):
        spans = [pl.ds(n * (cap // parts) * sub, cap // parts * sub) for n in range(parts)]
        return [
            pltpu.make_async_copy(table_in.at[span], late.at[span], sems.at[n]) for n, span in enumerate(spans)
        ]

    middle = (me == 1) | (me == 2)

    @pl.when(middle)
    def _():
        for copy in late_copies(from_b):
            copy.start()

    @pl.when(jnp.logical_not(middle))
    def _():
        for copy in late_copies(from_c):
            copy.start()

    height = n_out // parts
    blocks = [pl.ds(n * height, height) for n in range(parts)]
    fills = [
        pltpu.make_async_copy(table.at[span], acc.at[span], sems.at[parts + n]) for n, span in enumerate(blocks)
    ]
    for copy in fills:
        copy.start()
    for copy in late_copies(from_b) + fills:
        copy.wait()

    def add(c, carry):
        acc[names[0, at + c]] += late[pl.ds(pl.multiple_of(c * sub, sub), sub), :].astype(jnp.float32)
        return carry

    lax.fori_loop(0, cap, add, 0, unroll=4)
    flat = acc.reshape(n_out * sub, LANES)

    def emit(c, carry):
        rows = pl.ds(pl.multiple_of(c * 8, 8), 8)
        for t in range(sub):
            rows_buf[rows, t * LANES:(t + 1) * LANES] = flat[pl.ds(c * (8 * sub) + t, 8, stride=sub), :]
        return carry

    copies = []
    for n, rows in enumerate(blocks):
        lax.fori_loop(n * height // 8, (n + 1) * height // 8, emit, 0)
        copies.append(pltpu.make_async_copy(rows_buf.at[rows], out_ref.at[rows], sems.at[2 * parts + n]))
        copies[-1].start()
    for copy in copies:
        copy.wait()


def owner_sums(tables, last_names, from_b, from_c, sub):
    def whole(x):
        return pl.BlockSpec(x.shape, lambda i: (0,) * len(x.shape))

    table = jax.ShapeDtypeStruct((OSLOT, sub, LANES), jnp.float32)
    names = (NAME_ROWS, LANES)
    early = pl.pallas_call(
        early_kernel,
        out_shape=table,
        grid_spec=pl.GridSpec(
            grid=(1,),
            in_specs=[whole(x) for x in tables],
            out_specs=whole(table),
            scratch_shapes=[pltpu.VMEM(table.shape, jnp.float32)] * len(tables)
            + [
                pltpu.VMEM((len(tables),) + names, jnp.int32),
                pltpu.SMEM((len(tables),) + names, jnp.int32),
                pltpu.SemaphoreType.DMA,
            ],
        ),
        compiler_params=pltpu.CompilerParams(
            dimension_semantics=("arbitrary",), vmem_limit_bytes=20 * 1024 * 1024
        ),
        name="early_sums",
    )(*tables)
    return pl.pallas_call(
        last_kernel,
        out_shape=jax.ShapeDtypeStruct((OSLOT, sub * LANES), jnp.float32),
        grid_spec=pltpu.PrefetchScalarGridSpec(
            num_scalar_prefetch=1,
            grid=(1,),
            in_specs=[pl.BlockSpec(memory_space=pl.ANY)] * 3,
            out_specs=pl.BlockSpec(memory_space=pl.ANY),
            scratch_shapes=[
                pltpu.VMEM(table.shape, jnp.float32),
                pltpu.VMEM((from_b.shape[0] - NAME_ROWS, LANES), jnp.bfloat16),
                pltpu.VMEM((OSLOT, sub * LANES), jnp.float32),
                pltpu.SemaphoreType.DMA((3 * 4,)),
            ],
        ),
        compiler_params=pltpu.CompilerParams(
            dimension_semantics=("arbitrary",), vmem_limit_bytes=20 * 1024 * 1024
        ),
        name="owner_sums",
    )(last_names, early, from_b, from_c)


def swap(x, axis, d):
    return lax.ppermute(x, axis, [(i, i ^ d) for i in range(lax.axis_size(axis))])


def direct(p_tiles):
    return [swap(p_tiles, "blk", d) for d in range(2, lax.axis_size("blk"), 2)]


def body(a_tiles, a_cols, p_tiles, route_list, out_slot):
    groups = lax.axis_size("grp")
    rf, tile, cols = a_tiles.shape
    cap = out_slot.shape[1] // groups
    sub = tile * tile // LANES
    takes = [(1, 0), (3, 1), (0, 2), (2, 3)]

    def take(x):
        return lax.ppermute(x, "grp", takes)

    rows_sent = with_numbers(a_tiles, route_list, out_slot, a_cols)
    far = direct(p_tiles)
    p_took = take(p_tiles)
    a_took = take(rows_sent)
    far[0], p_took = lax.optimization_barrier((far[0], p_took))
    far_took = direct(p_took)
    mine = [p_tiles, jnp.concatenate(far)]
    other = [swap(x, "blk", 1) for x in mine]

    def tables_own(off, middle):
        return jnp.where(middle, jnp.where(off == 0, 0, jnp.where(off == 1, 3, off - 1)), jnp.where(off < 2, off, 3))

    def tables_took(off, middle):
        return jnp.where((off == 0) | ((off == 1) & middle), off, 2)

    spans = ((0, cap), (cap, cap), (2 * cap, cap))
    own, to_a, to_b = partial_sums(rows_sent, mine + other, tables_own, 3, spans, groups, cap)
    own, p_took, *far_took = lax.optimization_barrier((own, p_took, *far_took))
    to_a, to_b, a_took = lax.optimization_barrier((to_a, to_b, a_took))
    from_a = lax.ppermute(to_a, "grp", [(0, 1), (3, 2), (1, 3), (2, 0)])
    from_b = lax.ppermute(to_b, "grp", [(1, 2), (2, 1)])
    took = [p_took] + far_took
    pieces = took + [swap(x, "blk", 1) for x in took]
    spans = ((0, cap), (cap, cap))
    own_took, to_c = partial_sums(a_took, pieces, tables_took, 2, spans, groups, cap)
    from_c = lax.ppermute(to_c, "grp", [(1, 0), (2, 3)])
    last_names = swap(out_slot, "grp", groups - 1)
    return owner_sums([own, own_took, from_a], last_names, from_b, from_c, sub)


def solution(mesh):
    in_specs = (
        P(("blk", "grp"), None, None),
        P(("blk", "grp"), None),
        P(("blk", "grp"), None, None),
        P(("blk", "grp"), None),
        P(("blk", "grp"), None),
    )
    out_specs = P(("blk", "grp"), None)
    return jax.shard_map(body, mesh=mesh, in_specs=in_specs, out_specs=out_specs, check_vma=False)
```

```python
import functools

import jax
import jax.numpy as jnp
from jax import lax
from jax.experimental import pallas as pl
from jax.experimental.pallas import tpu as pltpu
from jax.sharding import PartitionSpec as P

OSLOT = 128
LANES = 128
ACCS = 4
AHEAD = 2
NAME_ROWS = 16
PART = 256
PARTS = 1


def log2(n):
    assert n & (n - 1) == 0
    return n.bit_length() - 1


def number_columns(n_places):
    return 0, n_places, 2 * n_places, 2 * n_places + LANES


def numbers_kernel(a_ref, route_ref, slot_ref, cols_ref, out_ref, wide):
    rf, tile, width = a_ref.shape
    out_ref[:rf * tile, :] = a_ref[...].reshape(rf * tile, width)
    wide[...] = jnp.zeros_like(wide)
    cols = cols_ref[...]
    parts = (route_ref[...], slot_ref[...], lax.shift_right_logical(cols, jnp.int32(log2(PART))), cols & (PART - 1))
    for at, part in zip(number_columns(route_ref.shape[1]), parts):
        wide[:part.shape[0], at:at + part.shape[1]] = part.astype(jnp.float32)
    out_ref[rf * tile:, :] = wide[...].astype(out_ref.dtype)


def with_numbers(a_tiles, route_list, out_slot, a_cols):
    rf, tile, width = a_tiles.shape
    return pl.pallas_call(
        numbers_kernel,
        out_shape=jax.ShapeDtypeStruct((rf * tile + NAME_ROWS, width), a_tiles.dtype),
        scratch_shapes=[pltpu.VMEM((NAME_ROWS, width), jnp.float32)],
        compiler_params=pltpu.CompilerParams(vmem_limit_bytes=56 * 1024 * 1024),
        cost_estimate=pl.CostEstimate(flops=1, bytes_accessed=1, transcendentals=0),
        name="with_numbers",
    )(a_tiles, route_list, out_slot, a_cols)


def partial_kernel(n_pieces, spans, cap, groups, table_of, rows_in, *refs):
    pieces, refs = refs[:n_pieces], refs[n_pieces:]
    outs, refs = refs[:len(spans)], refs[len(spans):]
    accs, (a_ref, lhs_ref, panel, y_buf, w_buf, *rest, sems) = refs[:ACCS], refs[ACCS:]
    packed_ref, place_vmem, idx_vmem, place_ref, idx_ref = rest
    tile = panel.shape[1]
    rf, tiles = a_ref.shape[0] // tile, a_ref.shape[1] // tile
    width = panel.shape[2] // tile
    sub = tile * tile // LANES
    n_tables = accs[0].shape[0] // cap
    chunk = 8

    n_places = width * tiles * width
    copies = [
        pltpu.make_async_copy(rows_in.at[pl.ds(rf * tile, NAME_ROWS)], packed_ref, sems.at[0]),
    ]
    for n in range(0, rf, PARTS):
        part = pl.ds(n * tile, PARTS * tile)
        copies.append(pltpu.make_async_copy(rows_in.at[part], a_ref.at[part], sems.at[len(copies)]))
    at = 0
    for piece in pieces:
        for n in range(0, piece.shape[0], rf // 2):
            part, whole = piece.at[pl.ds(n, rf // 2)], panel.at[pl.ds(at, rf // 2)]
            copies.append(pltpu.make_async_copy(part, whole, sems.at[len(copies)]))
            at += rf // 2
    for copy in copies:
        copy.start()
    copies.pop(0).wait()

    me, blk = lax.axis_index("grp"), lax.axis_index("blk")
    numbers = packed_ref[...].astype(jnp.float32).astype(jnp.int32)
    at_route, at_slot, at_high, at_low = number_columns(n_places)
    route = numbers[:rf, at_route:at_route + n_places]
    names = numbers[:1, at_slot:at_slot + n_places].astype(jnp.float32)
    owner = lax.shift_right_logical(route, jnp.int32(log2(cap)))
    table = table_of(owner ^ me, (me == 1) | (me == 2))
    place_vmem[...] = jnp.where(table < n_tables, table * cap + (route & (cap - 1)), n_tables * cap)
    cols = numbers[:rf, at_high:at_high + LANES] * PART + numbers[:rf, at_low:at_low + LANES]
    d = lax.shift_right_logical(cols, jnp.int32(log2(rf * groups))) ^ blk
    half = panel.shape[0] // (2 * rf)
    idx_vmem[...] = ((d & 1) * half + lax.shift_right_logical(d, jnp.int32(1))) * rf + (cols & (rf - 1))
    for n, (src, dst) in enumerate(((place_vmem, place_ref), (idx_vmem, idx_ref))):
        copy = pltpu.make_async_copy(src, dst, sems.at[sems.shape[0] - 2 + n])
        copy.start()
        copies.append(copy)

    def clear(c, carry):
        blocks = pl.ds(c * chunk, chunk)
        for acc in accs:
            acc[blocks] = jnp.zeros((chunk, sub, LANES), jnp.float32)
        return carry

    lax.fori_loop(0, n_tables * cap // chunk, clear, 0)
    for acc in accs:
        acc[n_tables * cap] = jnp.zeros((sub, LANES), jnp.float32)
    for copy in copies:
        copy.wait()

    columns = width * tile
    from_col = lax.broadcasted_iota(jnp.int32, (columns, columns), 0)
    to_col = lax.broadcasted_iota(jnp.int32, (columns, columns), 1)
    wanted = jnp.where(to_col < columns // 2, 2 * to_col, 2 * to_col - columns + 1)
    chosen = jnp.where(from_col == wanted, 1.0, 0.0).astype(jnp.bfloat16)
    for row in range(rf):
        split = jnp.dot(panel[row], chosen, preferred_element_type=jnp.float32)
        stacked = jnp.concatenate([split[:, :columns // 2], split[:, columns // 2:]], axis=0)
        lhs_ref[row] = jnp.transpose(stacked).astype(jnp.bfloat16)

    lane = lax.broadcasted_iota(jnp.int32, (tile, LANES), 1)
    lo = lane < tile

    def first_products(row, k):
        both = a_ref[pl.ds(pl.multiple_of(row * tile, tile), tile), k * tile:k * tile + LANES]
        none = jnp.zeros_like(both)
        left = jnp.concatenate([jnp.where(lo, both, none), jnp.where(lo, none, both)], axis=0)
        right = jnp.concatenate([panel[idx_ref[row, k]], panel[idx_ref[row, k + 1]]], axis=0)
        return jnp.dot(left, right, preferred_element_type=jnp.float32)

    def keep(u, y):
        for m in range(width // 2):
            x = y[:, m * LANES:(m + 1) * LANES]
            y_buf[u, :, 2 * m * LANES:(2 * m + 1) * LANES] = x.astype(jnp.bfloat16)
            y_buf[u, :, (2 * m + 1) * LANES:(2 * m + 2) * LANES] = pltpu.roll(x, tile, 1).astype(jnp.bfloat16)

    def second_product(row, u):
        lhs = lhs_ref[row]
        w = []
        for m in range(width // 2):
            x = y_buf[u, :, 2 * m * LANES:(2 * m + 1) * LANES]
            xr = y_buf[u, :, (2 * m + 1) * LANES:(2 * m + 2) * LANES]
            none = jnp.zeros_like(x)
            right = jnp.concatenate(
                [
                    jnp.concatenate([jnp.where(lo, x, none), jnp.where(lo, xr, none)], axis=1),
                    jnp.concatenate([jnp.where(lo, none, xr), jnp.where(lo, none, x)], axis=1),
                ],
                axis=0,
            )
            w.append(jnp.dot(lhs, right, preferred_element_type=jnp.float32))
        return w

    def add(row, k, w):
        for q in range(width):
            part = w[q // 2][:, q % 2 * LANES:(q % 2 + 1) * LANES]
            for s in range(0, width, ACCS):
                group = range(s, min(s + ACCS, width))
                places = [place_ref[row, (n * tiles + k) * width + q] for n in group]
                old = [acc[place] for acc, place in zip(accs, places)]
                for acc, place, was, n in zip(accs, places, old, group):
                    acc[place] = was + part[n * sub:(n + 1) * sub]

    def keep_two(u, y):
        keep(u, y[:tile])
        keep(u + 1, y[tile:])

    def hold(n, w):
        for m, part in enumerate(w):
            w_buf[n, :, m * 2 * LANES:(m + 1) * 2 * LANES] = part

    def held(n):
        return [w_buf[n, :, m * 2 * LANES:(m + 1) * 2 * LANES] for m in range(width // 2)]

    for k in range(0, tiles, 2):
        keep_two(k, first_products(0, k))
    for n in range(AHEAD):
        hold(n, second_product(0, n))

    def block_row(row, carry):
        following = jnp.minimum(row + 1, rf - 1)
        w = [held(n) for n in range(AHEAD)]
        for k in range(tiles):
            if k % 2 == 0:
                upcoming = first_products(following, k)
            ahead = k + AHEAD
            w.append(second_product(row, ahead) if ahead < tiles else second_product(following, ahead - tiles))
            add(row, k, w.pop(0))
            if k % 2 == 1:
                keep_two(k - 1, upcoming)
        for n in range(AHEAD):
            hold(n, w[n])
        return carry

    lax.fori_loop(0, rf, block_row, 0)

    named = jnp.zeros((NAME_ROWS, LANES), jnp.float32)
    here = lax.broadcasted_iota(jnp.int32, named.shape, 0)
    for n in range(groups * cap // LANES):
        part = names[:, n * LANES:(n + 1) * LANES]
        named = jnp.where(here == n, jnp.broadcast_to(part, named.shape), named)

    for (first, count), out in zip(spans, outs):

        def merge(c, carry):
            blocks = pl.ds(first + c * chunk, chunk)
            total = accs[0][blocks]
            for acc in accs[1:]:
                total = total + acc[blocks]
            rows = pl.ds(pl.multiple_of(c * (chunk * sub), chunk * sub), chunk * sub)
            out[rows, :] = total.reshape(chunk * sub, LANES).astype(out.dtype)
            return carry

        lax.fori_loop(0, count // chunk, merge, 0)
        out[count * sub:, :] = named.astype(out.dtype)


def partial_sums(rows_in, pieces, table_of, tables, spans, groups, cap):
    tile, cols = pieces[0].shape[1], rows_in.shape[1]
    rf = (rows_in.shape[0] - NAME_ROWS) // tile
    sub = tile * tile // LANES
    width = pieces[0].shape[2]
    rows = sum(x.shape[0] for x in pieces)
    n_places = (width // tile) ** 2 * (cols // tile)
    operands = [rows_in] + pieces
    panel_bytes = rows * tile * width * 2
    return pl.pallas_call(
        functools.partial(partial_kernel, len(pieces), spans, cap, groups, table_of),
        out_shape=[jax.ShapeDtypeStruct((n * sub + NAME_ROWS, LANES), jnp.bfloat16) for _, n in spans],
        grid_spec=pl.GridSpec(
            grid=(1,),
            in_specs=[pl.BlockSpec(memory_space=pl.ANY)] * len(operands),
            out_specs=[pl.BlockSpec((n * sub + NAME_ROWS, LANES), lambda i: (0, 0)) for _, n in spans],
            scratch_shapes=[pltpu.VMEM((tables * cap + 1, sub, LANES), jnp.float32)] * ACCS
            + [
                pltpu.VMEM((rf * tile, cols), jnp.bfloat16),
                pltpu.VMEM((rf, width // 2, 2 * tile), jnp.bfloat16),
                pltpu.VMEM((rows, tile, width), jnp.bfloat16),
                pltpu.VMEM((cols // tile, tile, 2 * width), jnp.bfloat16),
                pltpu.VMEM((AHEAD, width // 2, 2 * width), jnp.float32),
                pltpu.VMEM((NAME_ROWS, cols), jnp.bfloat16),
                pltpu.VMEM((rf, n_places), jnp.int32),
                pltpu.VMEM((rf, LANES), jnp.int32),
                pltpu.SMEM((rf, n_places), jnp.int32),
                pltpu.SMEM((rf, LANES), jnp.int32),
                pltpu.SemaphoreType.DMA((3 + rf // PARTS + 2 * rows // rf,)),
            ],
        ),
        compiler_params=pltpu.CompilerParams(
            dimension_semantics=("arbitrary",), vmem_limit_bytes=26 * 1024 * 1024 + panel_bytes
        ),
        cost_estimate=pl.CostEstimate(flops=1, bytes_accessed=1, transcendentals=0),
        name="partial_sums",
    )(*operands)


def early_kernel(*refs):
    tables, out_ref, accs, (vmem_names, smem_names, sem) = refs[:3], refs[3], refs[4:-3], refs[-3:]
    n_out, sub = out_ref.shape[:2]
    cap = (tables[0].shape[0] - NAME_ROWS) // sub
    chunk = 8
    at = lax.axis_index("grp") * cap
    row, lane = lax.div(at, jnp.int32(LANES)), lax.rem(at, jnp.int32(LANES))

    for n, x in enumerate(tables):
        vmem_names[n] = x[pl.ds(cap * sub, NAME_ROWS), :].astype(jnp.float32).astype(jnp.int32)
    copy = pltpu.make_async_copy(vmem_names, smem_names, sem)
    copy.start()

    def clear(c, carry):
        for acc in accs:
            acc[pl.ds(c * chunk, chunk)] = jnp.zeros((chunk, sub, LANES), jnp.float32)
        return carry

    lax.fori_loop(0, n_out // chunk, clear, 0)
    copy.wait()

    def add(c, carry):
        src = pl.ds(pl.multiple_of(c * sub, sub), sub)
        names = [smem_names[n, row, lane + c] for n in range(len(tables))]
        old = [acc[name] for acc, name in zip(accs, names)]
        for acc, name, was, x in zip(accs, names, old, tables):
            acc[name] = was + x[src, :].astype(jnp.float32)
        return carry

    lax.fori_loop(0, cap, add, 0, unroll=4)

    def merge(c, carry):
        blocks = pl.ds(c * chunk, chunk)
        total = accs[0][blocks]
        for acc in accs[1:]:
            total = total + acc[blocks]
        out_ref[blocks] = total
        return carry

    lax.fori_loop(0, n_out // chunk, merge, 0)


def last_kernel(table, from_b, from_c, out_ref, acc, late, rows_buf, vmem_names, smem_names, sems):
    n_out, sub = acc.shape[:2]
    cap = (late.shape[0] - NAME_ROWS) // sub
    me = lax.axis_index("grp")
    at = me * cap
    row, lane = lax.div(at, jnp.int32(LANES)), lax.rem(at, jnp.int32(LANES))
    parts = (sems.shape[0] - 2) // 3

    def late_copies(table_in):
        spans = [pl.ds(cap * sub, NAME_ROWS)]
        spans += [pl.ds(n * (cap // parts) * sub, cap // parts * sub) for n in range(parts)]
        return [
            pltpu.make_async_copy(table_in.at[span], late.at[span], sems.at[n]) for n, span in enumerate(spans)
        ]

    middle = (me == 1) | (me == 2)

    @pl.when(middle)
    def _():
        for copy in late_copies(from_b):
            copy.start()

    @pl.when(jnp.logical_not(middle))
    def _():
        for copy in late_copies(from_c):
            copy.start()

    height = n_out // parts
    blocks = [pl.ds(n * height, height) for n in range(parts)]
    fills = [
        pltpu.make_async_copy(table.at[span], acc.at[span], sems.at[1 + parts + n]) for n, span in enumerate(blocks)
    ]
    for copy in fills:
        copy.start()
    waiting = late_copies(from_b)
    waiting.pop(0).wait()
    vmem_names[...] = late[pl.ds(cap * sub, NAME_ROWS), :].astype(jnp.float32).astype(jnp.int32)
    copy = pltpu.make_async_copy(vmem_names, smem_names, sems.at[1 + 2 * parts])
    copy.start()
    for other in waiting + fills + [copy]:
        other.wait()

    def add(c, carry):
        acc[smem_names[row, lane + c]] += late[pl.ds(pl.multiple_of(c * sub, sub), sub), :].astype(jnp.float32)
        return carry

    lax.fori_loop(0, cap, add, 0, unroll=4)
    flat = acc.reshape(n_out * sub, LANES)

    def emit(c, carry):
        rows = pl.ds(pl.multiple_of(c * 8, 8), 8)
        for t in range(sub):
            rows_buf[rows, t * LANES:(t + 1) * LANES] = flat[pl.ds(c * (8 * sub) + t, 8, stride=sub), :]
        return carry

    copies = []
    for n, rows in enumerate(blocks):
        lax.fori_loop(n * height // 8, (n + 1) * height // 8, emit, 0)
        copies.append(pltpu.make_async_copy(rows_buf.at[rows], out_ref.at[rows], sems.at[2 + 2 * parts + n]))
        copies[-1].start()
    for copy in copies:
        copy.wait()


def owner_sums(tables, from_b, from_c, sub):
    def whole(x):
        return pl.BlockSpec(x.shape, lambda i: (0,) * len(x.shape))

    table = jax.ShapeDtypeStruct((OSLOT, sub, LANES), jnp.float32)
    names = (NAME_ROWS, LANES)
    early = pl.pallas_call(
        early_kernel,
        out_shape=table,
        grid_spec=pl.GridSpec(
            grid=(1,),
            in_specs=[whole(x) for x in tables],
            out_specs=whole(table),
            scratch_shapes=[pltpu.VMEM(table.shape, jnp.float32)] * len(tables)
            + [
                pltpu.VMEM((len(tables),) + names, jnp.int32),
                pltpu.SMEM((len(tables),) + names, jnp.int32),
                pltpu.SemaphoreType.DMA,
            ],
        ),
        compiler_params=pltpu.CompilerParams(
            dimension_semantics=("arbitrary",), vmem_limit_bytes=20 * 1024 * 1024
        ),
        name="early_sums",
    )(*tables)
    return pl.pallas_call(
        last_kernel,
        out_shape=jax.ShapeDtypeStruct((OSLOT, sub * LANES), jnp.float32),
        grid_spec=pl.GridSpec(
            grid=(1,),
            in_specs=[pl.BlockSpec(memory_space=pl.ANY)] * 3,
            out_specs=pl.BlockSpec(memory_space=pl.ANY),
            scratch_shapes=[
                pltpu.VMEM(table.shape, jnp.float32),
                pltpu.VMEM(from_b.shape, jnp.bfloat16),
                pltpu.VMEM((OSLOT, sub * LANES), jnp.float32),
                pltpu.VMEM(names, jnp.int32),
                pltpu.SMEM(names, jnp.int32),
                pltpu.SemaphoreType.DMA((2 + 3 * 8,)),
            ],
        ),
        compiler_params=pltpu.CompilerParams(
            dimension_semantics=("arbitrary",), vmem_limit_bytes=20 * 1024 * 1024
        ),
        name="owner_sums",
    )(early, from_b, from_c)


def swap(x, axis, d):
    return lax.ppermute(x, axis, [(i, i ^ d) for i in range(lax.axis_size(axis))])


def direct(p_tiles):
    return [swap(p_tiles, "blk", d) for d in range(2, lax.axis_size("blk"), 2)]


def body(a_tiles, a_cols, p_tiles, route_list, out_slot):
    groups = lax.axis_size("grp")
    rf, tile, cols = a_tiles.shape
    cap = out_slot.shape[1] // groups
    sub = tile * tile // LANES
    takes = [(1, 0), (3, 1), (0, 2), (2, 3)]

    def take(x):
        return lax.ppermute(x, "grp", takes)

    rows_sent = with_numbers(a_tiles, route_list, out_slot, a_cols)
    far = direct(p_tiles)
    p_took = take(p_tiles)
    a_took = take(rows_sent)
    far[0], p_took = lax.optimization_barrier((far[0], p_took))
    far_took = direct(p_took)
    mine = [p_tiles, jnp.concatenate(far)]
    other = [swap(x, "blk", 1) for x in mine]

    def tables_own(off, middle):
        return jnp.where(middle, jnp.where(off == 0, 0, jnp.where(off == 1, 3, off - 1)), jnp.where(off < 2, off, 3))

    def tables_took(off, middle):
        return jnp.where((off == 0) | ((off == 1) & middle), off, 2)

    spans = ((0, cap), (cap, cap), (2 * cap, cap))
    own, to_a, to_b = partial_sums(rows_sent, mine + other, tables_own, 3, spans, groups, cap)
    own, p_took, *far_took = lax.optimization_barrier((own, p_took, *far_took))
    to_a, to_b, a_took = lax.optimization_barrier((to_a, to_b, a_took))
    from_a = lax.ppermute(to_a, "grp", [(0, 1), (3, 2), (1, 3), (2, 0)])
    from_b = lax.ppermute(to_b, "grp", [(1, 2), (2, 1)])
    took = [p_took] + far_took
    pieces = took + [swap(x, "blk", 1) for x in took]
    spans = ((0, cap), (cap, cap))
    own_took, to_c = partial_sums(a_took, pieces, tables_took, 2, spans, groups, cap)
    from_c = lax.ppermute(to_c, "grp", [(1, 0), (2, 3)])
    return owner_sums([own, own_took, from_a], from_b, from_c, sub)


def solution(mesh):
    in_specs = (
        P(("blk", "grp"), None, None),
        P(("blk", "grp"), None),
        P(("blk", "grp"), None, None),
        P(("blk", "grp"), None),
        P(("blk", "grp"), None),
    )
    out_specs = P(("blk", "grp"), None)
    return jax.shard_map(body, mesh=mesh, in_specs=in_specs, out_specs=out_specs, check_vma=False)
```

```python
import functools

import jax
import jax.numpy as jnp
from jax import lax
from jax.experimental import pallas as pl
from jax.experimental.pallas import tpu as pltpu
from jax.sharding import PartitionSpec as P

OSLOT = 128
LANES = 128
ACCS = 4
AHEAD = 2
NAME_ROWS = 16
PART = 256
PARTS = 4


def log2(n):
    assert n & (n - 1) == 0
    return n.bit_length() - 1


def number_columns(n_places):
    return 0, n_places, 2 * n_places, 2 * n_places + LANES


def numbers_kernel(a_ref, route_ref, slot_ref, cols_ref, out_ref, wide):
    rf, tile, width = a_ref.shape
    out_ref[:rf * tile, :] = a_ref[...].reshape(rf * tile, width)
    wide[...] = jnp.zeros_like(wide)
    cols = cols_ref[...]
    parts = (route_ref[...], slot_ref[...], lax.shift_right_logical(cols, jnp.int32(log2(PART))), cols & (PART - 1))
    for at, part in zip(number_columns(route_ref.shape[1]), parts):
        wide[:part.shape[0], at:at + part.shape[1]] = part.astype(jnp.float32)
    out_ref[rf * tile:, :] = wide[...].astype(out_ref.dtype)


def with_numbers(a_tiles, route_list, out_slot, a_cols):
    rf, tile, width = a_tiles.shape
    return pl.pallas_call(
        numbers_kernel,
        out_shape=jax.ShapeDtypeStruct((rf * tile + NAME_ROWS, width), a_tiles.dtype),
        scratch_shapes=[pltpu.VMEM((NAME_ROWS, width), jnp.float32)],
        compiler_params=pltpu.CompilerParams(vmem_limit_bytes=56 * 1024 * 1024),
        cost_estimate=pl.CostEstimate(flops=1, bytes_accessed=1, transcendentals=0),
        name="with_numbers",
    )(a_tiles, route_list, out_slot, a_cols)


def partial_kernel(n_pieces, spans, cap, groups, table_of, rows_in, *refs):
    pieces, refs = refs[:n_pieces], refs[n_pieces:]
    outs, refs = refs[:len(spans)], refs[len(spans):]
    accs, (a_ref, lhs_ref, panel, y_buf, w_buf, *rest, sems) = refs[:ACCS], refs[ACCS:]
    packed_ref, place_vmem, idx_vmem, place_ref, idx_ref = rest
    tile = panel.shape[1]
    rf, tiles = a_ref.shape[0] // tile, a_ref.shape[1] // tile
    width = panel.shape[2] // tile
    sub = tile * tile // LANES
    n_tables = accs[0].shape[0] // cap
    chunk = 8

    n_places = width * tiles * width
    copies = [
        pltpu.make_async_copy(rows_in.at[pl.ds(rf * tile, NAME_ROWS)], packed_ref, sems.at[0]),
    ]
    for n in range(0, rf, PARTS):
        part = pl.ds(n * tile, PARTS * tile)
        copies.append(pltpu.make_async_copy(rows_in.at[part], a_ref.at[part], sems.at[len(copies)]))
    at = 0
    for piece in pieces:
        height = piece.shape[0]
        copies.append(pltpu.make_async_copy(piece, panel.at[pl.ds(at, height)], sems.at[len(copies)]))
        at += height
    for copy in copies:
        copy.start()
    copies.pop(0).wait()

    me, blk = lax.axis_index("grp"), lax.axis_index("blk")
    numbers = packed_ref[...].astype(jnp.float32).astype(jnp.int32)
    at_route, at_slot, at_high, at_low = number_columns(n_places)
    route = numbers[:rf, at_route:at_route + n_places]
    names = numbers[:1, at_slot:at_slot + n_places].astype(jnp.float32)
    owner = lax.shift_right_logical(route, jnp.int32(log2(cap)))
    table = table_of(owner ^ me, (me == 1) | (me == 2))
    place_vmem[...] = jnp.where(table < n_tables, table * cap + (route & (cap - 1)), n_tables * cap)
    cols = numbers[:rf, at_high:at_high + LANES] * PART + numbers[:rf, at_low:at_low + LANES]
    d = lax.shift_right_logical(cols, jnp.int32(log2(rf * groups))) ^ blk
    half = panel.shape[0] // (2 * rf)
    idx_vmem[...] = ((d & 1) * half + lax.shift_right_logical(d, jnp.int32(1))) * rf + (cols & (rf - 1))
    for n, (src, dst) in enumerate(((place_vmem, place_ref), (idx_vmem, idx_ref))):
        copy = pltpu.make_async_copy(src, dst, sems.at[sems.shape[0] - 2 + n])
        copy.start()
        copies.append(copy)

    def clear(c, carry):
        blocks = pl.ds(c * chunk, chunk)
        for acc in accs:
            acc[blocks] = jnp.zeros((chunk, sub, LANES), jnp.float32)
        return carry

    lax.fori_loop(0, n_tables * cap // chunk, clear, 0)
    for acc in accs:
        acc[n_tables * cap] = jnp.zeros((sub, LANES), jnp.float32)
    for copy in copies:
        copy.wait()

    columns = width * tile
    from_col = lax.broadcasted_iota(jnp.int32, (columns, columns), 0)
    to_col = lax.broadcasted_iota(jnp.int32, (columns, columns), 1)
    wanted = jnp.where(to_col < columns // 2, 2 * to_col, 2 * to_col - columns + 1)
    chosen = jnp.where(from_col == wanted, 1.0, 0.0).astype(jnp.bfloat16)
    for row in range(rf):
        split = jnp.dot(panel[row], chosen, preferred_element_type=jnp.float32)
        stacked = jnp.concatenate([split[:, :columns // 2], split[:, columns // 2:]], axis=0)
        lhs_ref[row] = jnp.transpose(stacked).astype(jnp.bfloat16)

    lane = lax.broadcasted_iota(jnp.int32, (tile, LANES), 1)
    lo = lane < tile

    def first_products(row, k):
        both = a_ref[pl.ds(pl.multiple_of(row * tile, tile), tile), k * tile:k * tile + LANES]
        none = jnp.zeros_like(both)
        left = jnp.concatenate([jnp.where(lo, both, none), jnp.where(lo, none, both)], axis=0)
        right = jnp.concatenate([panel[idx_ref[row, k]], panel[idx_ref[row, k + 1]]], axis=0)
        return jnp.dot(left, right, preferred_element_type=jnp.float32)

    def keep(u, y):
        for m in range(width // 2):
            x = y[:, m * LANES:(m + 1) * LANES]
            y_buf[u, :, 2 * m * LANES:(2 * m + 1) * LANES] = x.astype(jnp.bfloat16)
            y_buf[u, :, (2 * m + 1) * LANES:(2 * m + 2) * LANES] = pltpu.roll(x, tile, 1).astype(jnp.bfloat16)

    def second_product(row, u):
        lhs = lhs_ref[row]
        w = []
        for m in range(width // 2):
            x = y_buf[u, :, 2 * m * LANES:(2 * m + 1) * LANES]
            xr = y_buf[u, :, (2 * m + 1) * LANES:(2 * m + 2) * LANES]
            none = jnp.zeros_like(x)
            right = jnp.concatenate(
                [
                    jnp.concatenate([jnp.where(lo, x, none), jnp.where(lo, xr, none)], axis=1),
                    jnp.concatenate([jnp.where(lo, none, xr), jnp.where(lo, none, x)], axis=1),
                ],
                axis=0,
            )
            w.append(jnp.dot(lhs, right, preferred_element_type=jnp.float32))
        return w

    def add(row, k, w):
        for q in range(width):
            part = w[q // 2][:, q % 2 * LANES:(q % 2 + 1) * LANES]
            for s in range(0, width, ACCS):
                group = range(s, min(s + ACCS, width))
                places = [place_ref[row, (n * tiles + k) * width + q] for n in group]
                old = [acc[place] for acc, place in zip(accs, places)]
                for acc, place, was, n in zip(accs, places, old, group):
                    acc[place] = was + part[n * sub:(n + 1) * sub]

    def keep_two(u, y):
        keep(u, y[:tile])
        keep(u + 1, y[tile:])

    def hold(n, w):
        for m, part in enumerate(w):
            w_buf[n, :, m * 2 * LANES:(m + 1) * 2 * LANES] = part

    def held(n):
        return [w_buf[n, :, m * 2 * LANES:(m + 1) * 2 * LANES] for m in range(width // 2)]

    for k in range(0, tiles, 2):
        keep_two(k, first_products(0, k))
    for n in range(AHEAD):
        hold(n, second_product(0, n))

    def block_row(row, carry):
        following = jnp.minimum(row + 1, rf - 1)
        w = [held(n) for n in range(AHEAD)]
        for k in range(tiles):
            if k % 2 == 0:
                upcoming = first_products(following, k)
            ahead = k + AHEAD
            w.append(second_product(row, ahead) if ahead < tiles else second_product(following, ahead - tiles))
            add(row, k, w.pop(0))
            if k % 2 == 1:
                keep_two(k - 1, upcoming)
        for n in range(AHEAD):
            hold(n, w[n])
        return carry

    lax.fori_loop(0, rf, block_row, 0)

    named = jnp.zeros((NAME_ROWS, LANES), jnp.float32)
    here = lax.broadcasted_iota(jnp.int32, named.shape, 0)
    for n in range(groups * cap // LANES):
        part = names[:, n * LANES:(n + 1) * LANES]
        named = jnp.where(here == n, jnp.broadcast_to(part, named.shape), named)

    for (first, count), out in zip(spans, outs):

        def merge(c, carry):
            blocks = pl.ds(first + c * chunk, chunk)
            total = accs[0][blocks]
            for acc in accs[1:]:
                total = total + acc[blocks]
            rows = pl.ds(pl.multiple_of(c * (chunk * sub), chunk * sub), chunk * sub)
            out[rows, :] = total.reshape(chunk * sub, LANES).astype(out.dtype)
            return carry

        lax.fori_loop(0, count // chunk, merge, 0)
        out[count * sub:, :] = named.astype(out.dtype)


def partial_sums(rows_in, pieces, table_of, tables, spans, groups, cap):
    tile, cols = pieces[0].shape[1], rows_in.shape[1]
    rf = (rows_in.shape[0] - NAME_ROWS) // tile
    sub = tile * tile // LANES
    width = pieces[0].shape[2]
    rows = sum(x.shape[0] for x in pieces)
    n_places = (width // tile) ** 2 * (cols // tile)
    operands = [rows_in] + pieces
    panel_bytes = rows * tile * width * 2
    return pl.pallas_call(
        functools.partial(partial_kernel, len(pieces), spans, cap, groups, table_of),
        out_shape=[jax.ShapeDtypeStruct((n * sub + NAME_ROWS, LANES), jnp.bfloat16) for _, n in spans],
        grid_spec=pl.GridSpec(
            grid=(1,),
            in_specs=[pl.BlockSpec(memory_space=pl.ANY)] * len(operands),
            out_specs=[pl.BlockSpec((n * sub + NAME_ROWS, LANES), lambda i: (0, 0)) for _, n in spans],
            scratch_shapes=[pltpu.VMEM((tables * cap + 1, sub, LANES), jnp.float32)] * ACCS
            + [
                pltpu.VMEM((rf * tile, cols), jnp.bfloat16),
                pltpu.VMEM((rf, width // 2, 2 * tile), jnp.bfloat16),
                pltpu.VMEM((rows, tile, width), jnp.bfloat16),
                pltpu.VMEM((cols // tile, tile, 2 * width), jnp.bfloat16),
                pltpu.VMEM((AHEAD, width // 2, 2 * width), jnp.float32),
                pltpu.VMEM((NAME_ROWS, cols), jnp.bfloat16),
                pltpu.VMEM((rf, n_places), jnp.int32),
                pltpu.VMEM((rf, LANES), jnp.int32),
                pltpu.SMEM((rf, n_places), jnp.int32),
                pltpu.SMEM((rf, LANES), jnp.int32),
                pltpu.SemaphoreType.DMA((3 + rf // PARTS + len(pieces),)),
            ],
        ),
        compiler_params=pltpu.CompilerParams(
            dimension_semantics=("arbitrary",), vmem_limit_bytes=26 * 1024 * 1024 + panel_bytes
        ),
        cost_estimate=pl.CostEstimate(flops=1, bytes_accessed=1, transcendentals=0),
        name="partial_sums",
    )(*operands)


def early_kernel(*refs):
    tables, out_ref, accs, (vmem_names, smem_names, sem) = refs[:3], refs[3], refs[4:-3], refs[-3:]
    n_out, sub = out_ref.shape[:2]
    cap = (tables[0].shape[0] - NAME_ROWS) // sub
    chunk = 8
    at = lax.axis_index("grp") * cap
    row, lane = lax.div(at, jnp.int32(LANES)), lax.rem(at, jnp.int32(LANES))

    for n, x in enumerate(tables):
        vmem_names[n] = x[pl.ds(cap * sub, NAME_ROWS), :].astype(jnp.float32).astype(jnp.int32)
    copy = pltpu.make_async_copy(vmem_names, smem_names, sem)
    copy.start()

    def clear(c, carry):
        for acc in accs:
            acc[pl.ds(c * chunk, chunk)] = jnp.zeros((chunk, sub, LANES), jnp.float32)
        return carry

    lax.fori_loop(0, n_out // chunk, clear, 0)
    copy.wait()

    def add(c, carry):
        src = pl.ds(pl.multiple_of(c * sub, sub), sub)
        names = [smem_names[n, row, lane + c] for n in range(len(tables))]
        old = [acc[name] for acc, name in zip(accs, names)]
        for acc, name, was, x in zip(accs, names, old, tables):
            acc[name] = was + x[src, :].astype(jnp.float32)
        return carry

    lax.fori_loop(0, cap, add, 0, unroll=4)

    def merge(c, carry):
        blocks = pl.ds(c * chunk, chunk)
        total = accs[0][blocks]
        for acc in accs[1:]:
            total = total + acc[blocks]
        out_ref[blocks] = total
        return carry

    lax.fori_loop(0, n_out // chunk, merge, 0)


def last_kernel(table, from_b, from_c, out_ref, acc, late, rows_buf, vmem_names, smem_names, sems):
    n_out, sub = acc.shape[:2]
    cap = (late.shape[0] - NAME_ROWS) // sub
    me = lax.axis_index("grp")
    at = me * cap
    row, lane = lax.div(at, jnp.int32(LANES)), lax.rem(at, jnp.int32(LANES))
    parts = (sems.shape[0] - 2) // 3

    def late_copies(table_in):
        spans = [pl.ds(cap * sub, NAME_ROWS)]
        spans += [pl.ds(n * (cap // parts) * sub, cap // parts * sub) for n in range(parts)]
        return [
            pltpu.make_async_copy(table_in.at[span], late.at[span], sems.at[n]) for n, span in enumerate(spans)
        ]

    middle = (me == 1) | (me == 2)

    @pl.when(middle)
    def _():
        for copy in late_copies(from_b):
            copy.start()

    @pl.when(jnp.logical_not(middle))
    def _():
        for copy in late_copies(from_c):
            copy.start()

    height = n_out // parts
    blocks = [pl.ds(n * height, height) for n in range(parts)]
    fills = [
        pltpu.make_async_copy(table.at[span], acc.at[span], sems.at[1 + parts + n]) for n, span in enumerate(blocks)
    ]
    for copy in fills:
        copy.start()
    waiting = late_copies(from_b)
    waiting.pop(0).wait()
    vmem_names[...] = late[pl.ds(cap * sub, NAME_ROWS), :].astype(jnp.float32).astype(jnp.int32)
    copy = pltpu.make_async_copy(vmem_names, smem_names, sems.at[1 + 2 * parts])
    copy.start()
    for other in waiting + fills + [copy]:
        other.wait()

    def add(c, carry):
        acc[smem_names[row, lane + c]] += late[pl.ds(pl.multiple_of(c * sub, sub), sub), :].astype(jnp.float32)
        return carry

    lax.fori_loop(0, cap, add, 0, unroll=4)
    flat = acc.reshape(n_out * sub, LANES)

    def emit(c, carry):
        rows = pl.ds(pl.multiple_of(c * 8, 8), 8)
        for t in range(sub):
            rows_buf[rows, t * LANES:(t + 1) * LANES] = flat[pl.ds(c * (8 * sub) + t, 8, stride=sub), :]
        return carry

    copies = []
    for n, rows in enumerate(blocks):
        lax.fori_loop(n * height // 8, (n + 1) * height // 8, emit, 0)
        copies.append(pltpu.make_async_copy(rows_buf.at[rows], out_ref.at[rows], sems.at[2 + 2 * parts + n]))
        copies[-1].start()
    for copy in copies:
        copy.wait()


def owner_sums(tables, from_b, from_c, sub):
    def whole(x):
        return pl.BlockSpec(x.shape, lambda i: (0,) * len(x.shape))

    table = jax.ShapeDtypeStruct((OSLOT, sub, LANES), jnp.float32)
    names = (NAME_ROWS, LANES)
    early = pl.pallas_call(
        early_kernel,
        out_shape=table,
        grid_spec=pl.GridSpec(
            grid=(1,),
            in_specs=[whole(x) for x in tables],
            out_specs=whole(table),
            scratch_shapes=[pltpu.VMEM(table.shape, jnp.float32)] * len(tables)
            + [
                pltpu.VMEM((len(tables),) + names, jnp.int32),
                pltpu.SMEM((len(tables),) + names, jnp.int32),
                pltpu.SemaphoreType.DMA,
            ],
        ),
        compiler_params=pltpu.CompilerParams(
            dimension_semantics=("arbitrary",), vmem_limit_bytes=20 * 1024 * 1024
        ),
        name="early_sums",
    )(*tables)
    return pl.pallas_call(
        last_kernel,
        out_shape=jax.ShapeDtypeStruct((OSLOT, sub * LANES), jnp.float32),
        grid_spec=pl.GridSpec(
            grid=(1,),
            in_specs=[pl.BlockSpec(memory_space=pl.ANY)] * 3,
            out_specs=pl.BlockSpec(memory_space=pl.ANY),
            scratch_shapes=[
                pltpu.VMEM(table.shape, jnp.float32),
                pltpu.VMEM(from_b.shape, jnp.bfloat16),
                pltpu.VMEM((OSLOT, sub * LANES), jnp.float32),
                pltpu.VMEM(names, jnp.int32),
                pltpu.SMEM(names, jnp.int32),
                pltpu.SemaphoreType.DMA((2 + 3 * 4,)),
            ],
        ),
        compiler_params=pltpu.CompilerParams(
            dimension_semantics=("arbitrary",), vmem_limit_bytes=20 * 1024 * 1024
        ),
        name="owner_sums",
    )(early, from_b, from_c)


def swap(x, axis, d):
    return lax.ppermute(x, axis, [(i, i ^ d) for i in range(lax.axis_size(axis))])


def direct(p_tiles):
    return [swap(p_tiles, "blk", d) for d in range(2, lax.axis_size("blk"), 2)]


def body(a_tiles, a_cols, p_tiles, route_list, out_slot):
    groups = lax.axis_size("grp")
    rf, tile, cols = a_tiles.shape
    cap = out_slot.shape[1] // groups
    sub = tile * tile // LANES
    takes = [(1, 0), (3, 1), (0, 2), (2, 3)]

    def take(x):
        return lax.ppermute(x, "grp", takes)

    rows_sent = with_numbers(a_tiles, route_list, out_slot, a_cols)
    far = direct(p_tiles)
    p_took = take(p_tiles)
    a_took = take(rows_sent)
    far[0], p_took = lax.optimization_barrier((far[0], p_took))
    far_took = direct(p_took)
    mine = [p_tiles, jnp.concatenate(far)]
    other = [swap(x, "blk", 1) for x in mine]

    def tables_own(off, middle):
        return jnp.where(middle, jnp.where(off == 0, 0, jnp.where(off == 1, 3, off - 1)), jnp.where(off < 2, off, 3))

    def tables_took(off, middle):
        return jnp.where((off == 0) | ((off == 1) & middle), off, 2)

    spans = ((0, cap), (cap, cap), (2 * cap, cap))
    own, to_a, to_b = partial_sums(rows_sent, mine + other, tables_own, 3, spans, groups, cap)
    own, p_took, *far_took = lax.optimization_barrier((own, p_took, *far_took))
    to_a, to_b, a_took = lax.optimization_barrier((to_a, to_b, a_took))
    from_a = lax.ppermute(to_a, "grp", [(0, 1), (3, 2), (1, 3), (2, 0)])
    from_b = lax.ppermute(to_b, "grp", [(1, 2), (2, 1)])
    took = [p_took] + far_took
    pieces = took + [swap(x, "blk", 1) for x in took]
    spans = ((0, cap), (cap, cap))
    own_took, to_c = partial_sums(a_took, pieces, tables_took, 2, spans, groups, cap)
    from_c = lax.ppermute(to_c, "grp", [(1, 0), (2, 3)])
    return owner_sums([own, own_took, from_a], from_b, from_c, sub)


def solution(mesh):
    in_specs = (
        P(("blk", "grp"), None, None),
        P(("blk", "grp"), None),
        P(("blk", "grp"), None, None),
        P(("blk", "grp"), None),
        P(("blk", "grp"), None),
    )
    out_specs = P(("blk", "grp"), None)
    return jax.shard_map(body, mesh=mesh, in_specs=in_specs, out_specs=out_specs, check_vma=False)
```
